32 devices in a mesh: groups: 2 (over y), ctx: 4 (over z), dp: 4 (over x, core).
Axes of the slice: x: 2, y: 2, z: 4, core: 2. Of those that a mesh axis runs over, the one named last changes fastest.
Arguments:
- queries: bfloat16 [8, 512, 1024], P(('groups', 'dp'), 'ctx'), parts along dimension 0, may hold values from -6 to 6
- key_rows: bfloat16 [8, 512, 1024], P(('groups', 'dp'), 'ctx'), parts along dimension 0, may hold values from -6 to 6
- value_rows: bfloat16 [8, 512, 1024], P(('groups', 'dp'), 'ctx'), parts along dimension 0, may hold values from -6 to 6
- update_gate: bfloat16 [8, 512, 1024], P(('groups', 'dp'), 'ctx'), parts along dimension 0, may hold values from -6 to 6
- out_grad: bfloat16 [8, 512, 1024], P(('groups', 'dp'), 'ctx'), parts along dimension 0, may hold values from -6 to 6
- user_lengths: int32 [8, 4], P(('groups', 'dp')), parts along dimension 0, may hold values from 1 to 256, 512 in all within a row
- rel_bias: float32 [8, 8], replicated, may hold values from -1 to 1
- norm_gain: float32 [1024], replicated, may hold values from 0.5 to 1.5
Outputs:
- query_grad: bfloat16 [8, 512, 1024], P(('groups', 'dp'), 'ctx'), parts along dimension 0
- key_grad: bfloat16 [8, 512, 1024], P(('groups', 'dp'), 'ctx'), parts along dimension 0
- value_grad: bfloat16 [8, 512, 1024], P(('groups', 'dp'), 'ctx'), parts along dimension 0
- gate_grad: bfloat16 [8, 512, 1024], P(('groups', 'dp'), 'ctx'), parts along dimension 0
- bias_grad: float32 [16, 8], P('groups'), parts along dimension 0
- gain_grad: float32 [2048], P('groups'), parts along dimension 0
The draws below stay inside these ranges and needn't reach their ends.
There are 2 independent parts, one for each index of `groups`. The reference program is written for one: setup_inputs(seed, part) draws one part's arguments, and reference() takes and returns one part's arrays. A program takes and returns all parts, laid end to end along the dimension named above; an argument that names none is the same for every part. Nothing has to cross between parts.
Inputs may be any that keep to these rules, and one draw needn't show every extreme that they name: `user_lengths`: each row lists the event counts of the 4 users packed one after another into a sequence; a row sums to 512 and its largest entry is exactly 256.
All inputs are finite; a program needn't handle non-finite values.
Results may differ from the reference program's by a relative error of at most 0.0058.
Values may be sent and summed in bfloat16 or wider, within the bound.
No kernel may reach another device: no remote copies, remote signals or barrier semaphores. Data moves between devices by JAX's collectives and lax.ppermute only.
A program may use at most 64 MiB of HBM per device.

```python
import math
import jax
import jax.numpy as jnp
import numpy as np
from jax import lax

HEADS = 8
HEAD_DIM = 128
D = 1024
BUCKETS = 8
TOK_DEV = 128
SPAN = 2
MAX_LEN = 256
SEQ_LEN = 512
USERS = 4
SEQS = 4
N_CTX = 4


def steps_of(key, dims, shards, low, top_value):
    level, own = 1.0, jax.random.fold_in(key, 6)
    for dim, shards_of in shards:
        draws = jnp.exp(jax.random.uniform(jax.random.fold_in(own, dim), (shards_of,), jnp.float32, low / len(shards), top_value / len(shards)))
        level = level * jnp.repeat(draws, dims[dim] // shards_of).reshape([-1 if axis == dim else 1 for axis in range(len(dims))])
    return level


def length_profile(count, total, bound, lean):
    portions = [(1 << 20) // math.isqrt(rank ** lean) + 1 for rank in range(2, count + 1)]
    surplus, holding = total - bound - (count - 1), [1] * (count - 1)
    while surplus > 0:
        free = [i for i in range(count - 1) if holding[i] < bound]
        pool, left = sum([portions[i] for i in free]), surplus
        for i in free:
            extra = min(bound - holding[i], max(1, left * portions[i] // pool), surplus)
            holding[i] = holding[i] + extra
            surplus = surplus - extra
    return np.array([bound] + holding)


def ragged_sizes(stream_key, count, total, limit, lean):
    if count == 2:
        one = jax.random.randint(stream_key, (), max(1, total - limit), min(limit, total - 1) + 1)
        return jnp.stack([one, total - one])
    tallies = jnp.asarray(length_profile(count, total, limit, lean), jnp.int32)
    couples = (count - 1) // 2
    donor, taker = tallies[1:1 + 2 * couples:2], tallies[2:2 + 2 * couples:2]
    room = jnp.minimum(donor - 1, limit - taker)
    shifted = jax.random.randint(jax.random.fold_in(stream_key, 1), (couples,), 0, 1 << 20) % (room + 1)
    tallies = tallies.at[1:1 + 2 * couples:2].set(donor - shifted).at[2:2 + 2 * couples:2].set(taker + shifted)
    return tallies[jax.random.permutation(jax.random.fold_in(stream_key, 2), count)]


def noise(key, shape, width, bound, pieces=(), kind=jnp.bfloat16):
    gain = steps_of(key, shape, pieces, -0.22, 0.18) if pieces else 1.0
    entries = jax.random.normal(key, shape, jnp.float32) * width * gain
    return jnp.minimum(jnp.maximum(entries, -bound), bound).astype(kind)


def setup_inputs(seed: int = 0, part: int = 0) -> dict:
    splits = jax.random.split(jax.random.key(seed), 9)
    own_keys = jax.random.split(jax.random.fold_in(splits[8], part), 9)
    queries = noise(own_keys[0], (SEQS, SEQ_LEN, D), 1.0, 6.0, ((0, 4), (1, 4)))
    key_rows = noise(own_keys[1], (SEQS, SEQ_LEN, D), 1.0, 6.0, ((0, 4), (1, 4)))
    value_rows = noise(own_keys[2], (SEQS, SEQ_LEN, D), 1.0, 6.0, ((0, 4), (1, 4)))
    update_gate = noise(own_keys[3], (SEQS, SEQ_LEN, D), 1.0, 6.0, ((0, 4), (1, 4)))
    out_grad = noise(own_keys[4], (SEQS, SEQ_LEN, D), 1.0, 6.0, ((0, 4), (1, 4)))
    user_lengths = jax.vmap(lambda own: ragged_sizes(own, USERS, SEQ_LEN, MAX_LEN, 2))(jax.random.split(own_keys[5], SEQS)).reshape((SEQS, USERS)).astype(jnp.int32)
    rel_bias = jnp.clip(jax.random.uniform(splits[6], (BUCKETS, HEADS), jnp.float32, -1.0, 1.0), -1.0, 1.0)
    norm_gain = jnp.clip(1.0 + 0.1 * jax.random.normal(splits[7], (D,), jnp.float32), 0.5, 1.5)
    return dict(queries=queries, key_rows=key_rows, value_rows=value_rows, update_gate=update_gate, out_grad=out_grad, user_lengths=user_lengths, rel_bias=rel_bias, norm_gain=norm_gain)


EPSILON = 1e-05

def segment_of(positions, user_ends):
    return lax.optimization_barrier(jnp.sum((positions[:, None] >= user_ends[None, :]).astype(jnp.int32), axis=1))

def pair_mask(query_pos, key_pos, user_ends, seq_total, level_count):
    distance = query_pos[:, None] - key_pos[None, :]
    same_user = segment_of(query_pos, user_ends)[:, None] == segment_of(key_pos, user_ends)[None, :]
    inside = (key_pos[None, :] >= 0) & (query_pos[:, None] < seq_total)
    visible = (distance >= 0) & same_user & inside
    bucket = jnp.zeros(distance.shape, jnp.int32)
    for level in range(level_count - 1):
        bucket = bucket + (distance >= 2 ** level).astype(jnp.int32)
    return (visible, bucket)

def bias_values(bucket, rel_bias):
    total = jnp.zeros((rel_bias.shape[1],) + bucket.shape, jnp.float32)
    for level in range(rel_bias.shape[0]):
        total = jnp.where(bucket[None] == level, rel_bias[level][:, None, None], total)
    return total

def bias_sums(bucket, grads, level_count):
    return jnp.stack([lax.optimization_barrier(jnp.sum(jnp.where(bucket[None] == level, grads, 0.0), axis=(1, 2))) for level in range(level_count)])

def silu_slope(logits):
    sigma = jax.nn.sigmoid(logits)
    return sigma * (1.0 + logits * (1.0 - sigma))

def rounded(values):
    return lax.optimization_barrier(values.astype(jnp.bfloat16)).astype(jnp.float32)

def scores_of(query_blk, key_blk, bias):
    scaling = HEAD_DIM ** (-0.5)
    return jnp.einsum('qhd,khd->hqk', query_blk.astype(jnp.float32), key_blk.astype(jnp.float32)) * scaling + bias

def one_sequence(queries, key_rows, value_rows, update_gate, out_grad, lengths, rel_bias, norm_gain):
    row_count = TOK_DEV
    window = SPAN * row_count
    scaling = HEAD_DIM ** (-0.5)
    user_ends = jnp.cumsum(lengths).astype(jnp.int32)
    shape3 = (SEQ_LEN, HEADS, HEAD_DIM)
    query3 = queries.reshape(shape3)
    key3 = key_rows.reshape(shape3)
    value3 = value_rows.reshape(shape3)
    blank = jnp.zeros((window, HEADS, HEAD_DIM), jnp.bfloat16)
    key_front = jnp.concatenate([blank, key3], axis=0)
    value_front = jnp.concatenate([blank, value3], axis=0)
    starts = jnp.arange(N_CTX, dtype=jnp.int32) * row_count
    row_index = jnp.arange(row_count, dtype=jnp.int32)
    wide_index = jnp.arange(window + row_count, dtype=jnp.int32)

    def forward_block(start):
        query_blk = lax.dynamic_slice_in_dim(query3, start, row_count, 0)
        key_blk = lax.dynamic_slice_in_dim(key_front, start, window + row_count, 0)
        value_blk = lax.dynamic_slice_in_dim(value_front, start, window + row_count, 0)
        visible, bucket = pair_mask(start + row_index, start - window + wide_index, user_ends, SEQ_LEN, BUCKETS)
        logits = scores_of(query_blk, key_blk, bias_values(bucket, rel_bias))
        weights = rounded(jnp.where(visible[None], jax.nn.silu(logits), 0.0))
        return jnp.einsum('hqk,khd->qhd', weights, value_blk.astype(jnp.float32))
    attention = lax.map(forward_block, starts).reshape(SEQ_LEN, D)
    center = attention - lax.optimization_barrier(jnp.mean(attention, axis=1, keepdims=True))
    inverse = lax.rsqrt(lax.optimization_barrier(jnp.mean(center * center, axis=1, keepdims=True)) + EPSILON)
    normed = center * inverse
    grad_f = out_grad.astype(jnp.float32)
    gate_f = update_gate.astype(jnp.float32)
    gate_grad = (grad_f * normed * norm_gain).astype(jnp.bfloat16)
    gain_part = lax.optimization_barrier(jnp.sum(grad_f * gate_f * normed, axis=0))
    pushed = grad_f * gate_f * norm_gain
    attn_grad = inverse * (pushed - lax.optimization_barrier(jnp.mean(pushed, axis=1, keepdims=True)) - normed * lax.optimization_barrier(jnp.mean(pushed * normed, axis=1, keepdims=True)))
    grad3 = lax.optimization_barrier(attn_grad.astype(jnp.bfloat16)).reshape(shape3)

    def query_block_grads(start):
        query_blk = lax.dynamic_slice_in_dim(query3, start, row_count, 0)
        grad_blk = lax.dynamic_slice_in_dim(grad3, start, row_count, 0)
        key_blk = lax.dynamic_slice_in_dim(key_front, start, window + row_count, 0)
        value_blk = lax.dynamic_slice_in_dim(value_front, start, window + row_count, 0)
        visible, bucket = pair_mask(start + row_index, start - window + wide_index, user_ends, SEQ_LEN, BUCKETS)
        logits = scores_of(query_blk, key_blk, bias_values(bucket, rel_bias))
        weight_grad = jnp.einsum('qhd,khd->hqk', grad_blk.astype(jnp.float32), value_blk.astype(jnp.float32))
        logit_grad = jnp.where(visible[None], weight_grad * silu_slope(logits), 0.0)
        query_part = jnp.einsum('hqk,khd->qhd', rounded(logit_grad), key_blk.astype(jnp.float32))
        return (query_part, bias_sums(bucket, logit_grad, BUCKETS))
    query_parts, bias_parts = lax.map(query_block_grads, starts)
    query_grad = (query_parts.reshape(SEQ_LEN, D) * scaling).astype(jnp.bfloat16)
    query_back = jnp.concatenate([query3, blank], axis=0)
    grad_back = jnp.concatenate([grad3, blank], axis=0)

    def key_block_grads(start):
        key_blk = lax.dynamic_slice_in_dim(key3, start, row_count, 0)
        value_blk = lax.dynamic_slice_in_dim(value3, start, row_count, 0)
        query_blk = lax.dynamic_slice_in_dim(query_back, start, window + row_count, 0)
        grad_blk = lax.dynamic_slice_in_dim(grad_back, start, window + row_count, 0)
        visible, bucket = pair_mask(start + wide_index, start + row_index, user_ends, SEQ_LEN, BUCKETS)
        logits = scores_of(query_blk, key_blk, bias_values(bucket, rel_bias))
        weights = rounded(jnp.where(visible[None], jax.nn.silu(logits), 0.0))
        weight_grad = jnp.einsum('qhd,khd->hqk', grad_blk.astype(jnp.float32), value_blk.astype(jnp.float32))
        logit_grad = rounded(jnp.where(visible[None], weight_grad * silu_slope(logits), 0.0))
        key_part = jnp.einsum('hqk,qhd->khd', logit_grad, query_blk.astype(jnp.float32))
        value_part = jnp.einsum('hqk,qhd->khd', weights, grad_blk.astype(jnp.float32))
        return (key_part, value_part)
    key_parts, value_parts = lax.map(key_block_grads, starts)
    key_grad = (key_parts.reshape(SEQ_LEN, D) * scaling).astype(jnp.bfloat16)
    value_grad = value_parts.reshape(SEQ_LEN, D).astype(jnp.bfloat16)
    return (query_grad, key_grad, value_grad, gate_grad, lax.optimization_barrier(jnp.sum(bias_parts, axis=0)), gain_part)

def reference(queries, key_rows, value_rows, update_gate, out_grad, user_lengths, rel_bias, norm_gain):

    def per_sequence(items):
        return one_sequence(items[0], items[1], items[2], items[3], items[4], items[5], rel_bias, norm_gain)
    results = lax.map(per_sequence, (queries, key_rows, value_rows, update_gate, out_grad, user_lengths))
    return (results[0], results[1], results[2], results[3], lax.optimization_barrier(jnp.sum(results[4], axis=0)), lax.optimization_barrier(jnp.sum(results[5], axis=0)))
```

```python
from functools import partial

import jax
import jax.numpy as jnp
from jax import lax
from jax.experimental import pallas as pl
from jax.experimental.pallas import tpu as pltpu
from jax.sharding import PartitionSpec as P

EPSILON = 1e-05
VMEM_LIMIT = 24 * 1024 * 1024
F32 = jnp.float32
BF16 = jnp.bfloat16


def passed_along(array, axis, by):
    size = lax.axis_size(axis)
    pairs = [(i, i + by) for i in range(size) if 0 <= i + by < size]
    return lax.ppermute(array, axis, pairs)


def contract(left, right, left_dim, right_dim):
    return lax.dot_general(
        left, right, (((left_dim,), (right_dim,)), ((), ())), preferred_element_type=F32
    )


class Pair:
    def __init__(self, lengths, bias, query_block, hops, rows, flipped):
        self.bias = bias
        self.levels, self.heads = bias.shape
        shape = (rows, rows)
        query_dim, key_dim = (1, 0) if flipped else (0, 1)
        first = (lax.axis_index("ctx") + query_block) * rows
        line = (1, rows) if flipped else (rows, 1)
        query_pos = first + lax.broadcasted_iota(jnp.int32, line, query_dim)
        end = jnp.int32(0)
        start = jnp.zeros(line, jnp.int32)
        for user in range(lengths.shape[1]):
            end = end + lengths[0, user]
            start = jnp.where(query_pos >= end, end, start)
        key_pos = first - hops * rows + lax.broadcasted_iota(jnp.int32, shape, key_dim)
        seen = key_pos >= start
        if hops == 0:
            seen = seen & (key_pos <= query_pos)
        self.mask = jnp.where(seen, 1.0, 0.0).astype(F32)
        self.far = (hops - 1) * rows + 1 >= 2 ** (self.levels - 2)
        self.distance = None if self.far else query_pos - key_pos

    def half_bias(self, head):
        value = 0.5 * self.bias[self.levels - 1, head]
        if self.far:
            return value
        for level in range(self.levels - 2, -1, -1):
            value = jnp.where(self.distance < 2**level, 0.5 * self.bias[level, head], value)
        return value

    def half_logits(self, scores, head, scaling):
        return scores * (0.5 * scaling) + self.half_bias(head)

    def bias_rows(self, grads):
        sub = lax.broadcasted_iota(jnp.int32, (self.levels, grads.shape[1]), 0)
        if self.far:
            row = jnp.sum(grads, axis=0, keepdims=True)
            return jnp.where(sub == self.levels - 1, row, 0.0)
        total = jnp.zeros(sub.shape, F32)
        for level in range(self.levels):
            inside = None
            if level > 0:
                inside = self.distance >= 2 ** (level - 1)
            if level < self.levels - 1:
                below = self.distance < 2**level
                inside = below if inside is None else inside & below
            row = jnp.sum(jnp.where(inside, grads, 0.0), axis=0, keepdims=True)
            total = jnp.where(sub == level, row, total)
        return total


def weights_of(half, mask):
    return ((half + half * jnp.tanh(half)) * mask).astype(BF16)


def slope_of(half, tanh):
    return (0.5 + 0.5 * tanh) * (1.0 + half * (1.0 - tanh))


def columns(head, width):
    return slice(head * width, (head + 1) * width)


def forward_kernel(hop_list, query_block, scaling, lengths, bias, *refs):
    count = len(hop_list)
    query, keys, values = refs[0], refs[1 : 1 + count], refs[1 + count : 1 + 2 * count]
    total = refs[1 + 2 * count] if len(refs) > 2 + 2 * count else None
    out = refs[-1]
    rows = query.shape[0]
    heads = bias.shape[1]
    width = query.shape[1] // heads
    pairs = [Pair(lengths, bias, query_block, hops, rows, False) for hops in hop_list]
    for head in range(heads):
        cols = columns(head, width)
        part = None if total is None else total[:, cols]
        for pair, key, value in zip(pairs, keys, values):
            half = pair.half_logits(contract(query[:, cols], key[:, cols], 1, 1), head, scaling)
            added = contract(weights_of(half, pair.mask), value[:, cols], 1, 0)
            part = added if part is None else part + added
        out[:, cols] = part.astype(out.dtype)


def norm_kernel(total, far_part, out_grad, update_gate, gain, attn_grad, gate_grad, gain_grad):
    rows, features = total.shape
    step = 16
    gain_row = gain[...]
    gain_sum = jnp.zeros((8, features), F32)
    for low in range(0, rows, step):
        span = slice(low, low + step)
        attention = total[span, :] + far_part[span, :].astype(F32)
        center = attention - jnp.mean(attention, axis=1, keepdims=True)
        inverse = lax.rsqrt(jnp.mean(center * center, axis=1, keepdims=True) + EPSILON)
        normed = center * inverse
        grad_f = out_grad[span, :].astype(F32)
        gate_grad[span, :] = (grad_f * normed * gain_row).astype(BF16)
        gated = grad_f * update_gate[span, :].astype(F32)
        product = gated * normed
        for part in range(0, step, 8):
            gain_sum = gain_sum + product[part : part + 8, :]
        pushed = gated * gain_row
        attn_grad[span, :] = (
            inverse
            * (
                pushed
                - jnp.mean(pushed, axis=1, keepdims=True)
                - normed * jnp.mean(pushed * normed, axis=1, keepdims=True)
            )
        ).astype(BF16)
    gain_grad[...] = jnp.sum(gain_sum, axis=0, keepdims=True)


def backward_own_kernel(hop_list, scaling, lengths, bias, *refs):
    count = len(hop_list)
    query, grad = refs[:2]
    keys, values = refs[2 : 2 + count], refs[2 + count : 2 + 2 * count]
    query_out, key_out, value_out, bias_out = refs[2 + 2 * count :]
    rows = query.shape[0]
    heads = bias.shape[1]
    width = query.shape[1] // heads
    pairs = [Pair(lengths, bias, 0, hops, rows, hops == 0) for hops in hop_list]
    lane = lax.broadcasted_iota(jnp.int32, bias_out.shape, 1)
    bias_total = jnp.zeros(bias_out.shape, F32)
    for head in range(heads):
        cols = columns(head, width)
        query_h, grad_h = query[:, cols], grad[:, cols]
        query_part = None
        bias_part = None
        for pair, hops, key, value in zip(pairs, hop_list, keys, values):
            key_h, value_h = key[:, cols], value[:, cols]
            if hops == 0:
                half = pair.half_logits(contract(key_h, query_h, 1, 1), head, scaling)
                weight_grad = contract(value_h, grad_h, 1, 1)
            else:
                half = pair.half_logits(contract(query_h, key_h, 1, 1), head, scaling)
                weight_grad = contract(grad_h, value_h, 1, 1)
            tanh = jnp.tanh(half)
            logit_grad = weight_grad * (slope_of(half, tanh) * pair.mask)
            rounded = logit_grad.astype(BF16)
            if hops == 0:
                weights = ((half + half * tanh) * pair.mask).astype(BF16)
                key_out[:, cols] = contract(rounded, query_h, 1, 0)
                value_out[:, cols] = contract(weights, grad_h, 1, 0)
                added = contract(rounded, key_h, 0, 0)
            else:
                added = contract(rounded, key_h, 1, 0)
            query_part = added if query_part is None else query_part + added
            sums = pair.bias_rows(logit_grad)
            bias_part = sums if bias_part is None else bias_part + sums
        query_out[:, cols] = query_part
        bias_total = jnp.where(lane == head, jnp.sum(bias_part, axis=1, keepdims=True), bias_total)
    bias_out[...] = bias_total


def backward_far_kernel(hops, scaling, lengths, bias, *refs):
    query, grad, key, value, bias_in, gain_in, query_out, small_out = refs
    rows = query.shape[0]
    levels, heads = bias.shape
    width = query.shape[1] // heads
    pair = Pair(lengths, bias, 1, hops, rows, False)
    lane = lax.broadcasted_iota(jnp.int32, bias_in.shape, 1)
    bias_total = bias_in[...]
    for head in range(heads):
        cols = columns(head, width)
        key_h = key[:, cols]
        half = pair.half_logits(contract(query[:, cols], key_h, 1, 1), head, scaling)
        weight_grad = contract(grad[:, cols], value[:, cols], 1, 1)
        logit_grad = weight_grad * (slope_of(half, jnp.tanh(half)) * pair.mask)
        query_out[:, cols] = contract(logit_grad.astype(BF16), key_h, 1, 0).astype(BF16)
        sums = jnp.sum(pair.bias_rows(logit_grad), axis=1, keepdims=True)
        bias_total = bias_total + jnp.where(lane == head, sums, 0.0)
    lanes = small_out.shape[1]
    lines = gain_in.shape[1] // lanes
    for line in range(lines):
        small_out[line : line + 1, :] = gain_in[:, line * lanes : (line + 1) * lanes]
    small_out[lines:, :] = bias_total


def backward_key_kernel(hops, scaling, lengths, bias, *refs):
    query, grad, key, value, key_in, value_in, key_out, value_out = refs
    last = key_out.dtype == BF16
    rows = query.shape[0]
    heads = bias.shape[1]
    width = query.shape[1] // heads
    pair = Pair(lengths, bias, hops, hops, rows, True)
    for head in range(heads):
        cols = columns(head, width)
        query_h, grad_h = query[:, cols], grad[:, cols]
        half = pair.half_logits(contract(key[:, cols], query_h, 1, 1), head, scaling)
        weight_grad = contract(value[:, cols], grad_h, 1, 1)
        tanh = jnp.tanh(half)
        rounded = (weight_grad * (slope_of(half, tanh) * pair.mask)).astype(BF16)
        weights = ((half + half * tanh) * pair.mask).astype(BF16)
        key_part = key_in[:, cols] + contract(rounded, query_h, 1, 0)
        value_part = value_in[:, cols] + contract(weights, grad_h, 1, 0)
        if last:
            key_part = key_part * scaling
        key_out[:, cols] = key_part.astype(key_out.dtype)
        value_out[:, cols] = value_part.astype(value_out.dtype)


def on_device(kernel, outs, smem, vmem, flops):
    moved = sum(array.size * array.dtype.itemsize for array in (*vmem, *outs))
    return pl.pallas_call(
        kernel,
        out_shape=outs,
        in_specs=[pl.BlockSpec(memory_space=pltpu.SMEM)] * len(smem)
        + [pl.BlockSpec(memory_space=pltpu.VMEM)] * len(vmem),
        out_specs=[pl.BlockSpec(memory_space=pltpu.VMEM)] * len(outs),
        compiler_params=pltpu.CompilerParams(vmem_limit_bytes=VMEM_LIMIT),
        cost_estimate=pl.CostEstimate(flops=flops, bytes_accessed=moved, transcendentals=0),
    )(*smem, *vmem)


def summed_over(array, axes):
    for axis in axes:
        size = lax.axis_size(axis)
        step = 1
        while step < size:
            array = array + lax.ppermute(array, axis, [(i, i ^ step) for i in range(size)])
            step = 2 * step
    return array


def local(queries, key_rows, value_rows, update_gate, out_grad, user_lengths, rel_bias, norm_gain):
    rows, features = queries.shape[1:]
    levels, heads = rel_bias.shape
    scaling = (features // heads) ** (-0.5)
    query, key, value = queries[0], key_rows[0], value_rows[0]
    reach = min(3, lax.axis_size("ctx") // 2)
    smem = (user_lengths, rel_bias)
    unit = 2 * rows * rows * features
    wide = jax.ShapeDtypeStruct((rows, features), F32)
    narrow = jax.ShapeDtypeStruct((rows, features), BF16)

    keys, values = [key], [value]
    for _ in range(reach - 1):
        keys.append(passed_along(keys[-1], "ctx", 1))
        values.append(passed_along(values[-1], "ctx", 1))
    later_queries = [query] + [passed_along(query, "ctx", -hops) for hops in range(1, reach + 1)]

    (attention,) = on_device(
        partial(forward_kernel, (0,), 0, scaling), [wide], smem, (query, key, value), 2 * unit
    )
    (far_part,) = on_device(
        partial(forward_kernel, (reach,), 1, scaling),
        [narrow],
        smem,
        (later_queries[1], keys[reach - 1], values[reach - 1]),
        2 * unit,
    )
    far_part = passed_along(far_part, "ctx", 1)
    near = tuple(range(1, reach))
    if near:
        (attention,) = on_device(
            partial(forward_kernel, near, 0, scaling),
            [wide],
            smem,
            (query, *keys[1:], *values[1:], attention),
            2 * len(near) * unit,
        )
    attn_grad, gate_grad, gain_part = on_device(
        norm_kernel,
        [narrow, narrow, jax.ShapeDtypeStruct((1, features), F32)],
        (),
        (attention, far_part, out_grad[0], update_gate[0], norm_gain[None]),
        20 * rows * features,
    )
    later_grads = [attn_grad]
    for _ in range(reach):
        later_grads.append(passed_along(later_grads[-1], "ctx", -1))

    lanes = features // 8
    small = jax.ShapeDtypeStruct((levels, lanes), F32)
    query_total, key_total, value_total, bias_part = on_device(
        partial(backward_own_kernel, (0, *near), scaling),
        [wide, wide, wide, small],
        smem,
        (query, attn_grad, *keys, *values),
        (5 + 3 * len(near)) * unit,
    )
    query_part, sums = on_device(
        partial(backward_far_kernel, reach, scaling),
        [narrow, jax.ShapeDtypeStruct((8 + levels, lanes), F32)],
        smem,
        (later_queries[1], later_grads[1], keys[-1], values[-1], bias_part, gain_part),
        3 * unit,
    )
    query_part = passed_along(query_part, "ctx", 1)
    sums = summed_over(sums, ("dp", "ctx"))
    for hops in range(1, reach + 1):
        key_total, value_total = on_device(
            partial(backward_key_kernel, hops, scaling),
            [narrow if hops == reach else wide] * 2,
            smem,
            (later_queries[hops], later_grads[hops], key, value, key_total, value_total),
            4 * unit,
        )
    query_grad = ((query_total + query_part.astype(F32)) * scaling).astype(BF16)
    return (
        query_grad[None],
        key_total[None],
        value_total[None],
        gate_grad[None],
        sums[8:, :heads],
        sums[:8].reshape(features),
    )


def solution(mesh):
    in_specs = (
        P(("groups", "dp"), "ctx", None),
        P(("groups", "dp"), "ctx", None),
        P(("groups", "dp"), "ctx", None),
        P(("groups", "dp"), "ctx", None),
        P(("groups", "dp"), "ctx", None),
        P(("groups", "dp"), None),
        P(),
        P(),
    )
    out_specs = (
        P(("groups", "dp"), "ctx", None),
        P(("groups", "dp"), "ctx", None),
        P(("groups", "dp"), "ctx", None),
        P(("groups", "dp"), "ctx", None),
        P("groups", None),
        P("groups"),
    )
    return jax.shard_map(local, mesh=mesh, in_specs=in_specs, out_specs=out_specs, check_vma=False)
```

```python
from functools import partial

import jax
import jax.numpy as jnp
from jax import lax
from jax.experimental import pallas as pl
from jax.experimental.pallas import tpu as pltpu
from jax.sharding import PartitionSpec as P

EPSILON = 1e-05
VMEM_LIMIT = 24 * 1024 * 1024
F32 = jnp.float32
BF16 = jnp.bfloat16


def passed_along(array, axis, by):
    size = lax.axis_size(axis)
    pairs = [(i, i + by) for i in range(size) if 0 <= i + by < size]
    return lax.ppermute(array, axis, pairs)


def contract(left, right, left_dim, right_dim):
    return lax.dot_general(
        left, right, (((left_dim,), (right_dim,)), ((), ())), preferred_element_type=F32
    )


def user_starts(lengths, query_pos):
    end = jnp.int32(0)
    start = jnp.zeros(query_pos.shape, jnp.int32)
    for user in range(lengths.shape[1]):
        end = end + lengths[0, user]
        start = jnp.where(query_pos >= end, end, start)
    return start


class Pair:
    def __init__(self, mask, table, heads, hops, flipped=False):
        rows = mask.shape[0]
        self.table, self.heads, self.levels = table, heads, table.shape[0] // heads
        self.mask = mask[...]
        self.far = (hops - 1) * rows + 1 >= 2 ** (self.levels - 2)
        if not self.far:
            query_dim, key_dim = (1, 0) if flipped else (0, 1)
            query_row = lax.broadcasted_iota(jnp.int32, mask.shape, query_dim)
            key_row = lax.broadcasted_iota(jnp.int32, mask.shape, key_dim)
            self.distance = query_row - key_row + hops * rows

    def half_logits(self, scores, head, scaling):
        def level_row(level):
            at = level * self.heads + head
            return self.table[at : at + 1, :]

        value = level_row(self.levels - 1)
        if not self.far:
            for level in range(self.levels - 2, -1, -1):
                value = jnp.where(self.distance < 2**level, level_row(level), value)
        return scores * (0.5 * scaling) + value

    def bias_rows(self, grads):
        sub = lax.broadcasted_iota(jnp.int32, (self.levels, grads.shape[1]), 0)
        if self.far:
            row = jnp.sum(grads, axis=0, keepdims=True)
            return jnp.where(sub == self.levels - 1, row, 0.0)
        total = jnp.zeros(sub.shape, F32)
        for level in range(self.levels):
            inside = None
            if level > 0:
                inside = self.distance >= 2 ** (level - 1)
            if level < self.levels - 1:
                below = self.distance < 2**level
                inside = below if inside is None else inside & below
            row = jnp.sum(jnp.where(inside, grads, 0.0), axis=0, keepdims=True)
            total = jnp.where(sub == level, row, total)
        return total


def slope_of(half, tanh):
    return (0.5 + 0.5 * tanh) * (1.0 + half * (1.0 - tanh))


def columns(head, width):
    return slice(head * width, (head + 1) * width)


def in_stages(count, first, second, ahead=3):
    held = [first(i) for i in range(min(ahead, count))]
    for i in range(count):
        if i + ahead < count:
            held.append(first(i + ahead))
        second(i, held.pop(0))


def mask_kernel(plan, lengths, bias, table, *masks):
    levels, heads = bias.shape
    for level in range(levels):
        for head in range(heads):
            at = level * heads + head
            table[at : at + 1, :] = jnp.full((1, table.shape[1]), 0.5 * bias[level, head], F32)
    for (block, hops, flipped), mask in zip(plan, masks):
        rows = mask.shape[0]
        query_dim, key_dim = (1, 0) if flipped else (0, 1)
        line = (1, rows) if flipped else (rows, 1)
        first = (lax.axis_index("ctx") + block) * rows
        query_pos = first + lax.broadcasted_iota(jnp.int32, line, query_dim)
        key_pos = first - hops * rows + lax.broadcasted_iota(jnp.int32, mask.shape, key_dim)
        seen = (key_pos >= user_starts(lengths, query_pos)) & (key_pos <= query_pos)
        mask[...] = jnp.where(seen, 1.0, 0.0).astype(F32)


def forward_kernel(hop_list, heads, scaling, *refs):
    count = len(hop_list)
    table, masks, query = refs[0], refs[1 : 1 + count], refs[1 + count]
    keys, values = refs[2 + count : 2 + 2 * count], refs[2 + 2 * count : 2 + 3 * count]
    total = refs[2 + 3 * count] if len(refs) > 3 + 3 * count else None
    out = refs[-1]
    width = query.shape[1] // heads
    pairs = [Pair(mask, table, heads, hops) for mask, hops in zip(masks, hop_list)]

    def scores(head):
        cols = columns(head, width)
        return [contract(query[:, cols], key[:, cols], 1, 1) for key in keys]

    def attend(head, found):
        cols = columns(head, width)
        part = None if total is None else total[:, cols]
        for pair, score, value in zip(pairs, found, values):
            half = pair.half_logits(score, head, scaling)
            weights = ((half + half * jnp.tanh(half)) * pair.mask).astype(BF16)
            added = contract(weights, value[:, cols], 1, 0)
            part = added if part is None else part + added
        out[:, cols] = part.astype(out.dtype)

    in_stages(heads, scores, attend)


def norm_kernel(total, far_part, out_grad, update_gate, gain, attn_grad, gate_grad, gain_grad):
    rows, features = total.shape
    step = 16
    gain_row = gain[...]
    gain_sum = jnp.zeros((8, features), F32)
    for low in range(0, rows, step):
        span = slice(low, low + step)
        attention = total[span, :] + far_part[span, :].astype(F32)
        center = attention - jnp.mean(attention, axis=1, keepdims=True)
        inverse = lax.rsqrt(jnp.mean(center * center, axis=1, keepdims=True) + EPSILON)
        normed = center * inverse
        grad_f = out_grad[span, :].astype(F32)
        gate_grad[span, :] = (grad_f * normed * gain_row).astype(BF16)
        gated = grad_f * update_gate[span, :].astype(F32)
        product = gated * normed
        for part in range(0, step, 8):
            gain_sum = gain_sum + product[part : part + 8, :]
        pushed = gated * gain_row
        attn_grad[span, :] = (
            inverse
            * (
                pushed
                - jnp.mean(pushed, axis=1, keepdims=True)
                - normed * jnp.mean(pushed * normed, axis=1, keepdims=True)
            )
        ).astype(BF16)
    gain_grad[...] = jnp.sum(gain_sum, axis=0, keepdims=True)


def backward_own_kernel(hop_list, heads, scaling, *refs):
    count = len(hop_list)
    table, masks = refs[0], refs[1 : 1 + count]
    query, grad = refs[1 + count : 3 + count]
    keys, values = refs[3 + count : 3 + 2 * count], refs[3 + 2 * count : 3 + 3 * count]
    query_out, key_out, value_out, bias_out = refs[3 + 3 * count :]
    width = query.shape[1] // heads
    pairs = [
        Pair(mask, table, heads, hops, hops == 0) for mask, hops in zip(masks, hop_list)
    ]
    lane = lax.broadcasted_iota(jnp.int32, bias_out.shape, 1)
    bias_total = [jnp.zeros(bias_out.shape, F32)]

    def scores(head):
        cols = columns(head, width)
        query_h, grad_h = query[:, cols], grad[:, cols]
        found = []
        for hops, key, value in zip(hop_list, keys, values):
            key_h, value_h = key[:, cols], value[:, cols]
            if hops == 0:
                found.append((contract(key_h, query_h, 1, 1), contract(value_h, grad_h, 1, 1)))
            else:
                found.append((contract(query_h, key_h, 1, 1), contract(grad_h, value_h, 1, 1)))
        return found

    def differentiate(head, found):
        cols = columns(head, width)
        query_part, bias_part = None, None
        for pair, hops, key, (score, weight_grad) in zip(pairs, hop_list, keys, found):
            half = pair.half_logits(score, head, scaling)
            tanh = jnp.tanh(half)
            logit_grad = weight_grad * (slope_of(half, tanh) * pair.mask)
            rounded = logit_grad.astype(BF16)
            if hops == 0:
                weights = ((half + half * tanh) * pair.mask).astype(BF16)
                key_out[:, cols] = contract(rounded, query[:, cols], 1, 0)
                value_out[:, cols] = contract(weights, grad[:, cols], 1, 0)
                added = contract(rounded, key[:, cols], 0, 0)
            else:
                added = contract(rounded, key[:, cols], 1, 0)
            query_part = added if query_part is None else query_part + added
            sums = pair.bias_rows(logit_grad)
            bias_part = sums if bias_part is None else bias_part + sums
        query_out[:, cols] = query_part
        sums = jnp.sum(bias_part, axis=1, keepdims=True)
        bias_total[0] = jnp.where(lane == head, sums, bias_total[0])

    in_stages(heads, scores, differentiate, 1)
    bias_out[...] = bias_total[0]


def backward_far_kernel(hops, heads, scaling, *refs):
    table, mask, query, grad, key, value, bias_in, gain_in, query_out, small_out = refs
    width = query.shape[1] // heads
    pair = Pair(mask, table, heads, hops)
    lane = lax.broadcasted_iota(jnp.int32, bias_in.shape, 1)
    bias_total = [bias_in[...]]

    def scores(head):
        cols = columns(head, width)
        score = contract(query[:, cols], key[:, cols], 1, 1)
        return score, contract(grad[:, cols], value[:, cols], 1, 1)

    def differentiate(head, found):
        cols = columns(head, width)
        half = pair.half_logits(found[0], head, scaling)
        logit_grad = found[1] * (slope_of(half, jnp.tanh(half)) * pair.mask)
        query_out[:, cols] = contract(logit_grad.astype(BF16), key[:, cols], 1, 0).astype(BF16)
        sums = jnp.sum(pair.bias_rows(logit_grad), axis=1, keepdims=True)
        bias_total[0] = bias_total[0] + jnp.where(lane == head, sums, 0.0)

    in_stages(heads, scores, differentiate)
    lanes = small_out.shape[1]
    lines = gain_in.shape[1] // lanes
    for line in range(lines):
        small_out[line : line + 1, :] = gain_in[:, line * lanes : (line + 1) * lanes]
    small_out[lines:, :] = bias_total[0]


def backward_key_kernel(hops, heads, scaling, *refs):
    table, mask, query, grad, key, value, key_in, value_in, key_out, value_out = refs
    last = key_out.dtype == BF16
    width = query.shape[1] // heads
    pair = Pair(mask, table, heads, hops, True)

    def scores(head):
        cols = columns(head, width)
        score = contract(key[:, cols], query[:, cols], 1, 1)
        return score, contract(value[:, cols], grad[:, cols], 1, 1)

    def differentiate(head, found):
        cols = columns(head, width)
        half = pair.half_logits(found[0], head, scaling)
        tanh = jnp.tanh(half)
        rounded = (found[1] * (slope_of(half, tanh) * pair.mask)).astype(BF16)
        weights = ((half + half * tanh) * pair.mask).astype(BF16)
        key_part = key_in[:, cols] + contract(rounded, query[:, cols], 1, 0)
        value_part = value_in[:, cols] + contract(weights, grad[:, cols], 1, 0)
        if last:
            key_part = key_part * scaling
        key_out[:, cols] = key_part.astype(key_out.dtype)
        value_out[:, cols] = value_part.astype(value_out.dtype)

    in_stages(heads, scores, differentiate)


def query_kernel(scaling, total, part, out):
    out[...] = ((total[...] + part[...].astype(F32)) * scaling).astype(BF16)


def on_device(kernel, outs, args, smem=(), ahead=()):
    count = len(args)

    def body(*refs):
        kernel(*refs[: len(smem) + count], *refs[len(smem) + count + len(ahead) :])

    return pl.pallas_call(
        body,
        out_shape=outs,
        in_specs=[pl.BlockSpec(memory_space=pltpu.SMEM)] * len(smem)
        + [pl.BlockSpec(memory_space=pltpu.VMEM)] * count
        + [pl.BlockSpec(memory_space=pl.ANY)] * len(ahead),
        out_specs=[pl.BlockSpec(memory_space=pltpu.VMEM)] * len(outs),
        compiler_params=pltpu.CompilerParams(vmem_limit_bytes=VMEM_LIMIT),
        cost_estimate=pl.CostEstimate(flops=1000000, bytes_accessed=100000, transcendentals=0),
    )(*smem, *args, *ahead)


def summed_over(array, axes):
    return jnp.sum(lax.all_gather(array, axes), axis=0)


def local(queries, key_rows, value_rows, update_gate, out_grad, user_lengths, rel_bias, norm_gain):
    rows, features = queries.shape[1:]
    levels, heads = rel_bias.shape
    scaling = (features // heads) ** (-0.5)
    query, key, value = queries[0], key_rows[0], value_rows[0]
    reach = min(3, lax.axis_size("ctx") // 2)
    wide = jax.ShapeDtypeStruct((rows, features), F32)
    narrow = jax.ShapeDtypeStruct((rows, features), BF16)

    keys, values = [key], [value]
    for _ in range(reach - 1):
        keys.append(passed_along(keys[-1], "ctx", 1))
        values.append(passed_along(values[-1], "ctx", 1))
    later_queries = [query] + [passed_along(query, "ctx", -hops) for hops in range(1, reach + 1)]

    near = tuple(range(1, reach))
    plan = [(0, 0, False), (0, 0, True), (1, reach, False)]
    plan += [(0, hops, False) for hops in near]
    plan += [(hops, hops, True) for hops in range(1, reach + 1)]
    outs = [jax.ShapeDtypeStruct((levels * heads, rows), F32)]
    outs += [jax.ShapeDtypeStruct((rows, rows), F32)] * len(plan)
    table, *masks = on_device(partial(mask_kernel, plan), outs, (), (user_lengths, rel_bias))
    mask_of = dict(zip(plan, masks))
    near_masks = [mask_of[0, hops, False] for hops in near]
    (attention,) = on_device(
        partial(forward_kernel, (0,), heads, scaling),
        [wide],
        (table, mask_of[0, 0, False], query, key, value),
    )
    far = (table, mask_of[1, reach, False], later_queries[1])
    (far_part,) = on_device(
        partial(forward_kernel, (reach,), heads, scaling), [narrow], (*far, keys[-1], values[-1])
    )
    far_part = passed_along(far_part, "ctx", 1)
    if near:
        (attention,) = on_device(
            partial(forward_kernel, near, heads, scaling),
            [wide],
            (table, *near_masks, query, *keys[1:], *values[1:], attention),
        )
    attn_grad, gate_grad, gain_part = on_device(
        norm_kernel,
        [narrow, narrow, jax.ShapeDtypeStruct((1, features), F32)],
        (attention, far_part, out_grad[0], update_gate[0], norm_gain[None]),
        ahead=later_queries[2:],
    )
    later_grads = [attn_grad]
    for _ in range(reach):
        later_grads.append(passed_along(later_grads[-1], "ctx", -1))

    lanes = features // 8
    query_total, key_total, value_total, bias_part = on_device(
        partial(backward_own_kernel, (0, *near), heads, scaling),
        [wide, wide, wide, jax.ShapeDtypeStruct((levels, lanes), F32)],
        (table, mask_of[0, 0, True], *near_masks, query, attn_grad, *keys, *values),
    )
    query_part, sums = on_device(
        partial(backward_far_kernel, reach, heads, scaling),
        [narrow, jax.ShapeDtypeStruct((8 + levels, lanes), F32)],
        (*far, later_grads[1], keys[-1], values[-1], bias_part, gain_part),
    )
    query_part = passed_along(query_part, "ctx", 1)
    sums = summed_over(sums, ("ctx", "dp"))
    for hops in range(1, reach + 1):
        key_total, value_total = on_device(
            partial(backward_key_kernel, hops, heads, scaling),
            [narrow if hops == reach else wide] * 2,
            (
                table,
                mask_of[hops, hops, True],
                later_queries[hops],
                later_grads[hops],
                key,
                value,
                key_total,
                value_total,
            ),
        )
    (query_grad,) = on_device(partial(query_kernel, scaling), [narrow], (query_total, query_part))
    return (
        query_grad[None],
        key_total[None],
        value_total[None],
        gate_grad[None],
        sums[8:, :heads],
        sums[:8].reshape(features),
    )


def solution(mesh):
    in_specs = (
        P(("groups", "dp"), "ctx", None),
        P(("groups", "dp"), "ctx", None),
        P(("groups", "dp"), "ctx", None),
        P(("groups", "dp"), "ctx", None),
        P(("groups", "dp"), "ctx", None),
        P(("groups", "dp"), None),
        P(),
        P(),
    )
    out_specs = (
        P(("groups", "dp"), "ctx", None),
        P(("groups", "dp"), "ctx", None),
        P(("groups", "dp"), "ctx", None),
        P(("groups", "dp"), "ctx", None),
        P("groups", None),
        P("groups"),
    )
    return jax.shard_map(local, mesh=mesh, in_specs=in_specs, out_specs=out_specs, check_vma=False)
```

```python
from functools import partial

import jax
import jax.numpy as jnp
from jax import lax
from jax.experimental import pallas as pl
from jax.experimental.pallas import tpu as pltpu
from jax.sharding import PartitionSpec as P

EPSILON = 1e-05
VMEM_LIMIT = 24 * 1024 * 1024
F32 = jnp.float32
BF16 = jnp.bfloat16


def passed_along(array, axis, by):
    size = lax.axis_size(axis)
    pairs = [(i, i + by) for i in range(size) if 0 <= i + by < size]
    return lax.ppermute(array, axis, pairs)


def contract(left, right, left_dim, right_dim):
    return lax.dot_general(
        left, right, (((left_dim,), (right_dim,)), ((), ())), preferred_element_type=F32
    )


def user_starts(lengths, query_pos):
    end = jnp.int32(0)
    start = jnp.zeros(query_pos.shape, jnp.int32)
    for user in range(lengths.shape[1]):
        end = end + lengths[0, user]
        start = jnp.where(query_pos >= end, end, start)
    return start


class Pair:
    def __init__(self, mask, table, heads, hops, flipped=False):
        rows = mask.shape[0]
        self.table, self.heads, self.levels = table, heads, table.shape[0] // heads
        self.mask = mask[...]
        self.far = (hops - 1) * rows + 1 >= 2 ** (self.levels - 2)
        if not self.far:
            query_dim, key_dim = (1, 0) if flipped else (0, 1)
            query_row = lax.broadcasted_iota(jnp.int32, mask.shape, query_dim)
            key_row = lax.broadcasted_iota(jnp.int32, mask.shape, key_dim)
            self.distance = query_row - key_row + hops * rows

    def half_logits(self, scores, head, scaling):
        def level_row(level):
            at = level * self.heads + head
            return self.table[at : at + 1, :]

        value = level_row(self.levels - 1)
        if not self.far:
            for level in range(self.levels - 2, -1, -1):
                value = jnp.where(self.distance < 2**level, level_row(level), value)
        return scores * (0.5 * scaling) + value

    def bias_rows(self, grads):
        sub = lax.broadcasted_iota(jnp.int32, (self.levels, grads.shape[1]), 0)
        if self.far:
            row = jnp.sum(grads, axis=0, keepdims=True)
            return jnp.where(sub == self.levels - 1, row, 0.0)
        total = jnp.zeros(sub.shape, F32)
        for level in range(self.levels):
            inside = None
            if level > 0:
                inside = self.distance >= 2 ** (level - 1)
            if level < self.levels - 1:
                below = self.distance < 2**level
                inside = below if inside is None else inside & below
            row = jnp.sum(jnp.where(inside, grads, 0.0), axis=0, keepdims=True)
            total = jnp.where(sub == level, row, total)
        return total


def slope_of(half, tanh):
    return (0.5 + 0.5 * tanh) * (1.0 + half * (1.0 - tanh))


def columns(head, width):
    return slice(head * width, (head + 1) * width)


def in_stages(count, first, second, ahead=3):
    held = [first(i) for i in range(min(ahead, count))]
    for i in range(count):
        if i + ahead < count:
            held.append(first(i + ahead))
        second(i, held.pop(0))


def mask_kernel(plan, lengths, bias, table, *masks):
    levels, heads = bias.shape
    for level in range(levels):
        for head in range(heads):
            at = level * heads + head
            table[at : at + 1, :] = jnp.full((1, table.shape[1]), 0.5 * bias[level, head], F32)
    for (block, hops, flipped), mask in zip(plan, masks):
        rows = mask.shape[0]
        query_dim, key_dim = (1, 0) if flipped else (0, 1)
        line = (1, rows) if flipped else (rows, 1)
        first = (lax.axis_index("ctx") + block) * rows
        query_pos = first + lax.broadcasted_iota(jnp.int32, line, query_dim)
        key_pos = first - hops * rows + lax.broadcasted_iota(jnp.int32, mask.shape, key_dim)
        seen = (key_pos >= user_starts(lengths, query_pos)) & (key_pos <= query_pos)
        mask[...] = jnp.where(seen, 1.0, 0.0).astype(F32)


def forward_kernel(hop_list, heads, scaling, *refs):
    count = len(hop_list)
    table, masks, query = refs[0], refs[1 : 1 + count], refs[1 + count]
    keys, values = refs[2 + count : 2 + 2 * count], refs[2 + 2 * count : 2 + 3 * count]
    total = refs[2 + 3 * count] if len(refs) > 3 + 3 * count else None
    out = refs[-1]
    width = query.shape[1] // heads
    pairs = [Pair(mask, table, heads, hops) for mask, hops in zip(masks, hop_list)]

    def scores(head):
        cols = columns(head, width)
        return [contract(query[:, cols], key[:, cols], 1, 1) for key in keys]

    def attend(head, found):
        cols = columns(head, width)
        part = None if total is None else total[:, cols]
        for pair, score, value in zip(pairs, found, values):
            half = pair.half_logits(score, head, scaling)
            weights = ((half + half * jnp.tanh(half)) * pair.mask).astype(BF16)
            added = contract(weights, value[:, cols], 1, 0)
            part = added if part is None else part + added
        out[:, cols] = part.astype(out.dtype)

    in_stages(heads, scores, attend)


def norm_kernel(total, out_grad, update_gate, gain, attn_grad, gate_grad, gain_grad):
    rows, features = total.shape
    step = 16
    gain_row = gain[...]
    gain_sum = jnp.zeros((8, features), F32)
    for low in range(0, rows, step):
        span = slice(low, low + step)
        attention = total[span, :]
        center = attention - jnp.mean(attention, axis=1, keepdims=True)
        inverse = lax.rsqrt(jnp.mean(center * center, axis=1, keepdims=True) + EPSILON)
        normed = center * inverse
        grad_f = out_grad[span, :].astype(F32)
        gate_grad[span, :] = (grad_f * normed * gain_row).astype(BF16)
        gated = grad_f * update_gate[span, :].astype(F32)
        product = gated * normed
        for part in range(0, step, 8):
            gain_sum = gain_sum + product[part : part + 8, :]
        pushed = gated * gain_row
        attn_grad[span, :] = (
            inverse
            * (
                pushed
                - jnp.mean(pushed, axis=1, keepdims=True)
                - normed * jnp.mean(pushed * normed, axis=1, keepdims=True)
            )
        ).astype(BF16)
    gain_grad[...] = jnp.sum(gain_sum, axis=0, keepdims=True)


def backward_own_kernel(hop_list, heads, scaling, *refs):
    count = len(hop_list)
    table, masks = refs[0], refs[1 : 1 + count]
    query, grad = refs[1 + count : 3 + count]
    keys, values = refs[3 + count : 3 + 2 * count], refs[3 + 2 * count : 3 + 3 * count]
    gain_in, query_out, key_out, value_out, small_out = refs[3 + 3 * count :]
    width = query.shape[1] // heads
    pairs = [
        Pair(mask, table, heads, hops, hops == 0) for mask, hops in zip(masks, hop_list)
    ]
    lanes = small_out.shape[1]
    lines = gain_in.shape[1] // lanes
    levels = small_out.shape[0] - lines
    lane = lax.broadcasted_iota(jnp.int32, (levels, lanes), 1)
    bias_total = [jnp.zeros((levels, lanes), F32)]

    def scores(head):
        cols = columns(head, width)
        query_h, grad_h = query[:, cols], grad[:, cols]
        found = []
        for hops, key, value in zip(hop_list, keys, values):
            key_h, value_h = key[:, cols], value[:, cols]
            if hops == 0:
                found.append((contract(key_h, query_h, 1, 1), contract(value_h, grad_h, 1, 1)))
            else:
                found.append((contract(query_h, key_h, 1, 1), contract(grad_h, value_h, 1, 1)))
        return found

    def differentiate(head, found):
        cols = columns(head, width)
        query_part, bias_part = None, None
        for pair, hops, key, (score, weight_grad) in zip(pairs, hop_list, keys, found):
            half = pair.half_logits(score, head, scaling)
            tanh = jnp.tanh(half)
            logit_grad = weight_grad * (slope_of(half, tanh) * pair.mask)
            rounded = logit_grad.astype(BF16)
            if hops == 0:
                weights = ((half + half * tanh) * pair.mask).astype(BF16)
                key_out[:, cols] = contract(rounded, query[:, cols], 1, 0)
                value_out[:, cols] = contract(weights, grad[:, cols], 1, 0)
                added = contract(rounded, key[:, cols], 0, 0)
            else:
                added = contract(rounded, key[:, cols], 1, 0)
            query_part = added if query_part is None else query_part + added
            sums = pair.bias_rows(logit_grad)
            bias_part = sums if bias_part is None else bias_part + sums
        query_out[:, cols] = (query_part * scaling).astype(BF16)
        sums = jnp.sum(bias_part, axis=1, keepdims=True)
        bias_total[0] = jnp.where(lane == head, sums, bias_total[0])

    in_stages(heads, scores, differentiate, 1)
    for line in range(lines):
        small_out[line : line + 1, :] = gain_in[:, line * lanes : (line + 1) * lanes]
    small_out[lines:, :] = bias_total[0]


def backward_key_kernel(hops, heads, scaling, *refs):
    table, mask, query, grad, key, value, key_in, value_in, key_out, value_out = refs
    last = key_out.dtype == BF16
    width = query.shape[1] // heads
    pair = Pair(mask, table, heads, hops, True)

    def scores(head):
        cols = columns(head, width)
        score = contract(key[:, cols], query[:, cols], 1, 1)
        return score, contract(value[:, cols], grad[:, cols], 1, 1)

    def differentiate(head, found):
        cols = columns(head, width)
        half = pair.half_logits(found[0], head, scaling)
        tanh = jnp.tanh(half)
        rounded = (found[1] * (slope_of(half, tanh) * pair.mask)).astype(BF16)
        weights = ((half + half * tanh) * pair.mask).astype(BF16)
        key_part = key_in[:, cols] + contract(rounded, query[:, cols], 1, 0)
        value_part = value_in[:, cols] + contract(weights, grad[:, cols], 1, 0)
        if last:
            key_part = key_part * scaling
        key_out[:, cols] = key_part.astype(key_out.dtype)
        value_out[:, cols] = value_part.astype(value_out.dtype)

    in_stages(heads, scores, differentiate)


def on_device(kernel, outs, args, smem=(), ahead=()):
    count = len(args)

    def body(*refs):
        kernel(*refs[: len(smem) + count], *refs[len(smem) + count + len(ahead) :])

    return pl.pallas_call(
        body,
        out_shape=outs,
        in_specs=[pl.BlockSpec(memory_space=pltpu.SMEM)] * len(smem)
        + [pl.BlockSpec(memory_space=pltpu.VMEM)] * count
        + [pl.BlockSpec(memory_space=pl.ANY)] * len(ahead),
        out_specs=[pl.BlockSpec(memory_space=pltpu.VMEM)] * len(outs),
        compiler_params=pltpu.CompilerParams(vmem_limit_bytes=VMEM_LIMIT),
        cost_estimate=pl.CostEstimate(flops=1000000, bytes_accessed=100000, transcendentals=0),
    )(*smem, *args, *ahead)


def partners_of(axes):
    rounds = []
    for axis in axes:
        size = lax.axis_size(axis)
        step = 1
        while step < size:
            rounds.append((axis, [(i, i ^ step) for i in range(size)]))
            step = 2 * step
    return rounds


def local(queries, key_rows, value_rows, update_gate, out_grad, user_lengths, rel_bias, norm_gain):
    rows, features = queries.shape[1:]
    levels, heads = rel_bias.shape
    scaling = (features // heads) ** (-0.5)
    query, key, value = queries[0], key_rows[0], value_rows[0]
    reach = min(3, lax.axis_size("ctx") // 2)
    wide = jax.ShapeDtypeStruct((rows, features), F32)
    narrow = jax.ShapeDtypeStruct((rows, features), BF16)

    keys, values, later_queries = [key], [value], [query]
    for _ in range(reach):
        keys.append(passed_along(keys[-1], "ctx", 1))
        values.append(passed_along(values[-1], "ctx", 1))
        later_queries.append(passed_along(later_queries[-1], "ctx", -1))

    hop_list = tuple(range(reach + 1))
    plan = [(0, hops, False) for hops in hop_list] + [(hops, hops, True) for hops in hop_list]
    outs = [jax.ShapeDtypeStruct((levels * heads, rows), F32)]
    outs += [jax.ShapeDtypeStruct((rows, rows), F32)] * len(plan)
    table, *masks = on_device(partial(mask_kernel, plan), outs, (), (user_lengths, rel_bias))
    masks, flipped = masks[: reach + 1], masks[reach + 1 :]
    attention = ()
    for hops in hop_list:
        attention = on_device(
            partial(forward_kernel, (hops,), heads, scaling),
            [wide],
            (table, masks[hops], query, keys[hops], values[hops], *attention),
            ahead=later_queries[hops : hops + 1] if 0 < hops < reach else (),
        )
    attn_grad, gate_grad, gain_part = on_device(
        norm_kernel,
        [narrow, narrow, jax.ShapeDtypeStruct((1, features), F32)],
        (*attention, out_grad[0], update_gate[0], norm_gain[None]),
        ahead=later_queries[reach:],
    )
    lanes = features // 8
    query_grad, key_total, value_total, sums = on_device(
        partial(backward_own_kernel, hop_list, heads, scaling),
        [narrow, wide, wide, jax.ShapeDtypeStruct((8 + levels, lanes), F32)],
        (table, flipped[0], *masks[1:], query, attn_grad, *keys, *values, gain_part),
    )
    rounds = partners_of(("dp", "ctx"))
    later_grads = [attn_grad, passed_along(attn_grad, "ctx", -1)]
    for number, (axis, pairs) in enumerate(rounds, 1):
        sums = sums + lax.ppermute(sums, axis, pairs)
        if number < reach:
            arrived, sums = lax.optimization_barrier((later_grads[-1], sums))
            later_grads.append(passed_along(arrived, "ctx", -1))
    for hops in range(1, reach + 1):
        key_total, value_total = on_device(
            partial(backward_key_kernel, hops, heads, scaling),
            [narrow if hops == reach else wide] * 2,
            (
                table,
                flipped[hops],
                later_queries[hops],
                later_grads[hops],
                key,
                value,
                key_total,
                value_total,
            ),
        )
    return (
        query_grad[None],
        key_total[None],
        value_total[None],
        gate_grad[None],
        sums[8:, :heads],
        sums[:8].reshape(features),
    )


def solution(mesh):
    in_specs = (
        P(("groups", "dp"), "ctx", None),
        P(("groups", "dp"), "ctx", None),
        P(("groups", "dp"), "ctx", None),
        P(("groups", "dp"), "ctx", None),
        P(("groups", "dp"), "ctx", None),
        P(("groups", "dp"), None),
        P(),
        P(),
    )
    out_specs = (
        P(("groups", "dp"), "ctx", None),
        P(("groups", "dp"), "ctx", None),
        P(("groups", "dp"), "ctx", None),
        P(("groups", "dp"), "ctx", None),
        P("groups", None),
        P("groups"),
    )
    return jax.shard_map(local, mesh=mesh, in_specs=in_specs, out_specs=out_specs, check_vma=False)
```

```python
from functools import partial

import jax
import jax.numpy as jnp
from jax import lax
from jax.experimental import pallas as pl
from jax.experimental.pallas import tpu as pltpu
from jax.sharding import PartitionSpec as P

EPSILON = 1e-05
VMEM_LIMIT = 24 * 1024 * 1024
F32 = jnp.float32
BF16 = jnp.bfloat16


def passed_along(array, axis, by):
    size = lax.axis_size(axis)
    pairs = [(i, i + by) for i in range(size) if 0 <= i + by < size]
    return lax.ppermute(array, axis, pairs)


def contract(left, right, left_dim, right_dim):
    return lax.dot_general(
        left, right, (((left_dim,), (right_dim,)), ((), ())), preferred_element_type=F32
    )


def user_starts(lengths, query_pos):
    end = jnp.int32(0)
    start = jnp.zeros(query_pos.shape, jnp.int32)
    for user in range(lengths.shape[1]):
        end = end + lengths[0, user]
        start = jnp.where(query_pos >= end, end, start)
    return start


class Pair:
    def __init__(self, mask, table, heads, hops, flipped=False):
        rows = mask.shape[0]
        self.table, self.heads, self.levels = table, heads, table.shape[0] // heads
        self.mask = mask[...]
        self.far = (hops - 1) * rows + 1 >= 2 ** (self.levels - 2)
        if not self.far:
            query_dim, key_dim = (1, 0) if flipped else (0, 1)
            query_row = lax.broadcasted_iota(jnp.int32, mask.shape, query_dim)
            key_row = lax.broadcasted_iota(jnp.int32, mask.shape, key_dim)
            self.distance = query_row - key_row + hops * rows

    def half_logits(self, scores, head, scaling):
        def level_row(level):
            at = level * self.heads + head
            return self.table[at : at + 1, :]

        value = level_row(self.levels - 1)
        if not self.far:
            for level in range(self.levels - 2, -1, -1):
                value = jnp.where(self.distance < 2**level, level_row(level), value)
        return scores * (0.5 * scaling) + value

    def bias_rows(self, grads):
        sub = lax.broadcasted_iota(jnp.int32, (self.levels, grads.shape[1]), 0)
        if self.far:
            row = jnp.sum(grads, axis=0, keepdims=True)
            return jnp.where(sub == self.levels - 1, row, 0.0)
        total = jnp.zeros(sub.shape, F32)
        for level in range(self.levels):
            inside = None
            if level > 0:
                inside = self.distance >= 2 ** (level - 1)
            if level < self.levels - 1:
                below = self.distance < 2**level
                inside = below if inside is None else inside & below
            row = jnp.sum(jnp.where(inside, grads, 0.0), axis=0, keepdims=True)
            total = jnp.where(sub == level, row, total)
        return total


def slope_of(half, tanh):
    return (0.5 + 0.5 * tanh) * (1.0 + half * (1.0 - tanh))


def columns(head, width):
    return slice(head * width, (head + 1) * width)


def in_stages(count, first, second, ahead=3):
    held = [first(i) for i in range(min(ahead, count))]
    for i in range(count):
        if i + ahead < count:
            held.append(first(i + ahead))
        second(i, held.pop(0))


def attend(pairs, heads, scaling, query, keys, values, total, out):
    width = query.shape[1] // heads

    def scores(head):
        cols = columns(head, width)
        return [contract(query[:, cols], key[:, cols], 1, 1) for key in keys]

    def weigh(head, found):
        cols = columns(head, width)
        part = None if total is None else total[:, cols]
        for pair, score, value in zip(pairs, found, values):
            half = pair.half_logits(score, head, scaling)
            weights = ((half + half * jnp.tanh(half)) * pair.mask).astype(BF16)
            added = contract(weights, value[:, cols], 1, 0)
            part = added if part is None else part + added
        out[:, cols] = part.astype(out.dtype)

    in_stages(heads, scores, weigh)


def first_kernel(plan, heads, scaling, lengths, bias, *refs):
    inputs, refs = refs[:5], refs[5:]
    table, masks, refs = refs[0], refs[1 : 1 + len(plan)], refs[1 + len(plan) :]
    held, out, arrived = refs[:5], refs[5], refs[6]
    copies = [
        pltpu.make_async_copy(source, target, arrived.at[at])
        for at, (source, target) in enumerate(zip(inputs, held))
    ]
    for copy in copies:
        copy.start()
    levels = bias.shape[0]
    for level in range(levels):
        for head in range(heads):
            at = level * heads + head
            table[at : at + 1, :] = jnp.full((1, table.shape[1]), 0.5 * bias[level, head], F32)
    for (block, hops, flipped), mask in zip(plan, masks):
        rows = mask.shape[0]
        query_dim, key_dim = (1, 0) if flipped else (0, 1)
        line = (1, rows) if flipped else (rows, 1)
        first = (lax.axis_index("ctx") + block) * rows
        query_pos = first + lax.broadcasted_iota(jnp.int32, line, query_dim)
        key_pos = first - hops * rows + lax.broadcasted_iota(jnp.int32, mask.shape, key_dim)
        seen = (key_pos >= user_starts(lengths, query_pos)) & (key_pos <= query_pos)
        mask[...] = jnp.where(seen, 1.0, 0.0).astype(F32)
    for copy in copies:
        copy.wait()
    query, key, value = held[:3]
    pair = Pair(masks[0], table, heads, 0)
    attend([pair], heads, scaling, query, [key], [value], None, out)


def forward_kernel(hops, heads, scaling, table, mask, query, key, value, total, out):
    pair = Pair(mask, table, heads, hops)
    attend([pair], heads, scaling, query, [key], [value], total, out)


def normed_rows(attention):
    center = attention - jnp.mean(attention, axis=1, keepdims=True)
    inverse = lax.rsqrt(jnp.mean(center * center, axis=1, keepdims=True) + EPSILON)
    return center * inverse, inverse


def norm_kernel(hops, heads, scaling, *refs):
    table, mask, query, key, value, total, out_grad, update_gate, gain = refs[:9]
    attention, attn_grad, gain_grad = refs[9:]
    forward_kernel(hops, heads, scaling, table, mask, query, key, value, total, attention)
    rows, features = attention.shape
    step = 16
    gain_row = gain[...]
    gain_sum = jnp.zeros((8, features), F32)
    for low in range(0, rows, step):
        span = slice(low, low + step)
        normed, inverse = normed_rows(attention[span, :])
        gated = out_grad[span, :].astype(F32) * update_gate[span, :].astype(F32)
        product = gated * normed
        for part in range(0, step, 8):
            gain_sum = gain_sum + product[part : part + 8, :]
        pushed = gated * gain_row
        attn_grad[span, :] = (
            inverse
            * (
                pushed
                - jnp.mean(pushed, axis=1, keepdims=True)
                - normed * jnp.mean(pushed * normed, axis=1, keepdims=True)
            )
        ).astype(BF16)
    gain_grad[...] = jnp.sum(gain_sum, axis=0, keepdims=True)


def gate_kernel(attention, out_grad, gain, gate_grad):
    step = 16
    gain_row = gain[...]
    for low in range(0, attention.shape[0], step):
        span = slice(low, low + step)
        normed, _ = normed_rows(attention[span, :])
        gate_grad[span, :] = (out_grad[span, :].astype(F32) * normed * gain_row).astype(BF16)


def backward_query_kernel(hop_list, heads, scaling, *refs):
    count = len(hop_list)
    table, masks = refs[0], refs[1 : 1 + count]
    query, grad = refs[1 + count : 3 + count]
    keys, values = refs[3 + count : 3 + 2 * count], refs[3 + 2 * count : 3 + 3 * count]
    gain_in, query_out, small_out = refs[3 + 3 * count :]
    width = query.shape[1] // heads
    pairs = [Pair(mask, table, heads, hops) for mask, hops in zip(masks, hop_list)]
    lanes = small_out.shape[1]
    lines = gain_in.shape[1] // lanes
    levels = small_out.shape[0] - lines
    lane = lax.broadcasted_iota(jnp.int32, (levels, lanes), 1)
    bias_total = [jnp.zeros((levels, lanes), F32)]

    def scores(head):
        cols = columns(head, width)
        query_h, grad_h = query[:, cols], grad[:, cols]
        return [
            (contract(query_h, key[:, cols], 1, 1), contract(grad_h, value[:, cols], 1, 1))
            for key, value in zip(keys, values)
        ]

    def differentiate(head, found):
        cols = columns(head, width)
        query_part, bias_part = None, None
        for pair, key, (score, weight_grad) in zip(pairs, keys, found):
            half = pair.half_logits(score, head, scaling)
            logit_grad = weight_grad * (slope_of(half, jnp.tanh(half)) * pair.mask)
            added = contract(logit_grad.astype(BF16), key[:, cols], 1, 0)
            query_part = added if query_part is None else query_part + added
            sums = pair.bias_rows(logit_grad)
            bias_part = sums if bias_part is None else bias_part + sums
        query_out[:, cols] = (query_part * scaling).astype(BF16)
        sums = jnp.sum(bias_part, axis=1, keepdims=True)
        bias_total[0] = jnp.where(lane == head, sums, bias_total[0])

    in_stages(heads, scores, differentiate, 1)
    for line in range(lines):
        small_out[line : line + 1, :] = gain_in[:, line * lanes : (line + 1) * lanes]
    small_out[lines:, :] = bias_total[0]


def add_key_grads(hops, heads, scaling, table, mask, query, grad, key, value, sums, store):
    width = query.shape[1] // heads
    pair = Pair(mask, table, heads, hops, True)

    def scores(head):
        cols = columns(head, width)
        score = contract(key[:, cols], query[:, cols], 1, 1)
        return score, contract(value[:, cols], grad[:, cols], 1, 1)

    def differentiate(head, found):
        cols = columns(head, width)
        half = pair.half_logits(found[0], head, scaling)
        tanh = jnp.tanh(half)
        rounded = (found[1] * (slope_of(half, tanh) * pair.mask)).astype(BF16)
        weights = ((half + half * tanh) * pair.mask).astype(BF16)
        parts = [contract(rounded, query[:, cols], 1, 0), contract(weights, grad[:, cols], 1, 0)]
        store(head, cols, *[part + held[:, cols] for part, held in zip(parts, sums)] or parts)

    in_stages(heads, scores, differentiate)


def backward_key_kernel(hops, heads, scaling, *refs):
    key_out, value_out = refs[-2:]

    def store(head, cols, key_part, value_part):
        key_out[:, cols] = key_part
        value_out[:, cols] = value_part

    add_key_grads(hops, heads, scaling, *refs[:6], refs[6:-2], store)


def last_kernel(hops, heads, scaling, *refs):
    pieces = refs[8:-7]
    key_out, value_out, gain_out, bias_out, key_held, value_held, written = refs[-7:]
    copies = []
    group = 2

    def store(head, cols, key_part, value_part):
        key_held[:, cols] = (key_part * scaling).astype(BF16)
        value_held[:, cols] = value_part.astype(BF16)
        if (head + 1) % group == 0:
            done = slice(cols.stop - group * (cols.stop - cols.start), cols.stop)
            for held, out in ((key_held, key_out), (value_held, value_out)):
                at = written.at[len(copies)]
                copies.append(pltpu.make_async_copy(held.at[:, done], out.at[:, done], at))
                copies[-1].start()

    total = added_up([piece[...] for piece in pieces])
    lines = gain_out.shape[0]
    gain_out[...] = total[:lines]
    bias_out[...] = total[lines:, :heads]
    add_key_grads(hops, heads, scaling, *refs[:6], refs[6:8], store)
    for copy in copies:
        copy.wait()


def on_device(kernel, outs, args, smem=(), ahead=(), far=(), far_outs=0, scratch=()):
    count = len(smem) + len(far) + len(args)
    far = [pltpu.with_memory_space_constraint(array, pltpu.HBM) for array in far]

    def body(*refs):
        kernel(*refs[:count], *refs[count + len(ahead) :])

    vmem, anywhere = pl.BlockSpec(memory_space=pltpu.VMEM), pl.BlockSpec(memory_space=pl.ANY)
    return pl.pallas_call(
        body,
        out_shape=outs,
        in_specs=[pl.BlockSpec(memory_space=pltpu.SMEM)] * len(smem)
        + [pl.BlockSpec(memory_space=pltpu.HBM)] * len(far)
        + [vmem] * len(args)
        + [anywhere] * len(ahead),
        out_specs=[anywhere] * far_outs + [vmem] * (len(outs) - far_outs),
        scratch_shapes=scratch,
        compiler_params=pltpu.CompilerParams(vmem_limit_bytes=VMEM_LIMIT),
        cost_estimate=pl.CostEstimate(flops=1000000, bytes_accessed=100000, transcendentals=0),
    )(*smem, *far, *args, *ahead)


def rounds_of(axes):
    rounds = []
    for axis in axes:
        size = lax.axis_size(axis)
        step = 1
        while step < size:
            radix = 4 if size // step >= 4 else 2
            rounds.append((axis, [step * at for at in range(1, radix)]))
            step = radix * step
    return rounds


def exchanged(array, axis, distances):
    size = lax.axis_size(axis)
    return [array] + [
        lax.ppermute(array, axis, [(i, i ^ distance) for i in range(size)])
        for distance in distances
    ]


def added_up(pieces):
    while len(pieces) > 1:
        pieces = [left + right for left, right in zip(pieces[::2], pieces[1::2])]
    return pieces[0]


def local(queries, key_rows, value_rows, update_gate, out_grad, user_lengths, rel_bias, norm_gain):
    rows, features = queries.shape[1:]
    levels, heads = rel_bias.shape
    scaling = (features // heads) ** (-0.5)
    reach = min(3, lax.axis_size("ctx") // 2)
    wide = jax.ShapeDtypeStruct((rows, features), F32)
    narrow = jax.ShapeDtypeStruct((rows, features), BF16)
    inputs = (queries[0], key_rows[0], value_rows[0], update_gate[0], out_grad[0])
    gain = norm_gain[None]

    hop_list = tuple(range(reach + 1))
    plan = [(0, hops, False) for hops in hop_list] + [(hops, hops, True) for hops in hop_list]
    outs = [jax.ShapeDtypeStruct((levels * heads, rows), F32)]
    outs += [jax.ShapeDtypeStruct((rows, rows), F32)] * len(plan)
    outs += [narrow] * len(inputs) + [wide]
    table, *found = on_device(
        partial(first_kernel, plan, heads, scaling),
        outs,
        (),
        (user_lengths, rel_bias),
        far=inputs,
        scratch=[pltpu.SemaphoreType.DMA((len(inputs),))],
    )
    masks, flipped = found[: reach + 1], found[reach + 1 : 2 * reach + 2]
    query, key, value, gate, grad, attention = found[2 * reach + 2 :]

    later_queries = [query, passed_along(inputs[0], "ctx", -1)]
    keys = [key, passed_along(inputs[1], "ctx", 1)]
    values = [value, passed_along(inputs[2], "ctx", 1)]
    for hops in range(1, reach):
        keys.append(passed_along(keys[-1], "ctx", 1))
        if hops == 1:
            values[1], attention = lax.optimization_barrier((values[1], attention))
        values.append(passed_along(values[-1], "ctx", 1))
        later_queries.append(passed_along(later_queries[-1], "ctx", -1))
    for hops in range(1, reach):
        (attention,) = on_device(
            partial(forward_kernel, hops, heads, scaling),
            [wide],
            (table, masks[hops], query, keys[hops], values[hops], attention),
            ahead=later_queries[hops : hops + 1],
        )
    attention, attn_grad, gain_part = on_device(
        partial(norm_kernel, reach, heads, scaling),
        [wide, narrow, jax.ShapeDtypeStruct((1, features), F32)],
        (table, masks[-1], query, keys[-1], values[-1], attention, grad, gate, gain),
        ahead=later_queries[reach:],
    )

    lanes = features // 8
    query_grad, sums = on_device(
        partial(backward_query_kernel, hop_list, heads, scaling),
        [narrow, jax.ShapeDtypeStruct((8 + levels, lanes), F32)],
        (table, *masks, query, attn_grad, *keys, *values, gain_part),
    )
    later_grads = [attn_grad, passed_along(attn_grad, "ctx", -1)]
    pieces = [sums]
    first_pieces = None
    for number, (axis, distances) in enumerate(rounds_of(("dp", "ctx")), 1):
        pieces = exchanged(added_up(pieces), axis, distances)
        if number < reach:
            arrived, *pieces = lax.optimization_barrier((later_grads[-1], *pieces))
            later_grads.append(passed_along(arrived, "ctx", -1))
        first_pieces = first_pieces or pieces[1:2]
    key_grads = ()
    for hops in range(reach):
        key_grads = on_device(
            partial(backward_key_kernel, hops, heads, scaling),
            [wide] * 2,
            (table, flipped[hops], later_queries[hops], later_grads[hops], key, value, *key_grads),
            ahead=first_pieces,
        )
    (gate_grad,) = on_device(gate_kernel, [narrow], (attention, grad, gain), ahead=key_grads[:1])
    key_grad, value_grad, gain_grad, bias_grad = on_device(
        partial(last_kernel, reach, heads, scaling),
        [
            narrow,
            narrow,
            jax.ShapeDtypeStruct((8, lanes), F32),
            jax.ShapeDtypeStruct((levels, heads), F32),
        ],
        (
            table,
            flipped[reach],
            later_queries[reach],
            later_grads[reach],
            key,
            value,
            *key_grads,
            *pieces,
        ),
        far_outs=2,
        scratch=[pltpu.VMEM((rows, features), BF16)] * 2 + [pltpu.SemaphoreType.DMA((heads,))],
    )
    return (
        query_grad[None],
        key_grad[None],
        value_grad[None],
        gate_grad[None],
        bias_grad,
        gain_grad.reshape(features),
    )


def solution(mesh):
    in_specs = (
        P(("groups", "dp"), "ctx", None),
        P(("groups", "dp"), "ctx", None),
        P(("groups", "dp"), "ctx", None),
        P(("groups", "dp"), "ctx", None),
        P(("groups", "dp"), "ctx", None),
        P(("groups", "dp"), None),
        P(),
        P(),
    )
    out_specs = (
        P(("groups", "dp"), "ctx", None),
        P(("groups", "dp"), "ctx", None),
        P(("groups", "dp"), "ctx", None),
        P(("groups", "dp"), "ctx", None),
        P("groups", None),
        P("groups"),
    )
    return jax.shard_map(local, mesh=mesh, in_specs=in_specs, out_specs=out_specs, check_vma=False)
```

```python
from functools import partial

import jax
import jax.numpy as jnp
from jax import lax
from jax.experimental import pallas as pl
from jax.experimental.pallas import tpu as pltpu
from jax.sharding import PartitionSpec as P

EPSILON = 1e-05
VMEM_LIMIT = 24 * 1024 * 1024
F32 = jnp.float32
BF16 = jnp.bfloat16


def passed_along(array, axis, by):
    size = lax.axis_size(axis)
    pairs = [(i, i + by) for i in range(size) if 0 <= i + by < size]
    return lax.ppermute(array, axis, pairs)


def contract(left, right, left_dim, right_dim):
    return lax.dot_general(
        left, right, (((left_dim,), (right_dim,)), ((), ())), preferred_element_type=F32
    )


def user_starts(lengths, query_pos):
    end = jnp.int32(0)
    start = jnp.zeros(query_pos.shape, jnp.int32)
    for user in range(lengths.shape[1]):
        end = end + lengths[0, user]
        start = jnp.where(query_pos >= end, end, start)
    return start


class Pair:
    def __init__(self, mask, table, heads, hops, flipped=False, near=None):
        rows = mask.shape[0]
        self.table, self.heads, self.levels = table, heads, table.shape[0] // heads
        self.mask, self.hops, self.near = mask[...], hops, near
        self.far = (hops - 1) * rows + 1 >= 2 ** (self.levels - 2)
        if not self.far:
            query_dim, key_dim = (1, 0) if flipped else (0, 1)
            query_row = lax.broadcasted_iota(jnp.int32, mask.shape, query_dim)
            key_row = lax.broadcasted_iota(jnp.int32, mask.shape, key_dim)
            self.distance = query_row - key_row + hops * rows

    def half_bias(self, head):
        def level_row(level):
            at = level * self.heads + head
            return self.table[at : at + 1, :]

        value = level_row(self.levels - 1)
        if self.far:
            return value
        if self.near is not None:
            rows = self.mask.shape[0]
            close = self.near[head * rows : (head + 1) * rows, :]
            return close if self.hops == 0 else jnp.where(self.distance < rows, close, value)
        for level in range(self.levels - 2, -1, -1):
            value = jnp.where(self.distance < 2**level, level_row(level), value)
        return value

    def half_logits(self, scores, head, scaling):
        return scores * (0.5 * scaling) + self.half_bias(head)


def slope_of(half, tanh):
    return (0.5 + 0.5 * tanh) * (1.0 + half * (1.0 - tanh))


def columns(head, width):
    return slice(head * width, (head + 1) * width)


def in_stages(count, first, second, ahead=3):
    held = [first(i) for i in range(min(ahead, count))]
    for i in range(count):
        if i + ahead < count:
            held.append(first(i + ahead))
        second(i, held.pop(0))


def attend(pairs, heads, scaling, query, keys, values, total, out):
    width = query.shape[1] // heads

    def scores(head):
        cols = columns(head, width)
        return [contract(query[:, cols], key[:, cols], 1, 1) for key in keys]

    def weigh(head, found):
        cols = columns(head, width)
        part = None if total is None else total[:, cols]
        for pair, score, value in zip(pairs, found, values):
            half = pair.half_logits(score, head, scaling)
            weights = ((half + half * jnp.tanh(half)) * pair.mask).astype(BF16)
            added = contract(weights, value[:, cols], 1, 0)
            part = added if part is None else part + added
        out[:, cols] = part.astype(out.dtype)

    in_stages(heads, scores, weigh)


def first_kernel(plan, heads, scaling, lengths, bias, *refs):
    inputs, refs = refs[:5], refs[5:]
    table, near, masks, refs = refs[0], refs[1], refs[2 : 2 + len(plan)], refs[2 + len(plan) :]
    held, out, arrived = refs[:5], refs[5], refs[6]
    copies = [
        pltpu.make_async_copy(source, target, arrived.at[at])
        for at, (source, target) in enumerate(zip(inputs, held))
    ]
    for copy in copies:
        copy.start()
    levels = bias.shape[0]
    for level in range(levels):
        for head in range(heads):
            at = level * heads + head
            table[at : at + 1, :] = jnp.full((1, table.shape[1]), 0.5 * bias[level, head], F32)
    rows = masks[0].shape[0]
    apart = lax.broadcasted_iota(jnp.int32, (rows, rows), 0)
    apart = (apart - lax.broadcasted_iota(jnp.int32, (rows, rows), 1)) & (rows - 1)
    for head in range(heads):
        value = table[(levels - 1) * heads + head : (levels - 1) * heads + head + 1, :]
        for level in range(levels - 2, -1, -1):
            at = level * heads + head
            value = jnp.where(apart < 2**level, table[at : at + 1, :], value)
        near[head * rows : (head + 1) * rows, :] = value
    for (block, hops, flipped), mask in zip(plan, masks):
        query_dim, key_dim = (1, 0) if flipped else (0, 1)
        line = (1, rows) if flipped else (rows, 1)
        first = (lax.axis_index("ctx") + block) * rows
        query_pos = first + lax.broadcasted_iota(jnp.int32, line, query_dim)
        key_pos = first - hops * rows + lax.broadcasted_iota(jnp.int32, mask.shape, key_dim)
        seen = (key_pos >= user_starts(lengths, query_pos)) & (key_pos <= query_pos)
        mask[...] = jnp.where(seen, 1.0, 0.0).astype(F32)
    for copy in copies:
        copy.wait()
    query, key, value = held[:3]
    pair = Pair(masks[0], table, heads, 0, near=near)
    attend([pair], heads, scaling, query, [key], [value], None, out)


def forward_kernel(hops, heads, scaling, table, near, mask, query, key, value, total, out):
    pair = Pair(mask, table, heads, hops, near=near)
    attend([pair], heads, scaling, query, [key], [value], total, out)


def normed_rows(attention):
    center = attention - jnp.mean(attention, axis=1, keepdims=True)
    inverse = lax.rsqrt(jnp.mean(center * center, axis=1, keepdims=True) + EPSILON)
    return center * inverse, inverse


def norm_kernel(hops, heads, scaling, *refs):
    out_grad, update_gate, gain, attention, attn_grad, gain_grad = refs[-6:]
    forward_kernel(hops, heads, scaling, *refs[:-6], attention)
    rows, features = attention.shape
    step = 16
    gain_row = gain[...]
    gain_sum = jnp.zeros((8, features), F32)
    for low in range(0, rows, step):
        span = slice(low, low + step)
        normed, inverse = normed_rows(attention[span, :])
        gated = out_grad[span, :].astype(F32) * update_gate[span, :].astype(F32)
        product = gated * normed
        for part in range(0, step, 8):
            gain_sum = gain_sum + product[part : part + 8, :]
        pushed = gated * gain_row
        attn_grad[span, :] = (
            inverse
            * (
                pushed
                - jnp.mean(pushed, axis=1, keepdims=True)
                - normed * jnp.mean(pushed * normed, axis=1, keepdims=True)
            )
        ).astype(BF16)
    gain_grad[...] = jnp.sum(gain_sum, axis=0, keepdims=True)


def gate_kernel(attention, out_grad, gain, gate_grad):
    step = 16
    gain_row = gain[...]
    for low in range(0, attention.shape[0], step):
        span = slice(low, low + step)
        normed, _ = normed_rows(attention[span, :])
        gate_grad[span, :] = (out_grad[span, :].astype(F32) * normed * gain_row).astype(BF16)


def backward_query_kernel(hop_list, heads, scaling, *refs):
    count = len(hop_list)
    table, near, masks, refs = refs[0], refs[1], refs[2 : 2 + count], refs[2 + count :]
    query, grad, keys, values = refs[0], refs[1], refs[2 : 2 + count], refs[2 + count : 2 + 2 * count]
    gain_in, query_out, small_out = refs[2 + 2 * count :]
    rows, width = query.shape[0], query.shape[1] // heads
    pairs = [Pair(mask, table, heads, hops, near=near) for mask, hops in zip(masks, hop_list)]
    lanes = small_out.shape[1]
    lines = gain_in.shape[1] // lanes
    levels = small_out.shape[0] - lines
    lane = lax.broadcasted_iota(jnp.int32, (levels, lanes), 1)
    level_row = lax.broadcasted_iota(jnp.int32, (levels, lanes), 0)
    group = lax.broadcasted_iota(jnp.int32, (8, rows), 0)
    distance = (group - lax.broadcasted_iota(jnp.int32, (8, rows), 1)) & (rows - 1)
    bucket = sum((distance >= 2**level).astype(jnp.int32) for level in range(levels - 1))
    own = pairs[0].distance >= 0
    bias_total = [jnp.zeros((levels, lanes), F32)]

    def bias_sums(grads):
        close = jnp.where(own, grads[0], grads[1])
        rest = sum(grads[2:], jnp.where(own, grads[1], 0.0))
        by_place, far = jnp.zeros((8, rows), F32), jnp.zeros((8, rows), F32)
        for low in range(0, rows, 8):
            part = close[low : low + 8, :]
            by_place = by_place + (pltpu.roll(part, rows - low, 1) if low else part)
            far = far + rest[low : low + 8, :]
        sums = jnp.where(level_row == levels - 1, jnp.sum(far, axis=0, keepdims=True), 0.0)
        for level in range(levels):
            row = jnp.sum(jnp.where(bucket == level, by_place, 0.0), axis=0, keepdims=True)
            sums = sums + jnp.where(level_row == level, row, 0.0)
        return sums

    def scores(head):
        cols = columns(head, width)
        query_h, grad_h = query[:, cols], grad[:, cols]
        return [
            (contract(query_h, key[:, cols], 1, 1), contract(grad_h, value[:, cols], 1, 1))
            for key, value in zip(keys, values)
        ]

    def differentiate(head, found):
        cols = columns(head, width)
        query_part, grads = None, []
        for pair, key, (score, weight_grad) in zip(pairs, keys, found):
            half = pair.half_logits(score, head, scaling)
            grads.append(weight_grad * (slope_of(half, jnp.tanh(half)) * pair.mask))
            added = contract(grads[-1].astype(BF16), key[:, cols], 1, 0)
            query_part = added if query_part is None else query_part + added
        query_out[:, cols] = (query_part * scaling).astype(BF16)
        sums = jnp.sum(bias_sums(grads), axis=1, keepdims=True)
        bias_total[0] = jnp.where(lane == head, sums, bias_total[0])

    in_stages(heads, scores, differentiate, 1)
    for line in range(lines):
        small_out[line : line + 1, :] = gain_in[:, line * lanes : (line + 1) * lanes]
    small_out[lines:, :] = bias_total[0]


def add_key_grads(hops, heads, scaling, table, mask, query, grad, key, value, sums, store):
    width = query.shape[1] // heads
    pair = Pair(mask, table, heads, hops, True)

    def scores(head):
        cols = columns(head, width)
        score = contract(key[:, cols], query[:, cols], 1, 1)
        return score, contract(value[:, cols], grad[:, cols], 1, 1)

    def differentiate(head, found):
        cols = columns(head, width)
        half = pair.half_logits(found[0], head, scaling)
        tanh = jnp.tanh(half)
        rounded = (found[1] * (slope_of(half, tanh) * pair.mask)).astype(BF16)
        weights = ((half + half * tanh) * pair.mask).astype(BF16)
        parts = [contract(rounded, query[:, cols], 1, 0), contract(weights, grad[:, cols], 1, 0)]
        store(head, cols, *[part + held[:, cols] for part, held in zip(parts, sums)] or parts)

    in_stages(heads, scores, differentiate)


def backward_key_kernel(hops, heads, scaling, *refs):
    key_out, value_out = refs[-2:]

    def store(head, cols, key_part, value_part):
        key_out[:, cols] = key_part
        value_out[:, cols] = value_part

    add_key_grads(hops, heads, scaling, *refs[:6], refs[6:-2], store)


def last_kernel(hops, heads, scaling, *refs):
    pieces, outs, held = refs[8:-9], refs[-9:-5], refs[-5:-1]
    written = refs[-1]
    copies = []
    group = 2

    def write(at, cols):
        source, target = held[at].at[:, cols], outs[at].at[:, cols]
        copies.append(pltpu.make_async_copy(source, target, written.at[len(copies)]))
        copies[-1].start()

    def store(head, cols, key_part, value_part):
        held[0][:, cols] = (key_part * scaling).astype(BF16)
        held[1][:, cols] = value_part.astype(BF16)
        if (head + 1) % group == 0:
            done = slice(cols.stop - group * (cols.stop - cols.start), cols.stop)
            write(0, done)
            write(1, done)

    total = added_up([piece[...] for piece in pieces])
    lines = held[2].shape[0]
    held[2][...] = total[:lines]
    held[3][...] = total[lines:, :heads]
    for at in (2, 3):
        write(at, slice(0, held[at].shape[1]))
    add_key_grads(hops, heads, scaling, *refs[:6], refs[6:8], store)
    for copy in copies:
        copy.wait()


def on_device(kernel, outs, args, smem=(), ahead=(), far=(), far_outs=0, scratch=()):
    count = len(smem) + len(far) + len(args)
    far = [pltpu.with_memory_space_constraint(array, pltpu.HBM) for array in far]

    def body(*refs):
        kernel(*refs[:count], *refs[count + len(ahead) :])

    vmem, anywhere = pl.BlockSpec(memory_space=pltpu.VMEM), pl.BlockSpec(memory_space=pl.ANY)
    return pl.pallas_call(
        body,
        out_shape=outs,
        in_specs=[pl.BlockSpec(memory_space=pltpu.SMEM)] * len(smem)
        + [pl.BlockSpec(memory_space=pltpu.HBM)] * len(far)
        + [vmem] * len(args)
        + [anywhere] * len(ahead),
        out_specs=[anywhere] * far_outs + [vmem] * (len(outs) - far_outs),
        scratch_shapes=scratch,
        compiler_params=pltpu.CompilerParams(vmem_limit_bytes=VMEM_LIMIT),
        cost_estimate=pl.CostEstimate(flops=1000000, bytes_accessed=100000, transcendentals=0),
    )(*smem, *far, *args, *ahead)


def rounds_of(axes):
    rounds = []
    for axis in axes:
        size = lax.axis_size(axis)
        step = 1
        while step < size:
            radix = 4 if size // step >= 4 else 2
            rounds.append((axis, [step * at for at in range(1, radix)]))
            step = radix * step
    return rounds


def exchanged(array, axis, distances):
    size = lax.axis_size(axis)
    return [array] + [
        lax.ppermute(array, axis, [(i, i ^ distance) for i in range(size)])
        for distance in distances
    ]


def added_up(pieces):
    while len(pieces) > 1:
        pieces = [left + right for left, right in zip(pieces[::2], pieces[1::2])]
    return pieces[0]


def local(queries, key_rows, value_rows, update_gate, out_grad, user_lengths, rel_bias, norm_gain):
    rows, features = queries.shape[1:]
    levels, heads = rel_bias.shape
    scaling = (features // heads) ** (-0.5)
    reach = min(3, lax.axis_size("ctx") // 2)
    wide = jax.ShapeDtypeStruct((rows, features), F32)
    narrow = jax.ShapeDtypeStruct((rows, features), BF16)
    inputs = (queries[0], key_rows[0], value_rows[0], update_gate[0], out_grad[0])
    gain = norm_gain[None]

    arrived = [passed_along(inputs[at], "ctx", by) for at, by in ((1, 1), (2, 1), (0, -1))]

    hop_list = tuple(range(reach + 1))
    plan = [(0, hops, False) for hops in hop_list] + [(hops, hops, True) for hops in hop_list]
    outs = [jax.ShapeDtypeStruct((count * heads, rows), F32) for count in (levels, rows)]
    outs += [jax.ShapeDtypeStruct((rows, rows), F32)] * len(plan)
    outs += [narrow] * len(inputs) + [wide]
    table, near, *found = on_device(
        partial(first_kernel, plan, heads, scaling),
        outs,
        (),
        (user_lengths, rel_bias),
        far=inputs,
        ahead=arrived,
        scratch=[pltpu.SemaphoreType.DMA((len(inputs),))],
    )
    masks, flipped = found[: reach + 1], found[reach + 1 : 2 * reach + 2]
    query, key, value, gate, grad, attention = found[2 * reach + 2 :]

    later_queries = [query, *arrived[2:]]
    keys, values = [key, *arrived[:1]], [value, *arrived[1:2]]
    for hops in range(1, reach):
        keys.append(passed_along(keys[-1], "ctx", 1))
        values.append(passed_along(values[-1], "ctx", 1))
        later_queries.append(passed_along(later_queries[-1], "ctx", -1))
    for hops in range(1, reach):
        (attention,) = on_device(
            partial(forward_kernel, hops, heads, scaling),
            [wide],
            (table, near, masks[hops], query, keys[hops], values[hops], attention),
            ahead=later_queries[hops : hops + 1],
        )
    attention, attn_grad, gain_part = on_device(
        partial(norm_kernel, reach, heads, scaling),
        [wide, narrow, jax.ShapeDtypeStruct((1, features), F32)],
        (table, near, masks[-1], query, keys[-1], values[-1], attention, grad, gate, gain),
        ahead=later_queries[reach:],
    )

    lanes = features // 8
    query_grad, sums = on_device(
        partial(backward_query_kernel, hop_list, heads, scaling),
        [narrow, jax.ShapeDtypeStruct((8 + levels, lanes), F32)],
        (table, near, *masks, query, attn_grad, *keys, *values, gain_part),
    )
    later_grads = [attn_grad, passed_along(attn_grad, "ctx", -1)]
    pieces = [sums]
    first_pieces = None
    for number, (axis, distances) in enumerate(rounds_of(("ctx", "dp")), 1):
        pieces = exchanged(added_up(pieces), axis, distances)
        if number < reach:
            arrived, *pieces = lax.optimization_barrier((later_grads[-1], *pieces))
            later_grads.append(passed_along(arrived, "ctx", -1))
        first_pieces = first_pieces or pieces[1:2]
    key_grads = ()
    for hops in range(reach):
        key_grads = on_device(
            partial(backward_key_kernel, hops, heads, scaling),
            [wide] * 2,
            (table, flipped[hops], later_queries[hops], later_grads[hops], key, value, *key_grads),
            ahead=first_pieces,
        )
    (gate_grad,) = on_device(gate_kernel, [narrow], (attention, grad, gain), ahead=key_grads[:1])
    key_grad, value_grad, gain_grad, bias_grad = on_device(
        partial(last_kernel, reach, heads, scaling),
        [
            narrow,
            narrow,
            jax.ShapeDtypeStruct((8, lanes), F32),
            jax.ShapeDtypeStruct((levels, heads), F32),
        ],
        (
            table,
            flipped[reach],
            later_queries[reach],
            later_grads[reach],
            key,
            value,
            *key_grads,
            *pieces,
        ),
        far_outs=4,
        scratch=[pltpu.VMEM((rows, features), BF16)] * 2
        + [pltpu.VMEM((8, lanes), F32), pltpu.VMEM((levels, heads), F32)]
        + [pltpu.SemaphoreType.DMA((heads + 2,))],
    )
    return (
        query_grad[None],
        key_grad[None],
        value_grad[None],
        gate_grad[None],
        bias_grad,
        gain_grad.reshape(features),
    )


def solution(mesh):
    in_specs = (
        P(("groups", "dp"), "ctx", None),
        P(("groups", "dp"), "ctx", None),
        P(("groups", "dp"), "ctx", None),
        P(("groups", "dp"), "ctx", None),
        P(("groups", "dp"), "ctx", None),
        P(("groups", "dp"), None),
        P(),
        P(),
    )
    out_specs = (
        P(("groups", "dp"), "ctx", None),
        P(("groups", "dp"), "ctx", None),
        P(("groups", "dp"), "ctx", None),
        P(("groups", "dp"), "ctx", None),
        P("groups", None),
        P("groups"),
    )
    return jax.shard_map(local, mesh=mesh, in_specs=in_specs, out_specs=out_specs, check_vma=False)
```

```python
from functools import partial

import jax
import jax.numpy as jnp
from jax import lax
from jax.experimental import pallas as pl
from jax.experimental.pallas import tpu as pltpu
from jax.sharding import PartitionSpec as P

EPSILON = 1e-05
VMEM_LIMIT = 24 * 1024 * 1024
F32 = jnp.float32
BF16 = jnp.bfloat16


def passed_along(array, axis, by):
    size = lax.axis_size(axis)
    pairs = [(i, i + by) for i in range(size) if 0 <= i + by < size]
    return lax.ppermute(array, axis, pairs)


def contract(left, right, left_dim, right_dim):
    return lax.dot_general(
        left, right, (((left_dim,), (right_dim,)), ((), ())), preferred_element_type=F32
    )


def user_starts(lengths, query_pos):
    end = jnp.int32(0)
    start = jnp.zeros(query_pos.shape, jnp.int32)
    for user in range(lengths.shape[1]):
        end = end + lengths[0, user]
        start = jnp.where(query_pos >= end, end, start)
    return start


class Pair:
    def __init__(self, mask, table, heads, hops, flipped=False, near=None):
        rows = mask.shape[0]
        self.table, self.heads, self.levels = table, heads, table.shape[0] // heads
        self.mask, self.hops, self.near = mask[...], hops, near
        self.far = (hops - 1) * rows + 1 >= 2 ** (self.levels - 2)
        if not self.far:
            query_dim, key_dim = (1, 0) if flipped else (0, 1)
            query_row = lax.broadcasted_iota(jnp.int32, mask.shape, query_dim)
            key_row = lax.broadcasted_iota(jnp.int32, mask.shape, key_dim)
            self.distance = query_row - key_row + hops * rows

    def half_bias(self, head):
        def level_row(level):
            at = level * self.heads + head
            return self.table[at : at + 1, :]

        value = level_row(self.levels - 1)
        if self.far:
            return value
        if self.near is not None:
            rows = self.mask.shape[0]
            close = self.near[head * rows : (head + 1) * rows, :]
            return close if self.hops == 0 else jnp.where(self.distance < rows, close, value)
        for level in range(self.levels - 2, -1, -1):
            value = jnp.where(self.distance < 2**level, level_row(level), value)
        return value

    def half_logits(self, scores, head, scaling):
        return scores * (0.5 * scaling) + self.half_bias(head)


def slope_of(half, tanh):
    return (0.5 + 0.5 * tanh) * (1.0 + half * (1.0 - tanh))


def columns(head, width):
    return slice(head * width, (head + 1) * width)


def in_stages(count, first, second, ahead=3):
    held = [first(i) for i in range(min(ahead, count))]
    for i in range(count):
        if i + ahead < count:
            held.append(first(i + ahead))
        second(i, held.pop(0))


def attend(pairs, heads, scaling, query, keys, values, total, out):
    width = query.shape[1] // heads

    def scores(head):
        cols = columns(head, width)
        return [contract(query[:, cols], key[:, cols], 1, 1) for key in keys]

    def weigh(head, found):
        cols = columns(head, width)
        part = None if total is None else total[:, cols]
        for pair, score, value in zip(pairs, found, values):
            half = pair.half_logits(score, head, scaling)
            weights = ((half + half * jnp.tanh(half)) * pair.mask).astype(BF16)
            added = contract(weights, value[:, cols], 1, 0)
            part = added if part is None else part + added
        out[:, cols] = part.astype(out.dtype)

    in_stages(heads, scores, weigh)


def first_kernel(plan, heads, scaling, lengths, bias, *refs):
    inputs, refs = refs[:5], refs[5:]
    table, near, masks, refs = refs[0], refs[1], refs[2 : 2 + len(plan)], refs[2 + len(plan) :]
    held, out, arrived = refs[:5], refs[5], refs[6]
    copies = [
        pltpu.make_async_copy(source, target, arrived.at[at])
        for at, (source, target) in enumerate(zip(inputs, held))
    ]
    for copy in copies:
        copy.start()
    levels = bias.shape[0]
    for level in range(levels):
        for head in range(heads):
            at = level * heads + head
            table[at : at + 1, :] = jnp.full((1, table.shape[1]), 0.5 * bias[level, head], F32)
    rows = masks[0].shape[0]
    apart = lax.broadcasted_iota(jnp.int32, (rows, rows), 0)
    apart = (apart - lax.broadcasted_iota(jnp.int32, (rows, rows), 1)) & (rows - 1)
    for head in range(heads):
        value = table[(levels - 1) * heads + head : (levels - 1) * heads + head + 1, :]
        for level in range(levels - 2, -1, -1):
            at = level * heads + head
            value = jnp.where(apart < 2**level, table[at : at + 1, :], value)
        near[head * rows : (head + 1) * rows, :] = value
    for (block, hops, flipped), mask in zip(plan, masks):
        query_dim, key_dim = (1, 0) if flipped else (0, 1)
        line = (1, rows) if flipped else (rows, 1)
        first = (lax.axis_index("ctx") + block) * rows
        query_pos = first + lax.broadcasted_iota(jnp.int32, line, query_dim)
        key_pos = first - hops * rows + lax.broadcasted_iota(jnp.int32, mask.shape, key_dim)
        seen = (key_pos >= user_starts(lengths, query_pos)) & (key_pos <= query_pos)
        mask[...] = jnp.where(seen, 1.0, 0.0).astype(F32)
    for copy in copies:
        copy.wait()
    query, key, value = held[:3]
    pair = Pair(masks[0], table, heads, 0, near=near)
    attend([pair], heads, scaling, query, [key], [value], None, out)


def forward_kernel(hops, heads, scaling, table, near, mask, query, key, value, total, out):
    pair = Pair(mask, table, heads, hops, near=near)
    attend([pair], heads, scaling, query, [key], [value], total, out)


def normed_rows(attention):
    center = attention - jnp.mean(attention, axis=1, keepdims=True)
    inverse = lax.rsqrt(jnp.mean(center * center, axis=1, keepdims=True) + EPSILON)
    return center * inverse, inverse


def norm_kernel(hops, heads, scaling, *refs):
    out_grad, update_gate, gain, attention, attn_grad, gain_grad = refs[-6:]
    forward_kernel(hops, heads, scaling, *refs[:-6], attention)
    rows, features = attention.shape
    step = 16
    gain_row = gain[...]
    gain_sum = jnp.zeros((8, features), F32)
    for low in range(0, rows, step):
        span = slice(low, low + step)
        normed, inverse = normed_rows(attention[span, :])
        gated = out_grad[span, :].astype(F32) * update_gate[span, :].astype(F32)
        product = gated * normed
        for part in range(0, step, 8):
            gain_sum = gain_sum + product[part : part + 8, :]
        pushed = gated * gain_row
        attn_grad[span, :] = (
            inverse
            * (
                pushed
                - jnp.mean(pushed, axis=1, keepdims=True)
                - normed * jnp.mean(pushed * normed, axis=1, keepdims=True)
            )
        ).astype(BF16)
    gain_grad[...] = jnp.sum(gain_sum, axis=0, keepdims=True)


def gate_kernel(attention, out_grad, gain, gate_grad):
    step = 16
    gain_row = gain[...]
    for low in range(0, attention.shape[0], step):
        span = slice(low, low + step)
        normed, _ = normed_rows(attention[span, :])
        gate_grad[span, :] = (out_grad[span, :].astype(F32) * normed * gain_row).astype(BF16)


def backward_query_kernel(hop_list, heads, scaling, *refs):
    count = len(hop_list)
    table, near, masks, refs = refs[0], refs[1], refs[2 : 2 + count], refs[2 + count :]
    query, grad, keys, values = refs[0], refs[1], refs[2 : 2 + count], refs[2 + count : 2 + 2 * count]
    gain_in, query_out, small_out = refs[2 + 2 * count :]
    rows, width = query.shape[0], query.shape[1] // heads
    pairs = [Pair(mask, table, heads, hops, near=near) for mask, hops in zip(masks, hop_list)]
    lanes = small_out.shape[1]
    lines = gain_in.shape[1] // lanes
    levels = small_out.shape[0] - lines
    lane = lax.broadcasted_iota(jnp.int32, (levels, lanes), 1)
    level_row = lax.broadcasted_iota(jnp.int32, (levels, lanes), 0)
    group = lax.broadcasted_iota(jnp.int32, (8, rows), 0)
    distance = (group - lax.broadcasted_iota(jnp.int32, (8, rows), 1)) & (rows - 1)
    bucket = sum((distance >= 2**level).astype(jnp.int32) for level in range(levels - 1))
    own = pairs[0].distance >= 0
    bias_total = [jnp.zeros((levels, lanes), F32)]

    def bias_sums(grads):
        close = jnp.where(own, grads[0], grads[1])
        rest = sum(grads[2:], jnp.where(own, grads[1], 0.0))
        by_place, far = jnp.zeros((8, rows), F32), jnp.zeros((8, rows), F32)
        for low in range(0, rows, 8):
            part = close[low : low + 8, :]
            by_place = by_place + (pltpu.roll(part, rows - low, 1) if low else part)
            far = far + rest[low : low + 8, :]
        sums = jnp.where(level_row == levels - 1, jnp.sum(far, axis=0, keepdims=True), 0.0)
        for level in range(levels):
            row = jnp.sum(jnp.where(bucket == level, by_place, 0.0), axis=0, keepdims=True)
            sums = sums + jnp.where(level_row == level, row, 0.0)
        return sums

    def scores(head):
        cols = columns(head, width)
        query_h, grad_h = query[:, cols], grad[:, cols]
        return [
            (contract(query_h, key[:, cols], 1, 1), contract(grad_h, value[:, cols], 1, 1))
            for key, value in zip(keys, values)
        ]

    def differentiate(head, found):
        cols = columns(head, width)
        query_part, grads = None, []
        for pair, key, (score, weight_grad) in zip(pairs, keys, found):
            half = pair.half_logits(score, head, scaling)
            grads.append(weight_grad * (slope_of(half, jnp.tanh(half)) * pair.mask))
            added = contract(grads[-1].astype(BF16), key[:, cols], 1, 0)
            query_part = added if query_part is None else query_part + added
        query_out[:, cols] = (query_part * scaling).astype(BF16)
        sums = jnp.sum(bias_sums(grads), axis=1, keepdims=True)
        bias_total[0] = jnp.where(lane == head, sums, bias_total[0])

    in_stages(heads, scores, differentiate, 1)
    for line in range(lines):
        small_out[line : line + 1, :] = gain_in[:, line * lanes : (line + 1) * lanes]
    small_out[lines:, :] = bias_total[0]


def add_key_grads(hops, heads, scaling, table, mask, query, grad, key, value, sums, store):
    width = query.shape[1] // heads
    pair = Pair(mask, table, heads, hops, True)

    def scores(head):
        cols = columns(head, width)
        score = contract(key[:, cols], query[:, cols], 1, 1)
        return score, contract(value[:, cols], grad[:, cols], 1, 1)

    def differentiate(head, found):
        cols = columns(head, width)
        half = pair.half_logits(found[0], head, scaling)
        tanh = jnp.tanh(half)
        rounded = (found[1] * (slope_of(half, tanh) * pair.mask)).astype(BF16)
        weights = ((half + half * tanh) * pair.mask).astype(BF16)
        parts = [contract(rounded, query[:, cols], 1, 0), contract(weights, grad[:, cols], 1, 0)]
        store(head, cols, *[part + held[:, cols] for part, held in zip(parts, sums)] or parts)

    in_stages(heads, scores, differentiate)


def backward_key_kernel(hops, heads, scaling, *refs):
    key_out, value_out = refs[-2:]

    def store(head, cols, key_part, value_part):
        key_out[:, cols] = key_part
        value_out[:, cols] = value_part

    add_key_grads(hops, heads, scaling, *refs[:6], refs[6:-2], store)


def last_kernel(hops, heads, scaling, *refs):
    outs, held, written = refs[-5:-3], refs[-3:-1], refs[-1]
    copies = []
    group = 2

    def store(head, cols, key_part, value_part):
        held[0][:, cols] = (key_part * scaling).astype(BF16)
        held[1][:, cols] = value_part.astype(BF16)
        if (head + 1) % group == 0:
            done = slice(cols.stop - group * (cols.stop - cols.start), cols.stop)
            for source, target in zip(held, outs):
                at = written.at[len(copies)]
                copies.append(pltpu.make_async_copy(source.at[:, done], target.at[:, done], at))
                copies[-1].start()

    add_key_grads(hops, heads, scaling, *refs[:6], refs[6:-5], store)
    for copy in copies:
        copy.wait()


def sum_kernel(*refs):
    gain_out, bias_out = refs[-2:]
    total = added_up([piece[...] for piece in refs[:-2]])
    lines = gain_out.shape[0]
    gain_out[...] = total[:lines]
    bias_out[...] = total[lines:, : bias_out.shape[1]]


def on_device(kernel, outs, args, smem=(), ahead=(), far=(), far_outs=0, scratch=()):
    count = len(smem) + len(far) + len(args)
    far = [pltpu.with_memory_space_constraint(array, pltpu.HBM) for array in far]

    def body(*refs):
        kernel(*refs[:count], *refs[count + len(ahead) :])

    vmem, anywhere = pl.BlockSpec(memory_space=pltpu.VMEM), pl.BlockSpec(memory_space=pl.ANY)
    return pl.pallas_call(
        body,
        out_shape=outs,
        in_specs=[pl.BlockSpec(memory_space=pltpu.SMEM)] * len(smem)
        + [pl.BlockSpec(memory_space=pltpu.HBM)] * len(far)
        + [vmem] * len(args)
        + [anywhere] * len(ahead),
        out_specs=[anywhere] * far_outs + [vmem] * (len(outs) - far_outs),
        scratch_shapes=scratch,
        compiler_params=pltpu.CompilerParams(vmem_limit_bytes=VMEM_LIMIT),
        cost_estimate=pl.CostEstimate(flops=1000000, bytes_accessed=100000, transcendentals=0),
    )(*smem, *far, *args, *ahead)


def rounds_of(axes):
    rounds = []
    for axis in axes:
        size = lax.axis_size(axis)
        step = 1
        while step < size:
            radix = 4 if size // step >= 4 else 2
            rounds.append((axis, [step * at for at in range(1, radix)]))
            step = radix * step
    return rounds


def exchanged(array, axis, distances):
    size = lax.axis_size(axis)
    return [array] + [
        lax.ppermute(array, axis, [(i, i ^ distance) for i in range(size)])
        for distance in distances
    ]


def added_up(pieces):
    while len(pieces) > 1:
        pieces = [left + right for left, right in zip(pieces[::2], pieces[1::2])]
    return pieces[0]


def local(queries, key_rows, value_rows, update_gate, out_grad, user_lengths, rel_bias, norm_gain):
    rows, features = queries.shape[1:]
    levels, heads = rel_bias.shape
    scaling = (features // heads) ** (-0.5)
    reach = min(3, lax.axis_size("ctx") // 2)
    wide = jax.ShapeDtypeStruct((rows, features), F32)
    narrow = jax.ShapeDtypeStruct((rows, features), BF16)
    inputs = (queries[0], key_rows[0], value_rows[0], update_gate[0], out_grad[0])
    gain = norm_gain[None]

    arrived = [passed_along(inputs[at], "ctx", by) for at, by in ((1, 1), (2, 1), (0, -1))]

    hop_list = tuple(range(reach + 1))
    plan = [(0, hops, False) for hops in hop_list] + [(hops, hops, True) for hops in hop_list]
    outs = [jax.ShapeDtypeStruct((count * heads, rows), F32) for count in (levels, rows)]
    outs += [jax.ShapeDtypeStruct((rows, rows), F32)] * len(plan)
    outs += [narrow] * len(inputs) + [wide]
    table, near, *found = on_device(
        partial(first_kernel, plan, heads, scaling),
        outs,
        (),
        (user_lengths, rel_bias),
        far=inputs,
        scratch=[pltpu.SemaphoreType.DMA((len(inputs),))],
    )
    masks, flipped = found[: reach + 1], found[reach + 1 : 2 * reach + 2]
    query, key, value, gate, grad, attention = found[2 * reach + 2 :]

    later_queries = [query, arrived[2]]
    keys, values = [key, arrived[0]], [value, arrived[1]]
    for hops in range(1, reach):
        keys.append(passed_along(keys[-1], "ctx", 1))
        values.append(passed_along(values[-1], "ctx", 1))
        later_queries.append(passed_along(later_queries[-1], "ctx", -1))
    for hops in range(1, reach):
        (attention,) = on_device(
            partial(forward_kernel, hops, heads, scaling),
            [wide],
            (table, near, masks[hops], query, keys[hops], values[hops], attention),
            ahead=later_queries[hops : hops + 1],
        )
    attention, attn_grad, gain_part = on_device(
        partial(norm_kernel, reach, heads, scaling),
        [wide, narrow, jax.ShapeDtypeStruct((1, features), F32)],
        (table, near, masks[-1], query, keys[-1], values[-1], attention, grad, gate, gain),
    )

    lanes = features // 8
    query_grad, sums = on_device(
        partial(backward_query_kernel, hop_list, heads, scaling),
        [narrow, jax.ShapeDtypeStruct((8 + levels, lanes), F32)],
        (table, near, *masks, query, attn_grad, *keys, *values, gain_part),
        ahead=later_queries[reach:],
    )
    later_grads = [attn_grad, passed_along(attn_grad, "ctx", -1)]
    pieces = [sums]
    for axis, distances in rounds_of(("dp",)):
        pieces = exchanged(added_up(pieces), axis, distances)
    first_pieces = pieces[1:2]
    for hops in range(1, reach):
        arrived, *pieces = lax.optimization_barrier((later_grads[-1], *pieces))
        later_grads.append(passed_along(arrived, "ctx", -1))
    key_grads = ()
    for hops in range(reach):
        key_grads = on_device(
            partial(backward_key_kernel, hops, heads, scaling),
            [wide] * 2,
            (table, flipped[hops], later_queries[hops], later_grads[hops], key, value, *key_grads),
            ahead=first_pieces,
        )
    (gate_grad,) = on_device(gate_kernel, [narrow], (attention, grad, gain), ahead=key_grads[:1])
    (later_grads[-1], gate_grad, key_grads), *pieces = lax.optimization_barrier(
        ((later_grads[-1], gate_grad, key_grads), *pieces)
    )
    for axis, distances in rounds_of(("ctx",)):
        pieces = exchanged(added_up(pieces), axis, distances)
    key_grad, value_grad = on_device(
        partial(last_kernel, reach, heads, scaling),
        [narrow, narrow],
        (
            table,
            flipped[reach],
            later_queries[reach],
            later_grads[reach],
            key,
            value,
            *key_grads,
        ),
        far_outs=2,
        scratch=[pltpu.VMEM((rows, features), BF16)] * 2 + [pltpu.SemaphoreType.DMA((heads,))],
    )
    gain_grad, bias_grad = on_device(
        sum_kernel,
        [jax.ShapeDtypeStruct((8, lanes), F32), jax.ShapeDtypeStruct((levels, heads), F32)],
        pieces,
    )
    return (
        query_grad[None],
        key_grad[None],
        value_grad[None],
        gate_grad[None],
        bias_grad,
        gain_grad.reshape(features),
    )


def solution(mesh):
    in_specs = (
        P(("groups", "dp"), "ctx", None),
        P(("groups", "dp"), "ctx", None),
        P(("groups", "dp"), "ctx", None),
        P(("groups", "dp"), "ctx", None),
        P(("groups", "dp"), "ctx", None),
        P(("groups", "dp"), None),
        P(),
        P(),
    )
    out_specs = (
        P(("groups", "dp"), "ctx", None),
        P(("groups", "dp"), "ctx", None),
        P(("groups", "dp"), "ctx", None),
        P(("groups", "dp"), "ctx", None),
        P("groups", None),
        P("groups"),
    )
    return jax.shard_map(local, mesh=mesh, in_specs=in_specs, out_specs=out_specs, check_vma=False)
```

```python
from functools import partial

import jax
import jax.numpy as jnp
from jax import lax
from jax.experimental import pallas as pl
from jax.experimental.pallas import tpu as pltpu
from jax.sharding import PartitionSpec as P

EPSILON = 1e-05
VMEM_LIMIT = 24 * 1024 * 1024
F32 = jnp.float32
BF16 = jnp.bfloat16


def passed_along(array, axis, by):
    size = lax.axis_size(axis)
    pairs = [(i, i + by) for i in range(size) if 0 <= i + by < size]
    return lax.ppermute(array, axis, pairs)


def contract(left, right, left_dim, right_dim):
    return lax.dot_general(
        left, right, (((left_dim,), (right_dim,)), ((), ())), preferred_element_type=F32
    )


def user_starts(lengths, query_pos):
    end = jnp.int32(0)
    start = jnp.zeros(query_pos.shape, jnp.int32)
    for user in range(lengths.shape[1]):
        end = end + lengths[0, user]
        start = jnp.where(query_pos >= end, end, start)
    return start


class Pair:
    def __init__(self, mask, table, heads, hops, flipped=False, near=None):
        rows = mask.shape[0]
        self.table, self.heads, self.levels = table, heads, table.shape[0] // heads
        self.mask, self.hops, self.near = mask[...], hops, near
        self.far = (hops - 1) * rows + 1 >= 2 ** (self.levels - 2)
        if not self.far:
            query_dim, key_dim = (1, 0) if flipped else (0, 1)
            query_row = lax.broadcasted_iota(jnp.int32, mask.shape, query_dim)
            key_row = lax.broadcasted_iota(jnp.int32, mask.shape, key_dim)
            self.distance = query_row - key_row + hops * rows

    def half_bias(self, head):
        def level_row(level):
            at = level * self.heads + head
            return self.table[at : at + 1, :]

        value = level_row(self.levels - 1)
        if self.far:
            return value
        if self.near is not None:
            rows = self.mask.shape[0]
            close = self.near[head * rows : (head + 1) * rows, :]
            return close if self.hops == 0 else jnp.where(self.distance < rows, close, value)
        for level in range(self.levels - 2, -1, -1):
            value = jnp.where(self.distance < 2**level, level_row(level), value)
        return value

    def half_logits(self, scores, head, scaling):
        return scores * (0.5 * scaling) + self.half_bias(head)


def slope_of(half, tanh):
    return (0.5 + 0.5 * tanh) * (1.0 + half * (1.0 - tanh))


def columns(head, width):
    return slice(head * width, (head + 1) * width)


def in_stages(count, first, second, ahead=3):
    held = [first(i) for i in range(min(ahead, count))]
    for i in range(count):
        if i + ahead < count:
            held.append(first(i + ahead))
        second(i, held.pop(0))


def attend(pairs, heads, scaling, query, keys, values, total, out):
    width = query.shape[1] // heads

    def scores(head):
        cols = columns(head, width)
        return [contract(query[:, cols], key[:, cols], 1, 1) for key in keys]

    def weigh(head, found):
        cols = columns(head, width)
        part = None if total is None else total[:, cols]
        for pair, score, value in zip(pairs, found, values):
            half = pair.half_logits(score, head, scaling)
            weights = ((half + half * jnp.tanh(half)) * pair.mask).astype(BF16)
            added = contract(weights, value[:, cols], 1, 0)
            part = added if part is None else part + added
        out[:, cols] = part.astype(out.dtype)

    in_stages(heads, scores, weigh)


def first_kernel(plan, heads, scaling, lengths, bias, *refs):
    inputs, refs = refs[:5], refs[5:]
    table, near, masks, refs = refs[0], refs[1], refs[2 : 2 + len(plan)], refs[2 + len(plan) :]
    held, out, arrived = refs[:5], refs[5], refs[6]
    copies = [
        pltpu.make_async_copy(source, target, arrived.at[at])
        for at, (source, target) in enumerate(zip(inputs, held))
    ]
    for copy in copies:
        copy.start()
    levels = bias.shape[0]
    for level in range(levels):
        for head in range(heads):
            at = level * heads + head
            table[at : at + 1, :] = jnp.full((1, table.shape[1]), 0.5 * bias[level, head], F32)
    rows = masks[0].shape[0]
    apart = lax.broadcasted_iota(jnp.int32, (rows, rows), 0)
    apart = (apart - lax.broadcasted_iota(jnp.int32, (rows, rows), 1)) & (rows - 1)
    for head in range(heads):
        value = table[(levels - 1) * heads + head : (levels - 1) * heads + head + 1, :]
        for level in range(levels - 2, -1, -1):
            at = level * heads + head
            value = jnp.where(apart < 2**level, table[at : at + 1, :], value)
        near[head * rows : (head + 1) * rows, :] = value
    for (block, hops, flipped), mask in zip(plan, masks):
        query_dim, key_dim = (1, 0) if flipped else (0, 1)
        line = (1, rows) if flipped else (rows, 1)
        first = (lax.axis_index("ctx") + block) * rows
        query_pos = first + lax.broadcasted_iota(jnp.int32, line, query_dim)
        key_pos = first - hops * rows + lax.broadcasted_iota(jnp.int32, mask.shape, key_dim)
        seen = (key_pos >= user_starts(lengths, query_pos)) & (key_pos <= query_pos)
        mask[...] = jnp.where(seen, 1.0, 0.0).astype(F32)
    for copy in copies:
        copy.wait()
    query, key, value = held[:3]
    pair = Pair(masks[0], table, heads, 0, near=near)
    attend([pair], heads, scaling, query, [key], [value], None, out)


def forward_kernel(hops, heads, scaling, table, near, mask, query, key, value, total, out):
    pair = Pair(mask, table, heads, hops, near=near)
    attend([pair], heads, scaling, query, [key], [value], total, out)


def normed_rows(attention):
    center = attention - jnp.mean(attention, axis=1, keepdims=True)
    inverse = lax.rsqrt(jnp.mean(center * center, axis=1, keepdims=True) + EPSILON)
    return center * inverse, inverse


def norm_kernel(hops, heads, scaling, *refs):
    out_grad, update_gate, gain, attention, attn_grad, gain_grad = refs[-6:]
    forward_kernel(hops, heads, scaling, *refs[:-6], attention)
    rows, features = attention.shape
    step = 16
    gain_row = gain[...]
    gain_sum = jnp.zeros((8, features), F32)
    for low in range(0, rows, step):
        span = slice(low, low + step)
        normed, inverse = normed_rows(attention[span, :])
        gated = out_grad[span, :].astype(F32) * update_gate[span, :].astype(F32)
        product = gated * normed
        for part in range(0, step, 8):
            gain_sum = gain_sum + product[part : part + 8, :]
        pushed = gated * gain_row
        attn_grad[span, :] = (
            inverse
            * (
                pushed
                - jnp.mean(pushed, axis=1, keepdims=True)
                - normed * jnp.mean(pushed * normed, axis=1, keepdims=True)
            )
        ).astype(BF16)
    gain_grad[...] = jnp.sum(gain_sum, axis=0, keepdims=True)


def gate_kernel(attention, out_grad, gain, gate_grad):
    step = 16
    gain_row = gain[...]
    for low in range(0, attention.shape[0], step):
        span = slice(low, low + step)
        normed, _ = normed_rows(attention[span, :])
        gate_grad[span, :] = (out_grad[span, :].astype(F32) * normed * gain_row).astype(BF16)


def backward_query_kernel(hop_list, heads, scaling, *refs):
    count = len(hop_list)
    table, near, masks, refs = refs[0], refs[1], refs[2 : 2 + count], refs[2 + count :]
    query, grad, keys, values = refs[0], refs[1], refs[2 : 2 + count], refs[2 + count : 2 + 2 * count]
    gain_in, query_out, small_out = refs[2 + 2 * count :]
    rows, width = query.shape[0], query.shape[1] // heads
    pairs = [Pair(mask, table, heads, hops, near=near) for mask, hops in zip(masks, hop_list)]
    lanes = small_out.shape[1]
    lines = gain_in.shape[1] // lanes
    levels = small_out.shape[0] - lines
    lane = lax.broadcasted_iota(jnp.int32, (levels, lanes), 1)
    level_row = lax.broadcasted_iota(jnp.int32, (levels, lanes), 0)
    group = lax.broadcasted_iota(jnp.int32, (8, rows), 0)
    distance = (group - lax.broadcasted_iota(jnp.int32, (8, rows), 1)) & (rows - 1)
    bucket = sum((distance >= 2**level).astype(jnp.int32) for level in range(levels - 1))
    own = pairs[0].distance >= 0
    bias_total = [jnp.zeros((levels, lanes), F32)]

    def bias_sums(grads):
        close = jnp.where(own, grads[0], grads[1])
        rest = sum(grads[2:], jnp.where(own, grads[1], 0.0))
        by_place, far = jnp.zeros((8, rows), F32), jnp.zeros((8, rows), F32)
        for low in range(0, rows, 8):
            part = close[low : low + 8, :]
            by_place = by_place + (pltpu.roll(part, rows - low, 1) if low else part)
            far = far + rest[low : low + 8, :]
        sums = jnp.where(level_row == levels - 1, jnp.sum(far, axis=0, keepdims=True), 0.0)
        for level in range(levels):
            row = jnp.sum(jnp.where(bucket == level, by_place, 0.0), axis=0, keepdims=True)
            sums = sums + jnp.where(level_row == level, row, 0.0)
        return sums

    def scores(head):
        cols = columns(head, width)
        query_h, grad_h = query[:, cols], grad[:, cols]
        return [
            (contract(query_h, key[:, cols], 1, 1), contract(grad_h, value[:, cols], 1, 1))
            for key, value in zip(keys, values)
        ]

    def differentiate(head, found):
        cols = columns(head, width)
        query_part, grads = None, []
        for pair, key, (score, weight_grad) in zip(pairs, keys, found):
            half = pair.half_logits(score, head, scaling)
            grads.append(weight_grad * (slope_of(half, jnp.tanh(half)) * pair.mask))
            added = contract(grads[-1].astype(BF16), key[:, cols], 1, 0)
            query_part = added if query_part is None else query_part + added
        query_out[:, cols] = (query_part * scaling).astype(BF16)
        sums = jnp.sum(bias_sums(grads), axis=1, keepdims=True)
        bias_total[0] = jnp.where(lane == head, sums, bias_total[0])

    in_stages(heads, scores, differentiate, 1)
    for line in range(lines):
        small_out[line : line + 1, :] = gain_in[:, line * lanes : (line + 1) * lanes]
    small_out[lines:, :] = bias_total[0]


def add_key_grads(hops, heads, scaling, table, mask, query, grad, key, value, sums, store):
    width = query.shape[1] // heads
    pair = Pair(mask, table, heads, hops, True)

    def scores(head):
        cols = columns(head, width)
        score = contract(key[:, cols], query[:, cols], 1, 1)
        return score, contract(value[:, cols], grad[:, cols], 1, 1)

    def differentiate(head, found):
        cols = columns(head, width)
        half = pair.half_logits(found[0], head, scaling)
        tanh = jnp.tanh(half)
        rounded = (found[1] * (slope_of(half, tanh) * pair.mask)).astype(BF16)
        weights = ((half + half * tanh) * pair.mask).astype(BF16)
        parts = [contract(rounded, query[:, cols], 1, 0), contract(weights, grad[:, cols], 1, 0)]
        store(head, cols, *[part + held[:, cols] for part, held in zip(parts, sums)] or parts)

    in_stages(heads, scores, differentiate)


def backward_key_kernel(hops, heads, scaling, *refs):
    key_out, value_out = refs[-2:]

    def store(head, cols, key_part, value_part):
        key_out[:, cols] = key_part
        value_out[:, cols] = value_part

    add_key_grads(hops, heads, scaling, *refs[:6], refs[6:-2], store)


def last_kernel(hops, heads, scaling, *refs):
    outs, held, written = refs[-5:-3], refs[-3:-1], refs[-1]
    copies = []
    group = 2

    def store(head, cols, key_part, value_part):
        held[0][:, cols] = (key_part * scaling).astype(BF16)
        held[1][:, cols] = value_part.astype(BF16)
        if (head + 1) % group == 0:
            done = slice(cols.stop - group * (cols.stop - cols.start), cols.stop)
            for source, target in zip(held, outs):
                at = written.at[len(copies)]
                copies.append(pltpu.make_async_copy(source.at[:, done], target.at[:, done], at))
                copies[-1].start()

    add_key_grads(hops, heads, scaling, *refs[:6], refs[6:-5], store)
    for copy in copies:
        copy.wait()


def sum_kernel(pieces, gain_out, bias_out):
    total = jnp.sum(pieces[...], axis=0)
    lines = gain_out.shape[0]
    gain_out[...] = total[:lines]
    bias_out[...] = total[lines:, : bias_out.shape[1]]


def on_device(kernel, outs, args, smem=(), ahead=(), far=(), far_outs=0, scratch=()):
    count = len(smem) + len(far) + len(args)
    far = [pltpu.with_memory_space_constraint(array, pltpu.HBM) for array in far]

    def body(*refs):
        kernel(*refs[:count], *refs[count + len(ahead) :])

    vmem, anywhere = pl.BlockSpec(memory_space=pltpu.VMEM), pl.BlockSpec(memory_space=pl.ANY)
    return pl.pallas_call(
        body,
        out_shape=outs,
        in_specs=[pl.BlockSpec(memory_space=pltpu.SMEM)] * len(smem)
        + [pl.BlockSpec(memory_space=pltpu.HBM)] * len(far)
        + [vmem] * len(args)
        + [anywhere] * len(ahead),
        out_specs=[anywhere] * far_outs + [vmem] * (len(outs) - far_outs),
        scratch_shapes=scratch,
        compiler_params=pltpu.CompilerParams(vmem_limit_bytes=VMEM_LIMIT),
        cost_estimate=pl.CostEstimate(flops=1000000, bytes_accessed=100000, transcendentals=0),
    )(*smem, *far, *args, *ahead)


def local(queries, key_rows, value_rows, update_gate, out_grad, user_lengths, rel_bias, norm_gain):
    rows, features = queries.shape[1:]
    levels, heads = rel_bias.shape
    scaling = (features // heads) ** (-0.5)
    reach = min(3, lax.axis_size("ctx") // 2)
    wide = jax.ShapeDtypeStruct((rows, features), F32)
    narrow = jax.ShapeDtypeStruct((rows, features), BF16)
    inputs = (queries[0], key_rows[0], value_rows[0], update_gate[0], out_grad[0])
    gain = norm_gain[None]

    arrived = [passed_along(inputs[at], "ctx", by) for at, by in ((1, 1), (2, 1), (0, -1))]

    hop_list = tuple(range(reach + 1))
    plan = [(0, hops, False) for hops in hop_list] + [(hops, hops, True) for hops in hop_list]
    outs = [jax.ShapeDtypeStruct((count * heads, rows), F32) for count in (levels, rows)]
    outs += [jax.ShapeDtypeStruct((rows, rows), F32)] * len(plan)
    outs += [narrow] * len(inputs) + [wide]
    table, near, *found = on_device(
        partial(first_kernel, plan, heads, scaling),
        outs,
        (),
        (user_lengths, rel_bias),
        far=inputs,
        scratch=[pltpu.SemaphoreType.DMA((len(inputs),))],
    )
    masks, flipped = found[: reach + 1], found[reach + 1 : 2 * reach + 2]
    query, key, value, gate, grad, attention = found[2 * reach + 2 :]

    later_queries = [query, arrived[2]]
    keys, values = [key, arrived[0]], [value, arrived[1]]
    for hops in range(1, reach):
        keys.append(passed_along(keys[-1], "ctx", 1))
        values.append(passed_along(values[-1], "ctx", 1))
        later_queries.append(passed_along(later_queries[-1], "ctx", -1))
    for hops in range(1, reach):
        (attention,) = on_device(
            partial(forward_kernel, hops, heads, scaling),
            [wide],
            (table, near, masks[hops], query, keys[hops], values[hops], attention),
            ahead=later_queries[hops : hops + 1],
        )
    attention, attn_grad, gain_part = on_device(
        partial(norm_kernel, reach, heads, scaling),
        [wide, narrow, jax.ShapeDtypeStruct((1, features), F32)],
        (table, near, masks[-1], query, keys[-1], values[-1], attention, grad, gate, gain),
    )

    lanes = features // 8
    query_grad, sums = on_device(
        partial(backward_query_kernel, hop_list, heads, scaling),
        [narrow, jax.ShapeDtypeStruct((8 + levels, lanes), F32)],
        (table, near, *masks, query, attn_grad, *keys, *values, gain_part),
        ahead=later_queries[reach:],
    )
    later_grads = [attn_grad, passed_along(attn_grad, "ctx", -1)]
    for hops in range(1, reach):
        arrived, sums = lax.optimization_barrier((later_grads[-1], sums))
        later_grads.append(passed_along(arrived, "ctx", -1))
    key_grads = ()
    for hops in range(reach):
        key_grads = on_device(
            partial(backward_key_kernel, hops, heads, scaling),
            [wide] * 2,
            (table, flipped[hops], later_queries[hops], later_grads[hops], key, value, *key_grads),
        )
    (gate_grad,) = on_device(gate_kernel, [narrow], (attention, grad, gain), ahead=key_grads[:1])
    sums, key_grads, gate_grad = lax.optimization_barrier((sums, key_grads, gate_grad))
    for axes in [("ctx", "dp")] if lax.axis_size(("ctx", "dp")) <= 16 else ["ctx", "dp"]:
        size = lax.axis_size(axes)
        pieces = lax.all_to_all(jnp.broadcast_to(sums, (size, *sums.shape)), axes, 0, 0)
        sums = jnp.sum(pieces, axis=0)
    key_grad, value_grad = on_device(
        partial(last_kernel, reach, heads, scaling),
        [narrow, narrow],
        (
            table,
            flipped[reach],
            later_queries[reach],
            later_grads[reach],
            key,
            value,
            *key_grads,
        ),
        ahead=[pieces],
        far_outs=2,
        scratch=[pltpu.VMEM((rows, features), BF16)] * 2 + [pltpu.SemaphoreType.DMA((heads,))],
    )
    gain_grad, bias_grad = on_device(
        sum_kernel,
        [jax.ShapeDtypeStruct((8, lanes), F32), jax.ShapeDtypeStruct((levels, heads), F32)],
        [pieces],
    )
    return (
        query_grad[None],
        key_grad[None],
        value_grad[None],
        gate_grad[None],
        bias_grad,
        gain_grad.reshape(features),
    )


def solution(mesh):
    in_specs = (
        P(("groups", "dp"), "ctx", None),
        P(("groups", "dp"), "ctx", None),
        P(("groups", "dp"), "ctx", None),
        P(("groups", "dp"), "ctx", None),
        P(("groups", "dp"), "ctx", None),
        P(("groups", "dp"), None),
        P(),
        P(),
    )
    out_specs = (
        P(("groups", "dp"), "ctx", None),
        P(("groups", "dp"), "ctx", None),
        P(("groups", "dp"), "ctx", None),
        P(("groups", "dp"), "ctx", None),
        P("groups", None),
        P("groups"),
    )
    return jax.shard_map(local, mesh=mesh, in_specs=in_specs, out_specs=out_specs, check_vma=False)
```

```python
from functools import partial

import jax
import jax.numpy as jnp
from jax import lax
from jax.experimental import pallas as pl
from jax.experimental.pallas import tpu as pltpu
from jax.sharding import PartitionSpec as P

EPSILON = 1e-05
VMEM_LIMIT = 24 * 1024 * 1024
LONG = 4 * 10**9
F32 = jnp.float32
BF16 = jnp.bfloat16


def passed_along(array, axis, by):
    size = lax.axis_size(axis)
    pairs = [(i, i + by) for i in range(size) if 0 <= i + by < size]
    return lax.ppermute(array, axis, pairs)


def contract(left, right, left_dim, right_dim):
    return lax.dot_general(
        left, right, (((left_dim,), (right_dim,)), ((), ())), preferred_element_type=F32
    )


def user_starts(lengths, query_pos):
    end = jnp.int32(0)
    start = jnp.zeros(query_pos.shape, jnp.int32)
    for user in range(lengths.shape[1]):
        end = end + lengths[0, user]
        start = jnp.where(query_pos >= end, end, start)
    return start


class Pair:
    def __init__(self, mask, table, heads, hops, flipped=False, near=None):
        rows = mask.shape[0]
        self.table, self.heads, self.levels = table, heads, table.shape[0] // heads
        self.mask, self.hops, self.near = mask[...], hops, near
        self.far = (hops - 1) * rows + 1 >= 2 ** (self.levels - 2)
        if not self.far:
            query_dim, key_dim = (1, 0) if flipped else (0, 1)
            query_row = lax.broadcasted_iota(jnp.int32, mask.shape, query_dim)
            key_row = lax.broadcasted_iota(jnp.int32, mask.shape, key_dim)
            self.distance = query_row - key_row + hops * rows

    def half_bias(self, head):
        def level_row(level):
            at = level * self.heads + head
            return self.table[at : at + 1, :]

        value = level_row(self.levels - 1)
        if self.far:
            return value
        if self.near is not None:
            rows = self.mask.shape[0]
            close = self.near[head * rows : (head + 1) * rows, :]
            return close if self.hops == 0 else jnp.where(self.distance < rows, close, value)
        for level in range(self.levels - 2, -1, -1):
            value = jnp.where(self.distance < 2**level, level_row(level), value)
        return value

    def half_logits(self, scores, head, scaling):
        return scores * (0.5 * scaling) + self.half_bias(head)


def slope_of(half, tanh):
    return (0.5 + 0.5 * tanh) * (1.0 + half * (1.0 - tanh))


def columns(head, width):
    return slice(head * width, (head + 1) * width)


def in_stages(count, first, second, ahead=3):
    held = [first(i) for i in range(min(ahead, count))]
    for i in range(count):
        if i + ahead < count:
            held.append(first(i + ahead))
        second(i, held.pop(0))


def attend(pairs, heads, scaling, query, keys, values, total, out):
    width = query.shape[1] // heads

    def scores(head):
        cols = columns(head, width)
        return [contract(query[:, cols], key[:, cols], 1, 1) for key in keys]

    def weigh(head, found):
        cols = columns(head, width)
        part = None if total is None else total[:, cols]
        for pair, score, value in zip(pairs, found, values):
            half = pair.half_logits(score, head, scaling)
            weights = ((half + half * jnp.tanh(half)) * pair.mask).astype(BF16)
            added = contract(weights, value[:, cols], 1, 0)
            part = added if part is None else part + added
        out[:, cols] = part.astype(out.dtype)

    in_stages(heads, scores, weigh)


def first_kernel(plan, heads, scaling, lengths, bias, *refs):
    inputs, refs = refs[:5], refs[5:]
    table, near, masks, refs = refs[0], refs[1], refs[2 : 2 + len(plan)], refs[2 + len(plan) :]
    held, out, arrived = refs[:5], refs[5], refs[6]
    copies = [
        pltpu.make_async_copy(source, target, arrived.at[at])
        for at, (source, target) in enumerate(zip(inputs, held))
    ]
    for copy in copies:
        copy.start()
    levels = bias.shape[0]
    for level in range(levels):
        for head in range(heads):
            at = level * heads + head
            table[at : at + 1, :] = jnp.full((1, table.shape[1]), 0.5 * bias[level, head], F32)
    rows = masks[0].shape[0]
    apart = lax.broadcasted_iota(jnp.int32, (rows, rows), 0)
    apart = (apart - lax.broadcasted_iota(jnp.int32, (rows, rows), 1)) & (rows - 1)
    for head in range(heads):
        value = table[(levels - 1) * heads + head : (levels - 1) * heads + head + 1, :]
        for level in range(levels - 2, -1, -1):
            at = level * heads + head
            value = jnp.where(apart < 2**level, table[at : at + 1, :], value)
        near[head * rows : (head + 1) * rows, :] = value
    for (block, hops, flipped), mask in zip(plan, masks):
        query_dim, key_dim = (1, 0) if flipped else (0, 1)
        line = (1, rows) if flipped else (rows, 1)
        first = (lax.axis_index("ctx") + block) * rows
        query_pos = first + lax.broadcasted_iota(jnp.int32, line, query_dim)
        key_pos = first - hops * rows + lax.broadcasted_iota(jnp.int32, mask.shape, key_dim)
        seen = (key_pos >= user_starts(lengths, query_pos)) & (key_pos <= query_pos)
        mask[...] = jnp.where(seen, 1.0, 0.0).astype(F32)
    for copy in copies:
        copy.wait()
    query, key, value = held[:3]
    pair = Pair(masks[0], table, heads, 0, near=near)
    attend([pair], heads, scaling, query, [key], [value], None, out)


def forward_kernel(hops, heads, scaling, table, near, mask, query, key, value, total, out):
    pair = Pair(mask, table, heads, hops, near=near)
    attend([pair], heads, scaling, query, [key], [value], total, out)


def normed_rows(attention):
    center = attention - jnp.mean(attention, axis=1, keepdims=True)
    inverse = lax.rsqrt(jnp.mean(center * center, axis=1, keepdims=True) + EPSILON)
    return center * inverse, inverse


def norm_kernel(hops, heads, scaling, *refs):
    out_grad, update_gate, gain, attention, attn_grad, gain_grad = refs[-6:]
    forward_kernel(hops, heads, scaling, *refs[:-6], attention)
    rows, features = attention.shape
    step = 16
    gain_row = gain[...]
    gain_sum = jnp.zeros((8, features), F32)
    for low in range(0, rows, step):
        span = slice(low, low + step)
        normed, inverse = normed_rows(attention[span, :])
        gated = out_grad[span, :].astype(F32) * update_gate[span, :].astype(F32)
        product = gated * normed
        for part in range(0, step, 8):
            gain_sum = gain_sum + product[part : part + 8, :]
        pushed = gated * gain_row
        attn_grad[span, :] = (
            inverse
            * (
                pushed
                - jnp.mean(pushed, axis=1, keepdims=True)
                - normed * jnp.mean(pushed * normed, axis=1, keepdims=True)
            )
        ).astype(BF16)
    gain_grad[...] = jnp.sum(gain_sum, axis=0, keepdims=True)


def backward_query_kernel(hop_list, heads, scaling, *refs):
    count = len(hop_list)
    table, near, masks, refs = refs[0], refs[1], refs[2 : 2 + count], refs[2 + count :]
    query, grad, keys, values = refs[0], refs[1], refs[2 : 2 + count], refs[2 + count : 2 + 2 * count]
    gain_in, query_out, small_out = refs[2 + 2 * count :]
    rows, width = query.shape[0], query.shape[1] // heads
    pairs = [Pair(mask, table, heads, hops, near=near) for mask, hops in zip(masks, hop_list)]
    lanes = small_out.shape[1]
    lines = gain_in.shape[1] // lanes
    levels = small_out.shape[0] - lines
    lane = lax.broadcasted_iota(jnp.int32, (levels, lanes), 1)
    level_row = lax.broadcasted_iota(jnp.int32, (levels, lanes), 0)
    group = lax.broadcasted_iota(jnp.int32, (8, rows), 0)
    distance = (group - lax.broadcasted_iota(jnp.int32, (8, rows), 1)) & (rows - 1)
    bucket = sum((distance >= 2**level).astype(jnp.int32) for level in range(levels - 1))
    own = pairs[0].distance >= 0
    bias_total = [jnp.zeros((levels, lanes), F32)]

    def bias_sums(grads):
        close = jnp.where(own, grads[0], grads[1])
        rest = sum(grads[2:], jnp.where(own, grads[1], 0.0))
        by_place, far = jnp.zeros((8, rows), F32), jnp.zeros((8, rows), F32)
        for low in range(0, rows, 8):
            part = close[low : low + 8, :]
            by_place = by_place + (pltpu.roll(part, rows - low, 1) if low else part)
            far = far + rest[low : low + 8, :]
        sums = jnp.where(level_row == levels - 1, jnp.sum(far, axis=0, keepdims=True), 0.0)
        for level in range(levels):
            row = jnp.sum(jnp.where(bucket == level, by_place, 0.0), axis=0, keepdims=True)
            sums = sums + jnp.where(level_row == level, row, 0.0)
        return sums

    def scores(head):
        cols = columns(head, width)
        query_h, grad_h = query[:, cols], grad[:, cols]
        return [
            (contract(query_h, key[:, cols], 1, 1), contract(grad_h, value[:, cols], 1, 1))
            for key, value in zip(keys, values)
        ]

    def differentiate(head, found):
        cols = columns(head, width)
        query_part, grads = None, []
        for pair, key, (score, weight_grad) in zip(pairs, keys, found):
            half = pair.half_logits(score, head, scaling)
            grads.append(weight_grad * (slope_of(half, jnp.tanh(half)) * pair.mask))
            added = contract(grads[-1].astype(BF16), key[:, cols], 1, 0)
            query_part = added if query_part is None else query_part + added
        query_out[:, cols] = (query_part * scaling).astype(BF16)
        sums = jnp.sum(bias_sums(grads), axis=1, keepdims=True)
        bias_total[0] = jnp.where(lane == head, sums, bias_total[0])

    in_stages(heads, scores, differentiate, 1)
    for line in range(lines):
        small_out[line : line + 1, :] = gain_in[:, line * lanes : (line + 1) * lanes]
    small_out[lines:, :] = bias_total[0]


def add_key_grads(hops, heads, scaling, table, mask, query, grad, key, value, sums, store):
    width = query.shape[1] // heads
    pair = Pair(mask, table, heads, hops, True)

    def scores(head):
        cols = columns(head, width)
        score = contract(key[:, cols], query[:, cols], 1, 1)
        return score, contract(value[:, cols], grad[:, cols], 1, 1)

    def differentiate(head, found):
        cols = columns(head, width)
        half = pair.half_logits(found[0], head, scaling)
        tanh = jnp.tanh(half)
        rounded = (found[1] * (slope_of(half, tanh) * pair.mask)).astype(BF16)
        weights = ((half + half * tanh) * pair.mask).astype(BF16)
        parts = [contract(rounded, query[:, cols], 1, 0), contract(weights, grad[:, cols], 1, 0)]
        store(head, cols, *[part + held[:, cols] for part, held in zip(parts, sums)] or parts)

    in_stages(heads, scores, differentiate)


def into(key_out, value_out):
    def store(head, cols, key_part, value_part):
        key_out[:, cols] = key_part
        value_out[:, cols] = value_part

    return store


def own_key_kernel(heads, scaling, *refs):
    pieces, (key_out, value_out, shared) = refs[6:-3], refs[-3:]
    shared[...] = added_up([piece[...] for piece in pieces])
    add_key_grads(0, heads, scaling, *refs[:6], (), into(key_out, value_out))


def next_key_kernel(hops, heads, scaling, *refs):
    add_key_grads(hops, heads, scaling, *refs[:6], refs[6:8], into(*refs[8:]))


def gate_and_key_kernel(hops, heads, scaling, *refs):
    attention, out_grad, gain = refs[8:11]
    gate_out, key_out, value_out, held, written = refs[11:]
    step = 16
    gain_row = gain[...]
    for low in range(0, attention.shape[0], step):
        span = slice(low, low + step)
        normed, _ = normed_rows(attention[span, :])
        held[span, :] = (out_grad[span, :].astype(F32) * normed * gain_row).astype(BF16)
    copy = pltpu.make_async_copy(held, gate_out, written)
    copy.start()
    add_key_grads(hops, heads, scaling, *refs[:6], refs[6:8], into(key_out, value_out))
    copy.wait()


def last_kernel(hops, heads, scaling, *refs):
    outs, held, written = refs[-5:-3], refs[-3:-1], refs[-1]
    copies = []
    group = 2

    def store(head, cols, key_part, value_part):
        held[0][:, cols] = (key_part * scaling).astype(BF16)
        held[1][:, cols] = value_part.astype(BF16)
        if (head + 1) % group == 0:
            done = slice(cols.stop - group * (cols.stop - cols.start), cols.stop)
            for source, target in zip(held, outs):
                at = written.at[len(copies)]
                copies.append(pltpu.make_async_copy(source.at[:, done], target.at[:, done], at))
                copies[-1].start()

    add_key_grads(hops, heads, scaling, *refs[:6], refs[6:-5], store)
    for copy in copies:
        copy.wait()


def sum_kernel(*refs):
    gain_out, bias_out = refs[-2:]
    total = added_up([piece[...] for piece in refs[:-2]])
    lines = gain_out.shape[0]
    gain_out[...] = total[:lines]
    bias_out[...] = total[lines:, : bias_out.shape[1]]


def on_device(kernel, outs, args, smem=(), ahead=(), far=(), far_outs=0, scratch=(), flops=1000000):
    count = len(smem) + len(far) + len(args)
    far = [pltpu.with_memory_space_constraint(array, pltpu.HBM) for array in far]

    def body(*refs):
        kernel(*refs[:count], *refs[count + len(ahead) :])

    vmem, anywhere = pl.BlockSpec(memory_space=pltpu.VMEM), pl.BlockSpec(memory_space=pl.ANY)
    return pl.pallas_call(
        body,
        out_shape=outs,
        in_specs=[pl.BlockSpec(memory_space=pltpu.SMEM)] * len(smem)
        + [pl.BlockSpec(memory_space=pltpu.HBM)] * len(far)
        + [vmem] * len(args)
        + [anywhere] * len(ahead),
        out_specs=[anywhere] * far_outs + [vmem] * (len(outs) - far_outs),
        scratch_shapes=scratch,
        compiler_params=pltpu.CompilerParams(vmem_limit_bytes=VMEM_LIMIT),
        cost_estimate=pl.CostEstimate(flops=flops, bytes_accessed=100000, transcendentals=0),
    )(*smem, *far, *args, *ahead)


def added_up(pieces):
    while len(pieces) > 1:
        pieces = [left + right for left, right in zip(pieces[::2], pieces[1::2])]
    return pieces[0]


def exchanged(array, axis):
    size = lax.axis_size(axis)
    return [array] + [
        lax.ppermute(array, axis, [(i, i ^ distance) for i in range(size)])
        for distance in range(1, size)
    ]


def spread(array, axis, helpers):
    size, count = lax.axis_size(axis), lax.axis_size(helpers)
    found = []
    for low in range(0, size, count):
        pairs = [
            (i * count + m, (i ^ (low + m)) * count + m)
            for i in range(size)
            for m in range(min(count, size - low))
        ]
        found.append(lax.ppermute(array, (axis, helpers), pairs))
    return found


def local(queries, key_rows, value_rows, update_gate, out_grad, user_lengths, rel_bias, norm_gain):
    rows, features = queries.shape[1:]
    levels, heads = rel_bias.shape
    scaling = (features // heads) ** (-0.5)
    reach = min(3, lax.axis_size("ctx") // 2)
    wide = jax.ShapeDtypeStruct((rows, features), F32)
    narrow = jax.ShapeDtypeStruct((rows, features), BF16)
    inputs = (queries[0], key_rows[0], value_rows[0], update_gate[0], out_grad[0])
    gain = norm_gain[None]

    arrived = [passed_along(inputs[at], "ctx", by) for at, by in ((1, 1), (2, 1), (0, -1))]

    hop_list = tuple(range(reach + 1))
    plan = [(0, hops, False) for hops in hop_list] + [(hops, hops, True) for hops in hop_list]
    outs = [jax.ShapeDtypeStruct((count * heads, rows), F32) for count in (levels, rows)]
    outs += [jax.ShapeDtypeStruct((rows, rows), F32)] * len(plan)
    outs += [narrow] * len(inputs) + [wide]
    table, near, *found = on_device(
        partial(first_kernel, plan, heads, scaling),
        outs,
        (),
        (user_lengths, rel_bias),
        far=inputs,
        scratch=[pltpu.SemaphoreType.DMA((len(inputs),))],
    )
    masks, flipped = found[: reach + 1], found[reach + 1 : 2 * reach + 2]
    query, key, value, gate, grad, attention = found[2 * reach + 2 :]

    later_queries = [query, arrived[2]]
    keys, values = [key, arrived[0]], [value, arrived[1]]
    for hops in range(1, reach):
        keys.append(passed_along(keys[-1], "ctx", 1))
        values.append(passed_along(values[-1], "ctx", 1))
        later_queries.append(passed_along(later_queries[-1], "ctx", -1))
    for hops in range(1, reach):
        (attention,) = on_device(
            partial(forward_kernel, hops, heads, scaling),
            [wide],
            (table, near, masks[hops], query, keys[hops], values[hops], attention),
            ahead=later_queries[hops : hops + 1],
        )
    attention, attn_grad, gain_part = on_device(
        partial(norm_kernel, reach, heads, scaling),
        [wide, narrow, jax.ShapeDtypeStruct((1, features), F32)],
        (table, near, masks[-1], query, keys[-1], values[-1], attention, grad, gate, gain),
    )

    lanes = features // 8
    query_grad, sums = on_device(
        partial(backward_query_kernel, hop_list, heads, scaling),
        [narrow, jax.ShapeDtypeStruct((8 + levels, lanes), F32)],
        (table, near, *masks, query, attn_grad, *keys, *values, gain_part),
        ahead=later_queries[reach:],
    )
    later_grads = [attn_grad, passed_along(attn_grad, "ctx", -1)]
    sums = added_up(exchanged(sums, "dp"))

    def key_operands(hops):
        later = (later_queries[hops], later_grads[hops])
        return (table, flipped[hops], *later, key, value)

    *key_grads, shared = on_device(
        partial(own_key_kernel, heads, scaling),
        [wide, wide, jax.ShapeDtypeStruct(sums.shape, F32)],
        (*key_operands(0), *spread(sums, "ctx", "dp")),
        flops=LONG,
    )
    pieces = exchanged(shared, "dp")
    for hops in range(1, reach):
        arrived, sums = lax.optimization_barrier((later_grads[hops], sums))
        later_grads.append(passed_along(arrived, "ctx", -1))
        if hops == 1:
            gate_grad, *key_grads = on_device(
                partial(gate_and_key_kernel, hops, heads, scaling),
                [narrow, wide, wide],
                (*key_operands(hops), *key_grads, attention, grad, gain),
                ahead=[shared],
                far_outs=1,
                scratch=[pltpu.VMEM((rows, features), BF16), pltpu.SemaphoreType.DMA(())],
            )
        else:
            key_grads = on_device(
                partial(next_key_kernel, hops, heads, scaling),
                [wide] * 2,
                (*key_operands(hops), *key_grads),
            )
    key_grad, value_grad = on_device(
        partial(last_kernel, reach, heads, scaling),
        [narrow, narrow],
        (*key_operands(reach), *key_grads),
        far_outs=2,
        scratch=[pltpu.VMEM((rows, features), BF16)] * 2 + [pltpu.SemaphoreType.DMA((heads,))],
    )
    gain_grad, bias_grad = on_device(
        sum_kernel,
        [jax.ShapeDtypeStruct((8, lanes), F32), jax.ShapeDtypeStruct((levels, heads), F32)],
        pieces,
        ahead=key_grads[:1],
    )
    return (
        query_grad[None],
        key_grad[None],
        value_grad[None],
        gate_grad[None],
        bias_grad,
        gain_grad.reshape(features),
    )


def solution(mesh):
    in_specs = (
        P(("groups", "dp"), "ctx", None),
        P(("groups", "dp"), "ctx", None),
        P(("groups", "dp"), "ctx", None),
        P(("groups", "dp"), "ctx", None),
        P(("groups", "dp"), "ctx", None),
        P(("groups", "dp"), None),
        P(),
        P(),
    )
    out_specs = (
        P(("groups", "dp"), "ctx", None),
        P(("groups", "dp"), "ctx", None),
        P(("groups", "dp"), "ctx", None),
        P(("groups", "dp"), "ctx", None),
        P("groups", None),
        P("groups"),
    )
    return jax.shard_map(local, mesh=mesh, in_specs=in_specs, out_specs=out_specs, check_vma=False)
```

```python
from functools import partial

import jax
import jax.numpy as jnp
from jax import lax
from jax.experimental import pallas as pl
from jax.experimental.pallas import tpu as pltpu
from jax.sharding import PartitionSpec as P

EPSILON = 1e-05
VMEM_LIMIT = 24 * 1024 * 1024
F32 = jnp.float32
BF16 = jnp.bfloat16


def passed_along(array, axis, by):
    size = lax.axis_size(axis)
    pairs = [(i, i + by) for i in range(size) if 0 <= i + by < size]
    return lax.ppermute(array, axis, pairs)


def contract(left, right, left_dim, right_dim):
    return lax.dot_general(
        left, right, (((left_dim,), (right_dim,)), ((), ())), preferred_element_type=F32
    )


def user_starts(lengths, query_pos):
    end = jnp.int32(0)
    start = jnp.zeros(query_pos.shape, jnp.int32)
    for user in range(lengths.shape[1]):
        end = end + lengths[0, user]
        start = jnp.where(query_pos >= end, end, start)
    return start


class Pair:
    def __init__(self, mask, table, heads, hops, flipped=False, near=None):
        rows = mask.shape[0]
        self.table, self.heads, self.levels = table, heads, table.shape[0] // heads
        self.mask, self.hops, self.near = mask[...], hops, near
        self.far = (hops - 1) * rows + 1 >= 2 ** (self.levels - 2)
        if not self.far:
            query_dim, key_dim = (1, 0) if flipped else (0, 1)
            query_row = lax.broadcasted_iota(jnp.int32, mask.shape, query_dim)
            key_row = lax.broadcasted_iota(jnp.int32, mask.shape, key_dim)
            self.distance = query_row - key_row + hops * rows

    def half_bias(self, head):
        def level_row(level):
            at = level * self.heads + head
            return self.table[at : at + 1, :]

        value = level_row(self.levels - 1)
        if self.far:
            return value
        if self.near is not None:
            rows = self.mask.shape[0]
            close = self.near[head * rows : (head + 1) * rows, :]
            return close if self.hops == 0 else jnp.where(self.distance < rows, close, value)
        for level in range(self.levels - 2, -1, -1):
            value = jnp.where(self.distance < 2**level, level_row(level), value)
        return value

    def half_logits(self, scores, head, scaling):
        return scores * (0.5 * scaling) + self.half_bias(head)


def slope_of(half, tanh):
    return (0.5 + 0.5 * tanh) * (1.0 + half * (1.0 - tanh))


def columns(head, width):
    return slice(head * width, (head + 1) * width)


def in_stages(count, first, second, ahead=3):
    held = [first(i) for i in range(min(ahead, count))]
    for i in range(count):
        if i + ahead < count:
            held.append(first(i + ahead))
        second(i, held.pop(0))


def attend(pairs, heads, scaling, query, keys, values, total, out):
    width = query.shape[1] // heads

    def scores(head):
        cols = columns(head, width)
        return [contract(query[:, cols], key[:, cols], 1, 1) for key in keys]

    def weigh(head, found):
        cols = columns(head, width)
        part = None if total is None else total[:, cols]
        for pair, score, value in zip(pairs, found, values):
            half = pair.half_logits(score, head, scaling)
            weights = ((half + half * jnp.tanh(half)) * pair.mask).astype(BF16)
            added = contract(weights, value[:, cols], 1, 0)
            part = added if part is None else part + added
        out[:, cols] = part.astype(out.dtype)

    in_stages(heads, scores, weigh)


def first_kernel(plan, heads, scaling, lengths, bias, *refs):
    inputs, refs = refs[:5], refs[5:]
    table, near, masks, refs = refs[0], refs[1], refs[2 : 2 + len(plan)], refs[2 + len(plan) :]
    held, out, arrived = refs[:5], refs[5], refs[6]
    copies = [
        pltpu.make_async_copy(source, target, arrived.at[at])
        for at, (source, target) in enumerate(zip(inputs, held))
    ]
    for copy in copies:
        copy.start()
    levels = bias.shape[0]
    for level in range(levels):
        for head in range(heads):
            at = level * heads + head
            table[at : at + 1, :] = jnp.full((1, table.shape[1]), 0.5 * bias[level, head], F32)
    rows = masks[0].shape[0]
    apart = lax.broadcasted_iota(jnp.int32, (rows, rows), 0)
    apart = (apart - lax.broadcasted_iota(jnp.int32, (rows, rows), 1)) & (rows - 1)
    for head in range(heads):
        value = table[(levels - 1) * heads + head : (levels - 1) * heads + head + 1, :]
        for level in range(levels - 2, -1, -1):
            at = level * heads + head
            value = jnp.where(apart < 2**level, table[at : at + 1, :], value)
        near[head * rows : (head + 1) * rows, :] = value
    for (block, hops, flipped), mask in zip(plan, masks):
        query_dim, key_dim = (1, 0) if flipped else (0, 1)
        line = (1, rows) if flipped else (rows, 1)
        first = (lax.axis_index("ctx") + block) * rows
        query_pos = first + lax.broadcasted_iota(jnp.int32, line, query_dim)
        key_pos = first - hops * rows + lax.broadcasted_iota(jnp.int32, mask.shape, key_dim)
        seen = (key_pos >= user_starts(lengths, query_pos)) & (key_pos <= query_pos)
        mask[...] = jnp.where(seen, 1.0, 0.0).astype(F32)
    for copy in copies:
        copy.wait()
    query, key, value = held[:3]
    pair = Pair(masks[0], table, heads, 0, near=near)
    attend([pair], heads, scaling, query, [key], [value], None, out)


def forward_kernel(hops, heads, scaling, table, near, mask, query, key, value, total, out):
    pair = Pair(mask, table, heads, hops, near=near)
    attend([pair], heads, scaling, query, [key], [value], total, out)


def normed_rows(attention):
    center = attention - jnp.mean(attention, axis=1, keepdims=True)
    inverse = lax.rsqrt(jnp.mean(center * center, axis=1, keepdims=True) + EPSILON)
    return center * inverse, inverse


def norm_kernel(hops, heads, scaling, *refs):
    out_grad, update_gate, gain, attention, attn_grad, gain_grad = refs[-6:]
    forward_kernel(hops, heads, scaling, *refs[:-6], attention)
    rows, features = attention.shape
    step = 16
    gain_row = gain[...]
    gain_sum = jnp.zeros((8, features), F32)
    for low in range(0, rows, step):
        span = slice(low, low + step)
        normed, inverse = normed_rows(attention[span, :])
        gated = out_grad[span, :].astype(F32) * update_gate[span, :].astype(F32)
        product = gated * normed
        for part in range(0, step, 8):
            gain_sum = gain_sum + product[part : part + 8, :]
        pushed = gated * gain_row
        attn_grad[span, :] = (
            inverse
            * (
                pushed
                - jnp.mean(pushed, axis=1, keepdims=True)
                - normed * jnp.mean(pushed * normed, axis=1, keepdims=True)
            )
        ).astype(BF16)
    gain_grad[...] = jnp.sum(gain_sum, axis=0, keepdims=True)


def backward_query_kernel(hop_list, heads, scaling, *refs):
    count = len(hop_list)
    table, near, masks, refs = refs[0], refs[1], refs[2 : 2 + count], refs[2 + count :]
    query, grad, keys, values = refs[0], refs[1], refs[2 : 2 + count], refs[2 + count : 2 + 2 * count]
    gain_in, query_out, small_out = refs[2 + 2 * count :]
    rows, width = query.shape[0], query.shape[1] // heads
    pairs = [Pair(mask, table, heads, hops, near=near) for mask, hops in zip(masks, hop_list)]
    lanes = small_out.shape[1]
    lines = gain_in.shape[1] // lanes
    levels = small_out.shape[0] - lines
    lane = lax.broadcasted_iota(jnp.int32, (levels, lanes), 1)
    level_row = lax.broadcasted_iota(jnp.int32, (levels, lanes), 0)
    group = lax.broadcasted_iota(jnp.int32, (8, rows), 0)
    distance = (group - lax.broadcasted_iota(jnp.int32, (8, rows), 1)) & (rows - 1)
    bucket = sum((distance >= 2**level).astype(jnp.int32) for level in range(levels - 1))
    own = pairs[0].distance >= 0
    bias_total = [jnp.zeros((levels, lanes), F32)]

    def bias_sums(grads):
        close = jnp.where(own, grads[0], grads[1])
        rest = sum(grads[2:], jnp.where(own, grads[1], 0.0))
        by_place, far = jnp.zeros((8, rows), F32), jnp.zeros((8, rows), F32)
        for low in range(0, rows, 8):
            part = close[low : low + 8, :]
            by_place = by_place + (pltpu.roll(part, rows - low, 1) if low else part)
            far = far + rest[low : low + 8, :]
        sums = jnp.where(level_row == levels - 1, jnp.sum(far, axis=0, keepdims=True), 0.0)
        for level in range(levels):
            row = jnp.sum(jnp.where(bucket == level, by_place, 0.0), axis=0, keepdims=True)
            sums = sums + jnp.where(level_row == level, row, 0.0)
        return sums

    def scores(head):
        cols = columns(head, width)
        query_h, grad_h = query[:, cols], grad[:, cols]
        return [
            (contract(query_h, key[:, cols], 1, 1), contract(grad_h, value[:, cols], 1, 1))
            for key, value in zip(keys, values)
        ]

    def differentiate(head, found):
        cols = columns(head, width)
        query_part, grads = None, []
        for pair, key, (score, weight_grad) in zip(pairs, keys, found):
            half = pair.half_logits(score, head, scaling)
            grads.append(weight_grad * (slope_of(half, jnp.tanh(half)) * pair.mask))
            added = contract(grads[-1].astype(BF16), key[:, cols], 1, 0)
            query_part = added if query_part is None else query_part + added
        query_out[:, cols] = (query_part * scaling).astype(BF16)
        sums = jnp.sum(bias_sums(grads), axis=1, keepdims=True)
        bias_total[0] = jnp.where(lane == head, sums, bias_total[0])

    in_stages(heads, scores, differentiate, 1)
    for line in range(lines):
        small_out[line : line + 1, :] = gain_in[:, line * lanes : (line + 1) * lanes]
    small_out[lines:, :] = bias_total[0]


def add_key_grads(hops, heads, scaling, table, mask, query, grad, key, value, sums, store):
    width = query.shape[1] // heads
    pair = Pair(mask, table, heads, hops, True)

    def scores(head):
        cols = columns(head, width)
        score = contract(key[:, cols], query[:, cols], 1, 1)
        return score, contract(value[:, cols], grad[:, cols], 1, 1)

    def differentiate(head, found):
        cols = columns(head, width)
        half = pair.half_logits(found[0], head, scaling)
        tanh = jnp.tanh(half)
        rounded = (found[1] * (slope_of(half, tanh) * pair.mask)).astype(BF16)
        weights = ((half + half * tanh) * pair.mask).astype(BF16)
        parts = [contract(rounded, query[:, cols], 1, 0), contract(weights, grad[:, cols], 1, 0)]
        store(head, cols, *[part + held[:, cols] for part, held in zip(parts, sums)] or parts)

    in_stages(heads, scores, differentiate)


def into(key_out, value_out):
    def store(head, cols, key_part, value_part):
        key_out[:, cols] = key_part
        value_out[:, cols] = value_part

    return store


def next_key_kernel(hops, heads, scaling, *refs):
    add_key_grads(hops, heads, scaling, *refs[:6], refs[6:-2], into(*refs[-2:]))


def gate_and_key_kernel(hops, heads, scaling, *refs):
    attention, out_grad, gain = refs[8:11]
    gate_out, key_out, value_out, held, written = refs[11:]
    step = 16
    gain_row = gain[...]
    for low in range(0, attention.shape[0], step):
        span = slice(low, low + step)
        normed, _ = normed_rows(attention[span, :])
        held[span, :] = (out_grad[span, :].astype(F32) * normed * gain_row).astype(BF16)
    copy = pltpu.make_async_copy(held, gate_out, written)
    copy.start()
    add_key_grads(hops, heads, scaling, *refs[:6], refs[6:8], into(key_out, value_out))
    copy.wait()


def last_kernel(hops, heads, scaling, *refs):
    outs, held, written = refs[-5:-3], refs[-3:-1], refs[-1]
    copies = []
    group = 2

    def store(head, cols, key_part, value_part):
        held[0][:, cols] = (key_part * scaling).astype(BF16)
        held[1][:, cols] = value_part.astype(BF16)
        if (head + 1) % group == 0:
            done = slice(cols.stop - group * (cols.stop - cols.start), cols.stop)
            for source, target in zip(held, outs):
                at = written.at[len(copies)]
                copies.append(pltpu.make_async_copy(source.at[:, done], target.at[:, done], at))
                copies[-1].start()

    add_key_grads(hops, heads, scaling, *refs[:6], refs[6:-5], store)
    for copy in copies:
        copy.wait()


def sum_kernel(*refs):
    gain_out, bias_out = refs[-2:]
    total = added_up([piece[...] for piece in refs[:-2]])
    lines = gain_out.shape[0]
    gain_out[...] = total[:lines]
    bias_out[...] = total[lines:, : bias_out.shape[1]]


def on_device(kernel, outs, args, smem=(), ahead=(), far=(), far_outs=0, scratch=()):
    count = len(smem) + len(far) + len(args)
    far = [pltpu.with_memory_space_constraint(array, pltpu.HBM) for array in far]

    def body(*refs):
        kernel(*refs[:count], *refs[count + len(ahead) :])

    vmem, anywhere = pl.BlockSpec(memory_space=pltpu.VMEM), pl.BlockSpec(memory_space=pl.ANY)
    return pl.pallas_call(
        body,
        out_shape=outs,
        in_specs=[pl.BlockSpec(memory_space=pltpu.SMEM)] * len(smem)
        + [pl.BlockSpec(memory_space=pltpu.HBM)] * len(far)
        + [vmem] * len(args)
        + [anywhere] * len(ahead),
        out_specs=[anywhere] * far_outs + [vmem] * (len(outs) - far_outs),
        scratch_shapes=scratch,
        compiler_params=pltpu.CompilerParams(vmem_limit_bytes=VMEM_LIMIT),
        cost_estimate=pl.CostEstimate(flops=1000000, bytes_accessed=100000, transcendentals=0),
    )(*smem, *far, *args, *ahead)


def rounds_of(axes):
    rounds = []
    for axis in axes:
        size = lax.axis_size(axis)
        step = 1
        while step < size:
            radix = 4 if size // step >= 4 else 2
            rounds.append((axis, [step * at for at in range(1, radix)]))
            step = radix * step
    return rounds


def exchanged(array, axis, distances):
    size = lax.axis_size(axis)
    return [array] + [
        lax.ppermute(array, axis, [(i, i ^ distance) for i in range(size)])
        for distance in distances
    ]


def added_up(pieces):
    while len(pieces) > 1:
        pieces = [left + right for left, right in zip(pieces[::2], pieces[1::2])]
    return pieces[0]


def local(queries, key_rows, value_rows, update_gate, out_grad, user_lengths, rel_bias, norm_gain):
    rows, features = queries.shape[1:]
    levels, heads = rel_bias.shape
    scaling = (features // heads) ** (-0.5)
    reach = min(3, lax.axis_size("ctx") // 2)
    wide = jax.ShapeDtypeStruct((rows, features), F32)
    narrow = jax.ShapeDtypeStruct((rows, features), BF16)
    inputs = (queries[0], key_rows[0], value_rows[0], update_gate[0], out_grad[0])
    gain = norm_gain[None]

    arrived = [passed_along(inputs[at], "ctx", by) for at, by in ((1, 1), (2, 1), (0, -1))]

    hop_list = tuple(range(reach + 1))
    plan = [(0, hops, False) for hops in hop_list] + [(hops, hops, True) for hops in hop_list]
    outs = [jax.ShapeDtypeStruct((count * heads, rows), F32) for count in (levels, rows)]
    outs += [jax.ShapeDtypeStruct((rows, rows), F32)] * len(plan)
    outs += [narrow] * len(inputs) + [wide]
    table, near, *found = on_device(
        partial(first_kernel, plan, heads, scaling),
        outs,
        (),
        (user_lengths, rel_bias),
        far=inputs,
        scratch=[pltpu.SemaphoreType.DMA((len(inputs),))],
    )
    masks, flipped = found[: reach + 1], found[reach + 1 : 2 * reach + 2]
    query, key, value, gate, grad, attention = found[2 * reach + 2 :]

    later_queries = [query, arrived[2]]
    keys, values = [key, arrived[0]], [value, arrived[1]]
    for hops in range(1, reach):
        keys.append(passed_along(keys[-1], "ctx", 1))
        values.append(passed_along(values[-1], "ctx", 1))
        later_queries.append(passed_along(later_queries[-1], "ctx", -1))
    for hops in range(1, reach):
        (attention,) = on_device(
            partial(forward_kernel, hops, heads, scaling),
            [wide],
            (table, near, masks[hops], query, keys[hops], values[hops], attention),
            ahead=later_queries[hops : hops + 1],
        )
    attention, attn_grad, gain_part = on_device(
        partial(norm_kernel, reach, heads, scaling),
        [wide, narrow, jax.ShapeDtypeStruct((1, features), F32)],
        (table, near, masks[-1], query, keys[-1], values[-1], attention, grad, gate, gain),
    )

    lanes = features // 8
    query_grad, sums = on_device(
        partial(backward_query_kernel, hop_list, heads, scaling),
        [narrow, jax.ShapeDtypeStruct((8 + levels, lanes), F32)],
        (table, near, *masks, query, attn_grad, *keys, *values, gain_part),
        ahead=later_queries[reach:],
    )
    later_grads = [attn_grad, passed_along(attn_grad, "ctx", -1)]
    pieces = [sums]
    for axis, distances in rounds_of(("dp",)):
        pieces = exchanged(added_up(pieces), axis, distances)

    def key_operands(hops):
        later = (later_queries[hops], later_grads[hops])
        return (table, flipped[hops], *later, key, value)

    key_grads = on_device(
        partial(next_key_kernel, 0, heads, scaling),
        [wide] * 2,
        key_operands(0),
        ahead=pieces[1:2],
    )
    for hops in range(1, reach):
        arrived, *pieces = lax.optimization_barrier((later_grads[hops], *pieces))
        later_grads.append(passed_along(arrived, "ctx", -1))
        if hops == 1:
            gate_grad, *key_grads = on_device(
                partial(gate_and_key_kernel, hops, heads, scaling),
                [narrow, wide, wide],
                (*key_operands(hops), *key_grads, attention, grad, gain),
                far_outs=1,
                scratch=[pltpu.VMEM((rows, features), BF16), pltpu.SemaphoreType.DMA(())],
            )
        else:
            key_grads = on_device(
                partial(next_key_kernel, hops, heads, scaling),
                [wide] * 2,
                (*key_operands(hops), *key_grads),
            )
    key_grads, *pieces = lax.optimization_barrier((key_grads, *pieces))
    for axis, distances in rounds_of(("ctx",)):
        pieces = exchanged(added_up(pieces), axis, distances)
    key_grad, value_grad = on_device(
        partial(last_kernel, reach, heads, scaling),
        [narrow, narrow],
        (*key_operands(reach), *key_grads),
        far_outs=2,
        scratch=[pltpu.VMEM((rows, features), BF16)] * 2 + [pltpu.SemaphoreType.DMA((heads,))],
    )
    gain_grad, bias_grad = on_device(
        sum_kernel,
        [jax.ShapeDtypeStruct((8, lanes), F32), jax.ShapeDtypeStruct((levels, heads), F32)],
        pieces,
        ahead=[key_grad],
    )
    return (
        query_grad[None],
        key_grad[None],
        value_grad[None],
        gate_grad[None],
        bias_grad,
        gain_grad.reshape(features),
    )


def solution(mesh):
    in_specs = (
        P(("groups", "dp"), "ctx", None),
        P(("groups", "dp"), "ctx", None),
        P(("groups", "dp"), "ctx", None),
        P(("groups", "dp"), "ctx", None),
        P(("groups", "dp"), "ctx", None),
        P(("groups", "dp"), None),
        P(),
        P(),
    )
    out_specs = (
        P(("groups", "dp"), "ctx", None),
        P(("groups", "dp"), "ctx", None),
        P(("groups", "dp"), "ctx", None),
        P(("groups", "dp"), "ctx", None),
        P("groups", None),
        P("groups"),
    )
    return jax.shard_map(local, mesh=mesh, in_specs=in_specs, out_specs=out_specs, check_vma=False)
```

```python
from functools import partial

import jax
import jax.numpy as jnp
from jax import lax
from jax.experimental import pallas as pl
from jax.experimental.pallas import tpu as pltpu
from jax.sharding import PartitionSpec as P

EPSILON = 1e-05
VMEM_LIMIT = 24 * 1024 * 1024
F32 = jnp.float32
BF16 = jnp.bfloat16


def passed_along(array, axis, by):
    size = lax.axis_size(axis)
    pairs = [(i, i + by) for i in range(size) if 0 <= i + by < size]
    return lax.ppermute(array, axis, pairs)


def contract(left, right, left_dim, right_dim):
    return lax.dot_general(
        left, right, (((left_dim,), (right_dim,)), ((), ())), preferred_element_type=F32
    )


def user_starts(lengths, query_pos):
    end = jnp.int32(0)
    start = jnp.zeros(query_pos.shape, jnp.int32)
    for user in range(lengths.shape[1]):
        end = end + lengths[0, user]
        start = jnp.where(query_pos >= end, end, start)
    return start


class Pair:
    def __init__(self, mask, table, heads, hops, flipped=False, near=None):
        rows = mask.shape[0]
        self.table, self.heads, self.levels = table, heads, table.shape[0] // heads
        self.mask, self.hops, self.near = mask[...], hops, near
        self.far = (hops - 1) * rows + 1 >= 2 ** (self.levels - 2)
        if not self.far:
            query_dim, key_dim = (1, 0) if flipped else (0, 1)
            query_row = lax.broadcasted_iota(jnp.int32, mask.shape, query_dim)
            key_row = lax.broadcasted_iota(jnp.int32, mask.shape, key_dim)
            self.distance = query_row - key_row + hops * rows

    def half_bias(self, head):
        def level_row(level):
            at = level * self.heads + head
            return self.table[at : at + 1, :]

        value = level_row(self.levels - 1)
        if self.far:
            return value
        if self.near is not None:
            rows = self.mask.shape[0]
            close = self.near[head * rows : (head + 1) * rows, :]
            return close if self.hops == 0 else jnp.where(self.distance < rows, close, value)
        for level in range(self.levels - 2, -1, -1):
            value = jnp.where(self.distance < 2**level, level_row(level), value)
        return value

    def half_logits(self, scores, head, scaling):
        return scores * (0.5 * scaling) + self.half_bias(head)


def slope_of(half, tanh):
    return (0.5 + 0.5 * tanh) * (1.0 + half * (1.0 - tanh))


def columns(head, width):
    return slice(head * width, (head + 1) * width)


def in_stages(count, first, second, ahead=3):
    held = [first(i) for i in range(min(ahead, count))]
    for i in range(count):
        if i + ahead < count:
            held.append(first(i + ahead))
        second(i, held.pop(0))


def attend(pairs, heads, scaling, query, keys, values, total, out):
    width = query.shape[1] // heads

    def scores(head):
        cols = columns(head, width)
        return [contract(query[:, cols], key[:, cols], 1, 1) for key in keys]

    def weigh(head, found):
        cols = columns(head, width)
        part = None if total is None else total[:, cols]
        for pair, score, value in zip(pairs, found, values):
            half = pair.half_logits(score, head, scaling)
            weights = ((half + half * jnp.tanh(half)) * pair.mask).astype(BF16)
            added = contract(weights, value[:, cols], 1, 0)
            part = added if part is None else part + added
        out[:, cols] = part.astype(out.dtype)

    in_stages(heads, scores, weigh)


def first_kernel(plan, heads, scaling, lengths, bias, *refs):
    inputs, refs = refs[:5], refs[5:]
    table, near, masks, refs = refs[0], refs[1], refs[2 : 2 + len(plan)], refs[2 + len(plan) :]
    held, out, arrived = refs[:5], refs[5], refs[6]
    copies = [
        pltpu.make_async_copy(source, target, arrived.at[at])
        for at, (source, target) in enumerate(zip(inputs, held))
    ]
    for copy in copies:
        copy.start()
    levels = bias.shape[0]
    for level in range(levels):
        for head in range(heads):
            at = level * heads + head
            table[at : at + 1, :] = jnp.full((1, table.shape[1]), 0.5 * bias[level, head], F32)
    rows = masks[0].shape[0]
    apart = lax.broadcasted_iota(jnp.int32, (rows, rows), 0)
    apart = (apart - lax.broadcasted_iota(jnp.int32, (rows, rows), 1)) & (rows - 1)
    for head in range(heads):
        value = table[(levels - 1) * heads + head : (levels - 1) * heads + head + 1, :]
        for level in range(levels - 2, -1, -1):
            at = level * heads + head
            value = jnp.where(apart < 2**level, table[at : at + 1, :], value)
        near[head * rows : (head + 1) * rows, :] = value
    for (block, hops, flipped), mask in zip(plan, masks):
        query_dim, key_dim = (1, 0) if flipped else (0, 1)
        line = (1, rows) if flipped else (rows, 1)
        first = (lax.axis_index("ctx") + block) * rows
        query_pos = first + lax.broadcasted_iota(jnp.int32, line, query_dim)
        key_pos = first - hops * rows + lax.broadcasted_iota(jnp.int32, mask.shape, key_dim)
        seen = (key_pos >= user_starts(lengths, query_pos)) & (key_pos <= query_pos)
        mask[...] = jnp.where(seen, 1.0, 0.0).astype(F32)
    for copy in copies:
        copy.wait()
    query, key, value = held[:3]
    pair = Pair(masks[0], table, heads, 0, near=near)
    attend([pair], heads, scaling, query, [key], [value], None, out)


def forward_kernel(hops, heads, scaling, table, near, mask, query, key, value, total, out):
    pair = Pair(mask, table, heads, hops, near=near)
    attend([pair], heads, scaling, query, [key], [value], total, out)


def normed_rows(attention):
    center = attention - jnp.mean(attention, axis=1, keepdims=True)
    inverse = lax.rsqrt(jnp.mean(center * center, axis=1, keepdims=True) + EPSILON)
    return center * inverse, inverse


def norm_kernel(hops, heads, scaling, *refs):
    out_grad, update_gate, gain, attention, attn_grad, gain_grad = refs[-6:]
    forward_kernel(hops, heads, scaling, *refs[:-6], attention)
    rows, features = attention.shape
    step = 16
    gain_row = gain[...]
    gain_sum = jnp.zeros((8, features), F32)
    for low in range(0, rows, step):
        span = slice(low, low + step)
        normed, inverse = normed_rows(attention[span, :])
        gated = out_grad[span, :].astype(F32) * update_gate[span, :].astype(F32)
        product = gated * normed
        for part in range(0, step, 8):
            gain_sum = gain_sum + product[part : part + 8, :]
        pushed = gated * gain_row
        attn_grad[span, :] = (
            inverse
            * (
                pushed
                - jnp.mean(pushed, axis=1, keepdims=True)
                - normed * jnp.mean(pushed * normed, axis=1, keepdims=True)
            )
        ).astype(BF16)
    gain_grad[...] = jnp.sum(gain_sum, axis=0, keepdims=True)


def backward_query_kernel(hop_list, heads, scaling, *refs):
    count = len(hop_list)
    table, near, masks, refs = refs[0], refs[1], refs[2 : 2 + count], refs[2 + count :]
    query, grad, keys, values = refs[0], refs[1], refs[2 : 2 + count], refs[2 + count : 2 + 2 * count]
    gain_in, query_out, small_out = refs[2 + 2 * count :]
    rows, width = query.shape[0], query.shape[1] // heads
    pairs = [Pair(mask, table, heads, hops, near=near) for mask, hops in zip(masks, hop_list)]
    lanes = small_out.shape[1]
    lines = gain_in.shape[1] // lanes
    levels = small_out.shape[0] - lines
    lane = lax.broadcasted_iota(jnp.int32, (levels, lanes), 1)
    level_row = lax.broadcasted_iota(jnp.int32, (levels, lanes), 0)
    group = lax.broadcasted_iota(jnp.int32, (8, rows), 0)
    distance = (group - lax.broadcasted_iota(jnp.int32, (8, rows), 1)) & (rows - 1)
    bucket = sum((distance >= 2**level).astype(jnp.int32) for level in range(levels - 1))
    own = pairs[0].distance >= 0
    bias_total = [jnp.zeros((levels, lanes), F32)]

    def bias_sums(grads):
        close = jnp.where(own, grads[0], grads[1])
        rest = sum(grads[2:], jnp.where(own, grads[1], 0.0))
        by_place, far = jnp.zeros((8, rows), F32), jnp.zeros((8, rows), F32)
        for low in range(0, rows, 8):
            part = close[low : low + 8, :]
            by_place = by_place + (pltpu.roll(part, rows - low, 1) if low else part)
            far = far + rest[low : low + 8, :]
        sums = jnp.where(level_row == levels - 1, jnp.sum(far, axis=0, keepdims=True), 0.0)
        for level in range(levels):
            row = jnp.sum(jnp.where(bucket == level, by_place, 0.0), axis=0, keepdims=True)
            sums = sums + jnp.where(level_row == level, row, 0.0)
        return sums

    def scores(head):
        cols = columns(head, width)
        query_h, grad_h = query[:, cols], grad[:, cols]
        return [
            (contract(query_h, key[:, cols], 1, 1), contract(grad_h, value[:, cols], 1, 1))
            for key, value in zip(keys, values)
        ]

    def differentiate(head, found):
        cols = columns(head, width)
        query_part, grads = None, []
        for pair, key, (score, weight_grad) in zip(pairs, keys, found):
            half = pair.half_logits(score, head, scaling)
            grads.append(weight_grad * (slope_of(half, jnp.tanh(half)) * pair.mask))
            added = contract(grads[-1].astype(BF16), key[:, cols], 1, 0)
            query_part = added if query_part is None else query_part + added
        query_out[:, cols] = (query_part * scaling).astype(BF16)
        sums = jnp.sum(bias_sums(grads), axis=1, keepdims=True)
        bias_total[0] = jnp.where(lane == head, sums, bias_total[0])

    in_stages(heads, scores, differentiate, 1)
    for line in range(lines):
        small_out[line : line + 1, :] = gain_in[:, line * lanes : (line + 1) * lanes]
    small_out[lines:, :] = bias_total[0]


def add_key_grads(hops, heads, scaling, table, mask, query, grad, key, value, sums, store):
    width = query.shape[1] // heads
    pair = Pair(mask, table, heads, hops, True)

    def scores(head):
        cols = columns(head, width)
        score = contract(key[:, cols], query[:, cols], 1, 1)
        return score, contract(value[:, cols], grad[:, cols], 1, 1)

    def differentiate(head, found):
        cols = columns(head, width)
        half = pair.half_logits(found[0], head, scaling)
        tanh = jnp.tanh(half)
        rounded = (found[1] * (slope_of(half, tanh) * pair.mask)).astype(BF16)
        weights = ((half + half * tanh) * pair.mask).astype(BF16)
        parts = [contract(rounded, query[:, cols], 1, 0), contract(weights, grad[:, cols], 1, 0)]
        store(head, cols, *[part + held[:, cols] for part, held in zip(parts, sums)] or parts)

    in_stages(heads, scores, differentiate)


def into(key_out, value_out):
    def store(head, cols, key_part, value_part):
        key_out[:, cols] = key_part
        value_out[:, cols] = value_part

    return store


def next_key_kernel(hops, heads, scaling, *refs):
    add_key_grads(hops, heads, scaling, *refs[:6], refs[6:-2], into(*refs[-2:]))


def gate_and_key_kernel(hops, heads, scaling, *refs):
    attention, out_grad, gain = refs[8:11]
    gate_out, key_out, value_out, held, written = refs[11:]
    step = 16
    gain_row = gain[...]
    for low in range(0, attention.shape[0], step):
        span = slice(low, low + step)
        normed, _ = normed_rows(attention[span, :])
        held[span, :] = (out_grad[span, :].astype(F32) * normed * gain_row).astype(BF16)
    copy = pltpu.make_async_copy(held, gate_out, written)
    copy.start()
    add_key_grads(hops, heads, scaling, *refs[:6], refs[6:8], into(key_out, value_out))
    copy.wait()


def last_kernel(hops, heads, scaling, *refs):
    outs, held, written = refs[-5:-3], refs[-3:-1], refs[-1]
    copies = []
    group = 2

    def store(head, cols, key_part, value_part):
        held[0][:, cols] = (key_part * scaling).astype(BF16)
        held[1][:, cols] = value_part.astype(BF16)
        if (head + 1) % group == 0:
            done = slice(cols.stop - group * (cols.stop - cols.start), cols.stop)
            for source, target in zip(held, outs):
                at = written.at[len(copies)]
                copies.append(pltpu.make_async_copy(source.at[:, done], target.at[:, done], at))
                copies[-1].start()

    add_key_grads(hops, heads, scaling, *refs[:6], refs[6:-5], store)
    for copy in copies:
        copy.wait()


def sum_kernel(*refs):
    gain_out, bias_out = refs[-2:]
    total = added_up([piece[...] for piece in refs[:-2]])
    lines = gain_out.shape[0]
    gain_out[...] = total[:lines]
    bias_out[...] = total[lines:, : bias_out.shape[1]]


def on_device(kernel, outs, args, smem=(), ahead=(), far=(), far_outs=0, scratch=()):
    count = len(smem) + len(far) + len(args)
    far = [pltpu.with_memory_space_constraint(array, pltpu.HBM) for array in far]

    def body(*refs):
        kernel(*refs[:count], *refs[count + len(ahead) :])

    vmem, anywhere = pl.BlockSpec(memory_space=pltpu.VMEM), pl.BlockSpec(memory_space=pl.ANY)
    return pl.pallas_call(
        body,
        out_shape=outs,
        in_specs=[pl.BlockSpec(memory_space=pltpu.SMEM)] * len(smem)
        + [pl.BlockSpec(memory_space=pltpu.HBM)] * len(far)
        + [vmem] * len(args)
        + [anywhere] * len(ahead),
        out_specs=[anywhere] * far_outs + [vmem] * (len(outs) - far_outs),
        scratch_shapes=scratch,
        compiler_params=pltpu.CompilerParams(vmem_limit_bytes=VMEM_LIMIT),
        cost_estimate=pl.CostEstimate(flops=1000000, bytes_accessed=100000, transcendentals=0),
    )(*smem, *far, *args, *ahead)


def rounds_of(axes):
    rounds = []
    for axis in axes:
        size = lax.axis_size(axis)
        step = 1
        while step < size:
            radix = 4 if size // step >= 4 else 2
            rounds.append((axis, [step * at for at in range(1, radix)]))
            step = radix * step
    return rounds


def exchanged(array, axis, distances):
    size = lax.axis_size(axis)
    found = [
        lax.ppermute(array, axis, [(i, i ^ distance) for i in range(size)])
        for distance in reversed(distances)
    ]
    return [array] + found[::-1]


def added_up(pieces):
    while len(pieces) > 1:
        pieces = [left + right for left, right in zip(pieces[::2], pieces[1::2])]
    return pieces[0]


def local(queries, key_rows, value_rows, update_gate, out_grad, user_lengths, rel_bias, norm_gain):
    rows, features = queries.shape[1:]
    levels, heads = rel_bias.shape
    scaling = (features // heads) ** (-0.5)
    reach = min(3, lax.axis_size("ctx") // 2)
    wide = jax.ShapeDtypeStruct((rows, features), F32)
    narrow = jax.ShapeDtypeStruct((rows, features), BF16)
    inputs = (queries[0], key_rows[0], value_rows[0], update_gate[0], out_grad[0])
    gain = norm_gain[None]

    arrived = [passed_along(inputs[at], "ctx", by) for at, by in ((1, 1), (2, 1), (0, -1))]

    hop_list = tuple(range(reach + 1))
    plan = [(0, hops, False) for hops in hop_list] + [(hops, hops, True) for hops in hop_list]
    outs = [jax.ShapeDtypeStruct((count * heads, rows), F32) for count in (levels, rows)]
    outs += [jax.ShapeDtypeStruct((rows, rows), F32)] * len(plan)
    outs += [narrow] * len(inputs) + [wide]
    table, near, *found = on_device(
        partial(first_kernel, plan, heads, scaling),
        outs,
        (),
        (user_lengths, rel_bias),
        far=inputs,
        scratch=[pltpu.SemaphoreType.DMA((len(inputs),))],
    )
    masks, flipped = found[: reach + 1], found[reach + 1 : 2 * reach + 2]
    query, key, value, gate, grad, attention = found[2 * reach + 2 :]

    later_queries = [query, arrived[2]]
    keys, values = [key, arrived[0]], [value, arrived[1]]
    for hops in range(1, reach):
        keys.append(passed_along(keys[-1], "ctx", 1))
        values.append(passed_along(values[-1], "ctx", 1))
        later_queries.append(passed_along(later_queries[-1], "ctx", -1))
    for hops in range(1, reach):
        (attention,) = on_device(
            partial(forward_kernel, hops, heads, scaling),
            [wide],
            (table, near, masks[hops], query, keys[hops], values[hops], attention),
            ahead=later_queries[hops : hops + 1],
        )
    attention, attn_grad, gain_part = on_device(
        partial(norm_kernel, reach, heads, scaling),
        [wide, narrow, jax.ShapeDtypeStruct((1, features), F32)],
        (table, near, masks[-1], query, keys[-1], values[-1], attention, grad, gate, gain),
    )

    lanes = features // 8
    query_grad, sums = on_device(
        partial(backward_query_kernel, hop_list, heads, scaling),
        [narrow, jax.ShapeDtypeStruct((8 + levels, lanes), F32)],
        (table, near, *masks, query, attn_grad, *keys, *values, gain_part),
        ahead=later_queries[reach:],
    )
    later_grads = [attn_grad, passed_along(attn_grad, "ctx", -1)]
    pieces = [sums]
    for axis, distances in rounds_of(("dp",)):
        pieces = exchanged(added_up(pieces), axis, distances)

    def key_operands(hops):
        later = (later_queries[hops], later_grads[hops])
        return (table, flipped[hops], *later, key, value)

    key_grads = on_device(
        partial(next_key_kernel, 0, heads, scaling),
        [wide] * 2,
        key_operands(0),
        ahead=pieces[1:2],
    )
    for hops in range(1, reach):
        arrived, *pieces = lax.optimization_barrier((later_grads[hops], *pieces))
        later_grads.append(passed_along(arrived, "ctx", -1))
        if hops == 1:
            gate_grad, *key_grads = on_device(
                partial(gate_and_key_kernel, hops, heads, scaling),
                [narrow, wide, wide],
                (*key_operands(hops), *key_grads, attention, grad, gain),
                far_outs=1,
                scratch=[pltpu.VMEM((rows, features), BF16), pltpu.SemaphoreType.DMA(())],
            )
        else:
            key_grads = on_device(
                partial(next_key_kernel, hops, heads, scaling),
                [wide] * 2,
                (*key_operands(hops), *key_grads),
            )
    key_grads, *pieces = lax.optimization_barrier((key_grads, *pieces))
    for axis, distances in rounds_of(("ctx",)):
        pieces = exchanged(added_up(pieces), axis, distances)
    key_grad, value_grad = on_device(
        partial(last_kernel, reach, heads, scaling),
        [narrow, narrow],
        (*key_operands(reach), *key_grads),
        far_outs=2,
        scratch=[pltpu.VMEM((rows, features), BF16)] * 2 + [pltpu.SemaphoreType.DMA((heads,))],
    )
    key_grad, value_grad, pieces[0] = lax.optimization_barrier((key_grad, value_grad, pieces[0]))
    gain_grad, bias_grad = on_device(
        sum_kernel,
        [jax.ShapeDtypeStruct((8, lanes), F32), jax.ShapeDtypeStruct((levels, heads), F32)],
        pieces[::-1],
    )
    return (
        query_grad[None],
        key_grad[None],
        value_grad[None],
        gate_grad[None],
        bias_grad,
        gain_grad.reshape(features),
    )


def solution(mesh):
    in_specs = (
        P(("groups", "dp"), "ctx", None),
        P(("groups", "dp"), "ctx", None),
        P(("groups", "dp"), "ctx", None),
        P(("groups", "dp"), "ctx", None),
        P(("groups", "dp"), "ctx", None),
        P(("groups", "dp"), None),
        P(),
        P(),
    )
    out_specs = (
        P(("groups", "dp"), "ctx", None),
        P(("groups", "dp"), "ctx", None),
        P(("groups", "dp"), "ctx", None),
        P(("groups", "dp"), "ctx", None),
        P("groups", None),
        P("groups"),
    )
    return jax.shard_map(local, mesh=mesh, in_specs=in_specs, out_specs=out_specs, check_vma=False)
```

```python
from functools import partial

import jax
import jax.numpy as jnp
from jax import lax
from jax.experimental import pallas as pl
from jax.experimental.pallas import tpu as pltpu
from jax.sharding import PartitionSpec as P

EPSILON = 1e-05
VMEM_LIMIT = 24 * 1024 * 1024
F32 = jnp.float32
BF16 = jnp.bfloat16


def passed_along(array, axis, by, hop=1):
    size = lax.axis_size(axis)
    first, last = (hop - 1, size - 2) if by > 0 else (1, size - hop)
    return lax.ppermute(array, axis, [(i, i + by) for i in range(first, last + 1)])


def contract(left, right, left_dim, right_dim):
    return lax.dot_general(
        left, right, (((left_dim,), (right_dim,)), ((), ())), preferred_element_type=F32
    )


def user_starts(lengths, query_pos):
    end = jnp.int32(0)
    start = jnp.zeros(query_pos.shape, jnp.int32)
    for user in range(lengths.shape[1]):
        end = end + lengths[0, user]
        start = jnp.where(query_pos >= end, end, start)
    return start


class Pair:
    def __init__(self, mask, table, heads, hops, flipped=False, near=None):
        rows = mask.shape[0]
        self.table, self.heads, self.levels = table, heads, table.shape[0] // heads
        self.mask, self.hops, self.near = mask[...], hops, near
        self.far = (hops - 1) * rows + 1 >= 2 ** (self.levels - 2)
        if not self.far:
            query_dim, key_dim = (1, 0) if flipped else (0, 1)
            query_row = lax.broadcasted_iota(jnp.int32, mask.shape, query_dim)
            key_row = lax.broadcasted_iota(jnp.int32, mask.shape, key_dim)
            self.distance = query_row - key_row + hops * rows

    def half_bias(self, head):
        def level_row(level):
            at = level * self.heads + head
            return self.table[at : at + 1, :]

        value = level_row(self.levels - 1)
        if self.far:
            return value
        if self.near is not None:
            rows = self.mask.shape[0]
            close = self.near[head * rows : (head + 1) * rows, :]
            return close if self.hops == 0 else jnp.where(self.distance < rows, close, value)
        for level in range(self.levels - 2, -1, -1):
            value = jnp.where(self.distance < 2**level, level_row(level), value)
        return value

    def half_logits(self, scores, head, scaling):
        return scores * (0.5 * scaling) + self.half_bias(head)


def slope_of(half, tanh):
    return (0.5 + 0.5 * tanh) * (1.0 + half * (1.0 - tanh))


def columns(head, width):
    return slice(head * width, (head + 1) * width)


def in_stages(count, first, second, ahead=3):
    held = [first(i) for i in range(min(ahead, count))]
    for i in range(count):
        if i + ahead < count:
            held.append(first(i + ahead))
        second(i, held.pop(0))


def attend(pairs, heads, scaling, query, keys, values, total, out):
    width = query.shape[1] // heads

    def scores(head):
        cols = columns(head, width)
        return [contract(query[:, cols], key[:, cols], 1, 1) for key in keys]

    def weigh(head, found):
        cols = columns(head, width)
        part = None if total is None else total[:, cols]
        for pair, score, value in zip(pairs, found, values):
            half = pair.half_logits(score, head, scaling)
            weights = ((half + half * jnp.tanh(half)) * pair.mask).astype(BF16)
            added = contract(weights, value[:, cols], 1, 0)
            part = added if part is None else part + added
        out[:, cols] = part.astype(out.dtype)

    in_stages(heads, scores, weigh)


def first_kernel(plan, heads, scaling, lengths, bias, *refs):
    inputs, refs = refs[:5], refs[5:]
    table, near, masks, refs = refs[0], refs[1], refs[2 : 2 + len(plan)], refs[2 + len(plan) :]
    held, out, arrived = refs[:5], refs[5], refs[6]
    copies = [
        pltpu.make_async_copy(source, target, arrived.at[at])
        for at, (source, target) in enumerate(zip(inputs, held))
    ]
    for copy in copies:
        copy.start()
    levels = bias.shape[0]
    for level in range(levels):
        for head in range(heads):
            at = level * heads + head
            table[at : at + 1, :] = jnp.full((1, table.shape[1]), 0.5 * bias[level, head], F32)
    rows = masks[0].shape[0]
    apart = lax.broadcasted_iota(jnp.int32, (rows, rows), 0)
    apart = (apart - lax.broadcasted_iota(jnp.int32, (rows, rows), 1)) & (rows - 1)
    for head in range(heads):
        value = table[(levels - 1) * heads + head : (levels - 1) * heads + head + 1, :]
        for level in range(levels - 2, -1, -1):
            at = level * heads + head
            value = jnp.where(apart < 2**level, table[at : at + 1, :], value)
        near[head * rows : (head + 1) * rows, :] = value
    for (block, hops, flipped), mask in zip(plan, masks):
        query_dim, key_dim = (1, 0) if flipped else (0, 1)
        line = (1, rows) if flipped else (rows, 1)
        first = (lax.axis_index("ctx") + block) * rows
        query_pos = first + lax.broadcasted_iota(jnp.int32, line, query_dim)
        key_pos = first - hops * rows + lax.broadcasted_iota(jnp.int32, mask.shape, key_dim)
        seen = (key_pos >= user_starts(lengths, query_pos)) & (key_pos <= query_pos)
        mask[...] = jnp.where(seen, 1.0, 0.0).astype(F32)
    for copy in copies:
        copy.wait()
    query, key, value = held[:3]
    pair = Pair(masks[0], table, heads, 0, near=near)
    attend([pair], heads, scaling, query, [key], [value], None, out)


def forward_kernel(hops, heads, scaling, table, near, mask, query, key, value, total, out):
    pair = Pair(mask, table, heads, hops, near=near)
    attend([pair], heads, scaling, query, [key], [value], total, out)


def normed_rows(attention):
    center = attention - jnp.mean(attention, axis=1, keepdims=True)
    inverse = lax.rsqrt(jnp.mean(center * center, axis=1, keepdims=True) + EPSILON)
    return center * inverse, inverse


def norm_kernel(hops, heads, scaling, *refs):
    out_grad, update_gate, gain, attention, attn_grad, gain_grad = refs[-6:]
    forward_kernel(hops, heads, scaling, *refs[:-6], attention)
    rows, features = attention.shape
    step = 16
    gain_row = gain[...]
    gain_sum = jnp.zeros((8, features), F32)
    for low in range(0, rows, step):
        span = slice(low, low + step)
        normed, inverse = normed_rows(attention[span, :])
        gated = out_grad[span, :].astype(F32) * update_gate[span, :].astype(F32)
        product = gated * normed
        for part in range(0, step, 8):
            gain_sum = gain_sum + product[part : part + 8, :]
        pushed = gated * gain_row
        attn_grad[span, :] = (
            inverse
            * (
                pushed
                - jnp.mean(pushed, axis=1, keepdims=True)
                - normed * jnp.mean(pushed * normed, axis=1, keepdims=True)
            )
        ).astype(BF16)
    gain_grad[...] = jnp.sum(gain_sum, axis=0, keepdims=True)


def backward_query_kernel(hop_list, heads, scaling, *refs):
    count = len(hop_list)
    table, near, masks, refs = refs[0], refs[1], refs[2 : 2 + count], refs[2 + count :]
    query, grad, keys, values = refs[0], refs[1], refs[2 : 2 + count], refs[2 + count : 2 + 2 * count]
    gain_in, query_out, small_out = refs[2 + 2 * count :]
    rows, width = query.shape[0], query.shape[1] // heads
    pairs = [Pair(mask, table, heads, hops, near=near) for mask, hops in zip(masks, hop_list)]
    lanes = small_out.shape[1]
    lines = gain_in.shape[1] // lanes
    levels = small_out.shape[0] - lines
    lane = lax.broadcasted_iota(jnp.int32, (levels, lanes), 1)
    level_row = lax.broadcasted_iota(jnp.int32, (levels, lanes), 0)
    group = lax.broadcasted_iota(jnp.int32, (8, rows), 0)
    distance = (group - lax.broadcasted_iota(jnp.int32, (8, rows), 1)) & (rows - 1)
    bucket = sum((distance >= 2**level).astype(jnp.int32) for level in range(levels - 1))
    own = pairs[0].distance >= 0
    bias_total = [jnp.zeros((levels, lanes), F32)]

    def bias_sums(grads):
        close = jnp.where(own, grads[0], grads[1])
        rest = sum(grads[2:], jnp.where(own, grads[1], 0.0))
        by_place, far = jnp.zeros((8, rows), F32), jnp.zeros((8, rows), F32)
        for low in range(0, rows, 8):
            part = close[low : low + 8, :]
            by_place = by_place + (pltpu.roll(part, rows - low, 1) if low else part)
            far = far + rest[low : low + 8, :]
        sums = jnp.where(level_row == levels - 1, jnp.sum(far, axis=0, keepdims=True), 0.0)
        for level in range(levels):
            row = jnp.sum(jnp.where(bucket == level, by_place, 0.0), axis=0, keepdims=True)
            sums = sums + jnp.where(level_row == level, row, 0.0)
        return sums

    def scores(head):
        cols = columns(head, width)
        query_h, grad_h = query[:, cols], grad[:, cols]
        return [
            (contract(query_h, key[:, cols], 1, 1), contract(grad_h, value[:, cols], 1, 1))
            for key, value in zip(keys, values)
        ]

    def differentiate(head, found):
        cols = columns(head, width)
        query_part, grads = None, []
        for pair, key, (score, weight_grad) in zip(pairs, keys, found):
            half = pair.half_logits(score, head, scaling)
            grads.append(weight_grad * (slope_of(half, jnp.tanh(half)) * pair.mask))
            added = contract(grads[-1].astype(BF16), key[:, cols], 1, 0)
            query_part = added if query_part is None else query_part + added
        query_out[:, cols] = (query_part * scaling).astype(BF16)
        sums = jnp.sum(bias_sums(grads), axis=1, keepdims=True)
        bias_total[0] = jnp.where(lane == head, sums, bias_total[0])

    in_stages(heads, scores, differentiate, 1)
    for line in range(lines):
        small_out[line : line + 1, :] = gain_in[:, line * lanes : (line + 1) * lanes]
    small_out[lines:, :] = bias_total[0]


def add_key_grads(hops, heads, scaling, table, mask, query, grad, key, value, sums, store):
    width = query.shape[1] // heads
    pair = Pair(mask, table, heads, hops, True)

    def scores(head):
        cols = columns(head, width)
        score = contract(key[:, cols], query[:, cols], 1, 1)
        return score, contract(value[:, cols], grad[:, cols], 1, 1)

    def differentiate(head, found):
        cols = columns(head, width)
        half = pair.half_logits(found[0], head, scaling)
        tanh = jnp.tanh(half)
        rounded = (found[1] * (slope_of(half, tanh) * pair.mask)).astype(BF16)
        weights = ((half + half * tanh) * pair.mask).astype(BF16)
        parts = [contract(rounded, query[:, cols], 1, 0), contract(weights, grad[:, cols], 1, 0)]
        store(head, cols, *[part + held[:, cols] for part, held in zip(parts, sums)] or parts)

    in_stages(heads, scores, differentiate)


def into(key_out, value_out):
    def store(head, cols, key_part, value_part):
        key_out[:, cols] = key_part
        value_out[:, cols] = value_part

    return store


def next_key_kernel(hops, heads, scaling, *refs):
    add_key_grads(hops, heads, scaling, *refs[:6], refs[6:-2], into(*refs[-2:]))


def gate_and_key_kernel(hops, heads, scaling, *refs):
    attention, out_grad, gain = refs[8:11]
    gate_out, key_out, value_out, held, written = refs[11:]
    step = 16
    gain_row = gain[...]
    for low in range(0, attention.shape[0], step):
        span = slice(low, low + step)
        normed, _ = normed_rows(attention[span, :])
        held[span, :] = (out_grad[span, :].astype(F32) * normed * gain_row).astype(BF16)
    copy = pltpu.make_async_copy(held, gate_out, written)
    copy.start()
    add_key_grads(hops, heads, scaling, *refs[:6], refs[6:8], into(key_out, value_out))
    copy.wait()


def last_kernel(hops, heads, scaling, *refs):
    outs, held, written = refs[-5:-3], refs[-3:-1], refs[-1]
    copies = []
    group = 2

    def store(head, cols, key_part, value_part):
        held[0][:, cols] = (key_part * scaling).astype(BF16)
        held[1][:, cols] = value_part.astype(BF16)
        if (head + 1) % group == 0:
            done = slice(cols.stop - group * (cols.stop - cols.start), cols.stop)
            for source, target in zip(held, outs):
                at = written.at[len(copies)]
                copies.append(pltpu.make_async_copy(source.at[:, done], target.at[:, done], at))
                copies[-1].start()

    add_key_grads(hops, heads, scaling, *refs[:6], refs[6:-5], store)
    for copy in copies:
        copy.wait()


def sum_kernel(*refs):
    gain_out, bias_out = refs[-2:]
    total = added_up([piece[...] for piece in refs[:-2]])
    lines = gain_out.shape[0]
    gain_out[...] = total[:lines]
    bias_out[...] = total[lines:, : bias_out.shape[1]]


def on_device(kernel, outs, args, smem=(), ahead=(), far=(), far_outs=0, scratch=()):
    count = len(smem) + len(far) + len(args)
    far = [pltpu.with_memory_space_constraint(array, pltpu.HBM) for array in far]

    def body(*refs):
        kernel(*refs[:count], *refs[count + len(ahead) :])

    vmem, anywhere = pl.BlockSpec(memory_space=pltpu.VMEM), pl.BlockSpec(memory_space=pl.ANY)
    return pl.pallas_call(
        body,
        out_shape=outs,
        in_specs=[pl.BlockSpec(memory_space=pltpu.SMEM)] * len(smem)
        + [pl.BlockSpec(memory_space=pltpu.HBM)] * len(far)
        + [vmem] * len(args)
        + [anywhere] * len(ahead),
        out_specs=[anywhere] * far_outs + [vmem] * (len(outs) - far_outs),
        scratch_shapes=scratch,
        compiler_params=pltpu.CompilerParams(vmem_limit_bytes=VMEM_LIMIT),
        cost_estimate=pl.CostEstimate(flops=1000000, bytes_accessed=100000, transcendentals=0),
    )(*smem, *far, *args, *ahead)


def rounds_of(axes):
    rounds = []
    for axis in axes:
        size = lax.axis_size(axis)
        step = 1
        while step < size:
            radix = 4 if size // step >= 4 else 2
            rounds.append((axis, [step * at for at in range(1, radix)]))
            step = radix * step
    return rounds


def exchanged(array, axis, distances):
    size = lax.axis_size(axis)
    found = [
        lax.ppermute(array, axis, [(i, i ^ distance) for i in range(size)])
        for distance in reversed(distances)
    ]
    return [array] + found[::-1]


def added_up(pieces):
    while len(pieces) > 1:
        pieces = [left + right for left, right in zip(pieces[::2], pieces[1::2])]
    return pieces[0]


def local(queries, key_rows, value_rows, update_gate, out_grad, user_lengths, rel_bias, norm_gain):
    rows, features = queries.shape[1:]
    levels, heads = rel_bias.shape
    scaling = (features // heads) ** (-0.5)
    reach = min(3, lax.axis_size("ctx") // 2)
    wide = jax.ShapeDtypeStruct((rows, features), F32)
    narrow = jax.ShapeDtypeStruct((rows, features), BF16)
    inputs = (queries[0], key_rows[0], value_rows[0], update_gate[0], out_grad[0])
    gain = norm_gain[None]

    arrived = [passed_along(inputs[at], "ctx", by) for at, by in ((1, 1), (2, 1), (0, -1))]

    hop_list = tuple(range(reach + 1))
    plan = [(0, hops, False) for hops in hop_list] + [(hops, hops, True) for hops in hop_list]
    outs = [jax.ShapeDtypeStruct((count * heads, rows), F32) for count in (levels, rows)]
    outs += [jax.ShapeDtypeStruct((rows, rows), F32)] * len(plan)
    outs += [narrow] * len(inputs) + [wide]
    table, near, *found = on_device(
        partial(first_kernel, plan, heads, scaling),
        outs,
        (),
        (user_lengths, rel_bias),
        far=inputs,
        scratch=[pltpu.SemaphoreType.DMA((len(inputs),))],
    )
    masks, flipped = found[: reach + 1], found[reach + 1 : 2 * reach + 2]
    query, key, value, gate, grad, attention = found[2 * reach + 2 :]

    later_queries = [query, arrived[2]]
    keys, values = [key, arrived[0]], [value, arrived[1]]
    for hops in range(1, reach):
        keys.append(passed_along(keys[-1], "ctx", 1, hops + 1))
        values.append(passed_along(values[-1], "ctx", 1, hops + 1))
        later_queries.append(passed_along(later_queries[-1], "ctx", -1, hops + 1))
    for hops in range(1, reach):
        (attention,) = on_device(
            partial(forward_kernel, hops, heads, scaling),
            [wide],
            (table, near, masks[hops], query, keys[hops], values[hops], attention),
            ahead=later_queries[hops : hops + 1],
        )
    attention, attn_grad, gain_part = on_device(
        partial(norm_kernel, reach, heads, scaling),
        [wide, narrow, jax.ShapeDtypeStruct((1, features), F32)],
        (table, near, masks[-1], query, keys[-1], values[-1], attention, grad, gate, gain),
    )

    lanes = features // 8
    query_grad, sums = on_device(
        partial(backward_query_kernel, hop_list, heads, scaling),
        [narrow, jax.ShapeDtypeStruct((8 + levels, lanes), F32)],
        (table, near, *masks, query, attn_grad, *keys, *values, gain_part),
        ahead=later_queries[reach:],
    )
    later_grads = [attn_grad, passed_along(attn_grad, "ctx", -1)]
    pieces = [sums]
    for axis, distances in rounds_of(("dp",)):
        pieces = exchanged(added_up(pieces), axis, distances)

    def key_operands(hops):
        later = (later_queries[hops], later_grads[hops])
        return (table, flipped[hops], *later, key, value)

    key_grads = on_device(
        partial(next_key_kernel, 0, heads, scaling),
        [wide] * 2,
        key_operands(0),
        ahead=pieces[1:2],
    )
    for hops in range(1, reach):
        arrived, *pieces = lax.optimization_barrier((later_grads[hops], *pieces))
        later_grads.append(passed_along(arrived, "ctx", -1, hops + 1))
        if hops == 1:
            gate_grad, *key_grads = on_device(
                partial(gate_and_key_kernel, hops, heads, scaling),
                [narrow, wide, wide],
                (*key_operands(hops), *key_grads, attention, grad, gain),
                far_outs=1,
                scratch=[pltpu.VMEM((rows, features), BF16), pltpu.SemaphoreType.DMA(())],
            )
        else:
            key_grads = on_device(
                partial(next_key_kernel, hops, heads, scaling),
                [wide] * 2,
                (*key_operands(hops), *key_grads),
            )
    key_grads, *pieces = lax.optimization_barrier((key_grads, *pieces))
    for axis, distances in rounds_of(("ctx",)):
        pieces = exchanged(added_up(pieces), axis, distances)
    key_grad, value_grad = on_device(
        partial(last_kernel, reach, heads, scaling),
        [narrow, narrow],
        (*key_operands(reach), *key_grads),
        far_outs=2,
        scratch=[pltpu.VMEM((rows, features), BF16)] * 2 + [pltpu.SemaphoreType.DMA((heads,))],
    )
    key_grad, value_grad, pieces[0] = lax.optimization_barrier((key_grad, value_grad, pieces[0]))
    gain_grad, bias_grad = on_device(
        sum_kernel,
        [jax.ShapeDtypeStruct((8, lanes), F32), jax.ShapeDtypeStruct((levels, heads), F32)],
        pieces[::-1],
    )
    return (
        query_grad[None],
        key_grad[None],
        value_grad[None],
        gate_grad[None],
        bias_grad,
        gain_grad.reshape(features),
    )


def solution(mesh):
    in_specs = (
        P(("groups", "dp"), "ctx", None),
        P(("groups", "dp"), "ctx", None),
        P(("groups", "dp"), "ctx", None),
        P(("groups", "dp"), "ctx", None),
        P(("groups", "dp"), "ctx", None),
        P(("groups", "dp"), None),
        P(),
        P(),
    )
    out_specs = (
        P(("groups", "dp"), "ctx", None),
        P(("groups", "dp"), "ctx", None),
        P(("groups", "dp"), "ctx", None),
        P(("groups", "dp"), "ctx", None),
        P("groups", None),
        P("groups"),
    )
    return jax.shard_map(local, mesh=mesh, in_specs=in_specs, out_specs=out_specs, check_vma=False)
```

```python
from functools import partial

import jax
import jax.numpy as jnp
from jax import lax
from jax.experimental import pallas as pl
from jax.experimental.pallas import tpu as pltpu
from jax.sharding import PartitionSpec as P

EPSILON = 1e-05
VMEM_LIMIT = 24 * 1024 * 1024
F32 = jnp.float32
BF16 = jnp.bfloat16


def passed_along(array, axis, by, hop=1):
    size = lax.axis_size(axis)
    first, last = (hop - 1, size - 2) if by > 0 else (1, size - hop)
    return lax.ppermute(array, axis, [(i, i + by) for i in range(first, last + 1)])


def contract(left, right, left_dim, right_dim):
    return lax.dot_general(
        left, right, (((left_dim,), (right_dim,)), ((), ())), preferred_element_type=F32
    )


def user_starts(lengths, query_pos):
    end = jnp.int32(0)
    start = jnp.zeros(query_pos.shape, jnp.int32)
    for user in range(lengths.shape[1]):
        end = end + lengths[0, user]
        start = jnp.where(query_pos >= end, end, start)
    return start


class Pair:
    def __init__(self, mask, table, heads, hops, flipped=False, near=None):
        rows = mask.shape[0]
        self.table, self.heads, self.levels = table, heads, table.shape[0] // heads
        self.mask, self.hops, self.near = mask[...], hops, near
        self.far = (hops - 1) * rows + 1 >= 2 ** (self.levels - 2)
        if not self.far:
            query_dim, key_dim = (1, 0) if flipped else (0, 1)
            query_row = lax.broadcasted_iota(jnp.int32, mask.shape, query_dim)
            key_row = lax.broadcasted_iota(jnp.int32, mask.shape, key_dim)
            self.distance = query_row - key_row + hops * rows

    def half_bias(self, head):
        def level_row(level):
            at = level * self.heads + head
            return self.table[at : at + 1, :]

        value = level_row(self.levels - 1)
        if self.far:
            return value
        if self.near is not None:
            rows = self.mask.shape[0]
            close = self.near[head * rows : (head + 1) * rows, :]
            return close if self.hops == 0 else jnp.where(self.distance < rows, close, value)
        for level in range(self.levels - 2, -1, -1):
            value = jnp.where(self.distance < 2**level, level_row(level), value)
        return value

    def half_logits(self, scores, head, scaling):
        return scores * (0.5 * scaling) + self.half_bias(head)


def slope_of(half, tanh):
    return (0.5 + 0.5 * tanh) * (1.0 + half * (1.0 - tanh))


def columns(head, width):
    return slice(head * width, (head + 1) * width)


def in_stages(count, first, second, ahead=3):
    held = [first(i) for i in range(min(ahead, count))]
    for i in range(count):
        if i + ahead < count:
            held.append(first(i + ahead))
        second(i, held.pop(0))


def attend(pairs, heads, scaling, query, keys, values, total, out):
    width = query.shape[1] // heads

    def scores(head):
        cols = columns(head, width)
        return [contract(query[:, cols], key[:, cols], 1, 1) for key in keys]

    def weigh(head, found):
        cols = columns(head, width)
        part = None if total is None else total[:, cols]
        for pair, score, value in zip(pairs, found, values):
            half = pair.half_logits(score, head, scaling)
            weights = ((half + half * jnp.tanh(half)) * pair.mask).astype(BF16)
            added = contract(weights, value[:, cols], 1, 0)
            part = added if part is None else part + added
        out[:, cols] = part.astype(out.dtype)

    in_stages(heads, scores, weigh)


def first_kernel(plan, heads, scaling, lengths, bias, *refs):
    inputs, refs = refs[:5], refs[5:]
    table, near, masks, refs = refs[0], refs[1], refs[2 : 2 + len(plan)], refs[2 + len(plan) :]
    held, out, arrived = refs[:5], refs[5], refs[6]
    copies = [
        pltpu.make_async_copy(source, target, arrived.at[at])
        for at, (source, target) in enumerate(zip(inputs, held))
    ]
    for copy in copies:
        copy.start()
    levels = bias.shape[0]
    for level in range(levels):
        for head in range(heads):
            at = level * heads + head
            table[at : at + 1, :] = jnp.full((1, table.shape[1]), 0.5 * bias[level, head], F32)
    rows = masks[0].shape[0]
    apart = lax.broadcasted_iota(jnp.int32, (rows, rows), 0)
    apart = (apart - lax.broadcasted_iota(jnp.int32, (rows, rows), 1)) & (rows - 1)
    for head in range(heads):
        value = table[(levels - 1) * heads + head : (levels - 1) * heads + head + 1, :]
        for level in range(levels - 2, -1, -1):
            at = level * heads + head
            value = jnp.where(apart < 2**level, table[at : at + 1, :], value)
        near[head * rows : (head + 1) * rows, :] = value
    for (block, hops, flipped), mask in zip(plan, masks):
        query_dim, key_dim = (1, 0) if flipped else (0, 1)
        line = (1, rows) if flipped else (rows, 1)
        first = (lax.axis_index("ctx") + block) * rows
        query_pos = first + lax.broadcasted_iota(jnp.int32, line, query_dim)
        key_pos = first - hops * rows + lax.broadcasted_iota(jnp.int32, mask.shape, key_dim)
        seen = (key_pos >= user_starts(lengths, query_pos)) & (key_pos <= query_pos)
        mask[...] = jnp.where(seen, 1.0, 0.0).astype(F32)
    for copy in copies:
        copy.wait()
    query, key, value = held[:3]
    pair = Pair(masks[0], table, heads, 0, near=near)
    attend([pair], heads, scaling, query, [key], [value], None, out)


def forward_kernel(hops, heads, scaling, table, near, mask, query, key, value, total, out):
    pair = Pair(mask, table, heads, hops, near=near)
    attend([pair], heads, scaling, query, [key], [value], total, out)


def normed_rows(attention):
    center = attention - jnp.mean(attention, axis=1, keepdims=True)
    inverse = lax.rsqrt(jnp.mean(center * center, axis=1, keepdims=True) + EPSILON)
    return center * inverse, inverse


def weights_kernel(hops, heads, scaling, table, near, mask, query, key, weights):
    pair = Pair(mask, table, heads, hops, near=near)
    rows, width = query.shape[0], query.shape[1] // heads

    def scores(head):
        cols = columns(head, width)
        return contract(query[:, cols], key[:, cols], 1, 1)

    def weigh(head, found):
        half = pair.half_logits(found, head, scaling)
        lines = columns(head, rows)
        weights[lines, :] = ((half + half * jnp.tanh(half)) * pair.mask).astype(BF16)

    in_stages(heads, scores, weigh)


def norm_kernel(heads, *refs):
    weights, value, total, out_grad, update_gate, gain = refs[:6]
    attention, attn_grad, gain_grad = refs[6:]
    width = total.shape[1] // heads
    for head in range(heads):
        cols, lines = columns(head, width), columns(head, total.shape[0])
        attention[:, cols] = total[:, cols] + contract(weights[lines, :], value[:, cols], 1, 0)
    rows, features = attention.shape
    step = 16
    gain_row = gain[...]
    gain_sum = jnp.zeros((8, features), F32)
    for low in range(0, rows, step):
        span = slice(low, low + step)
        normed, inverse = normed_rows(attention[span, :])
        gated = out_grad[span, :].astype(F32) * update_gate[span, :].astype(F32)
        product = gated * normed
        for part in range(0, step, 8):
            gain_sum = gain_sum + product[part : part + 8, :]
        pushed = gated * gain_row
        attn_grad[span, :] = (
            inverse
            * (
                pushed
                - jnp.mean(pushed, axis=1, keepdims=True)
                - normed * jnp.mean(pushed * normed, axis=1, keepdims=True)
            )
        ).astype(BF16)
    gain_grad[...] = jnp.sum(gain_sum, axis=0, keepdims=True)


def backward_query_kernel(hop_list, heads, scaling, *refs):
    count = len(hop_list)
    table, near, masks, refs = refs[0], refs[1], refs[2 : 2 + count], refs[2 + count :]
    query, grad, keys, values = refs[0], refs[1], refs[2 : 2 + count], refs[2 + count : 2 + 2 * count]
    gain_in, query_out, small_out = refs[2 + 2 * count :]
    rows, width = query.shape[0], query.shape[1] // heads
    pairs = [Pair(mask, table, heads, hops, near=near) for mask, hops in zip(masks, hop_list)]
    lanes = small_out.shape[1]
    lines = gain_in.shape[1] // lanes
    levels = small_out.shape[0] - lines
    lane = lax.broadcasted_iota(jnp.int32, (levels, lanes), 1)
    level_row = lax.broadcasted_iota(jnp.int32, (levels, lanes), 0)
    group = lax.broadcasted_iota(jnp.int32, (8, rows), 0)
    distance = (group - lax.broadcasted_iota(jnp.int32, (8, rows), 1)) & (rows - 1)
    bucket = sum((distance >= 2**level).astype(jnp.int32) for level in range(levels - 1))
    own = pairs[0].distance >= 0
    bias_total = [jnp.zeros((levels, lanes), F32)]

    def bias_sums(grads):
        close = jnp.where(own, grads[0], grads[1])
        rest = sum(grads[2:], jnp.where(own, grads[1], 0.0))
        by_place, far = jnp.zeros((8, rows), F32), jnp.zeros((8, rows), F32)
        for low in range(0, rows, 8):
            part = close[low : low + 8, :]
            by_place = by_place + (pltpu.roll(part, rows - low, 1) if low else part)
            far = far + rest[low : low + 8, :]
        sums = jnp.where(level_row == levels - 1, jnp.sum(far, axis=0, keepdims=True), 0.0)
        for level in range(levels):
            row = jnp.sum(jnp.where(bucket == level, by_place, 0.0), axis=0, keepdims=True)
            sums = sums + jnp.where(level_row == level, row, 0.0)
        return sums

    def scores(head):
        cols = columns(head, width)
        query_h, grad_h = query[:, cols], grad[:, cols]
        return [
            (contract(query_h, key[:, cols], 1, 1), contract(grad_h, value[:, cols], 1, 1))
            for key, value in zip(keys, values)
        ]

    def differentiate(head, found):
        cols = columns(head, width)
        query_part, grads = None, []
        for pair, key, (score, weight_grad) in zip(pairs, keys, found):
            half = pair.half_logits(score, head, scaling)
            grads.append(weight_grad * (slope_of(half, jnp.tanh(half)) * pair.mask))
            added = contract(grads[-1].astype(BF16), key[:, cols], 1, 0)
            query_part = added if query_part is None else query_part + added
        query_out[:, cols] = (query_part * scaling).astype(BF16)
        sums = jnp.sum(bias_sums(grads), axis=1, keepdims=True)
        bias_total[0] = jnp.where(lane == head, sums, bias_total[0])

    in_stages(heads, scores, differentiate, 1)
    for line in range(lines):
        small_out[line : line + 1, :] = gain_in[:, line * lanes : (line + 1) * lanes]
    small_out[lines:, :] = bias_total[0]


def add_key_grads(hops, heads, scaling, table, mask, query, grad, key, value, sums, store):
    width = query.shape[1] // heads
    pair = Pair(mask, table, heads, hops, True)

    def scores(head):
        cols = columns(head, width)
        score = contract(key[:, cols], query[:, cols], 1, 1)
        return score, contract(value[:, cols], grad[:, cols], 1, 1)

    def differentiate(head, found):
        cols = columns(head, width)
        half = pair.half_logits(found[0], head, scaling)
        tanh = jnp.tanh(half)
        rounded = (found[1] * (slope_of(half, tanh) * pair.mask)).astype(BF16)
        weights = ((half + half * tanh) * pair.mask).astype(BF16)
        parts = [contract(rounded, query[:, cols], 1, 0), contract(weights, grad[:, cols], 1, 0)]
        store(head, cols, *[part + held[:, cols] for part, held in zip(parts, sums)] or parts)

    in_stages(heads, scores, differentiate)


def into(key_out, value_out):
    def store(head, cols, key_part, value_part):
        key_out[:, cols] = key_part
        value_out[:, cols] = value_part

    return store


def next_key_kernel(hops, heads, scaling, *refs):
    add_key_grads(hops, heads, scaling, *refs[:6], refs[6:-2], into(*refs[-2:]))


def gate_and_key_kernel(hops, heads, scaling, *refs):
    attention, out_grad, gain = refs[8:11]
    gate_out, key_out, value_out, held, written = refs[11:]
    step = 16
    gain_row = gain[...]
    for low in range(0, attention.shape[0], step):
        span = slice(low, low + step)
        normed, _ = normed_rows(attention[span, :])
        held[span, :] = (out_grad[span, :].astype(F32) * normed * gain_row).astype(BF16)
    copy = pltpu.make_async_copy(held, gate_out, written)
    copy.start()
    add_key_grads(hops, heads, scaling, *refs[:6], refs[6:8], into(key_out, value_out))
    copy.wait()


def slopes_kernel(hops, heads, scaling, table, mask, query, key, weights, slopes):
    pair = Pair(mask, table, heads, hops, True)
    rows, width = query.shape[0], query.shape[1] // heads

    def scores(head):
        cols = columns(head, width)
        return contract(key[:, cols], query[:, cols], 1, 1)

    def derive(head, found):
        half = pair.half_logits(found, head, scaling)
        tanh = jnp.tanh(half)
        lines = columns(head, rows)
        weights[lines, :] = ((half + half * tanh) * pair.mask).astype(BF16)
        slopes[lines, :] = slope_of(half, tanh) * pair.mask

    in_stages(heads, scores, derive)


def last_kernel(heads, scaling, *refs):
    weights, slopes, query, grad, value, key_in, value_in = refs[:7]
    pieces, outs, held, written = refs[7:-9], refs[-9:-5], refs[-5:-1], refs[-1]
    rows, width = query.shape[0], query.shape[1] // heads
    copies = []
    ends = [*range(1, heads - 1, 2), heads - 2, heads - 1]

    def write(at, cols):
        source, target = held[at].at[:, cols], outs[at].at[:, cols]
        copies.append(pltpu.make_async_copy(source, target, written.at[len(copies)]))
        copies[-1].start()

    total = added_up([piece[...] for piece in pieces])
    lines = held[2].shape[0]
    held[2][...] = total[:lines]
    held[3][...] = total[lines:, :heads]
    for at in (2, 3):
        write(at, slice(0, held[at].shape[1]))

    def scores(head):
        cols = columns(head, width)
        return contract(value[:, cols], grad[:, cols], 1, 1)

    def differentiate(head, found):
        cols, lines = columns(head, width), columns(head, rows)
        rounded = (found * slopes[lines, :]).astype(BF16)
        key_part = key_in[:, cols] + contract(rounded, query[:, cols], 1, 0)
        value_part = value_in[:, cols] + contract(weights[lines, :], grad[:, cols], 1, 0)
        held[0][:, cols] = (key_part * scaling).astype(BF16)
        held[1][:, cols] = value_part.astype(BF16)
        if head in ends:
            before = ends[ends.index(head) - 1] + 1 if head != ends[0] else 0
            for at in (0, 1):
                write(at, slice(before * width, cols.stop))

    in_stages(heads, scores, differentiate)
    for copy in copies:
        copy.wait()


def on_device(kernel, outs, args, smem=(), ahead=(), far=(), far_outs=0, scratch=()):
    count = len(smem) + len(far) + len(args)
    far = [pltpu.with_memory_space_constraint(array, pltpu.HBM) for array in far]

    def body(*refs):
        kernel(*refs[:count], *refs[count + len(ahead) :])

    vmem, anywhere = pl.BlockSpec(memory_space=pltpu.VMEM), pl.BlockSpec(memory_space=pl.ANY)
    return pl.pallas_call(
        body,
        out_shape=outs,
        in_specs=[pl.BlockSpec(memory_space=pltpu.SMEM)] * len(smem)
        + [pl.BlockSpec(memory_space=pltpu.HBM)] * len(far)
        + [vmem] * len(args)
        + [anywhere] * len(ahead),
        out_specs=[anywhere] * far_outs + [vmem] * (len(outs) - far_outs),
        scratch_shapes=scratch,
        compiler_params=pltpu.CompilerParams(vmem_limit_bytes=VMEM_LIMIT),
        cost_estimate=pl.CostEstimate(flops=1000000, bytes_accessed=100000, transcendentals=0),
    )(*smem, *far, *args, *ahead)


def rounds_of(axes):
    rounds = []
    for axis in axes:
        size = lax.axis_size(axis)
        step = 1
        while step < size:
            radix = 4 if size // step >= 4 else 2
            rounds.append((axis, [step * at for at in range(1, radix)]))
            step = radix * step
    return rounds


def exchanged(array, axis, distances):
    size = lax.axis_size(axis)
    found = [
        lax.ppermute(array, axis, [(i, i ^ distance) for i in range(size)])
        for distance in reversed(distances)
    ]
    return [array] + found[::-1]


def added_up(pieces):
    while len(pieces) > 1:
        pieces = [left + right for left, right in zip(pieces[::2], pieces[1::2])]
    return pieces[0]


def local(queries, key_rows, value_rows, update_gate, out_grad, user_lengths, rel_bias, norm_gain):
    rows, features = queries.shape[1:]
    levels, heads = rel_bias.shape
    scaling = (features // heads) ** (-0.5)
    reach = min(3, lax.axis_size("ctx") // 2)
    wide = jax.ShapeDtypeStruct((rows, features), F32)
    narrow = jax.ShapeDtypeStruct((rows, features), BF16)
    inputs = (queries[0], key_rows[0], value_rows[0], update_gate[0], out_grad[0])
    gain = norm_gain[None]

    arrived = [passed_along(inputs[at], "ctx", by) for at, by in ((1, 1), (2, 1), (0, -1))]

    hop_list = tuple(range(reach + 1))
    plan = [(0, hops, False) for hops in hop_list] + [(hops, hops, True) for hops in hop_list]
    outs = [jax.ShapeDtypeStruct((count * heads, rows), F32) for count in (levels, rows)]
    outs += [jax.ShapeDtypeStruct((rows, rows), F32)] * len(plan)
    outs += [narrow] * len(inputs) + [wide]
    table, near, *found = on_device(
        partial(first_kernel, plan, heads, scaling),
        outs,
        (),
        (user_lengths, rel_bias),
        far=inputs,
        scratch=[pltpu.SemaphoreType.DMA((len(inputs),))],
    )
    masks, flipped = found[: reach + 1], found[reach + 1 : 2 * reach + 2]
    query, key, value, gate, grad, attention = found[2 * reach + 2 :]

    later_queries = [query, arrived[2]]
    keys, values = [key, arrived[0]], [value, arrived[1]]
    for hops in range(1, reach):
        keys.append(passed_along(keys[-1], "ctx", 1, hops + 1))
        values.append(passed_along(values[-1], "ctx", 1, hops + 1))
        later_queries.append(passed_along(later_queries[-1], "ctx", -1, hops + 1))
    for hops in range(1, reach):
        (attention,) = on_device(
            partial(forward_kernel, hops, heads, scaling),
            [wide],
            (table, near, masks[hops], query, keys[hops], values[hops], attention),
            ahead=later_queries[hops : hops + 1],
        )
    stacked = (heads * rows, rows)
    (far_weights,) = on_device(
        partial(weights_kernel, reach, heads, scaling),
        [jax.ShapeDtypeStruct(stacked, BF16)],
        (table, near, masks[-1], query, keys[-1]),
        ahead=[attention],
    )
    attention, attn_grad, gain_part = on_device(
        partial(norm_kernel, heads),
        [wide, narrow, jax.ShapeDtypeStruct((1, features), F32)],
        (far_weights, values[-1], attention, grad, gate, gain),
    )

    lanes = features // 8
    query_grad, sums = on_device(
        partial(backward_query_kernel, hop_list, heads, scaling),
        [narrow, jax.ShapeDtypeStruct((8 + levels, lanes), F32)],
        (table, near, *masks, query, attn_grad, *keys, *values, gain_part),
        ahead=later_queries[reach:],
    )
    later_grads = [attn_grad, passed_along(attn_grad, "ctx", -1)]
    pieces = [sums]
    for axis, distances in rounds_of(("dp",)):
        pieces = exchanged(added_up(pieces), axis, distances)

    def key_operands(hops):
        later = (later_queries[hops], later_grads[hops])
        return (table, flipped[hops], *later, key, value)

    key_grads = on_device(
        partial(next_key_kernel, 0, heads, scaling),
        [wide] * 2,
        key_operands(0),
        ahead=pieces[1:2],
    )
    for hops in range(1, reach):
        arrived, *pieces = lax.optimization_barrier((later_grads[hops], *pieces))
        later_grads.append(passed_along(arrived, "ctx", -1, hops + 1))
        if hops == 1:
            gate_grad, *key_grads = on_device(
                partial(gate_and_key_kernel, hops, heads, scaling),
                [narrow, wide, wide],
                (*key_operands(hops), *key_grads, attention, grad, gain),
                far_outs=1,
                scratch=[pltpu.VMEM((rows, features), BF16), pltpu.SemaphoreType.DMA(())],
            )
        else:
            key_grads = on_device(
                partial(next_key_kernel, hops, heads, scaling),
                [wide] * 2,
                (*key_operands(hops), *key_grads),
            )
    far_tables = on_device(
        partial(slopes_kernel, reach, heads, scaling),
        [jax.ShapeDtypeStruct(stacked, BF16), jax.ShapeDtypeStruct(stacked, F32)],
        (table, flipped[reach], later_queries[reach], key),
        ahead=key_grads[:1],
    )
    key_grads, far_tables, *pieces = lax.optimization_barrier((key_grads, far_tables, *pieces))
    for axis, distances in rounds_of(("ctx",)):
        pieces = exchanged(added_up(pieces), axis, distances)
    small = [(8, lanes), (levels, heads)]
    key_grad, value_grad, gain_grad, bias_grad = on_device(
        partial(last_kernel, heads, scaling),
        [narrow, narrow, *[jax.ShapeDtypeStruct(shape, F32) for shape in small]],
        (
            *far_tables,
            later_queries[reach],
            later_grads[reach],
            value,
            *key_grads,
            *pieces[::-1],
        ),
        far_outs=4,
        scratch=[pltpu.VMEM((rows, features), BF16)] * 2
        + [pltpu.VMEM(shape, F32) for shape in small]
        + [pltpu.SemaphoreType.DMA((2 * heads + 2,))],
    )
    return (
        query_grad[None],
        key_grad[None],
        value_grad[None],
        gate_grad[None],
        bias_grad,
        gain_grad.reshape(features),
    )


def solution(mesh):
    in_specs = (
        P(("groups", "dp"), "ctx", None),
        P(("groups", "dp"), "ctx", None),
        P(("groups", "dp"), "ctx", None),
        P(("groups", "dp"), "ctx", None),
        P(("groups", "dp"), "ctx", None),
        P(("groups", "dp"), None),
        P(),
        P(),
    )
    out_specs = (
        P(("groups", "dp"), "ctx", None),
        P(("groups", "dp"), "ctx", None),
        P(("groups", "dp"), "ctx", None),
        P(("groups", "dp"), "ctx", None),
        P("groups", None),
        P("groups"),
    )
    return jax.shard_map(local, mesh=mesh, in_specs=in_specs, out_specs=out_specs, check_vma=False)
```

```python
from functools import partial

import jax
import jax.numpy as jnp
from jax import lax
from jax.experimental import pallas as pl
from jax.experimental.pallas import tpu as pltpu
from jax.sharding import PartitionSpec as P

EPSILON = 1e-05
VMEM_LIMIT = 24 * 1024 * 1024
F32 = jnp.float32
BF16 = jnp.bfloat16


def passed_along(array, axis, by, hop=1):
    size = lax.axis_size(axis)
    first, last = (hop - 1, size - 2) if by > 0 else (1, size - hop)
    return lax.ppermute(array, axis, [(i, i + by) for i in range(first, last + 1)])


def contract(left, right, left_dim, right_dim):
    return lax.dot_general(
        left, right, (((left_dim,), (right_dim,)), ((), ())), preferred_element_type=F32
    )


def user_starts(lengths, query_pos):
    end = jnp.int32(0)
    start = jnp.zeros(query_pos.shape, jnp.int32)
    for user in range(lengths.shape[1]):
        end = end + lengths[0, user]
        start = jnp.where(query_pos >= end, end, start)
    return start


class Pair:
    def __init__(self, mask, table, heads, hops, flipped=False, near=None):
        rows = mask.shape[0]
        self.table, self.heads, self.levels = table, heads, table.shape[0] // heads
        self.mask, self.hops, self.near = mask[...], hops, near
        self.far = (hops - 1) * rows + 1 >= 2 ** (self.levels - 2)
        if not self.far:
            query_dim, key_dim = (1, 0) if flipped else (0, 1)
            query_row = lax.broadcasted_iota(jnp.int32, mask.shape, query_dim)
            key_row = lax.broadcasted_iota(jnp.int32, mask.shape, key_dim)
            self.distance = query_row - key_row + hops * rows

    def half_bias(self, head):
        def level_row(level):
            at = level * self.heads + head
            return self.table[at : at + 1, :]

        value = level_row(self.levels - 1)
        if self.far:
            return value
        if self.near is not None:
            rows = self.mask.shape[0]
            close = self.near[head * rows : (head + 1) * rows, :]
            return close if self.hops == 0 else jnp.where(self.distance < rows, close, value)
        for level in range(self.levels - 2, -1, -1):
            value = jnp.where(self.distance < 2**level, level_row(level), value)
        return value

    def half_logits(self, scores, head, scaling):
        return scores * (0.5 * scaling) + self.half_bias(head)


def slope_of(half, tanh):
    return (0.5 + 0.5 * tanh) * (1.0 + half * (1.0 - tanh))


def columns(head, width):
    return slice(head * width, (head + 1) * width)


def in_stages(count, first, second, ahead=3):
    held = [first(i) for i in range(min(ahead, count))]
    for i in range(count):
        if i + ahead < count:
            held.append(first(i + ahead))
        second(i, held.pop(0))


def attend(pairs, heads, scaling, query, keys, values, total, out):
    width = query.shape[1] // heads

    def scores(head):
        cols = columns(head, width)
        return [contract(query[:, cols], key[:, cols], 1, 1) for key in keys]

    def weigh(head, found):
        cols = columns(head, width)
        part = None if total is None else total[:, cols]
        for pair, score, value in zip(pairs, found, values):
            half = pair.half_logits(score, head, scaling)
            weights = ((half + half * jnp.tanh(half)) * pair.mask).astype(BF16)
            added = contract(weights, value[:, cols], 1, 0)
            part = added if part is None else part + added
        out[:, cols] = part.astype(out.dtype)

    in_stages(heads, scores, weigh)


def first_kernel(plan, heads, scaling, lengths, bias, *refs):
    inputs, refs = refs[:5], refs[5:]
    table, near, masks, refs = refs[0], refs[1], refs[2 : 2 + len(plan)], refs[2 + len(plan) :]
    held, out, arrived = refs[:5], refs[5], refs[6]
    copies = [
        pltpu.make_async_copy(source, target, arrived.at[at])
        for at, (source, target) in enumerate(zip(inputs, held))
    ]
    for copy in copies:
        copy.start()
    levels = bias.shape[0]
    for level in range(levels):
        for head in range(heads):
            at = level * heads + head
            table[at : at + 1, :] = jnp.full((1, table.shape[1]), 0.5 * bias[level, head], F32)
    rows = masks[0].shape[0]
    apart = lax.broadcasted_iota(jnp.int32, (rows, rows), 0)
    apart = (apart - lax.broadcasted_iota(jnp.int32, (rows, rows), 1)) & (rows - 1)
    for head in range(heads):
        value = table[(levels - 1) * heads + head : (levels - 1) * heads + head + 1, :]
        for level in range(levels - 2, -1, -1):
            at = level * heads + head
            value = jnp.where(apart < 2**level, table[at : at + 1, :], value)
        near[head * rows : (head + 1) * rows, :] = value
    for (block, hops, flipped), mask in zip(plan, masks):
        query_dim, key_dim = (1, 0) if flipped else (0, 1)
        line = (1, rows) if flipped else (rows, 1)
        first = (lax.axis_index("ctx") + block) * rows
        query_pos = first + lax.broadcasted_iota(jnp.int32, line, query_dim)
        key_pos = first - hops * rows + lax.broadcasted_iota(jnp.int32, mask.shape, key_dim)
        seen = (key_pos >= user_starts(lengths, query_pos)) & (key_pos <= query_pos)
        mask[...] = jnp.where(seen, 1.0, 0.0).astype(F32)
    for copy in copies:
        copy.wait()
    query, key, value = held[:3]
    pair = Pair(masks[0], table, heads, 0, near=near)
    attend([pair], heads, scaling, query, [key], [value], None, out)


def forward_kernel(hops, heads, scaling, table, near, mask, query, key, value, total, out):
    pair = Pair(mask, table, heads, hops, near=near)
    attend([pair], heads, scaling, query, [key], [value], total, out)


def normed_rows(attention):
    center = attention - jnp.mean(attention, axis=1, keepdims=True)
    inverse = lax.rsqrt(jnp.mean(center * center, axis=1, keepdims=True) + EPSILON)
    return center * inverse, inverse


def weights_kernel(hops, heads, scaling, table, near, mask, query, key, weights):
    pair = Pair(mask, table, heads, hops, near=near)
    rows, width = query.shape[0], query.shape[1] // heads

    def scores(head):
        cols = columns(head, width)
        return contract(query[:, cols], key[:, cols], 1, 1)

    def weigh(head, found):
        half = pair.half_logits(found, head, scaling)
        lines = columns(head, rows)
        weights[lines, :] = ((half + half * jnp.tanh(half)) * pair.mask).astype(BF16)

    in_stages(heads, scores, weigh)


def norm_kernel(heads, *refs):
    weights, value, total, out_grad, update_gate, gain = refs[:6]
    attention, attn_grad, gain_grad = refs[6:]
    width = total.shape[1] // heads
    for head in range(heads):
        cols, lines = columns(head, width), columns(head, total.shape[0])
        attention[:, cols] = total[:, cols] + contract(weights[lines, :], value[:, cols], 1, 0)
    rows, features = attention.shape
    step = 16
    gain_row = gain[...]
    gain_sum = jnp.zeros((8, features), F32)
    for low in range(0, rows, step):
        span = slice(low, low + step)
        normed, inverse = normed_rows(attention[span, :])
        gated = out_grad[span, :].astype(F32) * update_gate[span, :].astype(F32)
        product = gated * normed
        for part in range(0, step, 8):
            gain_sum = gain_sum + product[part : part + 8, :]
        pushed = gated * gain_row
        attn_grad[span, :] = (
            inverse
            * (
                pushed
                - jnp.mean(pushed, axis=1, keepdims=True)
                - normed * jnp.mean(pushed * normed, axis=1, keepdims=True)
            )
        ).astype(BF16)
    gain_grad[...] = jnp.sum(gain_sum, axis=0, keepdims=True)


def backward_query_kernel(hop_list, heads, scaling, *refs):
    count = len(hop_list)
    table, near, masks, refs = refs[0], refs[1], refs[2 : 2 + count], refs[2 + count :]
    query, grad, keys, values = refs[0], refs[1], refs[2 : 2 + count], refs[2 + count : 2 + 2 * count]
    gain_in, query_out, small_out = refs[2 + 2 * count :]
    rows, width = query.shape[0], query.shape[1] // heads
    pairs = [Pair(mask, table, heads, hops, near=near) for mask, hops in zip(masks, hop_list)]
    lanes = small_out.shape[1]
    lines = gain_in.shape[1] // lanes
    levels = small_out.shape[0] - lines
    lane = lax.broadcasted_iota(jnp.int32, (levels, lanes), 1)
    level_row = lax.broadcasted_iota(jnp.int32, (levels, lanes), 0)
    group = lax.broadcasted_iota(jnp.int32, (8, rows), 0)
    distance = (group - lax.broadcasted_iota(jnp.int32, (8, rows), 1)) & (rows - 1)
    bucket = sum((distance >= 2**level).astype(jnp.int32) for level in range(levels - 1))
    own = pairs[0].distance >= 0
    bias_total = [jnp.zeros((levels, lanes), F32)]

    def bias_sums(grads):
        close = jnp.where(own, grads[0], grads[1])
        rest = sum(grads[2:], jnp.where(own, grads[1], 0.0))
        by_place, far = jnp.zeros((8, rows), F32), jnp.zeros((8, rows), F32)
        for low in range(0, rows, 8):
            part = close[low : low + 8, :]
            by_place = by_place + (pltpu.roll(part, rows - low, 1) if low else part)
            far = far + rest[low : low + 8, :]
        sums = jnp.where(level_row == levels - 1, jnp.sum(far, axis=0, keepdims=True), 0.0)
        for level in range(levels):
            row = jnp.sum(jnp.where(bucket == level, by_place, 0.0), axis=0, keepdims=True)
            sums = sums + jnp.where(level_row == level, row, 0.0)
        return sums

    def scores(head):
        cols = columns(head, width)
        query_h, grad_h = query[:, cols], grad[:, cols]
        return [
            (contract(query_h, key[:, cols], 1, 1), contract(grad_h, value[:, cols], 1, 1))
            for key, value in zip(keys, values)
        ]

    def differentiate(head, found):
        cols = columns(head, width)
        query_part, grads = None, []
        for pair, key, (score, weight_grad) in zip(pairs, keys, found):
            half = pair.half_logits(score, head, scaling)
            grads.append(weight_grad * (slope_of(half, jnp.tanh(half)) * pair.mask))
            added = contract(grads[-1].astype(BF16), key[:, cols], 1, 0)
            query_part = added if query_part is None else query_part + added
        query_out[:, cols] = (query_part * scaling).astype(BF16)
        sums = jnp.sum(bias_sums(grads), axis=1, keepdims=True)
        bias_total[0] = jnp.where(lane == head, sums, bias_total[0])

    in_stages(heads, scores, differentiate, 1)
    for line in range(lines):
        small_out[line : line + 1, :] = gain_in[:, line * lanes : (line + 1) * lanes]
    small_out[lines:, :] = bias_total[0]


def add_key_grads(hops, heads, scaling, table, mask, query, grad, key, value, sums, store):
    width = query.shape[1] // heads
    pair = Pair(mask, table, heads, hops, True)

    def scores(head):
        cols = columns(head, width)
        score = contract(key[:, cols], query[:, cols], 1, 1)
        return score, contract(value[:, cols], grad[:, cols], 1, 1)

    def differentiate(head, found):
        cols = columns(head, width)
        half = pair.half_logits(found[0], head, scaling)
        tanh = jnp.tanh(half)
        rounded = (found[1] * (slope_of(half, tanh) * pair.mask)).astype(BF16)
        weights = ((half + half * tanh) * pair.mask).astype(BF16)
        parts = [contract(rounded, query[:, cols], 1, 0), contract(weights, grad[:, cols], 1, 0)]
        store(head, cols, *[part + held[:, cols] for part, held in zip(parts, sums)] or parts)

    in_stages(heads, scores, differentiate)


def into(key_out, value_out):
    def store(head, cols, key_part, value_part):
        key_out[:, cols] = key_part
        value_out[:, cols] = value_part

    return store


def next_key_kernel(hops, heads, scaling, *refs):
    add_key_grads(hops, heads, scaling, *refs[:6], refs[6:-2], into(*refs[-2:]))


def gate_and_key_kernel(hops, heads, scaling, *refs):
    attention, out_grad, gain = refs[8:11]
    gate_out, key_out, value_out, held, written = refs[11:]
    step = 16
    gain_row = gain[...]
    for low in range(0, attention.shape[0], step):
        span = slice(low, low + step)
        normed, _ = normed_rows(attention[span, :])
        held[span, :] = (out_grad[span, :].astype(F32) * normed * gain_row).astype(BF16)
    copy = pltpu.make_async_copy(held, gate_out, written)
    copy.start()
    add_key_grads(hops, heads, scaling, *refs[:6], refs[6:8], into(key_out, value_out))
    copy.wait()


def slopes_kernel(hops, heads, scaling, table, mask, query, key, weights, slopes):
    pair = Pair(mask, table, heads, hops, True)
    rows, width = query.shape[0], query.shape[1] // heads

    def scores(head):
        cols = columns(head, width)
        return contract(key[:, cols], query[:, cols], 1, 1)

    def derive(head, found):
        half = pair.half_logits(found, head, scaling)
        tanh = jnp.tanh(half)
        lines = columns(head, rows)
        weights[lines, :] = ((half + half * tanh) * pair.mask).astype(BF16)
        slopes[lines, :] = slope_of(half, tanh) * pair.mask

    in_stages(heads, scores, derive)


def last_kernel(heads, scaling, *refs):
    weights, slopes, query, grad, value, key_in, value_in = refs[:7]
    outs, held, written = refs[7:9], refs[9:11], refs[11]
    rows, width = query.shape[0], query.shape[1] // heads
    copies = []
    ends = [*range(1, heads - 1, 2), heads - 2, heads - 1]

    def write(at, cols):
        source, target = held[at].at[:, cols], outs[at].at[:, cols]
        copies.append(pltpu.make_async_copy(source, target, written.at[len(copies)]))
        copies[-1].start()

    def scores(head):
        cols = columns(head, width)
        return contract(value[:, cols], grad[:, cols], 1, 1)

    def differentiate(head, found):
        cols, lines = columns(head, width), columns(head, rows)
        rounded = (found * slopes[lines, :]).astype(BF16)
        key_part = key_in[:, cols] + contract(rounded, query[:, cols], 1, 0)
        value_part = value_in[:, cols] + contract(weights[lines, :], grad[:, cols], 1, 0)
        held[0][:, cols] = (key_part * scaling).astype(BF16)
        held[1][:, cols] = value_part.astype(BF16)
        if head in ends:
            before = ends[ends.index(head) - 1] + 1 if head != ends[0] else 0
            for at in (0, 1):
                write(at, slice(before * width, cols.stop))

    in_stages(heads, scores, differentiate)
    for copy in copies:
        copy.wait()


def sum_kernel(*refs):
    gain_out, bias_out = refs[-2:]
    total = added_up([piece[...] for piece in refs[:-2]])
    lines = gain_out.shape[0]
    gain_out[...] = total[:lines]
    bias_out[...] = total[lines:, : bias_out.shape[1]]


def on_device(kernel, outs, args, smem=(), ahead=(), far=(), far_outs=0, scratch=()):
    count = len(smem) + len(far) + len(args)
    far = [pltpu.with_memory_space_constraint(array, pltpu.HBM) for array in far]

    def body(*refs):
        kernel(*refs[:count], *refs[count + len(ahead) :])

    vmem, anywhere = pl.BlockSpec(memory_space=pltpu.VMEM), pl.BlockSpec(memory_space=pl.ANY)
    return pl.pallas_call(
        body,
        out_shape=outs,
        in_specs=[pl.BlockSpec(memory_space=pltpu.SMEM)] * len(smem)
        + [pl.BlockSpec(memory_space=pltpu.HBM)] * len(far)
        + [vmem] * len(args)
        + [anywhere] * len(ahead),
        out_specs=[anywhere] * far_outs + [vmem] * (len(outs) - far_outs),
        scratch_shapes=scratch,
        compiler_params=pltpu.CompilerParams(vmem_limit_bytes=VMEM_LIMIT),
        cost_estimate=pl.CostEstimate(flops=1000000, bytes_accessed=100000, transcendentals=0),
    )(*smem, *far, *args, *ahead)


def rounds_of(axes):
    rounds = []
    for axis in axes:
        size = lax.axis_size(axis)
        step = 1
        while step < size:
            radix = 4 if size // step >= 4 else 2
            rounds.append((axis, [step * at for at in range(1, radix)]))
            step = radix * step
    return rounds


def exchanged(array, axis, distances):
    size = lax.axis_size(axis)
    found = [
        lax.ppermute(array, axis, [(i, i ^ distance) for i in range(size)])
        for distance in reversed(distances)
    ]
    return [array] + found[::-1]


def added_up(pieces):
    while len(pieces) > 1:
        pieces = [left + right for left, right in zip(pieces[::2], pieces[1::2])]
    return pieces[0]


def local(queries, key_rows, value_rows, update_gate, out_grad, user_lengths, rel_bias, norm_gain):
    rows, features = queries.shape[1:]
    levels, heads = rel_bias.shape
    scaling = (features // heads) ** (-0.5)
    reach = min(3, lax.axis_size("ctx") // 2)
    wide = jax.ShapeDtypeStruct((rows, features), F32)
    narrow = jax.ShapeDtypeStruct((rows, features), BF16)
    inputs = (queries[0], key_rows[0], value_rows[0], update_gate[0], out_grad[0])
    gain = norm_gain[None]

    arrived = [passed_along(inputs[at], "ctx", by) for at, by in ((1, 1), (2, 1), (0, -1))]

    hop_list = tuple(range(reach + 1))
    plan = [(0, hops, False) for hops in hop_list] + [(hops, hops, True) for hops in hop_list]
    outs = [jax.ShapeDtypeStruct((count * heads, rows), F32) for count in (levels, rows)]
    outs += [jax.ShapeDtypeStruct((rows, rows), F32)] * len(plan)
    outs += [narrow] * len(inputs) + [wide]
    table, near, *found = on_device(
        partial(first_kernel, plan, heads, scaling),
        outs,
        (),
        (user_lengths, rel_bias),
        far=inputs,
        scratch=[pltpu.SemaphoreType.DMA((len(inputs),))],
    )
    masks, flipped = found[: reach + 1], found[reach + 1 : 2 * reach + 2]
    query, key, value, gate, grad, attention = found[2 * reach + 2 :]

    later_queries = [query, arrived[2]]
    keys, values = [key, arrived[0]], [value, arrived[1]]
    for hops in range(1, reach):
        keys.append(passed_along(keys[-1], "ctx", 1, hops + 1))
        values.append(passed_along(values[-1], "ctx", 1, hops + 1))
        later_queries.append(passed_along(later_queries[-1], "ctx", -1, hops + 1))
    for hops in range(1, reach):
        (attention,) = on_device(
            partial(forward_kernel, hops, heads, scaling),
            [wide],
            (table, near, masks[hops], query, keys[hops], values[hops], attention),
            ahead=later_queries[hops : hops + 1],
        )
    stacked = (heads * rows, rows)
    (far_weights,) = on_device(
        partial(weights_kernel, reach, heads, scaling),
        [jax.ShapeDtypeStruct(stacked, BF16)],
        (table, near, masks[-1], query, keys[-1]),
        ahead=[attention],
    )
    attention, attn_grad, gain_part = on_device(
        partial(norm_kernel, heads),
        [wide, narrow, jax.ShapeDtypeStruct((1, features), F32)],
        (far_weights, values[-1], attention, grad, gate, gain),
    )

    lanes = features // 8
    query_grad, sums = on_device(
        partial(backward_query_kernel, hop_list, heads, scaling),
        [narrow, jax.ShapeDtypeStruct((8 + levels, lanes), F32)],
        (table, near, *masks, query, attn_grad, *keys, *values, gain_part),
        ahead=later_queries[reach:],
    )
    later_grads = [attn_grad, passed_along(attn_grad, "ctx", -1)]
    pieces = [sums]
    for axis, distances in rounds_of(("dp",)):
        pieces = exchanged(added_up(pieces), axis, distances)

    def key_operands(hops):
        later = (later_queries[hops], later_grads[hops])
        return (table, flipped[hops], *later, key, value)

    key_grads = on_device(
        partial(next_key_kernel, 0, heads, scaling),
        [wide] * 2,
        key_operands(0),
        ahead=pieces[1:2],
    )
    for hops in range(1, reach):
        arrived, *pieces = lax.optimization_barrier((later_grads[hops], *pieces))
        later_grads.append(passed_along(arrived, "ctx", -1, hops + 1))
        if hops == 1:
            gate_grad, *key_grads = on_device(
                partial(gate_and_key_kernel, hops, heads, scaling),
                [narrow, wide, wide],
                (*key_operands(hops), *key_grads, attention, grad, gain),
                far_outs=1,
                scratch=[pltpu.VMEM((rows, features), BF16), pltpu.SemaphoreType.DMA(())],
            )
        else:
            key_grads = on_device(
                partial(next_key_kernel, hops, heads, scaling),
                [wide] * 2,
                (*key_operands(hops), *key_grads),
            )
    far_tables = on_device(
        partial(slopes_kernel, reach, heads, scaling),
        [jax.ShapeDtypeStruct(stacked, BF16), jax.ShapeDtypeStruct(stacked, F32)],
        (table, flipped[reach], later_queries[reach], key),
        ahead=key_grads[:1],
    )
    key_grads, far_tables, *pieces = lax.optimization_barrier((key_grads, far_tables, *pieces))
    for axis, distances in rounds_of(("ctx",)):
        pieces = exchanged(added_up(pieces), axis, distances)
    key_grad, value_grad = on_device(
        partial(last_kernel, heads, scaling),
        [narrow, narrow],
        (*far_tables, later_queries[reach], later_grads[reach], value, *key_grads),
        far_outs=2,
        scratch=[pltpu.VMEM((rows, features), BF16)] * 2 + [pltpu.SemaphoreType.DMA((2 * heads,))],
    )
    key_grad, value_grad, pieces[0] = lax.optimization_barrier((key_grad, value_grad, pieces[0]))
    gain_grad, bias_grad = on_device(
        sum_kernel,
        [jax.ShapeDtypeStruct((8, lanes), F32), jax.ShapeDtypeStruct((levels, heads), F32)],
        pieces[::-1],
    )
    return (
        query_grad[None],
        key_grad[None],
        value_grad[None],
        gate_grad[None],
        bias_grad,
        gain_grad.reshape(features),
    )


def solution(mesh):
    in_specs = (
        P(("groups", "dp"), "ctx", None),
        P(("groups", "dp"), "ctx", None),
        P(("groups", "dp"), "ctx", None),
        P(("groups", "dp"), "ctx", None),
        P(("groups", "dp"), "ctx", None),
        P(("groups", "dp"), None),
        P(),
        P(),
    )
    out_specs = (
        P(("groups", "dp"), "ctx", None),
        P(("groups", "dp"), "ctx", None),
        P(("groups", "dp"), "ctx", None),
        P(("groups", "dp"), "ctx", None),
        P("groups", None),
        P("groups"),
    )
    return jax.shard_map(local, mesh=mesh, in_specs=in_specs, out_specs=out_specs, check_vma=False)
```

```python
from functools import partial

import jax
import jax.numpy as jnp
from jax import lax
from jax.experimental import pallas as pl
from jax.experimental.pallas import tpu as pltpu
from jax.sharding import PartitionSpec as P

EPSILON = 1e-05
VMEM_LIMIT = 24 * 1024 * 1024
F32 = jnp.float32
BF16 = jnp.bfloat16


def passed_along(array, axis, by, hop=1):
    size = lax.axis_size(axis)
    first, last = (hop - 1, size - 2) if by > 0 else (1, size - hop)
    return lax.ppermute(array, axis, [(i, i + by) for i in range(first, last + 1)])


def contract(left, right, left_dim, right_dim):
    return lax.dot_general(
        left, right, (((left_dim,), (right_dim,)), ((), ())), preferred_element_type=F32
    )


def user_starts(lengths, query_pos):
    end = jnp.int32(0)
    start = jnp.zeros(query_pos.shape, jnp.int32)
    for user in range(lengths.shape[1]):
        end = end + lengths[0, user]
        start = jnp.where(query_pos >= end, end, start)
    return start


class Pair:
    def __init__(self, mask, table, heads, hops, flipped=False, near=None):
        rows = table.shape[1]
        self.table, self.heads, self.levels = table, heads, table.shape[0] // heads
        self.mask, self.hops, self.near = mask[...], hops, near
        self.far = (hops - 1) * rows + 1 >= 2 ** (self.levels - 2)
        if not self.far:
            query_dim, key_dim = (1, 0) if flipped else (0, 1)
            query_row = lax.broadcasted_iota(jnp.int32, mask.shape, query_dim)
            key_row = lax.broadcasted_iota(jnp.int32, mask.shape, key_dim)
            self.distance = query_row - key_row + hops * rows

    def half_bias(self, head):
        def level_row(level):
            at = level * self.heads + head
            return self.table[at : at + 1, : self.mask.shape[1]]

        value = level_row(self.levels - 1)
        if self.far:
            return value
        if self.near is not None:
            rows = self.mask.shape[0]
            close = self.near[head * rows : (head + 1) * rows, :]
            return close if self.hops == 0 else jnp.where(self.distance < rows, close, value)
        for level in range(self.levels - 2, -1, -1):
            value = jnp.where(self.distance < 2**level, level_row(level), value)
        return value

    def half_logits(self, scores, head, scaling):
        return scores * (0.5 * scaling) + self.half_bias(head)


def slope_of(half, tanh):
    return (0.5 + 0.5 * tanh) * (1.0 + half * (1.0 - tanh))


def columns(head, width):
    return slice(head * width, (head + 1) * width)


def in_stages(count, first, second, ahead=3):
    held = [first(i) for i in range(min(ahead, count))]
    for i in range(count):
        if i + ahead < count:
            held.append(first(i + ahead))
        second(i, held.pop(0))


def attend(pairs, heads, scaling, query, keys, values, total, out):
    width = query.shape[1] // heads

    def scores(head):
        cols = columns(head, width)
        return [contract(query[:, cols], key[:, cols], 1, 1) for key in keys]

    def weigh(head, found):
        cols = columns(head, width)
        part = None if total is None else total[:, cols]
        for pair, score, value in zip(pairs, found, values):
            half = pair.half_logits(score, head, scaling)
            weights = ((half + half * jnp.tanh(half)) * pair.mask).astype(BF16)
            added = contract(weights, value[:, cols], 1, 0)
            part = added if part is None else part + added
        out[:, cols] = part.astype(out.dtype)

    in_stages(heads, scores, weigh)


def far_start(lengths, block, reach, rows):
    first = (lax.axis_index("ctx") + block) * rows
    end, start = jnp.int32(0), jnp.int32(0)
    for user in range(lengths.shape[1]):
        end = end + lengths[0, user]
        start = jnp.where(first >= end, end, start)
    return start - (first - reach * rows)


def first_kernel(plan, cut, heads, scaling, lengths, bias, *refs):
    inputs, refs = refs[:5], refs[5:]
    table, near, masks, refs = refs[0], refs[1], refs[2 : 2 + len(plan)], refs[2 + len(plan) :]
    late, refs = refs[0], refs[1:]
    held, out, arrived = refs[:5], refs[5], refs[6]
    copies = [
        pltpu.make_async_copy(source, target, arrived.at[at])
        for at, (source, target) in enumerate(zip(inputs, held))
    ]
    for copy in copies:
        copy.start()
    levels = bias.shape[0]
    for level in range(levels):
        for head in range(heads):
            at = level * heads + head
            table[at : at + 1, :] = jnp.full((1, table.shape[1]), 0.5 * bias[level, head], F32)
    rows = masks[0].shape[0]
    apart = lax.broadcasted_iota(jnp.int32, (rows, rows), 0)
    apart = (apart - lax.broadcasted_iota(jnp.int32, (rows, rows), 1)) & (rows - 1)
    for head in range(heads):
        value = table[(levels - 1) * heads + head : (levels - 1) * heads + head + 1, :]
        for level in range(levels - 2, -1, -1):
            at = level * heads + head
            value = jnp.where(apart < 2**level, table[at : at + 1, :], value)
        near[head * rows : (head + 1) * rows, :] = value
    for (block, hops, flipped), mask in zip(plan, masks):
        query_dim, key_dim = (1, 0) if flipped else (0, 1)
        line = (1, mask.shape[1]) if flipped else (mask.shape[0], 1)
        first = (lax.axis_index("ctx") + block) * rows
        query_pos = first + lax.broadcasted_iota(jnp.int32, line, query_dim)
        key_first = first - hops * rows + rows - mask.shape[key_dim]
        key_pos = key_first + lax.broadcasted_iota(jnp.int32, mask.shape, key_dim)
        seen = (key_pos >= user_starts(lengths, query_pos)) & (key_pos <= query_pos)
        value = jnp.where(seen, 1.0, 0.0).astype(F32)
        if mask.shape == (rows, rows):
            mask[...] = value
            continue
        at = 0 if mask.shape[0] == rows else 1
        is_late = jnp.where(far_start(lengths, block, hops, rows) > cut, 1.0, 0.0).astype(F32)
        late[8 * at : 8 * at + 8, :] = jnp.full((8, rows), is_late, F32)
        mask[...] = value * (is_late if at else 1.0 - is_late)
    for copy in copies:
        copy.wait()
    query, key, value = held[:3]
    pair = Pair(masks[0], table, heads, 0, near=near)
    attend([pair], heads, scaling, query, [key], [value], None, out)


def forward_kernel(hops, heads, scaling, table, near, mask, query, key, value, total, out):
    pair = Pair(mask, table, heads, hops, near=near)
    attend([pair], heads, scaling, query, [key], [value], total, out)


def normed_rows(attention):
    center = attention - jnp.mean(attention, axis=1, keepdims=True)
    inverse = lax.rsqrt(jnp.mean(center * center, axis=1, keepdims=True) + EPSILON)
    return center * inverse, inverse


def weights_kernel(hops, heads, scaling, table, near, mask, query, key, weights):
    pair = Pair(mask, table, heads, hops, near=near)
    rows, width = query.shape[0], query.shape[1] // heads

    def scores(head):
        cols = columns(head, width)
        return contract(query[:, cols], key[:, cols], 1, 1)

    def weigh(head, found):
        half = pair.half_logits(found, head, scaling)
        lines = columns(head, rows)
        weights[lines, :] = ((half + half * jnp.tanh(half)) * pair.mask).astype(BF16)

    in_stages(heads, scores, weigh)


def norm_kernel(heads, *refs):
    weights, value, total, out_grad, update_gate, gain = refs[:6]
    attention, attn_grad, gain_grad = refs[6:]
    width = total.shape[1] // heads
    for head in range(heads):
        cols, lines = columns(head, width), columns(head, total.shape[0])
        attention[:, cols] = total[:, cols] + contract(weights[lines, :], value[:, cols], 1, 0)
    rows, features = attention.shape
    step = 16
    gain_row = gain[...]
    gain_sum = jnp.zeros((8, features), F32)
    for low in range(0, rows, step):
        span = slice(low, low + step)
        normed, inverse = normed_rows(attention[span, :])
        gated = out_grad[span, :].astype(F32) * update_gate[span, :].astype(F32)
        product = gated * normed
        for part in range(0, step, 8):
            gain_sum = gain_sum + product[part : part + 8, :]
        pushed = gated * gain_row
        attn_grad[span, :] = (
            inverse
            * (
                pushed
                - jnp.mean(pushed, axis=1, keepdims=True)
                - normed * jnp.mean(pushed * normed, axis=1, keepdims=True)
            )
        ).astype(BF16)
    gain_grad[...] = jnp.sum(gain_sum, axis=0, keepdims=True)


def backward_query_kernel(hop_list, heads, scaling, *refs):
    count = len(hop_list)
    table, near, masks, refs = refs[0], refs[1], refs[2 : 2 + count], refs[2 + count :]
    query, grad, keys, values = refs[0], refs[1], refs[2 : 2 + count], refs[2 + count : 2 + 2 * count]
    gain_in, query_out, small_out = refs[2 + 2 * count :]
    rows, width = query.shape[0], query.shape[1] // heads
    pairs = [Pair(mask, table, heads, hops, near=near) for mask, hops in zip(masks, hop_list)]
    lanes = small_out.shape[1]
    lines = gain_in.shape[1] // lanes
    levels = small_out.shape[0] - lines
    lane = lax.broadcasted_iota(jnp.int32, (levels, lanes), 1)
    level_row = lax.broadcasted_iota(jnp.int32, (levels, lanes), 0)
    group = lax.broadcasted_iota(jnp.int32, (8, rows), 0)
    distance = (group - lax.broadcasted_iota(jnp.int32, (8, rows), 1)) & (rows - 1)
    bucket = sum((distance >= 2**level).astype(jnp.int32) for level in range(levels - 1))
    own = pairs[0].distance >= 0
    bias_total = [jnp.zeros((levels, lanes), F32)]

    def bias_sums(grads):
        close = jnp.where(own, grads[0], grads[1])
        rest = sum(grads[2:], jnp.where(own, grads[1], 0.0))
        by_place, far = jnp.zeros((8, rows), F32), jnp.zeros((8, rows), F32)
        for low in range(0, rows, 8):
            part = close[low : low + 8, :]
            by_place = by_place + (pltpu.roll(part, rows - low, 1) if low else part)
            far = far + rest[low : low + 8, :]
        sums = jnp.where(level_row == levels - 1, jnp.sum(far, axis=0, keepdims=True), 0.0)
        for level in range(levels):
            row = jnp.sum(jnp.where(bucket == level, by_place, 0.0), axis=0, keepdims=True)
            sums = sums + jnp.where(level_row == level, row, 0.0)
        return sums

    def scores(head):
        cols = columns(head, width)
        query_h, grad_h = query[:, cols], grad[:, cols]
        return [
            (contract(query_h, key[:, cols], 1, 1), contract(grad_h, value[:, cols], 1, 1))
            for key, value in zip(keys, values)
        ]

    def differentiate(head, found):
        cols = columns(head, width)
        query_part, grads = None, []
        for pair, key, (score, weight_grad) in zip(pairs, keys, found):
            half = pair.half_logits(score, head, scaling)
            grads.append(weight_grad * (slope_of(half, jnp.tanh(half)) * pair.mask))
            added = contract(grads[-1].astype(BF16), key[:, cols], 1, 0)
            query_part = added if query_part is None else query_part + added
        query_out[:, cols] = (query_part * scaling).astype(BF16)
        sums = jnp.sum(bias_sums(grads), axis=1, keepdims=True)
        bias_total[0] = jnp.where(lane == head, sums, bias_total[0])

    in_stages(heads, scores, differentiate, 1)
    for line in range(lines):
        small_out[line : line + 1, :] = gain_in[:, line * lanes : (line + 1) * lanes]
    small_out[lines:, :] = bias_total[0]


def add_key_grads(hops, heads, scaling, table, mask, query, grad, key, value, sums, store):
    width = query.shape[1] // heads
    pair = Pair(mask, table, heads, hops, True)

    def scores(head):
        cols = columns(head, width)
        score = contract(key[:, cols], query[:, cols], 1, 1)
        return score, contract(value[:, cols], grad[:, cols], 1, 1)

    def differentiate(head, found):
        cols = columns(head, width)
        half = pair.half_logits(found[0], head, scaling)
        tanh = jnp.tanh(half)
        rounded = (found[1] * (slope_of(half, tanh) * pair.mask)).astype(BF16)
        weights = ((half + half * tanh) * pair.mask).astype(BF16)
        parts = [contract(rounded, query[:, cols], 1, 0), contract(weights, grad[:, cols], 1, 0)]
        store(head, cols, *[part + held[:, cols] for part, held in zip(parts, sums)] or parts)

    in_stages(heads, scores, differentiate)


def into(key_out, value_out):
    def store(head, cols, key_part, value_part):
        key_out[:, cols] = key_part
        value_out[:, cols] = value_part

    return store


def next_key_kernel(hops, heads, scaling, *refs):
    add_key_grads(hops, heads, scaling, *refs[:6], refs[6:-2], into(*refs[-2:]))


def gate_and_key_kernel(hops, heads, scaling, *refs):
    attention, out_grad, gain = refs[8:11]
    gate_out, key_out, value_out, held, written = refs[11:]
    step = 16
    gain_row = gain[...]
    for low in range(0, attention.shape[0], step):
        span = slice(low, low + step)
        normed, _ = normed_rows(attention[span, :])
        held[span, :] = (out_grad[span, :].astype(F32) * normed * gain_row).astype(BF16)
    copy = pltpu.make_async_copy(held, gate_out, written)
    copy.start()
    add_key_grads(hops, heads, scaling, *refs[:6], refs[6:8], into(key_out, value_out))
    copy.wait()


def message_kernel(hops, heads, scaling, *refs):
    table, mask, late, query, grad, key, value, out = refs
    tail, cut, width = mask.shape[0], out.shape[0], query.shape[1] // heads
    pair = Pair(mask, table, heads, hops, True)
    is_late = late[8:9, :width] > 0.5

    def scores(head):
        cols = columns(head, width)
        score = contract(key[cut:, cols], query[:, cols], 1, 1)
        return score, contract(value[cut:, cols], grad[:, cols], 1, 1)

    def choose(head, found):
        cols = columns(head, width)
        half = pair.half_logits(found[0], head, scaling)
        tanh = jnp.tanh(half)
        rounded = (found[1] * (slope_of(half, tanh) * pair.mask)).astype(BF16)
        weights = ((half + half * tanh) * pair.mask).astype(BF16)
        parts = [contract(rounded, query[:, cols], 1, 0), contract(weights, grad[:, cols], 1, 0)]
        for at, part in enumerate(parts):
            lines = slice(at * tail, (at + 1) * tail)
            out[lines, cols] = jnp.where(is_late, part, grad[lines, cols].astype(F32)).astype(BF16)
        out[2 * tail :, cols] = grad[2 * tail : cut, cols]

    in_stages(heads, scores, choose)


def slopes_kernel(hops, heads, scaling, table, mask, query, key, weights, slopes):
    pair = Pair(mask, table, heads, hops, True)
    rows, cut, width = mask.shape[0], mask.shape[1], query.shape[1] // heads

    def scores(head):
        cols = columns(head, width)
        return contract(key[:, cols], query[:cut, cols], 1, 1)

    def derive(head, found):
        half = pair.half_logits(found, head, scaling)
        tanh = jnp.tanh(half)
        lines = columns(head, rows)
        weights[lines, :] = ((half + half * tanh) * pair.mask).astype(BF16)
        slopes[lines, :] = slope_of(half, tanh) * pair.mask

    in_stages(heads, scores, derive)


def last_kernel(heads, scaling, *refs):
    weights, slopes, late, query, message, value, key_in, value_in = refs[:8]
    outs, held, written = refs[8:10], refs[10:12], refs[12]
    rows, cut, width = query.shape[0], message.shape[0], query.shape[1] // heads
    tail = rows - cut
    is_late = late[0:1, :width]
    copies = []
    ends = [*range(1, heads - 1, 2), heads - 2, heads - 1]

    def write(at, cols):
        source, target = held[at].at[:, cols], outs[at].at[:, cols]
        copies.append(pltpu.make_async_copy(source, target, written.at[len(copies)]))
        copies[-1].start()

    def scores(head):
        cols = columns(head, width)
        return contract(value[:, cols], message[:, cols], 1, 1)

    def differentiate(head, found):
        cols, lines = columns(head, width), columns(head, rows)
        rounded = (found * slopes[lines, :]).astype(BF16)
        parts = [
            contract(rounded, query[:cut, cols], 1, 0),
            contract(weights[lines, :], message[:, cols], 1, 0),
        ]
        for at, (part, before) in enumerate(zip(parts, (key_in, value_in))):
            factor = 1.0 if at else scaling
            held[at][:cut, cols] = ((before[:cut, cols] + part[:cut]) * factor).astype(BF16)
            sent = message[at * tail : (at + 1) * tail, cols].astype(F32) * is_late
            held[at][cut:, cols] = ((before[cut:, cols] + part[cut:] + sent) * factor).astype(BF16)
        if head in ends:
            before = ends[ends.index(head) - 1] + 1 if head != ends[0] else 0
            for at in (0, 1):
                write(at, slice(before * width, cols.stop))

    in_stages(heads, scores, differentiate)
    for copy in copies:
        copy.wait()


def sum_kernel(*refs):
    gain_out, bias_out = refs[-2:]
    total = added_up([piece[...] for piece in refs[:-2]])
    lines = gain_out.shape[0]
    gain_out[...] = total[:lines]
    bias_out[...] = total[lines:, : bias_out.shape[1]]


def on_device(kernel, outs, args, smem=(), ahead=(), far=(), far_outs=0, scratch=()):
    count = len(smem) + len(far) + len(args)
    far = [pltpu.with_memory_space_constraint(array, pltpu.HBM) for array in far]

    def body(*refs):
        kernel(*refs[:count], *refs[count + len(ahead) :])

    vmem, anywhere = pl.BlockSpec(memory_space=pltpu.VMEM), pl.BlockSpec(memory_space=pl.ANY)
    return pl.pallas_call(
        body,
        out_shape=outs,
        in_specs=[pl.BlockSpec(memory_space=pltpu.SMEM)] * len(smem)
        + [pl.BlockSpec(memory_space=pltpu.HBM)] * len(far)
        + [vmem] * len(args)
        + [anywhere] * len(ahead),
        out_specs=[anywhere] * far_outs + [vmem] * (len(outs) - far_outs),
        scratch_shapes=scratch,
        compiler_params=pltpu.CompilerParams(vmem_limit_bytes=VMEM_LIMIT),
        cost_estimate=pl.CostEstimate(flops=1000000, bytes_accessed=100000, transcendentals=0),
    )(*smem, *far, *args, *ahead)


def rounds_of(axes):
    rounds = []
    for axis in axes:
        size = lax.axis_size(axis)
        step = 1
        while step < size:
            radix = 4 if size // step >= 4 else 2
            rounds.append((axis, [step * at for at in range(1, radix)]))
            step = radix * step
    return rounds


def exchanged(array, axis, distances):
    size = lax.axis_size(axis)
    found = [
        lax.ppermute(array, axis, [(i, i ^ distance) for i in range(size)])
        for distance in reversed(distances)
    ]
    return [array] + found[::-1]


def added_up(pieces):
    while len(pieces) > 1:
        pieces = [left + right for left, right in zip(pieces[::2], pieces[1::2])]
    return pieces[0]


def local(queries, key_rows, value_rows, update_gate, out_grad, user_lengths, rel_bias, norm_gain):
    rows, features = queries.shape[1:]
    levels, heads = rel_bias.shape
    scaling = (features // heads) ** (-0.5)
    reach = min(3, lax.axis_size("ctx") // 2)
    wide = jax.ShapeDtypeStruct((rows, features), F32)
    narrow = jax.ShapeDtypeStruct((rows, features), BF16)
    inputs = (queries[0], key_rows[0], value_rows[0], update_gate[0], out_grad[0])
    gain = norm_gain[None]

    arrived = [passed_along(inputs[at], "ctx", by) for at, by in ((1, 1), (2, 1), (0, -1))]

    hop_list = tuple(range(reach + 1))
    plan = [(0, hops, False) for hops in hop_list] + [(hops, hops, True) for hops in hop_list]
    plan += [(reach - 1, reach, True)]
    cut = rows - rows // 4
    shapes = [(rows, rows)] * (len(plan) - 2) + [(rows, cut), (rows - cut, rows), (16, rows)]
    outs = [jax.ShapeDtypeStruct((count * heads, rows), F32) for count in (levels, rows)]
    outs += [jax.ShapeDtypeStruct(shape, F32) for shape in shapes]
    outs += [narrow] * len(inputs) + [wide]
    table, near, *found = on_device(
        partial(first_kernel, plan, cut, heads, scaling),
        outs,
        (),
        (user_lengths, rel_bias),
        far=inputs,
        scratch=[pltpu.SemaphoreType.DMA((len(inputs),))],
    )
    masks, flipped = found[: reach + 1], found[reach + 1 : 2 * reach + 2]
    sender_mask, late, query, key, value, gate, grad, attention = found[2 * reach + 2 :]

    later_queries = [query, arrived[2]]
    keys, values = [key, arrived[0]], [value, arrived[1]]
    for hops in range(1, reach):
        keys.append(passed_along(keys[-1], "ctx", 1, hops + 1))
        values.append(passed_along(values[-1], "ctx", 1, hops + 1))
        later_queries.append(passed_along(later_queries[-1], "ctx", -1, hops + 1))
    for hops in range(1, reach):
        (attention,) = on_device(
            partial(forward_kernel, hops, heads, scaling),
            [wide],
            (table, near, masks[hops], query, keys[hops], values[hops], attention),
            ahead=later_queries[hops : hops + 1],
        )
    stacked = (heads * rows, rows)
    (far_weights,) = on_device(
        partial(weights_kernel, reach, heads, scaling),
        [jax.ShapeDtypeStruct(stacked, BF16)],
        (table, near, masks[-1], query, keys[-1]),
        ahead=[attention],
    )
    attention, attn_grad, gain_part = on_device(
        partial(norm_kernel, heads),
        [wide, narrow, jax.ShapeDtypeStruct((1, features), F32)],
        (far_weights, values[-1], attention, grad, gate, gain),
    )

    lanes = features // 8
    query_grad, sums = on_device(
        partial(backward_query_kernel, hop_list, heads, scaling),
        [narrow, jax.ShapeDtypeStruct((8 + levels, lanes), F32)],
        (table, near, *masks, query, attn_grad, *keys, *values, gain_part),
        ahead=later_queries[reach:],
    )
    later_grads = [attn_grad, passed_along(attn_grad, "ctx", -1)]
    pieces = [sums]
    for axis, distances in rounds_of(("dp",)):
        pieces = exchanged(added_up(pieces), axis, distances)

    def key_operands(hops):
        later = (later_queries[hops], later_grads[hops])
        return (table, flipped[hops], *later, key, value)

    key_grads = on_device(
        partial(next_key_kernel, 0, heads, scaling),
        [wide] * 2,
        key_operands(0),
        ahead=pieces[1:2],
    )
    for hops in range(1, reach):
        arrived, *pieces = lax.optimization_barrier((later_grads[hops], *pieces))
        if hops + 1 == reach:
            (arrived,) = on_device(
                partial(message_kernel, reach, heads, scaling),
                [jax.ShapeDtypeStruct((cut, features), BF16)],
                (table, sender_mask, late, later_queries[hops], arrived, keys[1], values[1]),
            )
        later_grads.append(passed_along(arrived, "ctx", -1, hops + 1))
        if hops == 1:
            gate_grad, *key_grads = on_device(
                partial(gate_and_key_kernel, hops, heads, scaling),
                [narrow, wide, wide],
                (*key_operands(hops), *key_grads, attention, grad, gain),
                far_outs=1,
                scratch=[pltpu.VMEM((rows, features), BF16), pltpu.SemaphoreType.DMA(())],
            )
        else:
            key_grads = on_device(
                partial(next_key_kernel, hops, heads, scaling),
                [wide] * 2,
                (*key_operands(hops), *key_grads),
            )
    far_tables = on_device(
        partial(slopes_kernel, reach, heads, scaling),
        [jax.ShapeDtypeStruct((heads * rows, cut), kind) for kind in (BF16, F32)],
        (table, flipped[reach], later_queries[reach], key),
        ahead=key_grads[:1],
    )
    key_grads, far_tables, *pieces = lax.optimization_barrier((key_grads, far_tables, *pieces))
    for axis, distances in rounds_of(("ctx",)):
        pieces = exchanged(added_up(pieces), axis, distances)
    key_grad, value_grad = on_device(
        partial(last_kernel, heads, scaling),
        [narrow, narrow],
        (*far_tables, late, later_queries[reach], later_grads[reach], value, *key_grads),
        far_outs=2,
        scratch=[pltpu.VMEM((rows, features), BF16)] * 2 + [pltpu.SemaphoreType.DMA((2 * heads,))],
    )
    key_grad, value_grad, pieces[0] = lax.optimization_barrier((key_grad, value_grad, pieces[0]))
    gain_grad, bias_grad = on_device(
        sum_kernel,
        [jax.ShapeDtypeStruct((8, lanes), F32), jax.ShapeDtypeStruct((levels, heads), F32)],
        pieces,
    )
    return (
        query_grad[None],
        key_grad[None],
        value_grad[None],
        gate_grad[None],
        bias_grad,
        gain_grad.reshape(features),
    )


def solution(mesh):
    in_specs = (
        P(("groups", "dp"), "ctx", None),
        P(("groups", "dp"), "ctx", None),
        P(("groups", "dp"), "ctx", None),
        P(("groups", "dp"), "ctx", None),
        P(("groups", "dp"), "ctx", None),
        P(("groups", "dp"), None),
        P(),
        P(),
    )
    out_specs = (
        P(("groups", "dp"), "ctx", None),
        P(("groups", "dp"), "ctx", None),
        P(("groups", "dp"), "ctx", None),
        P(("groups", "dp"), "ctx", None),
        P("groups", None),
        P("groups"),
    )
    return jax.shard_map(local, mesh=mesh, in_specs=in_specs, out_specs=out_specs, check_vma=False)
```

```python
from functools import partial

import jax
import jax.numpy as jnp
from jax import lax
from jax.experimental import pallas as pl
from jax.experimental.pallas import tpu as pltpu
from jax.sharding import PartitionSpec as P

EPSILON = 1e-05
VMEM_LIMIT = 24 * 1024 * 1024
F32 = jnp.float32
BF16 = jnp.bfloat16


def passed_along(array, axis, by, hop=1):
    size = lax.axis_size(axis)
    first, last = (hop - 1, size - 2) if by > 0 else (1, size - hop)
    return lax.ppermute(array, axis, [(i, i + by) for i in range(first, last + 1)])


def contract(left, right, left_dim, right_dim):
    return lax.dot_general(
        left, right, (((left_dim,), (right_dim,)), ((), ())), preferred_element_type=F32
    )


def user_starts(lengths, query_pos):
    end = jnp.int32(0)
    start = jnp.zeros(query_pos.shape, jnp.int32)
    for user in range(lengths.shape[1]):
        end = end + lengths[0, user]
        start = jnp.where(query_pos >= end, end, start)
    return start


class Pair:
    def __init__(self, mask, table, heads, hops, flipped=False, near=None):
        rows = table.shape[1]
        self.table, self.heads, self.levels = table, heads, table.shape[0] // heads
        self.mask, self.hops, self.near = mask[...], hops, near
        self.far = (hops - 1) * rows + 1 >= 2 ** (self.levels - 2)
        if not self.far:
            query_dim, key_dim = (1, 0) if flipped else (0, 1)
            query_row = lax.broadcasted_iota(jnp.int32, mask.shape, query_dim)
            key_row = lax.broadcasted_iota(jnp.int32, mask.shape, key_dim)
            self.distance = query_row - key_row + hops * rows

    def half_bias(self, head):
        def level_row(level):
            at = level * self.heads + head
            return self.table[at : at + 1, : self.mask.shape[1]]

        value = level_row(self.levels - 1)
        if self.far:
            return value
        if self.near is not None:
            rows = self.mask.shape[0]
            close = self.near[head * rows : (head + 1) * rows, :]
            return close if self.hops == 0 else jnp.where(self.distance < rows, close, value)
        for level in range(self.levels - 2, -1, -1):
            value = jnp.where(self.distance < 2**level, level_row(level), value)
        return value

    def half_logits(self, scores, head, scaling):
        return scores * (0.5 * scaling) + self.half_bias(head)


def slope_of(half, tanh):
    return (0.5 + 0.5 * tanh) * (1.0 + half * (1.0 - tanh))


def columns(head, width):
    return slice(head * width, (head + 1) * width)


def in_stages(count, first, second, ahead=3):
    held = [first(i) for i in range(min(ahead, count))]
    for i in range(count):
        if i + ahead < count:
            held.append(first(i + ahead))
        second(i, held.pop(0))


def attend(pairs, heads, scaling, query, keys, values, total, out):
    width = query.shape[1] // heads

    def scores(head):
        cols = columns(head, width)
        return [contract(query[:, cols], key[:, cols], 1, 1) for key in keys]

    def weigh(head, found):
        cols = columns(head, width)
        part = None if total is None else total[:, cols]
        for pair, score, value in zip(pairs, found, values):
            half = pair.half_logits(score, head, scaling)
            weights = ((half + half * jnp.tanh(half)) * pair.mask).astype(BF16)
            added = contract(weights, value[:, cols], 1, 0)
            part = added if part is None else part + added
        out[:, cols] = part.astype(out.dtype)

    in_stages(heads, scores, weigh)


def far_start(lengths, block, reach, rows):
    first = (lax.axis_index("ctx") + block) * rows
    end, start = jnp.int32(0), jnp.int32(0)
    for user in range(lengths.shape[1]):
        end = end + lengths[0, user]
        start = jnp.where(first >= end, end, start)
    return start - (first - reach * rows)


def first_kernel(plan, cut, heads, scaling, lengths, bias, *refs):
    inputs, refs = refs[:5], refs[5:]
    table, near, masks, refs = refs[0], refs[1], refs[2 : 2 + len(plan)], refs[2 + len(plan) :]
    late, refs = refs[0], refs[1:]
    held, out, arrived = refs[:5], refs[5], refs[6]
    copies = [
        pltpu.make_async_copy(source, target, arrived.at[at])
        for at, (source, target) in enumerate(zip(inputs, held))
    ]
    for copy in copies:
        copy.start()
    levels = bias.shape[0]
    for level in range(levels):
        for head in range(heads):
            at = level * heads + head
            table[at : at + 1, :] = jnp.full((1, table.shape[1]), 0.5 * bias[level, head], F32)
    rows = masks[0].shape[0]
    apart = lax.broadcasted_iota(jnp.int32, (rows, rows), 0)
    apart = (apart - lax.broadcasted_iota(jnp.int32, (rows, rows), 1)) & (rows - 1)
    for head in range(heads):
        value = table[(levels - 1) * heads + head : (levels - 1) * heads + head + 1, :]
        for level in range(levels - 2, -1, -1):
            at = level * heads + head
            value = jnp.where(apart < 2**level, table[at : at + 1, :], value)
        near[head * rows : (head + 1) * rows, :] = value
    for (block, hops, flipped), mask in zip(plan, masks):
        query_dim, key_dim = (1, 0) if flipped else (0, 1)
        line = (1, mask.shape[1]) if flipped else (mask.shape[0], 1)
        first = (lax.axis_index("ctx") + block) * rows
        query_pos = first + lax.broadcasted_iota(jnp.int32, line, query_dim)
        key_first = first - hops * rows + rows - mask.shape[key_dim]
        key_pos = key_first + lax.broadcasted_iota(jnp.int32, mask.shape, key_dim)
        seen = (key_pos >= user_starts(lengths, query_pos)) & (key_pos <= query_pos)
        value = jnp.where(seen, 1.0, 0.0).astype(F32)
        if mask.shape == (rows, rows):
            mask[...] = value
            continue
        at = 0 if mask.shape[0] == rows else 1
        is_late = jnp.where(far_start(lengths, block, hops, rows) > cut, 1.0, 0.0).astype(F32)
        late[8 * at : 8 * at + 8, :] = jnp.full((8, rows), is_late, F32)
        mask[...] = value * (is_late if at else 1.0 - is_late)
    for copy in copies:
        copy.wait()
    query, key, value = held[:3]
    pair = Pair(masks[0], table, heads, 0, near=near)
    attend([pair], heads, scaling, query, [key], [value], None, out)


def forward_kernel(hops, heads, scaling, table, near, mask, query, key, value, total, out):
    pair = Pair(mask, table, heads, hops, near=near)
    attend([pair], heads, scaling, query, [key], [value], total, out)


def normed_rows(attention):
    center = attention - jnp.mean(attention, axis=1, keepdims=True)
    inverse = lax.rsqrt(jnp.mean(center * center, axis=1, keepdims=True) + EPSILON)
    return center * inverse, inverse


def weights_kernel(hops, heads, scaling, table, near, mask, query, key, weights):
    pair = Pair(mask, table, heads, hops, near=near)
    rows, width = query.shape[0], query.shape[1] // heads

    def scores(head):
        cols = columns(head, width)
        return contract(query[:, cols], key[:, cols], 1, 1)

    def weigh(head, found):
        half = pair.half_logits(found, head, scaling)
        lines = columns(head, rows)
        weights[lines, :] = ((half + half * jnp.tanh(half)) * pair.mask).astype(BF16)

    in_stages(heads, scores, weigh)


def norm_kernel(heads, *refs):
    weights, value, total, out_grad, update_gate, gain = refs[:6]
    attention, attn_grad, gain_grad = refs[6:]
    width = total.shape[1] // heads
    for head in range(heads):
        cols, lines = columns(head, width), columns(head, total.shape[0])
        attention[:, cols] = total[:, cols] + contract(weights[lines, :], value[:, cols], 1, 0)
    rows, features = attention.shape
    step = 16
    gain_row = gain[...]
    gain_sum = jnp.zeros((8, features), F32)
    for low in range(0, rows, step):
        span = slice(low, low + step)
        normed, inverse = normed_rows(attention[span, :])
        gated = out_grad[span, :].astype(F32) * update_gate[span, :].astype(F32)
        product = gated * normed
        for part in range(0, step, 8):
            gain_sum = gain_sum + product[part : part + 8, :]
        pushed = gated * gain_row
        attn_grad[span, :] = (
            inverse
            * (
                pushed
                - jnp.mean(pushed, axis=1, keepdims=True)
                - normed * jnp.mean(pushed * normed, axis=1, keepdims=True)
            )
        ).astype(BF16)
    gain_grad[...] = jnp.sum(gain_sum, axis=0, keepdims=True)


def backward_query_kernel(hop_list, heads, scaling, *refs):
    count = len(hop_list)
    table, near, masks, refs = refs[0], refs[1], refs[2 : 2 + count], refs[2 + count :]
    query, grad, keys, values = refs[0], refs[1], refs[2 : 2 + count], refs[2 + count : 2 + 2 * count]
    gain_in, query_out, small_out = refs[2 + 2 * count :]
    rows, width = query.shape[0], query.shape[1] // heads
    pairs = [Pair(mask, table, heads, hops, near=near) for mask, hops in zip(masks, hop_list)]
    lanes = small_out.shape[1]
    lines = gain_in.shape[1] // lanes
    levels = small_out.shape[0] - lines
    lane = lax.broadcasted_iota(jnp.int32, (levels, lanes), 1)
    level_row = lax.broadcasted_iota(jnp.int32, (levels, lanes), 0)
    group = lax.broadcasted_iota(jnp.int32, (8, rows), 0)
    distance = (group - lax.broadcasted_iota(jnp.int32, (8, rows), 1)) & (rows - 1)
    bucket = sum((distance >= 2**level).astype(jnp.int32) for level in range(levels - 1))
    own = pairs[0].distance >= 0
    bias_total = [jnp.zeros((levels, lanes), F32)]

    def bias_sums(grads):
        close = jnp.where(own, grads[0], grads[1])
        rest = sum(grads[2:], jnp.where(own, grads[1], 0.0))
        by_place, far = jnp.zeros((8, rows), F32), jnp.zeros((8, rows), F32)
        for low in range(0, rows, 8):
            part = close[low : low + 8, :]
            by_place = by_place + (pltpu.roll(part, rows - low, 1) if low else part)
            far = far + rest[low : low + 8, :]
        sums = jnp.where(level_row == levels - 1, jnp.sum(far, axis=0, keepdims=True), 0.0)
        for level in range(levels):
            row = jnp.sum(jnp.where(bucket == level, by_place, 0.0), axis=0, keepdims=True)
            sums = sums + jnp.where(level_row == level, row, 0.0)
        return sums

    def scores(head):
        cols = columns(head, width)
        query_h, grad_h = query[:, cols], grad[:, cols]
        return [
            (contract(query_h, key[:, cols], 1, 1), contract(grad_h, value[:, cols], 1, 1))
            for key, value in zip(keys, values)
        ]

    def differentiate(head, found):
        cols = columns(head, width)
        query_part, grads = None, []
        for pair, key, (score, weight_grad) in zip(pairs, keys, found):
            half = pair.half_logits(score, head, scaling)
            grads.append(weight_grad * (slope_of(half, jnp.tanh(half)) * pair.mask))
            added = contract(grads[-1].astype(BF16), key[:, cols], 1, 0)
            query_part = added if query_part is None else query_part + added
        query_out[:, cols] = (query_part * scaling).astype(BF16)
        sums = jnp.sum(bias_sums(grads), axis=1, keepdims=True)
        bias_total[0] = jnp.where(lane == head, sums, bias_total[0])

    in_stages(heads, scores, differentiate, 1)
    for line in range(lines):
        small_out[line : line + 1, :] = gain_in[:, line * lanes : (line + 1) * lanes]
    small_out[lines:, :] = bias_total[0]


def add_key_grads(hops, heads, scaling, table, mask, query, grad, key, value, sums, store):
    width = query.shape[1] // heads
    pair = Pair(mask, table, heads, hops, True)

    def scores(head):
        cols = columns(head, width)
        score = contract(key[:, cols], query[:, cols], 1, 1)
        return score, contract(value[:, cols], grad[:, cols], 1, 1)

    def differentiate(head, found):
        cols = columns(head, width)
        half = pair.half_logits(found[0], head, scaling)
        tanh = jnp.tanh(half)
        rounded = (found[1] * (slope_of(half, tanh) * pair.mask)).astype(BF16)
        weights = ((half + half * tanh) * pair.mask).astype(BF16)
        parts = [contract(rounded, query[:, cols], 1, 0), contract(weights, grad[:, cols], 1, 0)]
        store(head, cols, *[part + held[:, cols] for part, held in zip(parts, sums)] or parts)

    in_stages(heads, scores, differentiate)


def into(key_out, value_out):
    def store(head, cols, key_part, value_part):
        key_out[:, cols] = key_part
        value_out[:, cols] = value_part

    return store


def next_key_kernel(hops, heads, scaling, *refs):
    add_key_grads(hops, heads, scaling, *refs[:6], refs[6:-2], into(*refs[-2:]))


def gate_and_key_kernel(hops, heads, scaling, *refs):
    attention, out_grad, gain = refs[8:11]
    gate_out, key_out, value_out, held, written = refs[11:]
    step = 16
    gain_row = gain[...]
    for low in range(0, attention.shape[0], step):
        span = slice(low, low + step)
        normed, _ = normed_rows(attention[span, :])
        held[span, :] = (out_grad[span, :].astype(F32) * normed * gain_row).astype(BF16)
    copy = pltpu.make_async_copy(held, gate_out, written)
    copy.start()
    add_key_grads(hops, heads, scaling, *refs[:6], refs[6:8], into(key_out, value_out))
    copy.wait()


def message_kernel(hops, heads, scaling, *refs):
    table, mask, late, query, grad, key, value, out = refs
    tail, cut, width = mask.shape[0], out.shape[0], query.shape[1] // heads
    pair = Pair(mask, table, heads, hops, True)
    is_late = late[8:9, :width] > 0.5

    def scores(head):
        cols = columns(head, width)
        score = contract(key[cut:, cols], query[:, cols], 1, 1)
        return score, contract(value[cut:, cols], grad[:, cols], 1, 1)

    def choose(head, found):
        cols = columns(head, width)
        half = pair.half_logits(found[0], head, scaling)
        tanh = jnp.tanh(half)
        rounded = (found[1] * (slope_of(half, tanh) * pair.mask)).astype(BF16)
        weights = ((half + half * tanh) * pair.mask).astype(BF16)
        parts = [contract(rounded, query[:, cols], 1, 0), contract(weights, grad[:, cols], 1, 0)]
        for at, part in enumerate(parts):
            lines = slice(at * tail, (at + 1) * tail)
            out[lines, cols] = jnp.where(is_late, part, grad[lines, cols].astype(F32)).astype(BF16)
        out[2 * tail :, cols] = grad[2 * tail : cut, cols]

    in_stages(heads, scores, choose)


def slopes_kernel(hops, heads, scaling, table, mask, query, key, weights, slopes):
    pair = Pair(mask, table, heads, hops, True)
    rows, cut, width = mask.shape[0], mask.shape[1], query.shape[1] // heads

    def scores(head):
        cols = columns(head, width)
        return contract(key[:, cols], query[:cut, cols], 1, 1)

    def derive(head, found):
        half = pair.half_logits(found, head, scaling)
        tanh = jnp.tanh(half)
        lines = columns(head, rows)
        weights[lines, :] = ((half + half * tanh) * pair.mask).astype(BF16)
        slopes[lines, :] = slope_of(half, tanh) * pair.mask

    in_stages(heads, scores, derive)


def last_kernel(heads, scaling, *refs):
    weights, slopes, late, query, message, value, key_in, value_in = refs[:8]
    outs, held, written = refs[8:10], refs[10:12], refs[12]
    rows, cut, width = query.shape[0], message.shape[0], query.shape[1] // heads
    tail = rows - cut
    is_late = late[0:1, :width]
    copies = []
    ends = [*range(1, heads - 1, 2), heads - 2, heads - 1]

    def write(at, cols):
        source, target = held[at].at[:, cols], outs[at].at[:, cols]
        copies.append(pltpu.make_async_copy(source, target, written.at[len(copies)]))
        copies[-1].start()

    def scores(head):
        cols = columns(head, width)
        return contract(value[:, cols], message[:, cols], 1, 1)

    def differentiate(head, found):
        cols, lines = columns(head, width), columns(head, rows)
        rounded = (found * slopes[lines, :]).astype(BF16)
        parts = [
            contract(rounded, query[:cut, cols], 1, 0),
            contract(weights[lines, :], message[:, cols], 1, 0),
        ]
        for at, (part, before) in enumerate(zip(parts, (key_in, value_in))):
            factor = 1.0 if at else scaling
            held[at][:cut, cols] = ((before[:cut, cols] + part[:cut]) * factor).astype(BF16)
            sent = message[at * tail : (at + 1) * tail, cols].astype(F32) * is_late
            held[at][cut:, cols] = ((before[cut:, cols] + part[cut:] + sent) * factor).astype(BF16)
        if head in ends:
            before = ends[ends.index(head) - 1] + 1 if head != ends[0] else 0
            for at in (0, 1):
                write(at, slice(before * width, cols.stop))

    in_stages(heads, scores, differentiate)
    for copy in copies:
        copy.wait()


def sum_kernel(*refs):
    gain_out, bias_out = refs[-2:]
    total = added_up([piece[...] for piece in refs[:-2]])
    lines = gain_out.shape[0]
    gain_out[...] = total[:lines]
    bias_out[...] = total[lines:, : bias_out.shape[1]]


def on_device(kernel, outs, args, smem=(), ahead=(), far=(), far_outs=0, scratch=()):
    count = len(smem) + len(far) + len(args)
    far = [pltpu.with_memory_space_constraint(array, pltpu.HBM) for array in far]

    def body(*refs):
        kernel(*refs[:count], *refs[count + len(ahead) :])

    vmem, anywhere = pl.BlockSpec(memory_space=pltpu.VMEM), pl.BlockSpec(memory_space=pl.ANY)
    return pl.pallas_call(
        body,
        out_shape=outs,
        in_specs=[pl.BlockSpec(memory_space=pltpu.SMEM)] * len(smem)
        + [pl.BlockSpec(memory_space=pltpu.HBM)] * len(far)
        + [vmem] * len(args)
        + [anywhere] * len(ahead),
        out_specs=[anywhere] * far_outs + [vmem] * (len(outs) - far_outs),
        scratch_shapes=scratch,
        compiler_params=pltpu.CompilerParams(vmem_limit_bytes=VMEM_LIMIT),
        cost_estimate=pl.CostEstimate(flops=1000000, bytes_accessed=100000, transcendentals=0),
    )(*smem, *far, *args, *ahead)


def rounds_of(axes):
    rounds = []
    for axis in axes:
        size = lax.axis_size(axis)
        step = 1
        while step < size:
            radix = 4 if size // step >= 4 else 2
            rounds.append((axis, [step * at for at in range(1, radix)]))
            step = radix * step
    return rounds


def exchanged(array, axis, distances):
    size = lax.axis_size(axis)
    found = [
        lax.ppermute(array, axis, [(i, i ^ distance) for i in range(size)])
        for distance in reversed(distances)
    ]
    return [array] + found[::-1]


def added_up(pieces):
    while len(pieces) > 1:
        pieces = [left + right for left, right in zip(pieces[::2], pieces[1::2])]
    return pieces[0]


def local(queries, key_rows, value_rows, update_gate, out_grad, user_lengths, rel_bias, norm_gain):
    rows, features = queries.shape[1:]
    levels, heads = rel_bias.shape
    scaling = (features // heads) ** (-0.5)
    reach = min(3, lax.axis_size("ctx") // 2)
    wide = jax.ShapeDtypeStruct((rows, features), F32)
    narrow = jax.ShapeDtypeStruct((rows, features), BF16)
    inputs = (queries[0], key_rows[0], value_rows[0], update_gate[0], out_grad[0])
    gain = norm_gain[None]

    arrived = [passed_along(inputs[at], "ctx", by) for at, by in ((1, 1), (2, 1), (0, -1))]

    hop_list = tuple(range(reach + 1))
    plan = [(0, hops, False) for hops in hop_list] + [(hops, hops, True) for hops in hop_list]
    plan += [(reach - 1, reach, True)]
    cut = rows - rows // 4
    shapes = [(rows, rows)] * (len(plan) - 2) + [(rows, cut), (rows - cut, rows), (16, rows)]
    outs = [jax.ShapeDtypeStruct((count * heads, rows), F32) for count in (levels, rows)]
    outs += [jax.ShapeDtypeStruct(shape, F32) for shape in shapes]
    outs += [narrow] * len(inputs) + [wide]
    table, near, *found = on_device(
        partial(first_kernel, plan, cut, heads, scaling),
        outs,
        (),
        (user_lengths, rel_bias),
        far=inputs,
        scratch=[pltpu.SemaphoreType.DMA((len(inputs),))],
    )
    masks, flipped = found[: reach + 1], found[reach + 1 : 2 * reach + 2]
    sender_mask, late, query, key, value, gate, grad, attention = found[2 * reach + 2 :]

    later_queries = [query, arrived[2]]
    keys, values = [key, arrived[0]], [value, arrived[1]]
    for hops in range(1, reach):
        keys.append(passed_along(keys[-1], "ctx", 1, hops + 1))
        values.append(passed_along(values[-1], "ctx", 1, hops + 1))
        later_queries.append(passed_along(later_queries[-1], "ctx", -1, hops + 1))
    for hops in range(1, reach):
        (attention,) = on_device(
            partial(forward_kernel, hops, heads, scaling),
            [wide],
            (table, near, masks[hops], query, keys[hops], values[hops], attention),
            ahead=later_queries[hops : hops + 1],
        )
    stacked = (heads * rows, rows)
    (far_weights,) = on_device(
        partial(weights_kernel, reach, heads, scaling),
        [jax.ShapeDtypeStruct(stacked, BF16)],
        (table, near, masks[-1], query, keys[-1]),
        ahead=[attention],
    )
    attention, attn_grad, gain_part = on_device(
        partial(norm_kernel, heads),
        [wide, narrow, jax.ShapeDtypeStruct((1, features), F32)],
        (far_weights, values[-1], attention, grad, gate, gain),
    )

    lanes = features // 8
    query_grad, sums = on_device(
        partial(backward_query_kernel, hop_list, heads, scaling),
        [narrow, jax.ShapeDtypeStruct((8 + levels, lanes), F32)],
        (table, near, *masks, query, attn_grad, *keys, *values, gain_part),
        ahead=later_queries[reach:],
    )
    later_grads = [attn_grad, passed_along(attn_grad, "ctx", -1)]
    pieces = [sums]
    for axis, distances in rounds_of(("dp",)):
        pieces = exchanged(added_up(pieces), axis, distances)

    def key_operands(hops):
        later = (later_queries[hops], later_grads[hops])
        return (table, flipped[hops], *later, key, value)

    key_grads = on_device(
        partial(next_key_kernel, 0, heads, scaling),
        [wide] * 2,
        key_operands(0),
        ahead=pieces[1:2],
    )
    for hops in range(1, reach):
        arrived, *pieces = lax.optimization_barrier((later_grads[hops], *pieces))
        if hops + 1 == reach:
            (arrived,) = on_device(
                partial(message_kernel, reach, heads, scaling),
                [jax.ShapeDtypeStruct((cut, features), BF16)],
                (table, sender_mask, late, later_queries[hops], arrived, keys[1], values[1]),
            )
        later_grads.append(passed_along(arrived, "ctx", -1, hops + 1))
        if hops == 1:
            gate_grad, *key_grads = on_device(
                partial(gate_and_key_kernel, hops, heads, scaling),
                [narrow, wide, wide],
                (*key_operands(hops), *key_grads, attention, grad, gain),
                far_outs=1,
                scratch=[pltpu.VMEM((rows, features), BF16), pltpu.SemaphoreType.DMA(())],
            )
        else:
            key_grads = on_device(
                partial(next_key_kernel, hops, heads, scaling),
                [wide] * 2,
                (*key_operands(hops), *key_grads),
            )
    far_tables = on_device(
        partial(slopes_kernel, reach, heads, scaling),
        [jax.ShapeDtypeStruct((heads * rows, cut), kind) for kind in (BF16, F32)],
        (table, flipped[reach], later_queries[reach], key),
        ahead=key_grads[:1],
    )
    for axis, distances in rounds_of(("ctx",)):
        pieces = exchanged(added_up(pieces), axis, distances)
    key_grad, value_grad = on_device(
        partial(last_kernel, heads, scaling),
        [narrow, narrow],
        (*far_tables, late, later_queries[reach], later_grads[reach], value, *key_grads),
        far_outs=2,
        scratch=[pltpu.VMEM((rows, features), BF16)] * 2 + [pltpu.SemaphoreType.DMA((2 * heads,))],
    )
    key_grad, value_grad, pieces[0] = lax.optimization_barrier((key_grad, value_grad, pieces[0]))
    gain_grad, bias_grad = on_device(
        sum_kernel,
        [jax.ShapeDtypeStruct((8, lanes), F32), jax.ShapeDtypeStruct((levels, heads), F32)],
        pieces[::-1],
    )
    return (
        query_grad[None],
        key_grad[None],
        value_grad[None],
        gate_grad[None],
        bias_grad,
        gain_grad.reshape(features),
    )


def solution(mesh):
    in_specs = (
        P(("groups", "dp"), "ctx", None),
        P(("groups", "dp"), "ctx", None),
        P(("groups", "dp"), "ctx", None),
        P(("groups", "dp"), "ctx", None),
        P(("groups", "dp"), "ctx", None),
        P(("groups", "dp"), None),
        P(),
        P(),
    )
    out_specs = (
        P(("groups", "dp"), "ctx", None),
        P(("groups", "dp"), "ctx", None),
        P(("groups", "dp"), "ctx", None),
        P(("groups", "dp"), "ctx", None),
        P("groups", None),
        P("groups"),
    )
    return jax.shard_map(local, mesh=mesh, in_specs=in_specs, out_specs=out_specs, check_vma=False)
```

```python
from functools import partial

import jax
import jax.numpy as jnp
from jax import lax
from jax.experimental import pallas as pl
from jax.experimental.pallas import tpu as pltpu
from jax.sharding import PartitionSpec as P

EPSILON = 1e-05
VMEM_LIMIT = 24 * 1024 * 1024
F32 = jnp.float32
BF16 = jnp.bfloat16


def passed_along(array, axis, by, hop=1):
    size = lax.axis_size(axis)
    first, last = (hop - 1, size - 2) if by > 0 else (1, size - hop)
    return lax.ppermute(array, axis, [(i, i + by) for i in range(first, last + 1)])


def contract(left, right, left_dim, right_dim):
    return lax.dot_general(
        left, right, (((left_dim,), (right_dim,)), ((), ())), preferred_element_type=F32
    )


def user_starts(lengths, query_pos):
    end = jnp.int32(0)
    start = jnp.zeros(query_pos.shape, jnp.int32)
    for user in range(lengths.shape[1]):
        end = end + lengths[0, user]
        start = jnp.where(query_pos >= end, end, start)
    return start


class Pair:
    def __init__(self, mask, table, heads, hops, flipped=False, near=None):
        rows = table.shape[1]
        self.table, self.heads, self.levels = table, heads, table.shape[0] // heads
        self.mask, self.hops, self.near = mask[...], hops, near
        self.far = (hops - 1) * rows + 1 >= 2 ** (self.levels - 2)
        if not self.far:
            query_dim, key_dim = (1, 0) if flipped else (0, 1)
            query_row = lax.broadcasted_iota(jnp.int32, mask.shape, query_dim)
            key_row = lax.broadcasted_iota(jnp.int32, mask.shape, key_dim)
            self.distance = query_row - key_row + hops * rows

    def half_bias(self, head):
        def level_row(level):
            at = level * self.heads + head
            return self.table[at : at + 1, : self.mask.shape[1]]

        value = level_row(self.levels - 1)
        if self.far:
            return value
        if self.near is not None:
            rows = self.mask.shape[0]
            close = self.near[head * rows : (head + 1) * rows, :]
            return close if self.hops == 0 else jnp.where(self.distance < rows, close, value)
        for level in range(self.levels - 2, -1, -1):
            value = jnp.where(self.distance < 2**level, level_row(level), value)
        return value

    def half_logits(self, scores, head, scaling):
        return scores * (0.5 * scaling) + self.half_bias(head)


def slope_of(half, tanh):
    return (0.5 + 0.5 * tanh) * (1.0 + half * (1.0 - tanh))


def columns(head, width):
    return slice(head * width, (head + 1) * width)


def in_stages(count, first, second, ahead=3):
    held = [first(i) for i in range(min(ahead, count))]
    for i in range(count):
        if i + ahead < count:
            held.append(first(i + ahead))
        second(i, held.pop(0))


def attend(pairs, heads, scaling, query, keys, values, total, out):
    width = query.shape[1] // heads

    def scores(head):
        cols = columns(head, width)
        return [contract(query[:, cols], key[:, cols], 1, 1) for key in keys]

    def weigh(head, found):
        cols = columns(head, width)
        part = None if total is None else total[:, cols]
        for pair, score, value in zip(pairs, found, values):
            half = pair.half_logits(score, head, scaling)
            weights = ((half + half * jnp.tanh(half)) * pair.mask).astype(BF16)
            added = contract(weights, value[:, cols], 1, 0)
            part = added if part is None else part + added
        out[:, cols] = part.astype(out.dtype)

    in_stages(heads, scores, weigh)


def far_start(lengths, block, reach, rows):
    first = (lax.axis_index("ctx") + block) * rows
    end, start = jnp.int32(0), jnp.int32(0)
    for user in range(lengths.shape[1]):
        end = end + lengths[0, user]
        start = jnp.where(first >= end, end, start)
    return start - (first - reach * rows)


def first_kernel(plan, cut, heads, scaling, lengths, bias, *refs):
    inputs, refs = refs[:5], refs[5:]
    table, near, masks, refs = refs[0], refs[1], refs[2 : 2 + len(plan)], refs[2 + len(plan) :]
    late, refs = refs[0], refs[1:]
    held, out, arrived = refs[:5], refs[5], refs[6]
    copies = [
        pltpu.make_async_copy(source, target, arrived.at[at])
        for at, (source, target) in enumerate(zip(inputs, held))
    ]
    for copy in copies:
        copy.start()
    levels = bias.shape[0]
    for level in range(levels):
        for head in range(heads):
            at = level * heads + head
            table[at : at + 1, :] = jnp.full((1, table.shape[1]), 0.5 * bias[level, head], F32)
    rows = masks[0].shape[0]
    apart = lax.broadcasted_iota(jnp.int32, (rows, rows), 0)
    apart = (apart - lax.broadcasted_iota(jnp.int32, (rows, rows), 1)) & (rows - 1)
    for head in range(heads):
        value = table[(levels - 1) * heads + head : (levels - 1) * heads + head + 1, :]
        for level in range(levels - 2, -1, -1):
            at = level * heads + head
            value = jnp.where(apart < 2**level, table[at : at + 1, :], value)
        near[head * rows : (head + 1) * rows, :] = value
    for (block, hops, flipped), mask in zip(plan, masks):
        query_dim, key_dim = (1, 0) if flipped else (0, 1)
        line = (1, mask.shape[1]) if flipped else (mask.shape[0], 1)
        first = (lax.axis_index("ctx") + block) * rows
        query_pos = first + lax.broadcasted_iota(jnp.int32, line, query_dim)
        key_first = first - hops * rows + rows - mask.shape[key_dim]
        key_pos = key_first + lax.broadcasted_iota(jnp.int32, mask.shape, key_dim)
        seen = (key_pos >= user_starts(lengths, query_pos)) & (key_pos <= query_pos)
        value = jnp.where(seen, 1.0, 0.0).astype(F32)
        if mask.shape == (rows, rows):
            mask[...] = value
            continue
        at = 0 if mask.shape[0] == rows else 1
        is_late = jnp.where(far_start(lengths, block, hops, rows) > cut, 1.0, 0.0).astype(F32)
        late[8 * at : 8 * at + 8, :] = jnp.full((8, rows), is_late, F32)
        mask[...] = value * (is_late if at else 1.0 - is_late)
    for copy in copies:
        copy.wait()
    query, key, value = held[:3]
    pair = Pair(masks[0], table, heads, 0, near=near)
    attend([pair], heads, scaling, query, [key], [value], None, out)


def forward_kernel(hops, heads, scaling, table, near, mask, query, key, value, total, out):
    pair = Pair(mask, table, heads, hops, near=near)
    attend([pair], heads, scaling, query, [key], [value], total, out)


def normed_rows(attention):
    center = attention - jnp.mean(attention, axis=1, keepdims=True)
    inverse = lax.rsqrt(jnp.mean(center * center, axis=1, keepdims=True) + EPSILON)
    return center * inverse, inverse


def weights_kernel(hops, heads, scaling, table, near, mask, query, key, weights):
    pair = Pair(mask, table, heads, hops, near=near)
    rows, width = query.shape[0], query.shape[1] // heads

    def scores(head):
        cols = columns(head, width)
        return contract(query[:, cols], key[:, cols], 1, 1)

    def weigh(head, found):
        half = pair.half_logits(found, head, scaling)
        lines = columns(head, rows)
        weights[lines, :] = ((half + half * jnp.tanh(half)) * pair.mask).astype(BF16)

    in_stages(heads, scores, weigh)


def norm_kernel(heads, *refs):
    weights, value, total, out_grad, update_gate, gain = refs[:6]
    kept, attn_grad, gain_grad = refs[6:]
    width = total.shape[1] // heads
    for head in range(heads):
        cols, lines = columns(head, width), columns(head, total.shape[0])
        kept[:, cols] = total[:, cols] + contract(weights[lines, :], value[:, cols], 1, 0)
    rows, features = kept.shape
    step = 16
    gain_row = gain[...]
    gain_sum = jnp.zeros((8, features), F32)
    for low in range(0, rows, step):
        span = slice(low, low + step)
        normed, inverse = normed_rows(kept[span, :])
        kept[span, :] = normed
        gated = out_grad[span, :].astype(F32) * update_gate[span, :].astype(F32)
        product = gated * normed
        for part in range(0, step, 8):
            gain_sum = gain_sum + product[part : part + 8, :]
        pushed = gated * gain_row
        attn_grad[span, :] = (
            inverse
            * (
                pushed
                - jnp.mean(pushed, axis=1, keepdims=True)
                - normed * jnp.mean(pushed * normed, axis=1, keepdims=True)
            )
        ).astype(BF16)
    gain_grad[...] = jnp.sum(gain_sum, axis=0, keepdims=True)


def backward_query_kernel(hop_list, heads, scaling, *refs):
    count = len(hop_list)
    table, near, masks, refs = refs[0], refs[1], refs[2 : 2 + count], refs[2 + count :]
    query, grad, keys, values = refs[0], refs[1], refs[2 : 2 + count], refs[2 + count : 2 + 2 * count]
    gain_in, query_out, small_out = refs[2 + 2 * count :]
    rows, width = query.shape[0], query.shape[1] // heads
    pairs = [Pair(mask, table, heads, hops, near=near) for mask, hops in zip(masks, hop_list)]
    lanes = small_out.shape[1]
    lines = gain_in.shape[1] // lanes
    levels = small_out.shape[0] - lines
    lane = lax.broadcasted_iota(jnp.int32, (levels, lanes), 1)
    level_row = lax.broadcasted_iota(jnp.int32, (levels, lanes), 0)
    group = lax.broadcasted_iota(jnp.int32, (8, rows), 0)
    distance = (group - lax.broadcasted_iota(jnp.int32, (8, rows), 1)) & (rows - 1)
    bucket = sum((distance >= 2**level).astype(jnp.int32) for level in range(levels - 1))
    own = pairs[0].distance >= 0
    bias_total = [jnp.zeros((levels, lanes), F32)]

    def bias_sums(grads):
        close = jnp.where(own, grads[0], grads[1])
        rest = sum(grads[2:], jnp.where(own, grads[1], 0.0))
        by_place, far = jnp.zeros((8, rows), F32), jnp.zeros((8, rows), F32)
        for low in range(0, rows, 8):
            part = close[low : low + 8, :]
            by_place = by_place + (pltpu.roll(part, rows - low, 1) if low else part)
            far = far + rest[low : low + 8, :]
        sums = jnp.where(level_row == levels - 1, jnp.sum(far, axis=0, keepdims=True), 0.0)
        for level in range(levels):
            row = jnp.sum(jnp.where(bucket == level, by_place, 0.0), axis=0, keepdims=True)
            sums = sums + jnp.where(level_row == level, row, 0.0)
        return sums

    def scores(head):
        cols = columns(head, width)
        query_h, grad_h = query[:, cols], grad[:, cols]
        return [
            (contract(query_h, key[:, cols], 1, 1), contract(grad_h, value[:, cols], 1, 1))
            for key, value in zip(keys, values)
        ]

    def differentiate(head, found):
        cols = columns(head, width)
        query_part, grads = None, []
        for pair, key, (score, weight_grad) in zip(pairs, keys, found):
            half = pair.half_logits(score, head, scaling)
            grads.append(weight_grad * (slope_of(half, jnp.tanh(half)) * pair.mask))
            added = contract(grads[-1].astype(BF16), key[:, cols], 1, 0)
            query_part = added if query_part is None else query_part + added
        query_out[:, cols] = (query_part * scaling).astype(BF16)
        sums = jnp.sum(bias_sums(grads), axis=1, keepdims=True)
        bias_total[0] = jnp.where(lane == head, sums, bias_total[0])

    in_stages(heads, scores, differentiate, 1)
    for line in range(lines):
        small_out[line : line + 1, :] = gain_in[:, line * lanes : (line + 1) * lanes]
    small_out[lines:, :] = bias_total[0]


def add_key_grads(hops, heads, scaling, table, mask, query, grad, key, value, sums, store):
    width = query.shape[1] // heads
    pair = Pair(mask, table, heads, hops, True)

    def scores(head):
        cols = columns(head, width)
        score = contract(key[:, cols], query[:, cols], 1, 1)
        return score, contract(value[:, cols], grad[:, cols], 1, 1)

    def differentiate(head, found):
        cols = columns(head, width)
        half = pair.half_logits(found[0], head, scaling)
        tanh = jnp.tanh(half)
        rounded = (found[1] * (slope_of(half, tanh) * pair.mask)).astype(BF16)
        weights = ((half + half * tanh) * pair.mask).astype(BF16)
        parts = [contract(rounded, query[:, cols], 1, 0), contract(weights, grad[:, cols], 1, 0)]
        store(head, cols, *[part + held[:, cols] for part, held in zip(parts, sums)] or parts)

    in_stages(heads, scores, differentiate)


def into(key_out, value_out):
    def store(head, cols, key_part, value_part):
        key_out[:, cols] = key_part
        value_out[:, cols] = value_part

    return store


def next_key_kernel(hops, heads, scaling, *refs):
    add_key_grads(hops, heads, scaling, *refs[:6], refs[6:-2], into(*refs[-2:]))


def gate_and_key_kernel(hops, heads, scaling, *refs):
    normed, out_grad, gain = refs[8:11]
    gate_out, key_out, value_out, held, written = refs[11:]
    step = 16
    gain_row = gain[...]
    for low in range(0, normed.shape[0], step):
        span = slice(low, low + step)
        held[span, :] = (out_grad[span, :].astype(F32) * normed[span, :] * gain_row).astype(BF16)
    copy = pltpu.make_async_copy(held, gate_out, written)
    copy.start()
    add_key_grads(hops, heads, scaling, *refs[:6], refs[6:8], into(key_out, value_out))
    copy.wait()


def message_kernel(heads, *refs):
    weights, slopes, late, query, grad, value, out = refs
    cut, width = out.shape[0], query.shape[1] // heads
    tail = query.shape[0] - cut
    is_late = late[8:9, :width] > 0.5

    def scores(head):
        cols = columns(head, width)
        return contract(value[cut:, cols], grad[:, cols], 1, 1)

    def choose(head, found):
        cols, lines = columns(head, width), columns(head, tail)
        rounded = (found * slopes[lines, :]).astype(BF16)
        parts = [
            contract(rounded, query[:, cols], 1, 0),
            contract(weights[lines, :], grad[:, cols], 1, 0),
        ]
        for at, part in enumerate(parts):
            lines = slice(at * tail, (at + 1) * tail)
            out[lines, cols] = jnp.where(is_late, part, grad[lines, cols].astype(F32)).astype(BF16)
        out[2 * tail :, cols] = grad[2 * tail : cut, cols]

    in_stages(heads, scores, choose)


def slopes_kernel(hops, heads, scaling, table, mask, query, key, weights, slopes):
    pair = Pair(mask, table, heads, hops, True)
    rows, cut, width = mask.shape[0], mask.shape[1], query.shape[1] // heads
    first = key.shape[0] - rows

    def scores(head):
        cols = columns(head, width)
        return contract(key[first:, cols], query[:cut, cols], 1, 1)

    def derive(head, found):
        half = pair.half_logits(found, head, scaling)
        tanh = jnp.tanh(half)
        lines = columns(head, rows)
        weights[lines, :] = ((half + half * tanh) * pair.mask).astype(BF16)
        slopes[lines, :] = slope_of(half, tanh) * pair.mask

    in_stages(heads, scores, derive)


def last_kernel(heads, scaling, *refs):
    weights, slopes, late, query, message, value, key_in, value_in = refs[:8]
    outs, held, written = refs[8:10], refs[10:12], refs[12]
    rows, cut, width = query.shape[0], message.shape[0], query.shape[1] // heads
    tail = rows - cut
    is_late = late[0:1, :width]
    copies = []
    ends = [*range(1, heads - 1, 2), heads - 2, heads - 1]

    def write(at, cols):
        source, target = held[at].at[:, cols], outs[at].at[:, cols]
        copies.append(pltpu.make_async_copy(source, target, written.at[len(copies)]))
        copies[-1].start()

    def scores(head):
        cols = columns(head, width)
        return contract(value[:, cols], message[:, cols], 1, 1)

    def differentiate(head, found):
        cols, lines = columns(head, width), columns(head, rows)
        rounded = (found * slopes[lines, :]).astype(BF16)
        parts = [
            contract(rounded, query[:cut, cols], 1, 0),
            contract(weights[lines, :], message[:, cols], 1, 0),
        ]
        for at, (part, before) in enumerate(zip(parts, (key_in, value_in))):
            factor = 1.0 if at else scaling
            held[at][:cut, cols] = ((before[:cut, cols] + part[:cut]) * factor).astype(BF16)
            sent = message[at * tail : (at + 1) * tail, cols].astype(F32) * is_late
            held[at][cut:, cols] = ((before[cut:, cols] + part[cut:] + sent) * factor).astype(BF16)
        if head in ends:
            before = ends[ends.index(head) - 1] + 1 if head != ends[0] else 0
            for at in (0, 1):
                write(at, slice(before * width, cols.stop))

    in_stages(heads, scores, differentiate)
    for copy in copies:
        copy.wait()


def sum_kernel(*refs):
    gain_out, bias_out = refs[-2:]
    total = added_up([piece[...] for piece in refs[:-2]])
    lines = gain_out.shape[0]
    gain_out[...] = total[:lines]
    bias_out[...] = total[lines:, : bias_out.shape[1]]


def on_device(kernel, outs, args, smem=(), ahead=(), far=(), far_outs=0, scratch=()):
    count = len(smem) + len(far) + len(args)
    far = [pltpu.with_memory_space_constraint(array, pltpu.HBM) for array in far]

    def body(*refs):
        kernel(*refs[:count], *refs[count + len(ahead) :])

    vmem, anywhere = pl.BlockSpec(memory_space=pltpu.VMEM), pl.BlockSpec(memory_space=pl.ANY)
    return pl.pallas_call(
        body,
        out_shape=outs,
        in_specs=[pl.BlockSpec(memory_space=pltpu.SMEM)] * len(smem)
        + [pl.BlockSpec(memory_space=pltpu.HBM)] * len(far)
        + [vmem] * len(args)
        + [anywhere] * len(ahead),
        out_specs=[anywhere] * far_outs + [vmem] * (len(outs) - far_outs),
        scratch_shapes=scratch,
        compiler_params=pltpu.CompilerParams(vmem_limit_bytes=VMEM_LIMIT),
        cost_estimate=pl.CostEstimate(flops=1000000, bytes_accessed=100000, transcendentals=0),
    )(*smem, *far, *args, *ahead)


def rounds_of(axes):
    rounds = []
    for axis in axes:
        size = lax.axis_size(axis)
        step = 1
        while step < size:
            radix = 4 if size // step >= 4 else 2
            rounds.append((axis, [step * at for at in range(1, radix)]))
            step = radix * step
    return rounds


def exchanged(array, axis, distances):
    size = lax.axis_size(axis)
    found = [
        lax.ppermute(array, axis, [(i, i ^ distance) for i in range(size)])
        for distance in reversed(distances)
    ]
    return [array] + found[::-1]


def added_up(pieces):
    while len(pieces) > 1:
        pieces = [left + right for left, right in zip(pieces[::2], pieces[1::2])]
    return pieces[0]


def local(queries, key_rows, value_rows, update_gate, out_grad, user_lengths, rel_bias, norm_gain):
    rows, features = queries.shape[1:]
    levels, heads = rel_bias.shape
    scaling = (features // heads) ** (-0.5)
    reach = min(3, lax.axis_size("ctx") // 2)
    wide = jax.ShapeDtypeStruct((rows, features), F32)
    narrow = jax.ShapeDtypeStruct((rows, features), BF16)
    inputs = (queries[0], key_rows[0], value_rows[0], update_gate[0], out_grad[0])
    gain = norm_gain[None]

    arrived = [passed_along(inputs[at], "ctx", by) for at, by in ((1, 1), (2, 1), (0, -1))]

    hop_list = tuple(range(reach + 1))
    plan = [(0, hops, False) for hops in hop_list] + [(hops, hops, True) for hops in hop_list]
    plan += [(reach - 1, reach, True)]
    cut = rows - rows // 4
    shapes = [(rows, rows)] * (len(plan) - 2) + [(rows, cut), (rows - cut, rows), (16, rows)]
    outs = [jax.ShapeDtypeStruct((count * heads, rows), F32) for count in (levels, rows)]
    outs += [jax.ShapeDtypeStruct(shape, F32) for shape in shapes]
    outs += [narrow] * len(inputs) + [wide]
    table, near, *found = on_device(
        partial(first_kernel, plan, cut, heads, scaling),
        outs,
        (),
        (user_lengths, rel_bias),
        far=inputs,
        scratch=[pltpu.SemaphoreType.DMA((len(inputs),))],
    )
    masks, flipped = found[: reach + 1], found[reach + 1 : 2 * reach + 2]
    sender_mask, late, query, key, value, gate, grad, attention = found[2 * reach + 2 :]

    later_queries = [query, arrived[2]]
    keys, values = [key, arrived[0]], [value, arrived[1]]
    for hops in range(1, reach):
        keys.append(passed_along(keys[-1], "ctx", 1, hops + 1))
        values.append(passed_along(values[-1], "ctx", 1, hops + 1))
        later_queries.append(passed_along(later_queries[-1], "ctx", -1, hops + 1))
    for hops in range(1, reach):
        (attention,) = on_device(
            partial(forward_kernel, hops, heads, scaling),
            [wide],
            (table, near, masks[hops], query, keys[hops], values[hops], attention),
            ahead=later_queries[hops : hops + 1],
        )
    stacked = (heads * rows, rows)
    (far_weights,) = on_device(
        partial(weights_kernel, reach, heads, scaling),
        [jax.ShapeDtypeStruct(stacked, BF16)],
        (table, near, masks[-1], query, keys[-1]),
        ahead=[attention],
    )
    normed, attn_grad, gain_part = on_device(
        partial(norm_kernel, heads),
        [wide, narrow, jax.ShapeDtypeStruct((1, features), F32)],
        (far_weights, values[-1], attention, grad, gate, gain),
    )

    sent_tables = on_device(
        partial(slopes_kernel, reach, heads, scaling),
        [jax.ShapeDtypeStruct((heads * (rows - cut), rows), kind) for kind in (BF16, F32)],
        (table, sender_mask, later_queries[reach - 1], keys[1]),
    )
    lanes = features // 8
    query_grad, sums = on_device(
        partial(backward_query_kernel, hop_list, heads, scaling),
        [narrow, jax.ShapeDtypeStruct((8 + levels, lanes), F32)],
        (table, near, *masks, query, attn_grad, *keys, *values, gain_part),
        ahead=[later_queries[reach], sent_tables[0]],
    )
    later_grads = [attn_grad, passed_along(attn_grad, "ctx", -1)]
    pieces = [sums]
    for axis, distances in rounds_of(("dp",)):
        pieces = exchanged(added_up(pieces), axis, distances)

    def key_operands(hops):
        later = (later_queries[hops], later_grads[hops])
        return (table, flipped[hops], *later, key, value)

    key_grads = on_device(
        partial(next_key_kernel, 0, heads, scaling),
        [wide] * 2,
        key_operands(0),
        ahead=pieces[1:2],
    )
    for hops in range(1, reach):
        arrived, *pieces = lax.optimization_barrier((later_grads[hops], *pieces))
        if hops + 1 == reach:
            (arrived,) = on_device(
                partial(message_kernel, heads),
                [jax.ShapeDtypeStruct((cut, features), BF16)],
                (*sent_tables, late, later_queries[hops], arrived, values[1]),
            )
        later_grads.append(passed_along(arrived, "ctx", -1, hops + 1))
        if hops == 1:
            gate_grad, *key_grads = on_device(
                partial(gate_and_key_kernel, hops, heads, scaling),
                [narrow, wide, wide],
                (*key_operands(hops), *key_grads, normed, grad, gain),
                far_outs=1,
                scratch=[pltpu.VMEM((rows, features), BF16), pltpu.SemaphoreType.DMA(())],
            )
        else:
            key_grads = on_device(
                partial(next_key_kernel, hops, heads, scaling),
                [wide] * 2,
                (*key_operands(hops), *key_grads),
            )
    far_tables = on_device(
        partial(slopes_kernel, reach, heads, scaling),
        [jax.ShapeDtypeStruct((heads * rows, cut), kind) for kind in (BF16, F32)],
        (table, flipped[reach], later_queries[reach], key),
        ahead=key_grads[:1],
    )
    for axis, distances in rounds_of(("ctx",)):
        pieces = exchanged(added_up(pieces), axis, distances)
    key_grad, value_grad = on_device(
        partial(last_kernel, heads, scaling),
        [narrow, narrow],
        (*far_tables, late, later_queries[reach], later_grads[reach], value, *key_grads),
        far_outs=2,
        scratch=[pltpu.VMEM((rows, features), BF16)] * 2 + [pltpu.SemaphoreType.DMA((2 * heads,))],
    )
    key_grad, value_grad, pieces[0] = lax.optimization_barrier((key_grad, value_grad, pieces[0]))
    gain_grad, bias_grad = on_device(
        sum_kernel,
        [jax.ShapeDtypeStruct((8, lanes), F32), jax.ShapeDtypeStruct((levels, heads), F32)],
        [*pieces[2:], *pieces[1::-1]],
    )
    return (
        query_grad[None],
        key_grad[None],
        value_grad[None],
        gate_grad[None],
        bias_grad,
        gain_grad.reshape(features),
    )


def solution(mesh):
    in_specs = (
        P(("groups", "dp"), "ctx", None),
        P(("groups", "dp"), "ctx", None),
        P(("groups", "dp"), "ctx", None),
        P(("groups", "dp"), "ctx", None),
        P(("groups", "dp"), "ctx", None),
        P(("groups", "dp"), None),
        P(),
        P(),
    )
    out_specs = (
        P(("groups", "dp"), "ctx", None),
        P(("groups", "dp"), "ctx", None),
        P(("groups", "dp"), "ctx", None),
        P(("groups", "dp"), "ctx", None),
        P("groups", None),
        P("groups"),
    )
    return jax.shard_map(local, mesh=mesh, in_specs=in_specs, out_specs=out_specs, check_vma=False)
```

```python
from functools import partial

import jax
import jax.numpy as jnp
from jax import lax
from jax.experimental import pallas as pl
from jax.experimental.pallas import tpu as pltpu
from jax.sharding import PartitionSpec as P

EPSILON = 1e-05
VMEM_LIMIT = 24 * 1024 * 1024
F32 = jnp.float32
BF16 = jnp.bfloat16


def passed_along(array, axis, by, hop=1):
    size = lax.axis_size(axis)
    first, last = (hop - 1, size - 2) if by > 0 else (1, size - hop)
    return lax.ppermute(array, axis, [(i, i + by) for i in range(first, last + 1)])


def contract(left, right, left_dim, right_dim):
    return lax.dot_general(
        left, right, (((left_dim,), (right_dim,)), ((), ())), preferred_element_type=F32
    )


def user_starts(lengths, query_pos):
    end = jnp.int32(0)
    start = jnp.zeros(query_pos.shape, jnp.int32)
    for user in range(lengths.shape[1]):
        end = end + lengths[0, user]
        start = jnp.where(query_pos >= end, end, start)
    return start


class Pair:
    def __init__(self, mask, table, heads, hops, flipped=False, near=None):
        rows = table.shape[1]
        self.table, self.heads, self.levels = table, heads, table.shape[0] // heads
        self.mask, self.hops, self.near = mask[...], hops, near
        self.far = (hops - 1) * rows + 1 >= 2 ** (self.levels - 2)
        if not self.far:
            query_dim, key_dim = (1, 0) if flipped else (0, 1)
            query_row = lax.broadcasted_iota(jnp.int32, mask.shape, query_dim)
            key_row = lax.broadcasted_iota(jnp.int32, mask.shape, key_dim)
            self.distance = query_row - key_row + hops * rows

    def half_bias(self, head):
        def level_row(level):
            at = level * self.heads + head
            return self.table[at : at + 1, : self.mask.shape[1]]

        value = level_row(self.levels - 1)
        if self.far:
            return value
        if self.near is not None:
            rows = self.mask.shape[0]
            close = self.near[head * rows : (head + 1) * rows, :]
            return close if self.hops == 0 else jnp.where(self.distance < rows, close, value)
        for level in range(self.levels - 2, -1, -1):
            value = jnp.where(self.distance < 2**level, level_row(level), value)
        return value

    def half_logits(self, scores, head, scaling):
        return scores * (0.5 * scaling) + self.half_bias(head)


def slope_of(half, tanh):
    return (0.5 + 0.5 * tanh) * (1.0 + half * (1.0 - tanh))


def columns(head, width):
    return slice(head * width, (head + 1) * width)


def in_stages(count, first, second, ahead=3):
    held = [first(i) for i in range(min(ahead, count))]
    for i in range(count):
        if i + ahead < count:
            held.append(first(i + ahead))
        second(i, held.pop(0))


def attend(pairs, heads, scaling, query, keys, values, total, out):
    width = query.shape[1] // heads

    def scores(head):
        cols = columns(head, width)
        return [contract(query[:, cols], key[:, cols], 1, 1) for key in keys]

    def weigh(head, found):
        cols = columns(head, width)
        part = None if total is None else total[:, cols]
        for pair, score, value in zip(pairs, found, values):
            half = pair.half_logits(score, head, scaling)
            weights = ((half + half * jnp.tanh(half)) * pair.mask).astype(BF16)
            added = contract(weights, value[:, cols], 1, 0)
            part = added if part is None else part + added
        out[:, cols] = part.astype(out.dtype)

    in_stages(heads, scores, weigh)


def far_start(lengths, block, reach, rows):
    first = (lax.axis_index("ctx") + block) * rows
    end, start = jnp.int32(0), jnp.int32(0)
    for user in range(lengths.shape[1]):
        end = end + lengths[0, user]
        start = jnp.where(first >= end, end, start)
    return start - (first - reach * rows)


def first_kernel(plan, cut, heads, scaling, lengths, bias, *refs):
    inputs, refs = refs[:5], refs[5:]
    table, near, masks, refs = refs[0], refs[1], refs[2 : 2 + len(plan)], refs[2 + len(plan) :]
    late, refs = refs[0], refs[1:]
    held, out, arrived = refs[:5], refs[5], refs[6]
    copies = [
        pltpu.make_async_copy(source, target, arrived.at[at])
        for at, (source, target) in enumerate(zip(inputs, held))
    ]
    for copy in copies:
        copy.start()
    levels = bias.shape[0]
    for level in range(levels):
        for head in range(heads):
            at = level * heads + head
            table[at : at + 1, :] = jnp.full((1, table.shape[1]), 0.5 * bias[level, head], F32)
    rows = masks[0].shape[0]
    apart = lax.broadcasted_iota(jnp.int32, (rows, rows), 0)
    apart = (apart - lax.broadcasted_iota(jnp.int32, (rows, rows), 1)) & (rows - 1)
    for head in range(heads):
        value = table[(levels - 1) * heads + head : (levels - 1) * heads + head + 1, :]
        for level in range(levels - 2, -1, -1):
            at = level * heads + head
            value = jnp.where(apart < 2**level, table[at : at + 1, :], value)
        near[head * rows : (head + 1) * rows, :] = value
    for (block, hops, flipped), mask in zip(plan, masks):
        query_dim, key_dim = (1, 0) if flipped else (0, 1)
        line = (1, mask.shape[1]) if flipped else (mask.shape[0], 1)
        first = (lax.axis_index("ctx") + block) * rows
        query_pos = first + lax.broadcasted_iota(jnp.int32, line, query_dim)
        key_first = first - hops * rows + rows - mask.shape[key_dim]
        key_pos = key_first + lax.broadcasted_iota(jnp.int32, mask.shape, key_dim)
        seen = (key_pos >= user_starts(lengths, query_pos)) & (key_pos <= query_pos)
        value = jnp.where(seen, 1.0, 0.0).astype(F32)
        if mask.shape == (rows, rows):
            mask[...] = value
            continue
        at = 0 if mask.shape[0] == rows else 1
        is_late = jnp.where(far_start(lengths, block, hops, rows) > cut, 1.0, 0.0).astype(F32)
        late[8 * at : 8 * at + 8, :] = jnp.full((8, rows), is_late, F32)
        mask[...] = value * (is_late if at else 1.0 - is_late)
    for copy in copies:
        copy.wait()
    query, key, value = held[:3]
    pair = Pair(masks[0], table, heads, 0, near=near)
    attend([pair], heads, scaling, query, [key], [value], None, out)


def forward_kernel(hops, heads, scaling, table, near, mask, query, key, value, total, out):
    pair = Pair(mask, table, heads, hops, near=near)
    attend([pair], heads, scaling, query, [key], [value], total, out)


def normed_rows(attention):
    center = attention - jnp.mean(attention, axis=1, keepdims=True)
    inverse = lax.rsqrt(jnp.mean(center * center, axis=1, keepdims=True) + EPSILON)
    return center * inverse, inverse


def weights_kernel(hops, heads, scaling, table, near, mask, query, key, weights):
    pair = Pair(mask, table, heads, hops, near=near)
    rows, width = query.shape[0], query.shape[1] // heads

    def scores(head):
        cols = columns(head, width)
        return contract(query[:, cols], key[:, cols], 1, 1)

    def weigh(head, found):
        half = pair.half_logits(found, head, scaling)
        lines = columns(head, rows)
        weights[lines, :] = ((half + half * jnp.tanh(half)) * pair.mask).astype(BF16)

    in_stages(heads, scores, weigh)


def norm_kernel(heads, *refs):
    weights, value, total, out_grad, update_gate, gain = refs[:6]
    attention, attn_grad, gain_grad = refs[6:]
    width = total.shape[1] // heads
    for head in range(heads):
        cols, lines = columns(head, width), columns(head, total.shape[0])
        attention[:, cols] = total[:, cols] + contract(weights[lines, :], value[:, cols], 1, 0)
    rows, features = attention.shape
    step = 16
    gain_row = gain[...]
    gain_sum = jnp.zeros((8, features), F32)
    for low in range(0, rows, step):
        span = slice(low, low + step)
        normed, inverse = normed_rows(attention[span, :])
        gated = out_grad[span, :].astype(F32) * update_gate[span, :].astype(F32)
        product = gated * normed
        for part in range(0, step, 8):
            gain_sum = gain_sum + product[part : part + 8, :]
        pushed = gated * gain_row
        attn_grad[span, :] = (
            inverse
            * (
                pushed
                - jnp.mean(pushed, axis=1, keepdims=True)
                - normed * jnp.mean(pushed * normed, axis=1, keepdims=True)
            )
        ).astype(BF16)
    gain_grad[...] = jnp.sum(gain_sum, axis=0, keepdims=True)


def backward_query_kernel(hop_list, heads, scaling, *refs):
    count = len(hop_list)
    table, near, masks, refs = refs[0], refs[1], refs[2 : 2 + count], refs[2 + count :]
    query, grad, keys, values = refs[0], refs[1], refs[2 : 2 + count], refs[2 + count : 2 + 2 * count]
    gain_in, query_out, small_out = refs[2 + 2 * count :]
    rows, width = query.shape[0], query.shape[1] // heads
    pairs = [Pair(mask, table, heads, hops, near=near) for mask, hops in zip(masks, hop_list)]
    lanes = small_out.shape[1]
    lines = gain_in.shape[1] // lanes
    levels = small_out.shape[0] - lines
    lane = lax.broadcasted_iota(jnp.int32, (levels, lanes), 1)
    level_row = lax.broadcasted_iota(jnp.int32, (levels, lanes), 0)
    group = lax.broadcasted_iota(jnp.int32, (8, rows), 0)
    distance = (group - lax.broadcasted_iota(jnp.int32, (8, rows), 1)) & (rows - 1)
    bucket = sum((distance >= 2**level).astype(jnp.int32) for level in range(levels - 1))
    own = pairs[0].distance >= 0
    bias_total = [jnp.zeros((levels, lanes), F32)]

    def bias_sums(grads):
        close = jnp.where(own, grads[0], grads[1])
        rest = sum(grads[2:], jnp.where(own, grads[1], 0.0))
        by_place, far = jnp.zeros((8, rows), F32), jnp.zeros((8, rows), F32)
        for low in range(0, rows, 8):
            part = close[low : low + 8, :]
            by_place = by_place + (pltpu.roll(part, rows - low, 1) if low else part)
            far = far + rest[low : low + 8, :]
        sums = jnp.where(level_row == levels - 1, jnp.sum(far, axis=0, keepdims=True), 0.0)
        for level in range(levels):
            row = jnp.sum(jnp.where(bucket == level, by_place, 0.0), axis=0, keepdims=True)
            sums = sums + jnp.where(level_row == level, row, 0.0)
        return sums

    def scores(head):
        cols = columns(head, width)
        query_h, grad_h = query[:, cols], grad[:, cols]
        return [
            (contract(query_h, key[:, cols], 1, 1), contract(grad_h, value[:, cols], 1, 1))
            for key, value in zip(keys, values)
        ]

    def differentiate(head, found):
        cols = columns(head, width)
        query_part, grads = None, []
        for pair, key, (score, weight_grad) in zip(pairs, keys, found):
            half = pair.half_logits(score, head, scaling)
            grads.append(weight_grad * (slope_of(half, jnp.tanh(half)) * pair.mask))
            added = contract(grads[-1].astype(BF16), key[:, cols], 1, 0)
            query_part = added if query_part is None else query_part + added
        query_out[:, cols] = (query_part * scaling).astype(BF16)
        sums = jnp.sum(bias_sums(grads), axis=1, keepdims=True)
        bias_total[0] = jnp.where(lane == head, sums, bias_total[0])

    in_stages(heads, scores, differentiate, 1)
    for line in range(lines):
        small_out[line : line + 1, :] = gain_in[:, line * lanes : (line + 1) * lanes]
    small_out[lines:, :] = bias_total[0]


def add_key_grads(hops, heads, scaling, table, mask, query, grad, key, value, sums, store):
    width = query.shape[1] // heads
    pair = Pair(mask, table, heads, hops, True)

    def scores(head):
        cols = columns(head, width)
        score = contract(key[:, cols], query[:, cols], 1, 1)
        return score, contract(value[:, cols], grad[:, cols], 1, 1)

    def differentiate(head, found):
        cols = columns(head, width)
        half = pair.half_logits(found[0], head, scaling)
        tanh = jnp.tanh(half)
        rounded = (found[1] * (slope_of(half, tanh) * pair.mask)).astype(BF16)
        weights = ((half + half * tanh) * pair.mask).astype(BF16)
        parts = [contract(rounded, query[:, cols], 1, 0), contract(weights, grad[:, cols], 1, 0)]
        store(head, cols, *[part + held[:, cols] for part, held in zip(parts, sums)] or parts)

    in_stages(heads, scores, differentiate)


def into(key_out, value_out):
    def store(head, cols, key_part, value_part):
        key_out[:, cols] = key_part
        value_out[:, cols] = value_part

    return store


def next_key_kernel(hops, heads, scaling, *refs):
    add_key_grads(hops, heads, scaling, *refs[:6], refs[6:-2], into(*refs[-2:]))


def gate_and_key_kernel(hops, heads, scaling, *refs):
    attention, out_grad, gain, query_grad = refs[8:12]
    gate_out, query_out, key_out, value_out, held, written = refs[12:]
    rows, step = attention.shape[0], 16
    part = rows // 4
    copies = []

    def write(source, target, low):
        lines = slice(low, low + part)
        copies.append(
            pltpu.make_async_copy(source.at[lines], target.at[lines], written.at[len(copies)])
        )
        copies[-1].start()

    for low in range(0, rows, part):
        write(query_grad, query_out, low)
    gain_row = gain[...]
    for low in range(0, rows, step):
        span = slice(low, low + step)
        normed, _ = normed_rows(attention[span, :])
        held[span, :] = (out_grad[span, :].astype(F32) * normed * gain_row).astype(BF16)
        if (low + step) % part == 0:
            write(held, gate_out, low + step - part)
    add_key_grads(hops, heads, scaling, *refs[:6], refs[6:8], into(key_out, value_out))
    for copy in copies:
        copy.wait()


def message_kernel(hops, heads, scaling, *refs):
    table, mask, late, query, grad, key, value, out = refs
    tail, cut, width = mask.shape[0], out.shape[0], query.shape[1] // heads
    pair = Pair(mask, table, heads, hops, True)
    is_late = late[8:9, :width] > 0.5

    def scores(head):
        cols = columns(head, width)
        score = contract(key[cut:, cols], query[:, cols], 1, 1)
        return score, contract(value[cut:, cols], grad[:, cols], 1, 1)

    def choose(head, found):
        cols = columns(head, width)
        half = pair.half_logits(found[0], head, scaling)
        tanh = jnp.tanh(half)
        rounded = (found[1] * (slope_of(half, tanh) * pair.mask)).astype(BF16)
        weights = ((half + half * tanh) * pair.mask).astype(BF16)
        parts = [contract(rounded, query[:, cols], 1, 0), contract(weights, grad[:, cols], 1, 0)]
        for at, part in enumerate(parts):
            lines = slice(at * tail, (at + 1) * tail)
            out[lines, cols] = jnp.where(is_late, part, grad[lines, cols].astype(F32)).astype(BF16)
        out[2 * tail :, cols] = grad[2 * tail : cut, cols]

    in_stages(heads, scores, choose)


def slopes_kernel(hops, heads, scaling, table, mask, query, key, weights, slopes):
    pair = Pair(mask, table, heads, hops, True)
    rows, cut, width = mask.shape[0], mask.shape[1], query.shape[1] // heads

    def scores(head):
        cols = columns(head, width)
        return contract(key[:, cols], query[:cut, cols], 1, 1)

    def derive(head, found):
        half = pair.half_logits(found, head, scaling)
        tanh = jnp.tanh(half)
        lines = columns(head, rows)
        weights[lines, :] = ((half + half * tanh) * pair.mask).astype(BF16)
        slopes[lines, :] = slope_of(half, tanh) * pair.mask

    in_stages(heads, scores, derive)


def last_kernel(heads, scaling, *refs):
    weights, slopes, late, query, message, value, key_in, value_in = refs[:8]
    outs, held, written = refs[8:10], refs[10:12], refs[12]
    rows, cut, width = query.shape[0], message.shape[0], query.shape[1] // heads
    tail = rows - cut
    is_late = late[0:1, :width]
    copies = []

    def write(at, cols):
        source, target = held[at].at[:, cols], outs[at].at[:, cols]
        copies.append(pltpu.make_async_copy(source, target, written.at[len(copies)]))
        copies[-1].start()

    def scores(head):
        cols = columns(head, width)
        return contract(value[:, cols], message[:, cols], 1, 1)

    def differentiate(head, found):
        cols, lines = columns(head, width), columns(head, rows)
        rounded = (found * slopes[lines, :]).astype(BF16)
        parts = [
            contract(rounded, query[:cut, cols], 1, 0),
            contract(weights[lines, :], message[:, cols], 1, 0),
        ]
        for at, (part, before) in enumerate(zip(parts, (key_in, value_in))):
            factor = 1.0 if at else scaling
            held[at][:cut, cols] = ((before[:cut, cols] + part[:cut]) * factor).astype(BF16)
            sent = message[at * tail : (at + 1) * tail, cols].astype(F32) * is_late
            held[at][cut:, cols] = ((before[cut:, cols] + part[cut:] + sent) * factor).astype(BF16)
        for at in (0, 1):
            write(at, cols)

    in_stages(heads, scores, differentiate)
    for copy in copies:
        copy.wait()


def sum_kernel(*refs):
    gain_out, bias_out = refs[-2:]
    total = added_up([piece[...] for piece in refs[:-2]])
    lines = gain_out.shape[0]
    gain_out[...] = total[:lines]
    bias_out[...] = total[lines:, : bias_out.shape[1]]


def on_device(kernel, outs, args, smem=(), ahead=(), far=(), far_outs=0, scratch=()):
    count = len(smem) + len(far) + len(args)
    far = [pltpu.with_memory_space_constraint(array, pltpu.HBM) for array in far]

    def body(*refs):
        kernel(*refs[:count], *refs[count + len(ahead) :])

    vmem, anywhere = pl.BlockSpec(memory_space=pltpu.VMEM), pl.BlockSpec(memory_space=pl.ANY)
    return pl.pallas_call(
        body,
        out_shape=outs,
        in_specs=[pl.BlockSpec(memory_space=pltpu.SMEM)] * len(smem)
        + [pl.BlockSpec(memory_space=pltpu.HBM)] * len(far)
        + [vmem] * len(args)
        + [anywhere] * len(ahead),
        out_specs=[anywhere] * far_outs + [vmem] * (len(outs) - far_outs),
        scratch_shapes=scratch,
        compiler_params=pltpu.CompilerParams(vmem_limit_bytes=VMEM_LIMIT),
        cost_estimate=pl.CostEstimate(flops=1000000, bytes_accessed=100000, transcendentals=0),
    )(*smem, *far, *args, *ahead)


def rounds_of(axes):
    rounds = []
    for axis in axes:
        size = lax.axis_size(axis)
        step = 1
        while step < size:
            radix = 4 if size // step >= 4 else 2
            rounds.append((axis, [step * at for at in range(1, radix)]))
            step = radix * step
    return rounds


def exchanged(array, axis, distances):
    size = lax.axis_size(axis)
    found = [
        lax.ppermute(array, axis, [(i, i ^ distance) for i in range(size)])
        for distance in reversed(distances)
    ]
    return [array] + found[::-1]


def added_up(pieces):
    while len(pieces) > 1:
        pieces = [left + right for left, right in zip(pieces[::2], pieces[1::2])]
    return pieces[0]


def local(queries, key_rows, value_rows, update_gate, out_grad, user_lengths, rel_bias, norm_gain):
    rows, features = queries.shape[1:]
    levels, heads = rel_bias.shape
    scaling = (features // heads) ** (-0.5)
    reach = min(3, lax.axis_size("ctx") // 2)
    wide = jax.ShapeDtypeStruct((rows, features), F32)
    narrow = jax.ShapeDtypeStruct((rows, features), BF16)
    inputs = (queries[0], key_rows[0], value_rows[0], update_gate[0], out_grad[0])
    gain = norm_gain[None]

    arrived = [passed_along(inputs[at], "ctx", by) for at, by in ((1, 1), (2, 1), (0, -1))]

    hop_list = tuple(range(reach + 1))
    plan = [(0, hops, False) for hops in hop_list] + [(hops, hops, True) for hops in hop_list]
    plan += [(reach - 1, reach, True)]
    cut = rows - rows // 4
    shapes = [(rows, rows)] * (len(plan) - 2) + [(rows, cut), (rows - cut, rows), (16, rows)]
    outs = [jax.ShapeDtypeStruct((count * heads, rows), F32) for count in (levels, rows)]
    outs += [jax.ShapeDtypeStruct(shape, F32) for shape in shapes]
    outs += [narrow] * len(inputs) + [wide]
    table, near, *found = on_device(
        partial(first_kernel, plan, cut, heads, scaling),
        outs,
        (),
        (user_lengths, rel_bias),
        far=inputs,
        scratch=[pltpu.SemaphoreType.DMA((len(inputs),))],
    )
    masks, flipped = found[: reach + 1], found[reach + 1 : 2 * reach + 2]
    sender_mask, late, query, key, value, gate, grad, attention = found[2 * reach + 2 :]

    later_queries = [query, arrived[2]]
    keys, values = [key, arrived[0]], [value, arrived[1]]
    for hops in range(1, reach):
        keys.append(passed_along(keys[-1], "ctx", 1, hops + 1))
        values.append(passed_along(values[-1], "ctx", 1, hops + 1))
        later_queries.append(passed_along(later_queries[-1], "ctx", -1, hops + 1))
    for hops in range(1, reach):
        (attention,) = on_device(
            partial(forward_kernel, hops, heads, scaling),
            [wide],
            (table, near, masks[hops], query, keys[hops], values[hops], attention),
            ahead=later_queries[hops : hops + 1],
        )
    stacked = (heads * rows, rows)
    (far_weights,) = on_device(
        partial(weights_kernel, reach, heads, scaling),
        [jax.ShapeDtypeStruct(stacked, BF16)],
        (table, near, masks[-1], query, keys[-1]),
        ahead=[attention],
    )
    attention, attn_grad, gain_part = on_device(
        partial(norm_kernel, heads),
        [wide, narrow, jax.ShapeDtypeStruct((1, features), F32)],
        (far_weights, values[-1], attention, grad, gate, gain),
    )

    lanes = features // 8
    query_grad, sums = on_device(
        partial(backward_query_kernel, hop_list, heads, scaling),
        [narrow, jax.ShapeDtypeStruct((8 + levels, lanes), F32)],
        (table, near, *masks, query, attn_grad, *keys, *values, gain_part),
        ahead=later_queries[reach:],
    )
    later_grads = [attn_grad, passed_along(attn_grad, "ctx", -1)]
    pieces = [sums]
    for axis, distances in rounds_of(("dp",)):
        pieces = exchanged(added_up(pieces), axis, distances)

    def key_operands(hops):
        later = (later_queries[hops], later_grads[hops])
        return (table, flipped[hops], *later, key, value)

    key_grads = on_device(
        partial(next_key_kernel, 0, heads, scaling),
        [wide] * 2,
        key_operands(0),
        ahead=pieces[1:2],
    )
    for hops in range(1, reach):
        arrived, *pieces = lax.optimization_barrier((later_grads[hops], *pieces))
        if hops + 1 == reach:
            (arrived,) = on_device(
                partial(message_kernel, reach, heads, scaling),
                [jax.ShapeDtypeStruct((cut, features), BF16)],
                (table, sender_mask, late, later_queries[hops], arrived, keys[1], values[1]),
            )
        later_grads.append(passed_along(arrived, "ctx", -1, hops + 1))
        if hops == 1:
            gate_grad, query_grad, *key_grads = on_device(
                partial(gate_and_key_kernel, hops, heads, scaling),
                [narrow, narrow, wide, wide],
                (*key_operands(hops), *key_grads, attention, grad, gain, query_grad),
                far_outs=2,
                scratch=[pltpu.VMEM((rows, features), BF16), pltpu.SemaphoreType.DMA((8,))],
            )
        else:
            key_grads = on_device(
                partial(next_key_kernel, hops, heads, scaling),
                [wide] * 2,
                (*key_operands(hops), *key_grads),
            )
    far_tables = on_device(
        partial(slopes_kernel, reach, heads, scaling),
        [jax.ShapeDtypeStruct((heads * rows, cut), kind) for kind in (BF16, F32)],
        (table, flipped[reach], later_queries[reach], key),
        ahead=key_grads[:1],
    )
    for axis, distances in rounds_of(("ctx",)):
        pieces = exchanged(added_up(pieces), axis, distances)
    key_grad, value_grad = on_device(
        partial(last_kernel, heads, scaling),
        [narrow, narrow],
        (*far_tables, late, later_queries[reach], later_grads[reach], value, *key_grads),
        far_outs=2,
        scratch=[pltpu.VMEM((rows, features), BF16)] * 2 + [pltpu.SemaphoreType.DMA((2 * heads,))],
    )
    key_grad, value_grad, pieces[0] = lax.optimization_barrier((key_grad, value_grad, pieces[0]))
    gain_grad, bias_grad = on_device(
        sum_kernel,
        [jax.ShapeDtypeStruct((8, lanes), F32), jax.ShapeDtypeStruct((levels, heads), F32)],
        pieces[::-1],
    )
    return (
        query_grad[None],
        key_grad[None],
        value_grad[None],
        gate_grad[None],
        bias_grad,
        gain_grad.reshape(features),
    )


def solution(mesh):
    in_specs = (
        P(("groups", "dp"), "ctx", None),
        P(("groups", "dp"), "ctx", None),
        P(("groups", "dp"), "ctx", None),
        P(("groups", "dp"), "ctx", None),
        P(("groups", "dp"), "ctx", None),
        P(("groups", "dp"), None),
        P(),
        P(),
    )
    out_specs = (
        P(("groups", "dp"), "ctx", None),
        P(("groups", "dp"), "ctx", None),
        P(("groups", "dp"), "ctx", None),
        P(("groups", "dp"), "ctx", None),
        P("groups", None),
        P("groups"),
    )
    return jax.shard_map(local, mesh=mesh, in_specs=in_specs, out_specs=out_specs, check_vma=False)
```

```python
from functools import partial

import jax
import jax.numpy as jnp
from jax import lax
from jax.experimental import pallas as pl
from jax.experimental.pallas import tpu as pltpu
from jax.sharding import PartitionSpec as P

EPSILON = 1e-05
VMEM_LIMIT = 24 * 1024 * 1024
F32 = jnp.float32
BF16 = jnp.bfloat16


def passed_along(array, axis, by, hop=1):
    size = lax.axis_size(axis)
    first, last = (hop - 1, size - 2) if by > 0 else (1, size - hop)
    return lax.ppermute(array, axis, [(i, i + by) for i in range(first, last + 1)])


def contract(left, right, left_dim, right_dim):
    return lax.dot_general(
        left, right, (((left_dim,), (right_dim,)), ((), ())), preferred_element_type=F32
    )


def user_starts(lengths, query_pos):
    end = jnp.int32(0)
    start = jnp.zeros(query_pos.shape, jnp.int32)
    for user in range(lengths.shape[1]):
        end = end + lengths[0, user]
        start = jnp.where(query_pos >= end, end, start)
    return start


class Pair:
    def __init__(self, mask, table, heads, hops, flipped=False, near=None):
        rows = table.shape[1]
        self.table, self.heads, self.levels = table, heads, table.shape[0] // heads
        self.mask, self.hops, self.near = mask[...], hops, near
        self.far = (hops - 1) * rows + 1 >= 2 ** (self.levels - 2)
        if not self.far:
            query_dim, key_dim = (1, 0) if flipped else (0, 1)
            query_row = lax.broadcasted_iota(jnp.int32, mask.shape, query_dim)
            key_row = lax.broadcasted_iota(jnp.int32, mask.shape, key_dim)
            self.distance = query_row - key_row + hops * rows

    def half_bias(self, head):
        def level_row(level):
            at = level * self.heads + head
            return self.table[at : at + 1, : self.mask.shape[1]]

        value = level_row(self.levels - 1)
        if self.far:
            return value
        if self.near is not None:
            rows = self.mask.shape[0]
            close = self.near[head * rows : (head + 1) * rows, :]
            return close if self.hops == 0 else jnp.where(self.distance < rows, close, value)
        for level in range(self.levels - 2, -1, -1):
            value = jnp.where(self.distance < 2**level, level_row(level), value)
        return value

    def half_logits(self, scores, head, scaling):
        return scores * (0.5 * scaling) + self.half_bias(head)


def slope_of(half, tanh):
    return (0.5 + 0.5 * tanh) * (1.0 + half * (1.0 - tanh))


def columns(head, width):
    return slice(head * width, (head + 1) * width)


def in_stages(count, first, second, ahead=3):
    held = [first(i) for i in range(min(ahead, count))]
    for i in range(count):
        if i + ahead < count:
            held.append(first(i + ahead))
        second(i, held.pop(0))


def attend(pairs, heads, scaling, query, keys, values, total, out):
    width = query.shape[1] // heads

    def scores(head):
        cols = columns(head, width)
        return [contract(query[:, cols], key[:, cols], 1, 1) for key in keys]

    def weigh(head, found):
        cols = columns(head, width)
        part = None if total is None else total[:, cols]
        for pair, score, value in zip(pairs, found, values):
            half = pair.half_logits(score, head, scaling)
            weights = ((half + half * jnp.tanh(half)) * pair.mask).astype(BF16)
            added = contract(weights, value[:, cols], 1, 0)
            part = added if part is None else part + added
        out[:, cols] = part.astype(out.dtype)

    in_stages(heads, scores, weigh)


def far_start(lengths, block, reach, rows):
    first = (lax.axis_index("ctx") + block) * rows
    end, start = jnp.int32(0), jnp.int32(0)
    for user in range(lengths.shape[1]):
        end = end + lengths[0, user]
        start = jnp.where(first >= end, end, start)
    return start - (first - reach * rows)


def first_kernel(plan, cut, heads, scaling, lengths, bias, *refs):
    inputs, refs = refs[:6], refs[6:]
    table, near, masks, refs = refs[0], refs[1], refs[2 : 2 + len(plan)], refs[2 + len(plan) :]
    late, refs = refs[0], refs[1:]
    held, out, arrived = refs[:6], refs[6], refs[7]
    copies = [
        pltpu.make_async_copy(source, target, arrived.at[at])
        for at, (source, target) in enumerate(zip(inputs, held))
    ]
    for copy in copies:
        copy.start()
    levels = bias.shape[0]
    for level in range(levels):
        for head in range(heads):
            at = level * heads + head
            table[at : at + 1, :] = jnp.full((1, table.shape[1]), 0.5 * bias[level, head], F32)
    rows = masks[0].shape[0]
    apart = lax.broadcasted_iota(jnp.int32, (rows, rows), 0)
    apart = (apart - lax.broadcasted_iota(jnp.int32, (rows, rows), 1)) & (rows - 1)
    for head in range(heads):
        value = table[(levels - 1) * heads + head : (levels - 1) * heads + head + 1, :]
        for level in range(levels - 2, -1, -1):
            at = level * heads + head
            value = jnp.where(apart < 2**level, table[at : at + 1, :], value)
        near[head * rows : (head + 1) * rows, :] = value
    for (block, hops, flipped), mask in zip(plan, masks):
        query_dim, key_dim = (1, 0) if flipped else (0, 1)
        line = (1, mask.shape[1]) if flipped else (mask.shape[0], 1)
        first = (lax.axis_index("ctx") + block) * rows
        query_pos = first + lax.broadcasted_iota(jnp.int32, line, query_dim)
        key_first = first - hops * rows + rows - mask.shape[key_dim]
        key_pos = key_first + lax.broadcasted_iota(jnp.int32, mask.shape, key_dim)
        seen = (key_pos >= user_starts(lengths, query_pos)) & (key_pos <= query_pos)
        value = jnp.where(seen, 1.0, 0.0).astype(F32)
        if mask.shape == (rows, rows):
            mask[...] = value
            continue
        at = 0 if mask.shape[0] == rows else 1
        is_late = jnp.where(far_start(lengths, block, hops, rows) > cut, 1.0, 0.0).astype(F32)
        late[8 * at : 8 * at + 8, :] = jnp.full((8, rows), is_late, F32)
        mask[...] = value * (is_late if at else 1.0 - is_late)
    for copy in copies:
        copy.wait()
    query, key, value = held[:3]
    pair = Pair(masks[0], table, heads, 0, near=near)
    attend([pair], heads, scaling, query, [key], [value], None, out)


def forward_kernel(hops, heads, scaling, table, near, mask, query, key, value, total, out):
    pair = Pair(mask, table, heads, hops, near=near)
    attend([pair], heads, scaling, query, [key], [value], total, out)


def normed_rows(attention):
    center = attention - jnp.mean(attention, axis=1, keepdims=True)
    inverse = lax.rsqrt(jnp.mean(center * center, axis=1, keepdims=True) + EPSILON)
    return center * inverse, inverse


def weights_kernel(hops, heads, scaling, table, near, mask, query, key, weights):
    pair = Pair(mask, table, heads, hops, near=near)
    rows, width = query.shape[0], query.shape[1] // heads

    def scores(head):
        cols = columns(head, width)
        return contract(query[:, cols], key[:, cols], 1, 1)

    def weigh(head, found):
        half = pair.half_logits(found, head, scaling)
        lines = columns(head, rows)
        weights[lines, :] = ((half + half * jnp.tanh(half)) * pair.mask).astype(BF16)

    in_stages(heads, scores, weigh)


def norm_kernel(heads, *refs):
    weights, value, total, out_grad, update_gate, gain = refs[:6]
    attention, attn_grad, gain_grad = refs[6:]
    width = total.shape[1] // heads
    for head in range(heads):
        cols, lines = columns(head, width), columns(head, total.shape[0])
        attention[:, cols] = total[:, cols] + contract(weights[lines, :], value[:, cols], 1, 0)
    rows, features = attention.shape
    step = 16
    gain_row = gain[...]
    gain_sum = jnp.zeros((8, features), F32)
    for low in range(0, rows, step):
        span = slice(low, low + step)
        normed, inverse = normed_rows(attention[span, :])
        gated = out_grad[span, :].astype(F32) * update_gate[span, :].astype(F32)
        product = gated * normed
        for part in range(0, step, 8):
            gain_sum = gain_sum + product[part : part + 8, :]
        pushed = gated * gain_row
        attn_grad[span, :] = (
            inverse
            * (
                pushed
                - jnp.mean(pushed, axis=1, keepdims=True)
                - normed * jnp.mean(pushed * normed, axis=1, keepdims=True)
            )
        ).astype(BF16)
    gain_grad[...] = jnp.sum(gain_sum, axis=0, keepdims=True)


def backward_query_kernel(hop_list, heads, scaling, *refs):
    count = len(hop_list)
    table, near, masks, refs = refs[0], refs[1], refs[2 : 2 + count], refs[2 + count :]
    query, grad, keys, values = refs[0], refs[1], refs[2 : 2 + count], refs[2 + count : 2 + 2 * count]
    gain_in, query_out, small_out = refs[2 + 2 * count :]
    rows, width = query.shape[0], query.shape[1] // heads
    pairs = [Pair(mask, table, heads, hops, near=near) for mask, hops in zip(masks, hop_list)]
    lanes = small_out.shape[1]
    lines = gain_in.shape[1] // lanes
    levels = small_out.shape[0] - lines
    lane = lax.broadcasted_iota(jnp.int32, (levels, lanes), 1)
    level_row = lax.broadcasted_iota(jnp.int32, (levels, lanes), 0)
    group = lax.broadcasted_iota(jnp.int32, (8, rows), 0)
    distance = (group - lax.broadcasted_iota(jnp.int32, (8, rows), 1)) & (rows - 1)
    bucket = sum((distance >= 2**level).astype(jnp.int32) for level in range(levels - 1))
    own = pairs[0].distance >= 0
    bias_total = [jnp.zeros((levels, lanes), F32)]

    def bias_sums(grads):
        close = jnp.where(own, grads[0], grads[1])
        rest = sum(grads[2:], jnp.where(own, grads[1], 0.0))
        by_place, far = jnp.zeros((8, rows), F32), jnp.zeros((8, rows), F32)
        for low in range(0, rows, 8):
            part = close[low : low + 8, :]
            by_place = by_place + (pltpu.roll(part, rows - low, 1) if low else part)
            far = far + rest[low : low + 8, :]
        sums = jnp.where(level_row == levels - 1, jnp.sum(far, axis=0, keepdims=True), 0.0)
        for level in range(levels):
            row = jnp.sum(jnp.where(bucket == level, by_place, 0.0), axis=0, keepdims=True)
            sums = sums + jnp.where(level_row == level, row, 0.0)
        return sums

    def scores(head):
        cols = columns(head, width)
        query_h, grad_h = query[:, cols], grad[:, cols]
        return [
            (contract(query_h, key[:, cols], 1, 1), contract(grad_h, value[:, cols], 1, 1))
            for key, value in zip(keys, values)
        ]

    def differentiate(head, found):
        cols = columns(head, width)
        query_part, grads = None, []
        for pair, key, (score, weight_grad) in zip(pairs, keys, found):
            half = pair.half_logits(score, head, scaling)
            grads.append(weight_grad * (slope_of(half, jnp.tanh(half)) * pair.mask))
            added = contract(grads[-1].astype(BF16), key[:, cols], 1, 0)
            query_part = added if query_part is None else query_part + added
        query_out[:, cols] = (query_part * scaling).astype(BF16)
        sums = jnp.sum(bias_sums(grads), axis=1, keepdims=True)
        bias_total[0] = jnp.where(lane == head, sums, bias_total[0])

    in_stages(heads, scores, differentiate, 1)
    for line in range(lines):
        small_out[line : line + 1, :] = gain_in[:, line * lanes : (line + 1) * lanes]
    small_out[lines:, :] = bias_total[0]


def add_key_grads(hops, heads, scaling, table, mask, query, grad, key, value, sums, store):
    width = query.shape[1] // heads
    pair = Pair(mask, table, heads, hops, True)

    def scores(head):
        cols = columns(head, width)
        score = contract(key[:, cols], query[:, cols], 1, 1)
        return score, contract(value[:, cols], grad[:, cols], 1, 1)

    def differentiate(head, found):
        cols = columns(head, width)
        half = pair.half_logits(found[0], head, scaling)
        tanh = jnp.tanh(half)
        rounded = (found[1] * (slope_of(half, tanh) * pair.mask)).astype(BF16)
        weights = ((half + half * tanh) * pair.mask).astype(BF16)
        parts = [contract(rounded, query[:, cols], 1, 0), contract(weights, grad[:, cols], 1, 0)]
        store(head, cols, *[part + held[:, cols] for part, held in zip(parts, sums)] or parts)

    in_stages(heads, scores, differentiate)


def into(key_out, value_out):
    def store(head, cols, key_part, value_part):
        key_out[:, cols] = key_part
        value_out[:, cols] = value_part

    return store


def next_key_kernel(hops, heads, scaling, *refs):
    add_key_grads(hops, heads, scaling, *refs[:6], refs[6:-2], into(*refs[-2:]))


def gate_and_key_kernel(hops, heads, scaling, *refs):
    attention, out_grad, gain, query_grad = refs[8:12]
    gate_out, query_out, key_out, value_out, held, written = refs[12:]
    rows, step = attention.shape[0], 16
    part = rows // 4
    copies = []

    def write(source, target, low):
        lines = slice(low, low + part)
        copies.append(
            pltpu.make_async_copy(source.at[lines], target.at[lines], written.at[len(copies)])
        )
        copies[-1].start()

    for low in range(0, rows, part):
        write(query_grad, query_out, low)
    gain_row = gain[...]
    for low in range(0, rows, step):
        span = slice(low, low + step)
        normed, _ = normed_rows(attention[span, :])
        held[span, :] = (out_grad[span, :].astype(F32) * normed * gain_row).astype(BF16)
        if (low + step) % part == 0:
            write(held, gate_out, low + step - part)
    add_key_grads(hops, heads, scaling, *refs[:6], refs[6:8], into(key_out, value_out))
    for copy in copies:
        copy.wait()


def message_kernel(hops, heads, scaling, *refs):
    table, mask, late, query, grad, key, value, out = refs
    tail, cut, width = mask.shape[0], out.shape[0], query.shape[1] // heads
    pair = Pair(mask, table, heads, hops, True)
    is_late = late[8:9, :width] > 0.5

    def scores(head):
        cols = columns(head, width)
        score = contract(key[cut:, cols], query[:, cols], 1, 1)
        return score, contract(value[cut:, cols], grad[:, cols], 1, 1)

    def choose(head, found):
        cols = columns(head, width)
        half = pair.half_logits(found[0], head, scaling)
        tanh = jnp.tanh(half)
        rounded = (found[1] * (slope_of(half, tanh) * pair.mask)).astype(BF16)
        weights = ((half + half * tanh) * pair.mask).astype(BF16)
        parts = [contract(rounded, query[:, cols], 1, 0), contract(weights, grad[:, cols], 1, 0)]
        for at, part in enumerate(parts):
            lines = slice(at * tail, (at + 1) * tail)
            out[lines, cols] = jnp.where(is_late, part, grad[lines, cols].astype(F32)).astype(BF16)
        out[2 * tail :, cols] = grad[2 * tail : cut, cols]

    in_stages(heads, scores, choose)


def slopes_kernel(hops, heads, scaling, table, mask, query, key, weights, slopes):
    pair = Pair(mask, table, heads, hops, True)
    rows, cut, width = mask.shape[0], mask.shape[1], query.shape[1] // heads

    def scores(head):
        cols = columns(head, width)
        return contract(key[:, cols], query[:cut, cols], 1, 1)

    def derive(head, found):
        half = pair.half_logits(found, head, scaling)
        tanh = jnp.tanh(half)
        lines = columns(head, rows)
        weights[lines, :] = ((half + half * tanh) * pair.mask).astype(BF16)
        slopes[lines, :] = slope_of(half, tanh) * pair.mask

    in_stages(heads, scores, derive)


def last_kernel(heads, scaling, *refs):
    weights, slopes, late, query, message, value, key_in, value_in = refs[:8]
    outs, held, written = refs[8:10], refs[10:12], refs[12]
    rows, cut, width = query.shape[0], message.shape[0], query.shape[1] // heads
    tail = rows - cut
    is_late = late[0:1, :width]
    copies = []

    def write(at, cols):
        source, target = held[at].at[:, cols], outs[at].at[:, cols]
        copies.append(pltpu.make_async_copy(source, target, written.at[len(copies)]))
        copies[-1].start()

    def scores(head):
        cols = columns(head, width)
        return contract(value[:, cols], message[:, cols], 1, 1)

    def differentiate(head, found):
        cols, lines = columns(head, width), columns(head, rows)
        rounded = (found * slopes[lines, :]).astype(BF16)
        parts = [
            contract(rounded, query[:cut, cols], 1, 0),
            contract(weights[lines, :], message[:, cols], 1, 0),
        ]
        for at, (part, before) in enumerate(zip(parts, (key_in, value_in))):
            factor = 1.0 if at else scaling
            held[at][:cut, cols] = ((before[:cut, cols] + part[:cut]) * factor).astype(BF16)
            sent = message[at * tail : (at + 1) * tail, cols].astype(F32) * is_late
            held[at][cut:, cols] = ((before[cut:, cols] + part[cut:] + sent) * factor).astype(BF16)
        for at in (0, 1):
            write(at, cols)

    in_stages(heads, scores, differentiate)
    for copy in copies:
        copy.wait()


def sum_kernel(*refs):
    gain_out, bias_out = refs[-2:]
    total = added_up([piece[...] for piece in refs[:-2]])
    lines = gain_out.shape[0]
    gain_out[...] = total[:lines]
    bias_out[...] = total[lines:, : bias_out.shape[1]]


def on_device(kernel, outs, args, smem=(), ahead=(), far=(), far_outs=0, scratch=()):
    count = len(smem) + len(far) + len(args)
    far = [pltpu.with_memory_space_constraint(array, pltpu.HBM) for array in far]

    def body(*refs):
        kernel(*refs[:count], *refs[count + len(ahead) :])

    vmem, anywhere = pl.BlockSpec(memory_space=pltpu.VMEM), pl.BlockSpec(memory_space=pl.ANY)
    return pl.pallas_call(
        body,
        out_shape=outs,
        in_specs=[pl.BlockSpec(memory_space=pltpu.SMEM)] * len(smem)
        + [pl.BlockSpec(memory_space=pltpu.HBM)] * len(far)
        + [vmem] * len(args)
        + [anywhere] * len(ahead),
        out_specs=[anywhere] * far_outs + [vmem] * (len(outs) - far_outs),
        scratch_shapes=scratch,
        compiler_params=pltpu.CompilerParams(vmem_limit_bytes=VMEM_LIMIT),
        cost_estimate=pl.CostEstimate(flops=1000000, bytes_accessed=100000, transcendentals=0),
    )(*smem, *far, *args, *ahead)


def rounds_of(axes):
    rounds = []
    for axis in axes:
        size = lax.axis_size(axis)
        step = 1
        while step < size:
            radix = 4 if size // step >= 4 else 2
            rounds.append((axis, [step * at for at in range(1, radix)]))
            step = radix * step
    return rounds


def exchanged(array, axis, distances):
    size = lax.axis_size(axis)
    found = [
        lax.ppermute(array, axis, [(i, i ^ distance) for i in range(size)])
        for distance in reversed(distances)
    ]
    return [array] + found[::-1]


def added_up(pieces):
    while len(pieces) > 1:
        pieces = [left + right for left, right in zip(pieces[::2], pieces[1::2])]
    return pieces[0]


def local(queries, key_rows, value_rows, update_gate, out_grad, user_lengths, rel_bias, norm_gain):
    rows, features = queries.shape[1:]
    levels, heads = rel_bias.shape
    scaling = (features // heads) ** (-0.5)
    reach = min(3, lax.axis_size("ctx") // 2)
    wide = jax.ShapeDtypeStruct((rows, features), F32)
    narrow = jax.ShapeDtypeStruct((rows, features), BF16)
    inputs = (queries[0], key_rows[0], value_rows[0], update_gate[0], out_grad[0], norm_gain[None])

    arrived = [passed_along(inputs[at], "ctx", by) for at, by in ((1, 1), (2, 1), (0, -1))]

    hop_list = tuple(range(reach + 1))
    plan = [(0, hops, False) for hops in hop_list] + [(hops, hops, True) for hops in hop_list]
    plan += [(reach - 1, reach, True)]
    cut = rows - rows // 4
    shapes = [(rows, rows)] * (len(plan) - 2) + [(rows, cut), (rows - cut, rows), (16, rows)]
    outs = [jax.ShapeDtypeStruct((count * heads, rows), F32) for count in (levels, rows)]
    outs += [jax.ShapeDtypeStruct(shape, F32) for shape in shapes]
    outs += [jax.ShapeDtypeStruct(array.shape, array.dtype) for array in inputs] + [wide]
    table, near, *found = on_device(
        partial(first_kernel, plan, cut, heads, scaling),
        outs,
        (),
        (user_lengths, rel_bias),
        far=inputs,
        scratch=[pltpu.SemaphoreType.DMA((len(inputs),))],
    )
    masks, flipped = found[: reach + 1], found[reach + 1 : 2 * reach + 2]
    sender_mask, late, query, key, value, gate, grad, gain, attention = found[2 * reach + 2 :]

    later_queries = [query, arrived[2]]
    keys, values = [key, arrived[0]], [value, arrived[1]]
    for hops in range(1, reach):
        keys.append(passed_along(keys[-1], "ctx", 1, hops + 1))
        values.append(passed_along(values[-1], "ctx", 1, hops + 1))
        later_queries.append(passed_along(later_queries[-1], "ctx", -1, hops + 1))
    for hops in range(1, reach):
        (attention,) = on_device(
            partial(forward_kernel, hops, heads, scaling),
            [wide],
            (table, near, masks[hops], query, keys[hops], values[hops], attention),
            ahead=later_queries[hops : hops + 1],
        )
    stacked = (heads * rows, rows)
    (far_weights,) = on_device(
        partial(weights_kernel, reach, heads, scaling),
        [jax.ShapeDtypeStruct(stacked, BF16)],
        (table, near, masks[-1], query, keys[-1]),
        ahead=[attention],
    )
    attention, attn_grad, gain_part = on_device(
        partial(norm_kernel, heads),
        [wide, narrow, jax.ShapeDtypeStruct((1, features), F32)],
        (far_weights, values[-1], attention, grad, gate, gain),
    )

    lanes = features // 8
    query_grad, sums = on_device(
        partial(backward_query_kernel, hop_list, heads, scaling),
        [narrow, jax.ShapeDtypeStruct((8 + levels, lanes), F32)],
        (table, near, *masks, query, attn_grad, *keys, *values, gain_part),
        ahead=later_queries[reach:],
    )
    later_grads = [attn_grad, passed_along(attn_grad, "ctx", -1)]
    pieces = [sums]
    for axis, distances in rounds_of(("dp",)):
        pieces = exchanged(added_up(pieces), axis, distances)

    def key_operands(hops):
        later = (later_queries[hops], later_grads[hops])
        return (table, flipped[hops], *later, key, value)

    key_grads = on_device(
        partial(next_key_kernel, 0, heads, scaling),
        [wide] * 2,
        key_operands(0),
        ahead=pieces[1:2],
    )
    for hops in range(1, reach):
        arrived, *pieces = lax.optimization_barrier((later_grads[hops], *pieces))
        if hops + 1 == reach:
            (arrived,) = on_device(
                partial(message_kernel, reach, heads, scaling),
                [jax.ShapeDtypeStruct((cut, features), BF16)],
                (table, sender_mask, late, later_queries[hops], arrived, keys[1], values[1]),
            )
        later_grads.append(passed_along(arrived, "ctx", -1, hops + 1))
        if hops == 1:
            gate_grad, query_grad, *key_grads = on_device(
                partial(gate_and_key_kernel, hops, heads, scaling),
                [narrow, narrow, wide, wide],
                (*key_operands(hops), *key_grads, attention, grad, gain, query_grad),
                far_outs=2,
                scratch=[pltpu.VMEM((rows, features), BF16), pltpu.SemaphoreType.DMA((8,))],
            )
        else:
            key_grads = on_device(
                partial(next_key_kernel, hops, heads, scaling),
                [wide] * 2,
                (*key_operands(hops), *key_grads),
            )
    far_tables = on_device(
        partial(slopes_kernel, reach, heads, scaling),
        [jax.ShapeDtypeStruct((heads * rows, cut), kind) for kind in (BF16, F32)],
        (table, flipped[reach], later_queries[reach], key),
        ahead=key_grads[:1],
    )
    for axis, distances in rounds_of(("ctx",)):
        pieces = exchanged(added_up(pieces), axis, distances)
    key_grad, value_grad = on_device(
        partial(last_kernel, heads, scaling),
        [narrow, narrow],
        (*far_tables, late, later_queries[reach], later_grads[reach], value, *key_grads),
        far_outs=2,
        scratch=[pltpu.VMEM((rows, features), BF16)] * 2 + [pltpu.SemaphoreType.DMA((2 * heads,))],
    )
    key_grad, value_grad, pieces[0] = lax.optimization_barrier((key_grad, value_grad, pieces[0]))
    gain_grad, bias_grad = on_device(
        sum_kernel,
        [jax.ShapeDtypeStruct((8, lanes), F32), jax.ShapeDtypeStruct((levels, heads), F32)],
        pieces[::-1],
    )
    return (
        query_grad[None],
        key_grad[None],
        value_grad[None],
        gate_grad[None],
        bias_grad,
        gain_grad.reshape(features),
    )


def solution(mesh):
    in_specs = (
        P(("groups", "dp"), "ctx", None),
        P(("groups", "dp"), "ctx", None),
        P(("groups", "dp"), "ctx", None),
        P(("groups", "dp"), "ctx", None),
        P(("groups", "dp"), "ctx", None),
        P(("groups", "dp"), None),
        P(),
        P(),
    )
    out_specs = (
        P(("groups", "dp"), "ctx", None),
        P(("groups", "dp"), "ctx", None),
        P(("groups", "dp"), "ctx", None),
        P(("groups", "dp"), "ctx", None),
        P("groups", None),
        P("groups"),
    )
    return jax.shard_map(local, mesh=mesh, in_specs=in_specs, out_specs=out_specs, check_vma=False)
```

```python
from functools import partial

import jax
import jax.numpy as jnp
from jax import lax
from jax.experimental import pallas as pl
from jax.experimental.pallas import tpu as pltpu
from jax.sharding import PartitionSpec as P

EPSILON = 1e-05
VMEM_LIMIT = 24 * 1024 * 1024
F32 = jnp.float32
BF16 = jnp.bfloat16


def passed_along(array, axis, by, hop=1):
    size = lax.axis_size(axis)
    first, last = (hop - 1, size - 2) if by > 0 else (1, size - hop)
    return lax.ppermute(array, axis, [(i, i + by) for i in range(first, last + 1)])


def contract(left, right, left_dim, right_dim):
    return lax.dot_general(
        left, right, (((left_dim,), (right_dim,)), ((), ())), preferred_element_type=F32
    )


def user_starts(lengths, query_pos):
    end = jnp.int32(0)
    start = jnp.zeros(query_pos.shape, jnp.int32)
    for user in range(lengths.shape[1]):
        end = end + lengths[0, user]
        start = jnp.where(query_pos >= end, end, start)
    return start


class Pair:
    def __init__(self, mask, table, heads, hops, flipped=False, near=None):
        rows = table.shape[1]
        self.table, self.heads, self.levels = table, heads, table.shape[0] // heads
        self.mask, self.hops, self.near = mask[...], hops, near
        self.far = (hops - 1) * rows + 1 >= 2 ** (self.levels - 2)
        if not self.far:
            query_dim, key_dim = (1, 0) if flipped else (0, 1)
            query_row = lax.broadcasted_iota(jnp.int32, mask.shape, query_dim)
            key_row = lax.broadcasted_iota(jnp.int32, mask.shape, key_dim)
            self.distance = query_row - key_row + hops * rows

    def half_bias(self, head):
        def level_row(level):
            at = level * self.heads + head
            return self.table[at : at + 1, : self.mask.shape[1]]

        value = level_row(self.levels - 1)
        if self.far:
            return value
        if self.near is not None:
            rows = self.mask.shape[0]
            close = self.near[head * rows : (head + 1) * rows, :]
            return close if self.hops == 0 else jnp.where(self.distance < rows, close, value)
        for level in range(self.levels - 2, -1, -1):
            value = jnp.where(self.distance < 2**level, level_row(level), value)
        return value

    def half_logits(self, scores, head, scaling):
        return scores * (0.5 * scaling) + self.half_bias(head)


def slope_of(half, tanh):
    return (0.5 + 0.5 * tanh) * (1.0 + half * (1.0 - tanh))


def columns(head, width):
    return slice(head * width, (head + 1) * width)


def in_stages(count, first, second, ahead=3):
    held = [first(i) for i in range(min(ahead, count))]
    for i in range(count):
        if i + ahead < count:
            held.append(first(i + ahead))
        second(i, held.pop(0))


def attend(pairs, heads, scaling, query, keys, values, total, out):
    width = query.shape[1] // heads

    def scores(head):
        cols = columns(head, width)
        return [contract(query[:, cols], key[:, cols], 1, 1) for key in keys]

    def weigh(head, found):
        cols = columns(head, width)
        part = None if total is None else total[:, cols]
        for pair, score, value in zip(pairs, found, values):
            half = pair.half_logits(score, head, scaling)
            weights = ((half + half * jnp.tanh(half)) * pair.mask).astype(BF16)
            added = contract(weights, value[:, cols], 1, 0)
            part = added if part is None else part + added
        out[:, cols] = part.astype(out.dtype)

    in_stages(heads, scores, weigh)


def far_start(lengths, block, reach, rows):
    first = (lax.axis_index("ctx") + block) * rows
    end, start = jnp.int32(0), jnp.int32(0)
    for user in range(lengths.shape[1]):
        end = end + lengths[0, user]
        start = jnp.where(first >= end, end, start)
    return start - (first - reach * rows)


def first_kernel(plan, cut, heads, scaling, lengths, bias, *refs):
    inputs, refs = refs[:6], refs[6:]
    table, near, masks, refs = refs[0], refs[1], refs[2 : 2 + len(plan)], refs[2 + len(plan) :]
    late, refs = refs[0], refs[1:]
    held, out, arrived = refs[:6], refs[6], refs[7]
    copies = [
        pltpu.make_async_copy(source, target, arrived.at[at])
        for at, (source, target) in enumerate(zip(inputs, held))
    ]
    for copy in copies:
        copy.start()
    levels = bias.shape[0]
    for level in range(levels):
        for head in range(heads):
            at = level * heads + head
            table[at : at + 1, :] = jnp.full((1, table.shape[1]), 0.5 * bias[level, head], F32)
    rows = masks[0].shape[0]
    apart = lax.broadcasted_iota(jnp.int32, (rows, rows), 0)
    apart = (apart - lax.broadcasted_iota(jnp.int32, (rows, rows), 1)) & (rows - 1)
    for head in range(heads):
        value = table[(levels - 1) * heads + head : (levels - 1) * heads + head + 1, :]
        for level in range(levels - 2, -1, -1):
            at = level * heads + head
            value = jnp.where(apart < 2**level, table[at : at + 1, :], value)
        near[head * rows : (head + 1) * rows, :] = value
    for (block, hops, flipped), mask in zip(plan, masks):
        query_dim, key_dim = (1, 0) if flipped else (0, 1)
        line = (1, mask.shape[1]) if flipped else (mask.shape[0], 1)
        first = (lax.axis_index("ctx") + block) * rows
        query_pos = first + lax.broadcasted_iota(jnp.int32, line, query_dim)
        key_first = first - hops * rows + rows - mask.shape[key_dim]
        key_pos = key_first + lax.broadcasted_iota(jnp.int32, mask.shape, key_dim)
        seen = (key_pos >= user_starts(lengths, query_pos)) & (key_pos <= query_pos)
        value = jnp.where(seen, 1.0, 0.0).astype(F32)
        if mask.shape == (rows, rows):
            mask[...] = value
            continue
        at = 0 if mask.shape[0] == rows else 1
        is_late = jnp.where(far_start(lengths, block, hops, rows) > cut, 1.0, 0.0).astype(F32)
        late[8 * at : 8 * at + 8, :] = jnp.full((8, rows), is_late, F32)
        mask[...] = value * (is_late if at else 1.0 - is_late)
    for copy in copies:
        copy.wait()
    query, key, value = held[:3]
    pair = Pair(masks[0], table, heads, 0, near=near)
    attend([pair], heads, scaling, query, [key], [value], None, out)


def forward_kernel(hops, heads, scaling, table, near, mask, query, key, value, total, out):
    pair = Pair(mask, table, heads, hops, near=near)
    attend([pair], heads, scaling, query, [key], [value], total, out)


def normed_rows(attention):
    center = attention - jnp.mean(attention, axis=1, keepdims=True)
    inverse = lax.rsqrt(jnp.mean(center * center, axis=1, keepdims=True) + EPSILON)
    return center * inverse, inverse


def weights_kernel(hops, heads, scaling, table, near, mask, query, key, weights):
    pair = Pair(mask, table, heads, hops, near=near)
    rows, width = query.shape[0], query.shape[1] // heads

    def scores(head):
        cols = columns(head, width)
        return contract(query[:, cols], key[:, cols], 1, 1)

    def weigh(head, found):
        half = pair.half_logits(found, head, scaling)
        lines = columns(head, rows)
        weights[lines, :] = ((half + half * jnp.tanh(half)) * pair.mask).astype(BF16)

    in_stages(heads, scores, weigh)


def norm_kernel(heads, *refs):
    weights, value, total, out_grad, update_gate, gain = refs[:6]
    attention, attn_grad, gain_grad = refs[6:]
    width = total.shape[1] // heads
    for head in range(heads):
        cols, lines = columns(head, width), columns(head, total.shape[0])
        attention[:, cols] = total[:, cols] + contract(weights[lines, :], value[:, cols], 1, 0)
    rows, features = attention.shape
    step = 16
    gain_row = gain[...]
    gain_sum = jnp.zeros((8, features), F32)
    for low in range(0, rows, step):
        span = slice(low, low + step)
        normed, inverse = normed_rows(attention[span, :])
        gated = out_grad[span, :].astype(F32) * update_gate[span, :].astype(F32)
        product = gated * normed
        for part in range(0, step, 8):
            gain_sum = gain_sum + product[part : part + 8, :]
        pushed = gated * gain_row
        attn_grad[span, :] = (
            inverse
            * (
                pushed
                - jnp.mean(pushed, axis=1, keepdims=True)
                - normed * jnp.mean(pushed * normed, axis=1, keepdims=True)
            )
        ).astype(BF16)
    gain_grad[...] = jnp.sum(gain_sum, axis=0, keepdims=True)


def backward_query_kernel(hop_list, heads, scaling, *refs):
    count = len(hop_list)
    table, near, masks, refs = refs[0], refs[1], refs[2 : 2 + count], refs[2 + count :]
    query, grad, keys, values = refs[0], refs[1], refs[2 : 2 + count], refs[2 + count : 2 + 2 * count]
    gain_in, query_out, small_out = refs[2 + 2 * count :]
    rows, width = query.shape[0], query.shape[1] // heads
    pairs = [Pair(mask, table, heads, hops, near=near) for mask, hops in zip(masks, hop_list)]
    lanes = small_out.shape[1]
    lines = gain_in.shape[1] // lanes
    levels = small_out.shape[0] - lines
    lane = lax.broadcasted_iota(jnp.int32, (levels, lanes), 1)
    level_row = lax.broadcasted_iota(jnp.int32, (levels, lanes), 0)
    group = lax.broadcasted_iota(jnp.int32, (8, rows), 0)
    distance = (group - lax.broadcasted_iota(jnp.int32, (8, rows), 1)) & (rows - 1)
    bucket = sum((distance >= 2**level).astype(jnp.int32) for level in range(levels - 1))
    own = pairs[0].distance >= 0
    bias_total = [jnp.zeros((levels, lanes), F32)]

    def bias_sums(grads):
        close = jnp.where(own, grads[0], grads[1])
        rest = sum(grads[2:], jnp.where(own, grads[1], 0.0))
        by_place, far = jnp.zeros((8, rows), F32), jnp.zeros((8, rows), F32)
        for low in range(0, rows, 8):
            part = close[low : low + 8, :]
            by_place = by_place + (pltpu.roll(part, rows - low, 1) if low else part)
            far = far + rest[low : low + 8, :]
        sums = jnp.where(level_row == levels - 1, jnp.sum(far, axis=0, keepdims=True), 0.0)
        for level in range(levels):
            row = jnp.sum(jnp.where(bucket == level, by_place, 0.0), axis=0, keepdims=True)
            sums = sums + jnp.where(level_row == level, row, 0.0)
        return sums

    def scores(head):
        cols = columns(head, width)
        query_h, grad_h = query[:, cols], grad[:, cols]
        return [
            (contract(query_h, key[:, cols], 1, 1), contract(grad_h, value[:, cols], 1, 1))
            for key, value in zip(keys, values)
        ]

    def differentiate(head, found):
        cols = columns(head, width)
        query_part, grads = None, []
        for pair, key, (score, weight_grad) in zip(pairs, keys, found):
            half = pair.half_logits(score, head, scaling)
            grads.append(weight_grad * (slope_of(half, jnp.tanh(half)) * pair.mask))
            added = contract(grads[-1].astype(BF16), key[:, cols], 1, 0)
            query_part = added if query_part is None else query_part + added
        query_out[:, cols] = (query_part * scaling).astype(BF16)
        sums = jnp.sum(bias_sums(grads), axis=1, keepdims=True)
        bias_total[0] = jnp.where(lane == head, sums, bias_total[0])

    in_stages(heads, scores, differentiate, 1)
    for line in range(lines):
        small_out[line : line + 1, :] = gain_in[:, line * lanes : (line + 1) * lanes]
    small_out[lines:, :] = bias_total[0]


def add_key_grads(hops, heads, scaling, table, mask, query, grad, key, value, sums, store):
    width = query.shape[1] // heads
    pair = Pair(mask, table, heads, hops, True)

    def scores(head):
        cols = columns(head, width)
        score = contract(key[:, cols], query[:, cols], 1, 1)
        return score, contract(value[:, cols], grad[:, cols], 1, 1)

    def differentiate(head, found):
        cols = columns(head, width)
        half = pair.half_logits(found[0], head, scaling)
        tanh = jnp.tanh(half)
        rounded = (found[1] * (slope_of(half, tanh) * pair.mask)).astype(BF16)
        weights = ((half + half * tanh) * pair.mask).astype(BF16)
        parts = [contract(rounded, query[:, cols], 1, 0), contract(weights, grad[:, cols], 1, 0)]
        store(head, cols, *[part + held[:, cols] for part, held in zip(parts, sums)] or parts)

    in_stages(heads, scores, differentiate)


def into(key_out, value_out):
    def store(head, cols, key_part, value_part):
        key_out[:, cols] = key_part
        value_out[:, cols] = value_part

    return store


def next_key_kernel(hops, heads, scaling, *refs):
    add_key_grads(hops, heads, scaling, *refs[:6], refs[6:-2], into(*refs[-2:]))


def gate_and_key_kernel(hops, heads, scaling, *refs):
    attention, out_grad, gain, query_grad = refs[8:12]
    gate_out, query_out, key_out, value_out, held, written = refs[12:]
    rows, step = attention.shape[0], 16
    part = rows // 4
    copies = []

    def write(source, target, low):
        lines = slice(low, low + part)
        copies.append(
            pltpu.make_async_copy(source.at[lines], target.at[lines], written.at[len(copies)])
        )
        copies[-1].start()

    for low in range(0, rows, part):
        write(query_grad, query_out, low)
    gain_row = gain[...]
    for low in range(0, rows, step):
        span = slice(low, low + step)
        normed, _ = normed_rows(attention[span, :])
        held[span, :] = (out_grad[span, :].astype(F32) * normed * gain_row).astype(BF16)
        if (low + step) % part == 0:
            write(held, gate_out, low + step - part)
    add_key_grads(hops, heads, scaling, *refs[:6], refs[6:8], into(key_out, value_out))
    for copy in copies:
        copy.wait()


def message_kernel(hops, heads, scaling, *refs):
    table, mask, late, query, grad, key, value, out = refs
    tail, cut, width = mask.shape[0], out.shape[0], query.shape[1] // heads
    pair = Pair(mask, table, heads, hops, True)
    is_late = late[8:9, :width] > 0.5

    def scores(head):
        cols = columns(head, width)
        score = contract(key[cut:, cols], query[:, cols], 1, 1)
        return score, contract(value[cut:, cols], grad[:, cols], 1, 1)

    def choose(head, found):
        cols = columns(head, width)
        half = pair.half_logits(found[0], head, scaling)
        tanh = jnp.tanh(half)
        rounded = (found[1] * (slope_of(half, tanh) * pair.mask)).astype(BF16)
        weights = ((half + half * tanh) * pair.mask).astype(BF16)
        parts = [contract(rounded, query[:, cols], 1, 0), contract(weights, grad[:, cols], 1, 0)]
        for at, part in enumerate(parts):
            lines = slice(at * tail, (at + 1) * tail)
            out[lines, cols] = jnp.where(is_late, part, grad[lines, cols].astype(F32)).astype(BF16)
        out[2 * tail :, cols] = grad[2 * tail : cut, cols]

    in_stages(heads, scores, choose)


def slopes_kernel(hops, heads, scaling, table, mask, query, key, weights, slopes):
    pair = Pair(mask, table, heads, hops, True)
    rows, cut, width = mask.shape[0], mask.shape[1], query.shape[1] // heads

    def scores(head):
        cols = columns(head, width)
        return contract(key[:, cols], query[:cut, cols], 1, 1)

    def derive(head, found):
        half = pair.half_logits(found, head, scaling)
        tanh = jnp.tanh(half)
        lines = columns(head, rows)
        weights[lines, :] = ((half + half * tanh) * pair.mask).astype(BF16)
        slopes[lines, :] = slope_of(half, tanh) * pair.mask

    in_stages(heads, scores, derive)


def last_kernel(heads, scaling, *refs):
    weights, slopes, late, query, message, value, key_in, value_in = refs[:8]
    outs, held, written = refs[8:10], refs[10:12], refs[12]
    rows, cut, width = query.shape[0], message.shape[0], query.shape[1] // heads
    tail = rows - cut
    is_late = late[0:1, :width]
    copies = []

    def write(at, cols):
        source, target = held[at].at[:, cols], outs[at].at[:, cols]
        copies.append(pltpu.make_async_copy(source, target, written.at[len(copies)]))
        copies[-1].start()

    def scores(head):
        cols = columns(head, width)
        return contract(value[:, cols], message[:, cols], 1, 1)

    def differentiate(head, found):
        cols, lines = columns(head, width), columns(head, rows)
        rounded = (found * slopes[lines, :]).astype(BF16)
        parts = [
            contract(rounded, query[:cut, cols], 1, 0),
            contract(weights[lines, :], message[:, cols], 1, 0),
        ]
        for at, (part, before) in enumerate(zip(parts, (key_in, value_in))):
            factor = 1.0 if at else scaling
            held[at][:cut, cols] = ((before[:cut, cols] + part[:cut]) * factor).astype(BF16)
            sent = message[at * tail : (at + 1) * tail, cols].astype(F32) * is_late
            held[at][cut:, cols] = ((before[cut:, cols] + part[cut:] + sent) * factor).astype(BF16)
        for at in (0, 1):
            write(at, cols)

    in_stages(heads, scores, differentiate)
    for copy in copies:
        copy.wait()


def sum_kernel(*refs):
    gain_out, bias_out = refs[-2:]
    total = added_up([piece[...] for piece in refs[:-2]])
    lines = gain_out.shape[0]
    gain_out[...] = total[:lines]
    bias_out[...] = total[lines:, : bias_out.shape[1]]


def on_device(kernel, outs, args, smem=(), ahead=(), far=(), far_outs=0, scratch=()):
    count = len(smem) + len(far) + len(args)
    far = [pltpu.with_memory_space_constraint(array, pltpu.HBM) for array in far]

    def body(*refs):
        kernel(*refs[:count], *refs[count + len(ahead) :])

    vmem, anywhere = pl.BlockSpec(memory_space=pltpu.VMEM), pl.BlockSpec(memory_space=pl.ANY)
    return pl.pallas_call(
        body,
        out_shape=outs,
        in_specs=[pl.BlockSpec(memory_space=pltpu.SMEM)] * len(smem)
        + [pl.BlockSpec(memory_space=pltpu.HBM)] * len(far)
        + [vmem] * len(args)
        + [anywhere] * len(ahead),
        out_specs=[anywhere] * far_outs + [vmem] * (len(outs) - far_outs),
        scratch_shapes=scratch,
        compiler_params=pltpu.CompilerParams(vmem_limit_bytes=VMEM_LIMIT),
        cost_estimate=pl.CostEstimate(flops=1000000, bytes_accessed=100000, transcendentals=0),
    )(*smem, *far, *args, *ahead)


def rounds_of(axes):
    rounds = []
    for axis in axes:
        size = lax.axis_size(axis)
        step = 1
        while step < size:
            radix = 4 if size // step >= 4 else 2
            rounds.append((axis, [step * at for at in range(1, radix)]))
            step = radix * step
    return rounds


def exchanged(array, axis, distances):
    size = lax.axis_size(axis)
    found = [
        lax.ppermute(array, axis, [(i, i ^ distance) for i in range(size)])
        for distance in reversed(distances)
    ]
    return [array] + found[::-1]


def added_up(pieces):
    while len(pieces) > 1:
        pieces = [left + right for left, right in zip(pieces[::2], pieces[1::2])]
    return pieces[0]


def local(queries, key_rows, value_rows, update_gate, out_grad, user_lengths, rel_bias, norm_gain):
    rows, features = queries.shape[1:]
    levels, heads = rel_bias.shape
    scaling = (features // heads) ** (-0.5)
    reach = min(3, lax.axis_size("ctx") // 2)
    wide = jax.ShapeDtypeStruct((rows, features), F32)
    narrow = jax.ShapeDtypeStruct((rows, features), BF16)
    inputs = (queries[0], key_rows[0], value_rows[0], update_gate[0], out_grad[0], norm_gain[None])

    arrived = [passed_along(inputs[at], "ctx", by) for at, by in ((1, 1), (2, 1), (0, -1))]

    hop_list = tuple(range(reach + 1))
    plan = [(0, hops, False) for hops in hop_list] + [(hops, hops, True) for hops in hop_list]
    plan += [(reach - 1, reach, True)]
    cut = rows - rows // 4
    shapes = [(rows, rows)] * (len(plan) - 2) + [(rows, cut), (rows - cut, rows), (16, rows)]
    outs = [jax.ShapeDtypeStruct((count * heads, rows), F32) for count in (levels, rows)]
    outs += [jax.ShapeDtypeStruct(shape, F32) for shape in shapes]
    outs += [jax.ShapeDtypeStruct(array.shape, array.dtype) for array in inputs] + [wide]
    table, near, *found = on_device(
        partial(first_kernel, plan, cut, heads, scaling),
        outs,
        (),
        (user_lengths, rel_bias),
        far=inputs,
        scratch=[pltpu.SemaphoreType.DMA((len(inputs),))],
    )
    masks, flipped = found[: reach + 1], found[reach + 1 : 2 * reach + 2]
    sender_mask, late, query, key, value, gate, grad, gain, attention = found[2 * reach + 2 :]

    later_queries = [query, arrived[2]]
    keys, values = [key, arrived[0]], [value, arrived[1]]
    for hops in range(1, reach):
        keys.append(passed_along(keys[-1], "ctx", 1, hops + 1))
        values.append(passed_along(values[-1], "ctx", 1, hops + 1))
        later_queries.append(passed_along(later_queries[-1], "ctx", -1, hops + 1))
    for hops in range(1, reach):
        (attention,) = on_device(
            partial(forward_kernel, hops, heads, scaling),
            [wide],
            (table, near, masks[hops], query, keys[hops], values[hops], attention),
            ahead=later_queries[hops : hops + 1],
        )
    stacked = (heads * rows, rows)
    (far_weights,) = on_device(
        partial(weights_kernel, reach, heads, scaling),
        [jax.ShapeDtypeStruct(stacked, BF16)],
        (table, near, masks[-1], query, keys[-1]),
        ahead=[attention],
    )
    attention, attn_grad, gain_part = on_device(
        partial(norm_kernel, heads),
        [wide, narrow, jax.ShapeDtypeStruct((1, features), F32)],
        (far_weights, values[-1], attention, grad, gate, gain),
    )

    lanes = features // 8
    query_grad, sums = on_device(
        partial(backward_query_kernel, hop_list, heads, scaling),
        [narrow, jax.ShapeDtypeStruct((8 + levels, lanes), F32)],
        (table, near, *masks, query, attn_grad, *keys, *values, gain_part),
        ahead=later_queries[reach:],
    )
    later_grads = [attn_grad, passed_along(attn_grad, "ctx", -1)]
    pieces = [sums]
    for axis, distances in rounds_of(("dp",)):
        pieces = exchanged(added_up(pieces), axis, distances)

    def key_operands(hops):
        later = (later_queries[hops], later_grads[hops])
        return (table, flipped[hops], *later, key, value)

    key_grads = on_device(
        partial(next_key_kernel, 0, heads, scaling),
        [wide] * 2,
        key_operands(0),
    )
    far_tables = on_device(
        partial(slopes_kernel, reach, heads, scaling),
        [jax.ShapeDtypeStruct((heads * rows, cut), kind) for kind in (BF16, F32)],
        (table, flipped[reach], later_queries[reach], key),
    )
    for hops in range(1, reach):
        arrived, *pieces = lax.optimization_barrier((later_grads[hops], *pieces))
        if hops + 1 == reach:
            (arrived,) = on_device(
                partial(message_kernel, reach, heads, scaling),
                [jax.ShapeDtypeStruct((cut, features), BF16)],
                (table, sender_mask, late, later_queries[hops], arrived, keys[1], values[1]),
                ahead=[key_grads[0], far_tables[0]],
            )
        later_grads.append(passed_along(arrived, "ctx", -1, hops + 1))
        if hops == 1:
            gate_grad, query_grad, *key_grads = on_device(
                partial(gate_and_key_kernel, hops, heads, scaling),
                [narrow, narrow, wide, wide],
                (*key_operands(hops), *key_grads, attention, grad, gain, query_grad),
                far_outs=2,
                scratch=[pltpu.VMEM((rows, features), BF16), pltpu.SemaphoreType.DMA((8,))],
            )
        else:
            key_grads = on_device(
                partial(next_key_kernel, hops, heads, scaling),
                [wide] * 2,
                (*key_operands(hops), *key_grads),
            )
    for axis, distances in rounds_of(("ctx",)):
        pieces = exchanged(added_up(pieces), axis, distances)
    key_grad, value_grad = on_device(
        partial(last_kernel, heads, scaling),
        [narrow, narrow],
        (*far_tables, late, later_queries[reach], later_grads[reach], value, *key_grads),
        far_outs=2,
        scratch=[pltpu.VMEM((rows, features), BF16)] * 2 + [pltpu.SemaphoreType.DMA((2 * heads,))],
    )
    key_grad, value_grad, pieces[0] = lax.optimization_barrier((key_grad, value_grad, pieces[0]))
    gain_grad, bias_grad = on_device(
        sum_kernel,
        [jax.ShapeDtypeStruct((8, lanes), F32), jax.ShapeDtypeStruct((levels, heads), F32)],
        pieces,
    )
    return (
        query_grad[None],
        key_grad[None],
        value_grad[None],
        gate_grad[None],
        bias_grad,
        gain_grad.reshape(features),
    )


def solution(mesh):
    in_specs = (
        P(("groups", "dp"), "ctx", None),
        P(("groups", "dp"), "ctx", None),
        P(("groups", "dp"), "ctx", None),
        P(("groups", "dp"), "ctx", None),
        P(("groups", "dp"), "ctx", None),
        P(("groups", "dp"), None),
        P(),
        P(),
    )
    out_specs = (
        P(("groups", "dp"), "ctx", None),
        P(("groups", "dp"), "ctx", None),
        P(("groups", "dp"), "ctx", None),
        P(("groups", "dp"), "ctx", None),
        P("groups", None),
        P("groups"),
    )
    return jax.shard_map(local, mesh=mesh, in_specs=in_specs, out_specs=out_specs, check_vma=False)
```

```python
from functools import partial

import jax
import jax.numpy as jnp
from jax import lax
from jax.experimental import pallas as pl
from jax.experimental.pallas import tpu as pltpu
from jax.sharding import PartitionSpec as P

EPSILON = 1e-05
VMEM_LIMIT = 24 * 1024 * 1024
LONG = 4 * 10**9
F32 = jnp.float32
BF16 = jnp.bfloat16


def passed_along(array, axis, by, hop=1):
    size = lax.axis_size(axis)
    first, last = (hop - 1, size - 2) if by > 0 else (1, size - hop)
    return lax.ppermute(array, axis, [(i, i + by) for i in range(first, last + 1)])


def contract(left, right, left_dim, right_dim):
    return lax.dot_general(
        left, right, (((left_dim,), (right_dim,)), ((), ())), preferred_element_type=F32
    )


def user_starts(lengths, query_pos):
    end = jnp.int32(0)
    start = jnp.zeros(query_pos.shape, jnp.int32)
    for user in range(lengths.shape[1]):
        end = end + lengths[0, user]
        start = jnp.where(query_pos >= end, end, start)
    return start


class Pair:
    def __init__(self, mask, table, heads, hops, flipped=False, near=None):
        rows = table.shape[1]
        self.table, self.heads, self.levels = table, heads, table.shape[0] // heads
        self.mask, self.hops, self.near = mask[...], hops, near
        self.far = (hops - 1) * rows + 1 >= 2 ** (self.levels - 2)
        if not self.far:
            query_dim, key_dim = (1, 0) if flipped else (0, 1)
            query_row = lax.broadcasted_iota(jnp.int32, mask.shape, query_dim)
            key_row = lax.broadcasted_iota(jnp.int32, mask.shape, key_dim)
            self.distance = query_row - key_row + hops * rows

    def half_bias(self, head):
        def level_row(level):
            at = level * self.heads + head
            return self.table[at : at + 1, : self.mask.shape[1]]

        value = level_row(self.levels - 1)
        if self.far:
            return value
        if self.near is not None:
            rows = self.mask.shape[0]
            close = self.near[head * rows : (head + 1) * rows, :]
            return close if self.hops == 0 else jnp.where(self.distance < rows, close, value)
        for level in range(self.levels - 2, -1, -1):
            value = jnp.where(self.distance < 2**level, level_row(level), value)
        return value

    def half_logits(self, scores, head, scaling):
        return scores * (0.5 * scaling) + self.half_bias(head)


def slope_of(half, tanh):
    return (0.5 + 0.5 * tanh) * (1.0 + half * (1.0 - tanh))


def columns(head, width):
    return slice(head * width, (head + 1) * width)


def in_stages(count, first, second, ahead=3):
    held = [first(i) for i in range(min(ahead, count))]
    for i in range(count):
        if i + ahead < count:
            held.append(first(i + ahead))
        second(i, held.pop(0))


def attend(pairs, heads, scaling, query, keys, values, total, out):
    width = query.shape[1] // heads

    def scores(head):
        cols = columns(head, width)
        return [contract(query[:, cols], key[:, cols], 1, 1) for key in keys]

    def weigh(head, found):
        cols = columns(head, width)
        part = None if total is None else total[:, cols]
        for pair, score, value in zip(pairs, found, values):
            half = pair.half_logits(score, head, scaling)
            weights = ((half + half * jnp.tanh(half)) * pair.mask).astype(BF16)
            added = contract(weights, value[:, cols], 1, 0)
            part = added if part is None else part + added
        out[:, cols] = part.astype(out.dtype)

    in_stages(heads, scores, weigh)


def far_start(lengths, block, reach, rows):
    first = (lax.axis_index("ctx") + block) * rows
    end, start = jnp.int32(0), jnp.int32(0)
    for user in range(lengths.shape[1]):
        end = end + lengths[0, user]
        start = jnp.where(first >= end, end, start)
    return start - (first - reach * rows)


def first_kernel(plan, cut, heads, scaling, lengths, bias, *refs):
    inputs, refs = refs[:6], refs[6:]
    table, near, masks, refs = refs[0], refs[1], refs[2 : 2 + len(plan)], refs[2 + len(plan) :]
    late, refs = refs[0], refs[1:]
    held, out, arrived = refs[:6], refs[6], refs[7]
    copies = [
        pltpu.make_async_copy(source, target, arrived.at[at])
        for at, (source, target) in enumerate(zip(inputs, held))
    ]
    for copy in copies:
        copy.start()
    levels = bias.shape[0]
    for level in range(levels):
        for head in range(heads):
            at = level * heads + head
            table[at : at + 1, :] = jnp.full((1, table.shape[1]), 0.5 * bias[level, head], F32)
    rows = masks[0].shape[0]
    apart = lax.broadcasted_iota(jnp.int32, (rows, rows), 0)
    apart = (apart - lax.broadcasted_iota(jnp.int32, (rows, rows), 1)) & (rows - 1)
    for head in range(heads):
        value = table[(levels - 1) * heads + head : (levels - 1) * heads + head + 1, :]
        for level in range(levels - 2, -1, -1):
            at = level * heads + head
            value = jnp.where(apart < 2**level, table[at : at + 1, :], value)
        near[head * rows : (head + 1) * rows, :] = value
    for (block, hops, flipped), mask in zip(plan, masks):
        query_dim, key_dim = (1, 0) if flipped else (0, 1)
        line = (1, mask.shape[1]) if flipped else (mask.shape[0], 1)
        first = (lax.axis_index("ctx") + block) * rows
        query_pos = first + lax.broadcasted_iota(jnp.int32, line, query_dim)
        key_first = first - hops * rows + rows - mask.shape[key_dim]
        key_pos = key_first + lax.broadcasted_iota(jnp.int32, mask.shape, key_dim)
        seen = (key_pos >= user_starts(lengths, query_pos)) & (key_pos <= query_pos)
        value = jnp.where(seen, 1.0, 0.0).astype(F32)
        if mask.shape == (rows, rows):
            mask[...] = value
            continue
        at = 0 if mask.shape[0] == rows else 1
        is_late = jnp.where(far_start(lengths, block, hops, rows) > cut, 1.0, 0.0).astype(F32)
        late[8 * at : 8 * at + 8, :] = jnp.full((8, rows), is_late, F32)
        mask[...] = value * (is_late if at else 1.0 - is_late)
    for copy in copies:
        copy.wait()
    query, key, value = held[:3]
    pair = Pair(masks[0], table, heads, 0, near=near)
    attend([pair], heads, scaling, query, [key], [value], None, out)


def forward_kernel(hops, heads, scaling, table, near, mask, query, key, value, total, out):
    pair = Pair(mask, table, heads, hops, near=near)
    attend([pair], heads, scaling, query, [key], [value], total, out)


def normed_rows(attention):
    center = attention - jnp.mean(attention, axis=1, keepdims=True)
    inverse = lax.rsqrt(jnp.mean(center * center, axis=1, keepdims=True) + EPSILON)
    return center * inverse, inverse


def weights_kernel(hops, heads, scaling, table, near, mask, query, key, weights):
    pair = Pair(mask, table, heads, hops, near=near)
    rows, width = query.shape[0], query.shape[1] // heads

    def scores(head):
        cols = columns(head, width)
        return contract(query[:, cols], key[:, cols], 1, 1)

    def weigh(head, found):
        half = pair.half_logits(found, head, scaling)
        lines = columns(head, rows)
        weights[lines, :] = ((half + half * jnp.tanh(half)) * pair.mask).astype(BF16)

    in_stages(heads, scores, weigh)


def norm_kernel(heads, *refs):
    weights, value, total, out_grad, update_gate, gain = refs[:6]
    attention, attn_grad, gain_grad = refs[6:]
    width = total.shape[1] // heads
    for head in range(heads):
        cols, lines = columns(head, width), columns(head, total.shape[0])
        attention[:, cols] = total[:, cols] + contract(weights[lines, :], value[:, cols], 1, 0)
    rows, features = attention.shape
    step = 16
    gain_row = gain[...]
    gain_sum = jnp.zeros((8, features), F32)
    for low in range(0, rows, step):
        span = slice(low, low + step)
        normed, inverse = normed_rows(attention[span, :])
        gated = out_grad[span, :].astype(F32) * update_gate[span, :].astype(F32)
        product = gated * normed
        for part in range(0, step, 8):
            gain_sum = gain_sum + product[part : part + 8, :]
        pushed = gated * gain_row
        attn_grad[span, :] = (
            inverse
            * (
                pushed
                - jnp.mean(pushed, axis=1, keepdims=True)
                - normed * jnp.mean(pushed * normed, axis=1, keepdims=True)
            )
        ).astype(BF16)
    gain_grad[...] = jnp.sum(gain_sum, axis=0, keepdims=True)


def backward_query_kernel(hop_list, heads, scaling, *refs):
    count = len(hop_list)
    table, near, masks, refs = refs[0], refs[1], refs[2 : 2 + count], refs[2 + count :]
    query, grad, keys, values = refs[0], refs[1], refs[2 : 2 + count], refs[2 + count : 2 + 2 * count]
    gain_in, query_out, small_out = refs[2 + 2 * count :]
    rows, width = query.shape[0], query.shape[1] // heads
    pairs = [Pair(mask, table, heads, hops, near=near) for mask, hops in zip(masks, hop_list)]
    lanes = small_out.shape[1]
    lines = gain_in.shape[1] // lanes
    levels = small_out.shape[0] - lines
    lane = lax.broadcasted_iota(jnp.int32, (levels, lanes), 1)
    level_row = lax.broadcasted_iota(jnp.int32, (levels, lanes), 0)
    group = lax.broadcasted_iota(jnp.int32, (8, rows), 0)
    distance = (group - lax.broadcasted_iota(jnp.int32, (8, rows), 1)) & (rows - 1)
    bucket = sum((distance >= 2**level).astype(jnp.int32) for level in range(levels - 1))
    own = pairs[0].distance >= 0
    bias_total = [jnp.zeros((levels, lanes), F32)]

    def bias_sums(grads):
        close = jnp.where(own, grads[0], grads[1])
        rest = sum(grads[2:], jnp.where(own, grads[1], 0.0))
        by_place, far = jnp.zeros((8, rows), F32), jnp.zeros((8, rows), F32)
        for low in range(0, rows, 8):
            part = close[low : low + 8, :]
            by_place = by_place + (pltpu.roll(part, rows - low, 1) if low else part)
            far = far + rest[low : low + 8, :]
        sums = jnp.where(level_row == levels - 1, jnp.sum(far, axis=0, keepdims=True), 0.0)
        for level in range(levels):
            row = jnp.sum(jnp.where(bucket == level, by_place, 0.0), axis=0, keepdims=True)
            sums = sums + jnp.where(level_row == level, row, 0.0)
        return sums

    def scores(head):
        cols = columns(head, width)
        query_h, grad_h = query[:, cols], grad[:, cols]
        return [
            (contract(query_h, key[:, cols], 1, 1), contract(grad_h, value[:, cols], 1, 1))
            for key, value in zip(keys, values)
        ]

    def differentiate(head, found):
        cols = columns(head, width)
        query_part, grads = None, []
        for pair, key, (score, weight_grad) in zip(pairs, keys, found):
            half = pair.half_logits(score, head, scaling)
            grads.append(weight_grad * (slope_of(half, jnp.tanh(half)) * pair.mask))
            added = contract(grads[-1].astype(BF16), key[:, cols], 1, 0)
            query_part = added if query_part is None else query_part + added
        query_out[:, cols] = (query_part * scaling).astype(BF16)
        sums = jnp.sum(bias_sums(grads), axis=1, keepdims=True)
        bias_total[0] = jnp.where(lane == head, sums, bias_total[0])

    in_stages(heads, scores, differentiate, 1)
    for line in range(lines):
        small_out[line : line + 1, :] = gain_in[:, line * lanes : (line + 1) * lanes]
    small_out[lines:, :] = bias_total[0]


def add_key_grads(hops, heads, scaling, table, mask, query, grad, key, value, sums, store):
    width = query.shape[1] // heads
    pair = Pair(mask, table, heads, hops, True)

    def scores(head):
        cols = columns(head, width)
        score = contract(key[:, cols], query[:, cols], 1, 1)
        return score, contract(value[:, cols], grad[:, cols], 1, 1)

    def differentiate(head, found):
        cols = columns(head, width)
        half = pair.half_logits(found[0], head, scaling)
        tanh = jnp.tanh(half)
        rounded = (found[1] * (slope_of(half, tanh) * pair.mask)).astype(BF16)
        weights = ((half + half * tanh) * pair.mask).astype(BF16)
        parts = [contract(rounded, query[:, cols], 1, 0), contract(weights, grad[:, cols], 1, 0)]
        store(head, cols, *[part + held[:, cols] for part, held in zip(parts, sums)] or parts)

    in_stages(heads, scores, differentiate)


def into(key_out, value_out):
    def store(head, cols, key_part, value_part):
        key_out[:, cols] = key_part
        value_out[:, cols] = value_part

    return store


def next_key_kernel(hops, heads, scaling, *refs):
    add_key_grads(hops, heads, scaling, *refs[:6], refs[6:-2], into(*refs[-2:]))


def gate_and_key_kernel(hops, heads, scaling, *refs):
    attention, out_grad, gain, query_grad = refs[8:12]
    gate_out, query_out, key_out, value_out, held, written = refs[12:]
    rows, step = attention.shape[0], 16
    part = rows // 4
    copies = []

    def write(source, target, low):
        lines = slice(low, low + part)
        copies.append(
            pltpu.make_async_copy(source.at[lines], target.at[lines], written.at[len(copies)])
        )
        copies[-1].start()

    for low in range(0, rows, part):
        write(query_grad, query_out, low)
    gain_row = gain[...]
    for low in range(0, rows, step):
        span = slice(low, low + step)
        normed, _ = normed_rows(attention[span, :])
        held[span, :] = (out_grad[span, :].astype(F32) * normed * gain_row).astype(BF16)
        if (low + step) % part == 0:
            write(held, gate_out, low + step - part)
    add_key_grads(hops, heads, scaling, *refs[:6], refs[6:8], into(key_out, value_out))
    for copy in copies:
        copy.wait()


def message_kernel(hops, heads, scaling, *refs):
    table, mask, late, query, grad, key, value, out = refs
    tail, cut, width = mask.shape[0], out.shape[0], query.shape[1] // heads
    pair = Pair(mask, table, heads, hops, True)
    is_late = late[8:9, :width] > 0.5

    def scores(head):
        cols = columns(head, width)
        score = contract(key[cut:, cols], query[:, cols], 1, 1)
        return score, contract(value[cut:, cols], grad[:, cols], 1, 1)

    def choose(head, found):
        cols = columns(head, width)
        half = pair.half_logits(found[0], head, scaling)
        tanh = jnp.tanh(half)
        rounded = (found[1] * (slope_of(half, tanh) * pair.mask)).astype(BF16)
        weights = ((half + half * tanh) * pair.mask).astype(BF16)
        parts = [contract(rounded, query[:, cols], 1, 0), contract(weights, grad[:, cols], 1, 0)]
        for at, part in enumerate(parts):
            lines = slice(at * tail, (at + 1) * tail)
            out[lines, cols] = jnp.where(is_late, part, grad[lines, cols].astype(F32)).astype(BF16)
        out[2 * tail :, cols] = grad[2 * tail : cut, cols]

    in_stages(heads, scores, choose)


def slopes_kernel(hops, heads, scaling, table, mask, query, key, weights, slopes):
    pair = Pair(mask, table, heads, hops, True)
    rows, cut, width = mask.shape[0], mask.shape[1], query.shape[1] // heads

    def scores(head):
        cols = columns(head, width)
        return contract(key[:, cols], query[:cut, cols], 1, 1)

    def derive(head, found):
        half = pair.half_logits(found, head, scaling)
        tanh = jnp.tanh(half)
        lines = columns(head, rows)
        weights[lines, :] = ((half + half * tanh) * pair.mask).astype(BF16)
        slopes[lines, :] = slope_of(half, tanh) * pair.mask

    in_stages(heads, scores, derive)


def last_kernel(heads, scaling, *refs):
    weights, slopes, late, query, message, value, key_in, value_in = refs[:8]
    outs, held, written = refs[8:10], refs[10:12], refs[12]
    rows, cut, width = query.shape[0], message.shape[0], query.shape[1] // heads
    tail = rows - cut
    is_late = late[0:1, :width]
    copies = []

    def write(at, cols):
        source, target = held[at].at[:, cols], outs[at].at[:, cols]
        copies.append(pltpu.make_async_copy(source, target, written.at[len(copies)]))
        copies[-1].start()

    def scores(head):
        cols = columns(head, width)
        return contract(value[:, cols], message[:, cols], 1, 1)

    def differentiate(head, found):
        cols, lines = columns(head, width), columns(head, rows)
        rounded = (found * slopes[lines, :]).astype(BF16)
        parts = [
            contract(rounded, query[:cut, cols], 1, 0),
            contract(weights[lines, :], message[:, cols], 1, 0),
        ]
        for at, (part, before) in enumerate(zip(parts, (key_in, value_in))):
            factor = 1.0 if at else scaling
            held[at][:cut, cols] = ((before[:cut, cols] + part[:cut]) * factor).astype(BF16)
            sent = message[at * tail : (at + 1) * tail, cols].astype(F32) * is_late
            held[at][cut:, cols] = ((before[cut:, cols] + part[cut:] + sent) * factor).astype(BF16)
        for at in (0, 1):
            write(at, cols)

    in_stages(heads, scores, differentiate)
    for copy in copies:
        copy.wait()


def pair_kernel(left, right, out):
    out[...] = left[...] + right[...]


def sum_kernel(*refs):
    gain_out, bias_out = refs[-2:]
    total = added_up([piece[...] for piece in refs[:-2]])
    lines = gain_out.shape[0]
    gain_out[...] = total[:lines]
    bias_out[...] = total[lines:, : bias_out.shape[1]]


def on_device(kernel, outs, args, smem=(), ahead=(), far=(), far_outs=0, scratch=(), flops=1000000):
    count = len(smem) + len(far) + len(args)
    far = [pltpu.with_memory_space_constraint(array, pltpu.HBM) for array in far]

    def body(*refs):
        kernel(*refs[:count], *refs[count + len(ahead) :])

    vmem, anywhere = pl.BlockSpec(memory_space=pltpu.VMEM), pl.BlockSpec(memory_space=pl.ANY)
    return pl.pallas_call(
        body,
        out_shape=outs,
        in_specs=[pl.BlockSpec(memory_space=pltpu.SMEM)] * len(smem)
        + [pl.BlockSpec(memory_space=pltpu.HBM)] * len(far)
        + [vmem] * len(args)
        + [anywhere] * len(ahead),
        out_specs=[anywhere] * far_outs + [vmem] * (len(outs) - far_outs),
        scratch_shapes=scratch,
        compiler_params=pltpu.CompilerParams(vmem_limit_bytes=VMEM_LIMIT),
        cost_estimate=pl.CostEstimate(flops=flops, bytes_accessed=100000, transcendentals=0),
    )(*smem, *far, *args, *ahead)


def rounds_of(axes, first=1):
    rounds = []
    for axis in axes:
        size = lax.axis_size(axis)
        step = first
        while step < size:
            radix = 4 if size // step >= 4 else 2
            rounds.append((axis, [step * at for at in range(1, radix)]))
            step = radix * step
    return rounds


def exchanged(array, axis, distances):
    size = lax.axis_size(axis)
    found = [
        lax.ppermute(array, axis, [(i, i ^ distance) for i in range(size)])
        for distance in reversed(distances)
    ]
    return [array] + found[::-1]


def added_up(pieces):
    while len(pieces) > 1:
        pieces = [left + right for left, right in zip(pieces[::2], pieces[1::2])]
    return pieces[0]


def local(queries, key_rows, value_rows, update_gate, out_grad, user_lengths, rel_bias, norm_gain):
    rows, features = queries.shape[1:]
    levels, heads = rel_bias.shape
    scaling = (features // heads) ** (-0.5)
    reach = min(3, lax.axis_size("ctx") // 2)
    wide = jax.ShapeDtypeStruct((rows, features), F32)
    narrow = jax.ShapeDtypeStruct((rows, features), BF16)
    inputs = (queries[0], key_rows[0], value_rows[0], update_gate[0], out_grad[0], norm_gain[None])

    arrived = [passed_along(inputs[at], "ctx", by) for at, by in ((1, 1), (2, 1), (0, -1))]

    hop_list = tuple(range(reach + 1))
    plan = [(0, hops, False) for hops in hop_list] + [(hops, hops, True) for hops in hop_list]
    plan += [(reach - 1, reach, True)]
    cut = rows - rows // 4
    shapes = [(rows, rows)] * (len(plan) - 2) + [(rows, cut), (rows - cut, rows), (16, rows)]
    outs = [jax.ShapeDtypeStruct((count * heads, rows), F32) for count in (levels, rows)]
    outs += [jax.ShapeDtypeStruct(shape, F32) for shape in shapes]
    outs += [jax.ShapeDtypeStruct(array.shape, array.dtype) for array in inputs] + [wide]
    table, near, *found = on_device(
        partial(first_kernel, plan, cut, heads, scaling),
        outs,
        (),
        (user_lengths, rel_bias),
        far=inputs,
        scratch=[pltpu.SemaphoreType.DMA((len(inputs),))],
    )
    masks, flipped = found[: reach + 1], found[reach + 1 : 2 * reach + 2]
    sender_mask, late, query, key, value, gate, grad, gain, attention = found[2 * reach + 2 :]

    later_queries = [query, arrived[2]]
    keys, values = [key, arrived[0]], [value, arrived[1]]
    for hops in range(1, reach):
        keys.append(passed_along(keys[-1], "ctx", 1, hops + 1))
        values.append(passed_along(values[-1], "ctx", 1, hops + 1))
        later_queries.append(passed_along(later_queries[-1], "ctx", -1, hops + 1))
    for hops in range(1, reach):
        (attention,) = on_device(
            partial(forward_kernel, hops, heads, scaling),
            [wide],
            (table, near, masks[hops], query, keys[hops], values[hops], attention),
            ahead=later_queries[hops : hops + 1],
        )
    stacked = (heads * rows, rows)
    (far_weights,) = on_device(
        partial(weights_kernel, reach, heads, scaling),
        [jax.ShapeDtypeStruct(stacked, BF16)],
        (table, near, masks[-1], query, keys[-1]),
        ahead=[attention],
    )
    attention, attn_grad, gain_part = on_device(
        partial(norm_kernel, heads),
        [wide, narrow, jax.ShapeDtypeStruct((1, features), F32)],
        (far_weights, values[-1], attention, grad, gate, gain),
    )

    lanes = features // 8
    query_grad, sums = on_device(
        partial(backward_query_kernel, hop_list, heads, scaling),
        [narrow, jax.ShapeDtypeStruct((8 + levels, lanes), F32)],
        (table, near, *masks, query, attn_grad, *keys, *values, gain_part),
        ahead=later_queries[reach:],
    )
    later_grads = [attn_grad, passed_along(attn_grad, "ctx", -1)]
    pieces = [sums]
    for axis, distances in rounds_of(("dp",)):
        pieces = exchanged(added_up(pieces), axis, distances)

    def key_operands(hops):
        later = (later_queries[hops], later_grads[hops])
        return (table, flipped[hops], *later, key, value)

    key_grads = on_device(
        partial(next_key_kernel, 0, heads, scaling),
        [wide] * 2,
        key_operands(0),
    )
    far_tables = on_device(
        partial(slopes_kernel, reach, heads, scaling),
        [jax.ShapeDtypeStruct((heads * rows, cut), kind) for kind in (BF16, F32)],
        (table, flipped[reach], later_queries[reach], key),
    )
    key_grads, far_tables, *pieces = lax.optimization_barrier((key_grads, far_tables, *pieces))
    sums = added_up(pieces)
    [(axis, distances), *rest] = [("ctx", [1]), *rounds_of(("ctx",), 2)]
    (paired,) = on_device(
        pair_kernel,
        [jax.ShapeDtypeStruct(sums.shape, F32)],
        exchanged(sums, axis, distances),
        flops=LONG,
    )
    for hops in range(1, reach):
        arrived, sums = lax.optimization_barrier((later_grads[hops], sums))
        if hops + 1 == reach:
            (arrived,) = on_device(
                partial(message_kernel, reach, heads, scaling),
                [jax.ShapeDtypeStruct((cut, features), BF16)],
                (table, sender_mask, late, later_queries[hops], arrived, keys[1], values[1]),
                ahead=[key_grads[0], far_tables[0]],
            )
        later_grads.append(passed_along(arrived, "ctx", -1, hops + 1))
        if hops == 1:
            gate_grad, query_grad, *key_grads = on_device(
                partial(gate_and_key_kernel, hops, heads, scaling),
                [narrow, narrow, wide, wide],
                (*key_operands(hops), *key_grads, attention, grad, gain, query_grad),
                far_outs=2,
                scratch=[pltpu.VMEM((rows, features), BF16), pltpu.SemaphoreType.DMA((8,))],
            )
        else:
            key_grads = on_device(
                partial(next_key_kernel, hops, heads, scaling),
                [wide] * 2,
                (*key_operands(hops), *key_grads),
            )
    pieces = [paired]
    for axis, distances in rest:
        pieces = exchanged(added_up(pieces), axis, distances)
    key_grad, value_grad = on_device(
        partial(last_kernel, heads, scaling),
        [narrow, narrow],
        (*far_tables, late, later_queries[reach], later_grads[reach], value, *key_grads),
        far_outs=2,
        scratch=[pltpu.VMEM((rows, features), BF16)] * 2 + [pltpu.SemaphoreType.DMA((2 * heads,))],
    )
    key_grad, value_grad, pieces[0] = lax.optimization_barrier((key_grad, value_grad, pieces[0]))
    gain_grad, bias_grad = on_device(
        sum_kernel,
        [jax.ShapeDtypeStruct((8, lanes), F32), jax.ShapeDtypeStruct((levels, heads), F32)],
        pieces,
    )
    return (
        query_grad[None],
        key_grad[None],
        value_grad[None],
        gate_grad[None],
        bias_grad,
        gain_grad.reshape(features),
    )


def solution(mesh):
    in_specs = (
        P(("groups", "dp"), "ctx", None),
        P(("groups", "dp"), "ctx", None),
        P(("groups", "dp"), "ctx", None),
        P(("groups", "dp"), "ctx", None),
        P(("groups", "dp"), "ctx", None),
        P(("groups", "dp"), None),
        P(),
        P(),
    )
    out_specs = (
        P(("groups", "dp"), "ctx", None),
        P(("groups", "dp"), "ctx", None),
        P(("groups", "dp"), "ctx", None),
        P(("groups", "dp"), "ctx", None),
        P("groups", None),
        P("groups"),
    )
    return jax.shard_map(local, mesh=mesh, in_specs=in_specs, out_specs=out_specs, check_vma=False)
```

```python
from functools import partial

import jax
import jax.numpy as jnp
from jax import lax
from jax.experimental import pallas as pl
from jax.experimental.pallas import tpu as pltpu
from jax.sharding import PartitionSpec as P

EPSILON = 1e-05
VMEM_LIMIT = 24 * 1024 * 1024
LONG = 4 * 10**9
F32 = jnp.float32
BF16 = jnp.bfloat16


def passed_along(array, axis, by, hop=1):
    size = lax.axis_size(axis)
    first, last = (hop - 1, size - 2) if by > 0 else (1, size - hop)
    return lax.ppermute(array, axis, [(i, i + by) for i in range(first, last + 1)])


def contract(left, right, left_dim, right_dim):
    return lax.dot_general(
        left, right, (((left_dim,), (right_dim,)), ((), ())), preferred_element_type=F32
    )


def user_starts(lengths, query_pos):
    end = jnp.int32(0)
    start = jnp.zeros(query_pos.shape, jnp.int32)
    for user in range(lengths.shape[1]):
        end = end + lengths[0, user]
        start = jnp.where(query_pos >= end, end, start)
    return start


class Pair:
    def __init__(self, mask, table, heads, hops, flipped=False, near=None):
        rows = table.shape[1]
        self.table, self.heads, self.levels = table, heads, table.shape[0] // heads
        self.mask, self.hops, self.near = mask[...], hops, near
        self.far = (hops - 1) * rows + 1 >= 2 ** (self.levels - 2)
        if not self.far:
            query_dim, key_dim = (1, 0) if flipped else (0, 1)
            query_row = lax.broadcasted_iota(jnp.int32, mask.shape, query_dim)
            key_row = lax.broadcasted_iota(jnp.int32, mask.shape, key_dim)
            self.distance = query_row - key_row + hops * rows

    def half_bias(self, head):
        def level_row(level):
            at = level * self.heads + head
            return self.table[at : at + 1, : self.mask.shape[1]]

        value = level_row(self.levels - 1)
        if self.far:
            return value
        if self.near is not None:
            rows = self.mask.shape[0]
            close = self.near[head * rows : (head + 1) * rows, :]
            return close if self.hops == 0 else jnp.where(self.distance < rows, close, value)
        for level in range(self.levels - 2, -1, -1):
            value = jnp.where(self.distance < 2**level, level_row(level), value)
        return value

    def half_logits(self, scores, head, scaling):
        return scores * (0.5 * scaling) + self.half_bias(head)


def slope_of(half, tanh):
    return (0.5 + 0.5 * tanh) * (1.0 + half * (1.0 - tanh))


def columns(head, width):
    return slice(head * width, (head + 1) * width)


def in_stages(count, first, second, ahead=3):
    held = [first(i) for i in range(min(ahead, count))]
    for i in range(count):
        if i + ahead < count:
            held.append(first(i + ahead))
        second(i, held.pop(0))


def attend(pairs, heads, scaling, query, keys, values, total, out):
    width = query.shape[1] // heads

    def scores(head):
        cols = columns(head, width)
        return [contract(query[:, cols], key[:, cols], 1, 1) for key in keys]

    def weigh(head, found):
        cols = columns(head, width)
        part = None if total is None else total[:, cols]
        for pair, score, value in zip(pairs, found, values):
            half = pair.half_logits(score, head, scaling)
            weights = ((half + half * jnp.tanh(half)) * pair.mask).astype(BF16)
            added = contract(weights, value[:, cols], 1, 0)
            part = added if part is None else part + added
        out[:, cols] = part.astype(out.dtype)

    in_stages(heads, scores, weigh)


def far_start(lengths, block, reach, rows):
    first = (lax.axis_index("ctx") + block) * rows
    end, start = jnp.int32(0), jnp.int32(0)
    for user in range(lengths.shape[1]):
        end = end + lengths[0, user]
        start = jnp.where(first >= end, end, start)
    return start - (first - reach * rows)


def first_kernel(plan, cut, heads, scaling, lengths, bias, *refs):
    inputs, refs = refs[:6], refs[6:]
    table, near, masks, refs = refs[0], refs[1], refs[2 : 2 + len(plan)], refs[2 + len(plan) :]
    late, refs = refs[0], refs[1:]
    held, out, arrived = refs[:6], refs[6], refs[7]
    copies = [
        pltpu.make_async_copy(source, target, arrived.at[at])
        for at, (source, target) in enumerate(zip(inputs, held))
    ]
    for copy in copies:
        copy.start()
    levels = bias.shape[0]
    for level in range(levels):
        for head in range(heads):
            at = level * heads + head
            table[at : at + 1, :] = jnp.full((1, table.shape[1]), 0.5 * bias[level, head], F32)
    rows = masks[0].shape[0]
    apart = lax.broadcasted_iota(jnp.int32, (rows, rows), 0)
    apart = (apart - lax.broadcasted_iota(jnp.int32, (rows, rows), 1)) & (rows - 1)
    for head in range(heads):
        value = table[(levels - 1) * heads + head : (levels - 1) * heads + head + 1, :]
        for level in range(levels - 2, -1, -1):
            at = level * heads + head
            value = jnp.where(apart < 2**level, table[at : at + 1, :], value)
        near[head * rows : (head + 1) * rows, :] = value
    for (block, hops, flipped), mask in zip(plan, masks):
        query_dim, key_dim = (1, 0) if flipped else (0, 1)
        line = (1, mask.shape[1]) if flipped else (mask.shape[0], 1)
        first = (lax.axis_index("ctx") + block) * rows
        query_pos = first + lax.broadcasted_iota(jnp.int32, line, query_dim)
        key_first = first - hops * rows + rows - mask.shape[key_dim]
        key_pos = key_first + lax.broadcasted_iota(jnp.int32, mask.shape, key_dim)
        seen = (key_pos >= user_starts(lengths, query_pos)) & (key_pos <= query_pos)
        value = jnp.where(seen, 1.0, 0.0).astype(F32)
        if mask.shape == (rows, rows):
            mask[...] = value
            continue
        at = 0 if mask.shape[0] == rows else 1
        is_late = jnp.where(far_start(lengths, block, hops, rows) > cut, 1.0, 0.0).astype(F32)
        late[8 * at : 8 * at + 8, :] = jnp.full((8, rows), is_late, F32)
        mask[...] = value * (is_late if at else 1.0 - is_late)
    for copy in copies:
        copy.wait()
    query, key, value = held[:3]
    pair = Pair(masks[0], table, heads, 0, near=near)
    attend([pair], heads, scaling, query, [key], [value], None, out)


def forward_kernel(hops, heads, scaling, table, near, mask, query, key, value, total, out):
    pair = Pair(mask, table, heads, hops, near=near)
    attend([pair], heads, scaling, query, [key], [value], total, out)


def normed_rows(attention):
    center = attention - jnp.mean(attention, axis=1, keepdims=True)
    inverse = lax.rsqrt(jnp.mean(center * center, axis=1, keepdims=True) + EPSILON)
    return center * inverse, inverse


def weights_kernel(hops, heads, scaling, table, near, mask, query, key, weights):
    pair = Pair(mask, table, heads, hops, near=near)
    rows, width = query.shape[0], query.shape[1] // heads

    def scores(head):
        cols = columns(head, width)
        return contract(query[:, cols], key[:, cols], 1, 1)

    def weigh(head, found):
        half = pair.half_logits(found, head, scaling)
        lines = columns(head, rows)
        weights[lines, :] = ((half + half * jnp.tanh(half)) * pair.mask).astype(BF16)

    in_stages(heads, scores, weigh)


def norm_kernel(heads, *refs):
    weights, value, total, out_grad, update_gate, gain = refs[:6]
    attention, attn_grad, gain_grad = refs[6:]
    width = total.shape[1] // heads
    for head in range(heads):
        cols, lines = columns(head, width), columns(head, total.shape[0])
        attention[:, cols] = total[:, cols] + contract(weights[lines, :], value[:, cols], 1, 0)
    rows, features = attention.shape
    step = 16
    gain_row = gain[...]
    gain_sum = jnp.zeros((8, features), F32)
    for low in range(0, rows, step):
        span = slice(low, low + step)
        normed, inverse = normed_rows(attention[span, :])
        gated = out_grad[span, :].astype(F32) * update_gate[span, :].astype(F32)
        product = gated * normed
        for part in range(0, step, 8):
            gain_sum = gain_sum + product[part : part + 8, :]
        pushed = gated * gain_row
        attn_grad[span, :] = (
            inverse
            * (
                pushed
                - jnp.mean(pushed, axis=1, keepdims=True)
                - normed * jnp.mean(pushed * normed, axis=1, keepdims=True)
            )
        ).astype(BF16)
    gain_grad[...] = jnp.sum(gain_sum, axis=0, keepdims=True)


def backward_query_kernel(hop_list, heads, scaling, *refs):
    count = len(hop_list)
    table, near, masks, refs = refs[0], refs[1], refs[2 : 2 + count], refs[2 + count :]
    query, grad, keys, values = refs[0], refs[1], refs[2 : 2 + count], refs[2 + count : 2 + 2 * count]
    gain_in, query_out, small_out = refs[2 + 2 * count :]
    rows, width = query.shape[0], query.shape[1] // heads
    pairs = [Pair(mask, table, heads, hops, near=near) for mask, hops in zip(masks, hop_list)]
    lanes = small_out.shape[1]
    lines = gain_in.shape[1] // lanes
    levels = small_out.shape[0] - lines
    lane = lax.broadcasted_iota(jnp.int32, (levels, lanes), 1)
    level_row = lax.broadcasted_iota(jnp.int32, (levels, lanes), 0)
    group = lax.broadcasted_iota(jnp.int32, (8, rows), 0)
    distance = (group - lax.broadcasted_iota(jnp.int32, (8, rows), 1)) & (rows - 1)
    bucket = sum((distance >= 2**level).astype(jnp.int32) for level in range(levels - 1))
    own = pairs[0].distance >= 0
    bias_total = [jnp.zeros((levels, lanes), F32)]

    def bias_sums(grads):
        close = jnp.where(own, grads[0], grads[1])
        rest = sum(grads[2:], jnp.where(own, grads[1], 0.0))
        by_place, far = jnp.zeros((8, rows), F32), jnp.zeros((8, rows), F32)
        for low in range(0, rows, 8):
            part = close[low : low + 8, :]
            by_place = by_place + (pltpu.roll(part, rows - low, 1) if low else part)
            far = far + rest[low : low + 8, :]
        sums = jnp.where(level_row == levels - 1, jnp.sum(far, axis=0, keepdims=True), 0.0)
        for level in range(levels):
            row = jnp.sum(jnp.where(bucket == level, by_place, 0.0), axis=0, keepdims=True)
            sums = sums + jnp.where(level_row == level, row, 0.0)
        return sums

    def scores(head):
        cols = columns(head, width)
        query_h, grad_h = query[:, cols], grad[:, cols]
        return [
            (contract(query_h, key[:, cols], 1, 1), contract(grad_h, value[:, cols], 1, 1))
            for key, value in zip(keys, values)
        ]

    def differentiate(head, found):
        cols = columns(head, width)
        query_part, grads = None, []
        for pair, key, (score, weight_grad) in zip(pairs, keys, found):
            half = pair.half_logits(score, head, scaling)
            grads.append(weight_grad * (slope_of(half, jnp.tanh(half)) * pair.mask))
            added = contract(grads[-1].astype(BF16), key[:, cols], 1, 0)
            query_part = added if query_part is None else query_part + added
        query_out[:, cols] = (query_part * scaling).astype(BF16)
        sums = jnp.sum(bias_sums(grads), axis=1, keepdims=True)
        bias_total[0] = jnp.where(lane == head, sums, bias_total[0])

    in_stages(heads, scores, differentiate, 1)
    for line in range(lines):
        small_out[line : line + 1, :] = gain_in[:, line * lanes : (line + 1) * lanes]
    small_out[lines:, :] = bias_total[0]


def add_key_grads(hops, heads, scaling, table, mask, query, grad, key, value, sums, store):
    width = query.shape[1] // heads
    pair = Pair(mask, table, heads, hops, True)

    def scores(head):
        cols = columns(head, width)
        score = contract(key[:, cols], query[:, cols], 1, 1)
        return score, contract(value[:, cols], grad[:, cols], 1, 1)

    def differentiate(head, found):
        cols = columns(head, width)
        half = pair.half_logits(found[0], head, scaling)
        tanh = jnp.tanh(half)
        rounded = (found[1] * (slope_of(half, tanh) * pair.mask)).astype(BF16)
        weights = ((half + half * tanh) * pair.mask).astype(BF16)
        parts = [contract(rounded, query[:, cols], 1, 0), contract(weights, grad[:, cols], 1, 0)]
        store(head, cols, *[part + held[:, cols] for part, held in zip(parts, sums)] or parts)

    in_stages(heads, scores, differentiate)


def into(key_out, value_out):
    def store(head, cols, key_part, value_part):
        key_out[:, cols] = key_part
        value_out[:, cols] = value_part

    return store


def next_key_kernel(hops, heads, scaling, *refs):
    add_key_grads(hops, heads, scaling, *refs[:6], refs[6:-2], into(*refs[-2:]))


def gate_and_key_kernel(hops, heads, scaling, *refs):
    attention, out_grad, gain, query_grad = refs[8:12]
    gate_out, query_out, key_out, value_out, held, written = refs[12:]
    rows, step = attention.shape[0], 16
    part = rows // 4
    copies = []

    def write(source, target, low):
        lines = slice(low, low + part)
        copies.append(
            pltpu.make_async_copy(source.at[lines], target.at[lines], written.at[len(copies)])
        )
        copies[-1].start()

    for low in range(0, rows, part):
        write(query_grad, query_out, low)
    gain_row = gain[...]
    for low in range(0, rows, step):
        span = slice(low, low + step)
        normed, _ = normed_rows(attention[span, :])
        held[span, :] = (out_grad[span, :].astype(F32) * normed * gain_row).astype(BF16)
        if (low + step) % part == 0:
            write(held, gate_out, low + step - part)
    add_key_grads(hops, heads, scaling, *refs[:6], refs[6:8], into(key_out, value_out))
    for copy in copies:
        copy.wait()


def message_kernel(hops, heads, scaling, *refs):
    table, mask, late, query, grad, key, value, out = refs
    tail, cut, width = mask.shape[0], out.shape[0], query.shape[1] // heads
    pair = Pair(mask, table, heads, hops, True)
    is_late = late[8:9, :width] > 0.5

    def scores(head):
        cols = columns(head, width)
        score = contract(key[cut:, cols], query[:, cols], 1, 1)
        return score, contract(value[cut:, cols], grad[:, cols], 1, 1)

    def choose(head, found):
        cols = columns(head, width)
        half = pair.half_logits(found[0], head, scaling)
        tanh = jnp.tanh(half)
        rounded = (found[1] * (slope_of(half, tanh) * pair.mask)).astype(BF16)
        weights = ((half + half * tanh) * pair.mask).astype(BF16)
        parts = [contract(rounded, query[:, cols], 1, 0), contract(weights, grad[:, cols], 1, 0)]
        for at, part in enumerate(parts):
            lines = slice(at * tail, (at + 1) * tail)
            out[lines, cols] = jnp.where(is_late, part, grad[lines, cols].astype(F32)).astype(BF16)
        out[2 * tail :, cols] = grad[2 * tail : cut, cols]

    in_stages(heads, scores, choose)


def slopes_kernel(hops, heads, scaling, table, mask, query, key, weights, slopes):
    pair = Pair(mask, table, heads, hops, True)
    rows, cut, width = mask.shape[0], mask.shape[1], query.shape[1] // heads

    def scores(head):
        cols = columns(head, width)
        return contract(key[:, cols], query[:cut, cols], 1, 1)

    def derive(head, found):
        half = pair.half_logits(found, head, scaling)
        tanh = jnp.tanh(half)
        lines = columns(head, rows)
        weights[lines, :] = ((half + half * tanh) * pair.mask).astype(BF16)
        slopes[lines, :] = slope_of(half, tanh) * pair.mask

    in_stages(heads, scores, derive)


def last_kernel(heads, scaling, *refs):
    weights, slopes, late, query, message, value, key_in, value_in = refs[:8]
    outs, held, written = refs[8:10], refs[10:12], refs[12]
    rows, cut, width = query.shape[0], message.shape[0], query.shape[1] // heads
    tail = rows - cut
    is_late = late[0:1, :width]
    copies = []

    def write(at, cols):
        source, target = held[at].at[:, cols], outs[at].at[:, cols]
        copies.append(pltpu.make_async_copy(source, target, written.at[len(copies)]))
        copies[-1].start()

    def scores(head):
        cols = columns(head, width)
        return contract(value[:, cols], message[:, cols], 1, 1)

    def differentiate(head, found):
        cols, lines = columns(head, width), columns(head, rows)
        rounded = (found * slopes[lines, :]).astype(BF16)
        parts = [
            contract(rounded, query[:cut, cols], 1, 0),
            contract(weights[lines, :], message[:, cols], 1, 0),
        ]
        for at, (part, before) in enumerate(zip(parts, (key_in, value_in))):
            factor = 1.0 if at else scaling
            held[at][:cut, cols] = ((before[:cut, cols] + part[:cut]) * factor).astype(BF16)
            sent = message[at * tail : (at + 1) * tail, cols].astype(F32) * is_late
            held[at][cut:, cols] = ((before[cut:, cols] + part[cut:] + sent) * factor).astype(BF16)
        for at in (0, 1):
            write(at, cols)

    in_stages(heads, scores, differentiate)
    for copy in copies:
        copy.wait()


def pair_kernel(left, right, out):
    out[...] = left[...] + right[...]


def sum_kernel(*refs):
    gain_out, bias_out = refs[-2:]
    total = added_up([piece[...] for piece in refs[:-2]])
    lines = gain_out.shape[0]
    gain_out[...] = total[:lines]
    bias_out[...] = total[lines:, : bias_out.shape[1]]


def on_device(kernel, outs, args, smem=(), ahead=(), far=(), far_outs=0, scratch=(), flops=1000000):
    count = len(smem) + len(far) + len(args)
    far = [pltpu.with_memory_space_constraint(array, pltpu.HBM) for array in far]

    def body(*refs):
        kernel(*refs[:count], *refs[count + len(ahead) :])

    vmem, anywhere = pl.BlockSpec(memory_space=pltpu.VMEM), pl.BlockSpec(memory_space=pl.ANY)
    return pl.pallas_call(
        body,
        out_shape=outs,
        in_specs=[pl.BlockSpec(memory_space=pltpu.SMEM)] * len(smem)
        + [pl.BlockSpec(memory_space=pltpu.HBM)] * len(far)
        + [vmem] * len(args)
        + [anywhere] * len(ahead),
        out_specs=[anywhere] * far_outs + [vmem] * (len(outs) - far_outs),
        scratch_shapes=scratch,
        compiler_params=pltpu.CompilerParams(vmem_limit_bytes=VMEM_LIMIT),
        cost_estimate=pl.CostEstimate(flops=flops, bytes_accessed=100000, transcendentals=0),
    )(*smem, *far, *args, *ahead)


def rounds_of(axes, first=1):
    rounds = []
    for axis in axes:
        size = lax.axis_size(axis)
        step = first
        while step < size:
            radix = 4 if size // step >= 4 else 2
            rounds.append((axis, [step * at for at in range(1, radix)]))
            step = radix * step
    return rounds


def exchanged(array, axis, distances):
    size = lax.axis_size(axis)
    found = [
        lax.ppermute(array, axis, [(i, i ^ distance) for i in range(size)])
        for distance in reversed(distances)
    ]
    return [array] + found[::-1]


def added_up(pieces):
    while len(pieces) > 1:
        pieces = [left + right for left, right in zip(pieces[::2], pieces[1::2])]
    return pieces[0]


def local(queries, key_rows, value_rows, update_gate, out_grad, user_lengths, rel_bias, norm_gain):
    rows, features = queries.shape[1:]
    levels, heads = rel_bias.shape
    scaling = (features // heads) ** (-0.5)
    reach = min(3, lax.axis_size("ctx") // 2)
    wide = jax.ShapeDtypeStruct((rows, features), F32)
    narrow = jax.ShapeDtypeStruct((rows, features), BF16)
    inputs = (queries[0], key_rows[0], value_rows[0], update_gate[0], out_grad[0], norm_gain[None])

    arrived = [passed_along(inputs[at], "ctx", by) for at, by in ((1, 1), (2, 1), (0, -1))]

    hop_list = tuple(range(reach + 1))
    plan = [(0, hops, False) for hops in hop_list] + [(hops, hops, True) for hops in hop_list]
    plan += [(reach - 1, reach, True)]
    cut = rows - rows // 4
    shapes = [(rows, rows)] * (len(plan) - 2) + [(rows, cut), (rows - cut, rows), (16, rows)]
    outs = [jax.ShapeDtypeStruct((count * heads, rows), F32) for count in (levels, rows)]
    outs += [jax.ShapeDtypeStruct(shape, F32) for shape in shapes]
    outs += [jax.ShapeDtypeStruct(array.shape, array.dtype) for array in inputs] + [wide]
    table, near, *found = on_device(
        partial(first_kernel, plan, cut, heads, scaling),
        outs,
        (),
        (user_lengths, rel_bias),
        far=inputs,
        scratch=[pltpu.SemaphoreType.DMA((len(inputs),))],
    )
    masks, flipped = found[: reach + 1], found[reach + 1 : 2 * reach + 2]
    sender_mask, late, query, key, value, gate, grad, gain, attention = found[2 * reach + 2 :]

    later_queries = [query, arrived[2]]
    keys, values = [key, arrived[0]], [value, arrived[1]]
    for hops in range(1, reach):
        keys.append(passed_along(keys[-1], "ctx", 1, hops + 1))
        values.append(passed_along(values[-1], "ctx", 1, hops + 1))
        later_queries.append(passed_along(later_queries[-1], "ctx", -1, hops + 1))
    for hops in range(1, reach):
        (attention,) = on_device(
            partial(forward_kernel, hops, heads, scaling),
            [wide],
            (table, near, masks[hops], query, keys[hops], values[hops], attention),
            ahead=later_queries[hops : hops + 1],
        )
    stacked = (heads * rows, rows)
    (far_weights,) = on_device(
        partial(weights_kernel, reach, heads, scaling),
        [jax.ShapeDtypeStruct(stacked, BF16)],
        (table, near, masks[-1], query, keys[-1]),
        ahead=[attention],
    )
    attention, attn_grad, gain_part = on_device(
        partial(norm_kernel, heads),
        [wide, narrow, jax.ShapeDtypeStruct((1, features), F32)],
        (far_weights, values[-1], attention, grad, gate, gain),
    )

    lanes = features // 8
    query_grad, sums = on_device(
        partial(backward_query_kernel, hop_list, heads, scaling),
        [narrow, jax.ShapeDtypeStruct((8 + levels, lanes), F32)],
        (table, near, *masks, query, attn_grad, *keys, *values, gain_part),
        ahead=later_queries[reach:],
    )
    later_grads = [attn_grad, passed_along(attn_grad, "ctx", -1)]
    pieces = [sums]
    for axis, distances in rounds_of(("dp",)):
        pieces = exchanged(added_up(pieces), axis, distances)

    def key_operands(hops):
        later = (later_queries[hops], later_grads[hops])
        return (table, flipped[hops], *later, key, value)

    key_grads = on_device(
        partial(next_key_kernel, 0, heads, scaling),
        [wide] * 2,
        key_operands(0),
    )
    far_tables = on_device(
        partial(slopes_kernel, reach, heads, scaling),
        [jax.ShapeDtypeStruct((heads * rows, cut), kind) for kind in (BF16, F32)],
        (table, flipped[reach], later_queries[reach], key),
    )
    key_grads, far_tables, *pieces = lax.optimization_barrier((key_grads, far_tables, *pieces[::-1]))
    sums = added_up(pieces[::-1])
    [(axis, distances), *rest] = [("ctx", [1]), *rounds_of(("ctx",), 2)]
    (paired,) = on_device(
        pair_kernel,
        [jax.ShapeDtypeStruct(sums.shape, F32)],
        exchanged(sums, axis, distances),
        flops=LONG,
    )
    for hops in range(1, reach):
        arrived, sums = lax.optimization_barrier((later_grads[hops], sums))
        if hops + 1 == reach:
            (arrived,) = on_device(
                partial(message_kernel, reach, heads, scaling),
                [jax.ShapeDtypeStruct((cut, features), BF16)],
                (table, sender_mask, late, later_queries[hops], arrived, keys[1], values[1]),
                ahead=[key_grads[0], far_tables[0]],
            )
        later_grads.append(passed_along(arrived, "ctx", -1, hops + 1))
        if hops == 1:
            gate_grad, query_grad, *key_grads = on_device(
                partial(gate_and_key_kernel, hops, heads, scaling),
                [narrow, narrow, wide, wide],
                (*key_operands(hops), *key_grads, attention, grad, gain, query_grad),
                far_outs=2,
                scratch=[pltpu.VMEM((rows, features), BF16), pltpu.SemaphoreType.DMA((8,))],
            )
        else:
            key_grads = on_device(
                partial(next_key_kernel, hops, heads, scaling),
                [wide] * 2,
                (*key_operands(hops), *key_grads),
            )
    pieces = [paired]
    for axis, distances in rest:
        pieces = exchanged(added_up(pieces), axis, distances)
    key_grads, pieces[0] = lax.optimization_barrier((key_grads, pieces[0]))
    gain_grad, bias_grad = on_device(
        sum_kernel,
        [jax.ShapeDtypeStruct((8, lanes), F32), jax.ShapeDtypeStruct((levels, heads), F32)],
        pieces,
    )
    later_grads[reach], gain_grad, bias_grad = lax.optimization_barrier(
        (later_grads[reach], gain_grad, bias_grad)
    )
    key_grad, value_grad = on_device(
        partial(last_kernel, heads, scaling),
        [narrow, narrow],
        (*far_tables, late, later_queries[reach], later_grads[reach], value, *key_grads),
        far_outs=2,
        scratch=[pltpu.VMEM((rows, features), BF16)] * 2 + [pltpu.SemaphoreType.DMA((2 * heads,))],
    )
    return (
        query_grad[None],
        key_grad[None],
        value_grad[None],
        gate_grad[None],
        bias_grad,
        gain_grad.reshape(features),
    )


def solution(mesh):
    in_specs = (
        P(("groups", "dp"), "ctx", None),
        P(("groups", "dp"), "ctx", None),
        P(("groups", "dp"), "ctx", None),
        P(("groups", "dp"), "ctx", None),
        P(("groups", "dp"), "ctx", None),
        P(("groups", "dp"), None),
        P(),
        P(),
    )
    out_specs = (
        P(("groups", "dp"), "ctx", None),
        P(("groups", "dp"), "ctx", None),
        P(("groups", "dp"), "ctx", None),
        P(("groups", "dp"), "ctx", None),
        P("groups", None),
        P("groups"),
    )
    return jax.shard_map(local, mesh=mesh, in_specs=in_specs, out_specs=out_specs, check_vma=False)
```

```python
from functools import partial

import jax
import jax.numpy as jnp
from jax import lax
from jax.experimental import pallas as pl
from jax.experimental.pallas import tpu as pltpu
from jax.sharding import PartitionSpec as P

EPSILON = 1e-05
VMEM_LIMIT = 24 * 1024 * 1024
F32 = jnp.float32
BF16 = jnp.bfloat16


def passed_along(array, axis, by, hop=1):
    size = lax.axis_size(axis)
    first, last = (hop - 1, size - 2) if by > 0 else (1, size - hop)
    return lax.ppermute(array, axis, [(i, i + by) for i in range(first, last + 1)])


def contract(left, right, left_dim, right_dim):
    return lax.dot_general(
        left, right, (((left_dim,), (right_dim,)), ((), ())), preferred_element_type=F32
    )


def user_starts(lengths, query_pos):
    end = jnp.int32(0)
    start = jnp.zeros(query_pos.shape, jnp.int32)
    for user in range(lengths.shape[1]):
        end = end + lengths[0, user]
        start = jnp.where(query_pos >= end, end, start)
    return start


class Pair:
    def __init__(self, mask, table, heads, hops, flipped=False, near=None):
        rows = table.shape[1]
        self.table, self.heads, self.levels = table, heads, table.shape[0] // heads
        self.mask, self.hops, self.near = mask[...], hops, near
        self.far = (hops - 1) * rows + 1 >= 2 ** (self.levels - 2)
        if not self.far:
            query_dim, key_dim = (1, 0) if flipped else (0, 1)
            query_row = lax.broadcasted_iota(jnp.int32, mask.shape, query_dim)
            key_row = lax.broadcasted_iota(jnp.int32, mask.shape, key_dim)
            self.distance = query_row - key_row + hops * rows

    def half_bias(self, head):
        def level_row(level):
            at = level * self.heads + head
            return self.table[at : at + 1, : self.mask.shape[1]]

        value = level_row(self.levels - 1)
        if self.far:
            return value
        if self.near is not None:
            rows = self.mask.shape[0]
            close = self.near[head * rows : (head + 1) * rows, :]
            return close if self.hops == 0 else jnp.where(self.distance < rows, close, value)
        for level in range(self.levels - 2, -1, -1):
            value = jnp.where(self.distance < 2**level, level_row(level), value)
        return value

    def half_logits(self, scores, head, scaling):
        return scores * (0.5 * scaling) + self.half_bias(head)


def slope_of(half, tanh):
    return (0.5 + 0.5 * tanh) * (1.0 + half * (1.0 - tanh))


def columns(head, width):
    return slice(head * width, (head + 1) * width)


def in_stages(count, first, second, ahead=3):
    held = [first(i) for i in range(min(ahead, count))]
    for i in range(count):
        if i + ahead < count:
            held.append(first(i + ahead))
        second(i, held.pop(0))


def attend(pairs, heads, scaling, query, keys, values, total, out):
    width = query.shape[1] // heads

    def scores(head):
        cols = columns(head, width)
        return [contract(query[:, cols], key[:, cols], 1, 1) for key in keys]

    def weigh(head, found):
        cols = columns(head, width)
        part = None if total is None else total[:, cols]
        for pair, score, value in zip(pairs, found, values):
            half = pair.half_logits(score, head, scaling)
            weights = ((half + half * jnp.tanh(half)) * pair.mask).astype(BF16)
            added = contract(weights, value[:, cols], 1, 0)
            part = added if part is None else part + added
        out[:, cols] = part.astype(out.dtype)

    in_stages(heads, scores, weigh)


def far_start(lengths, block, reach, rows):
    first = (lax.axis_index("ctx") + block) * rows
    end, start = jnp.int32(0), jnp.int32(0)
    for user in range(lengths.shape[1]):
        end = end + lengths[0, user]
        start = jnp.where(first >= end, end, start)
    return start - (first - reach * rows)


def first_kernel(plan, cut, heads, scaling, lengths, bias, *refs):
    inputs, refs = refs[:6], refs[6:]
    table, near, masks, refs = refs[0], refs[1], refs[2 : 2 + len(plan)], refs[2 + len(plan) :]
    late, refs = refs[0], refs[1:]
    held, out, arrived = refs[:6], refs[6], refs[7]
    copies = [
        pltpu.make_async_copy(source, target, arrived.at[at])
        for at, (source, target) in enumerate(zip(inputs, held))
    ]
    for copy in copies:
        copy.start()
    levels = bias.shape[0]
    for level in range(levels):
        for head in range(heads):
            at = level * heads + head
            table[at : at + 1, :] = jnp.full((1, table.shape[1]), 0.5 * bias[level, head], F32)
    rows = masks[0].shape[0]
    apart = lax.broadcasted_iota(jnp.int32, (rows, rows), 0)
    apart = (apart - lax.broadcasted_iota(jnp.int32, (rows, rows), 1)) & (rows - 1)
    for head in range(heads):
        value = table[(levels - 1) * heads + head : (levels - 1) * heads + head + 1, :]
        for level in range(levels - 2, -1, -1):
            at = level * heads + head
            value = jnp.where(apart < 2**level, table[at : at + 1, :], value)
        near[head * rows : (head + 1) * rows, :] = value
    for (block, hops, flipped), mask in zip(plan, masks):
        query_dim, key_dim = (1, 0) if flipped else (0, 1)
        line = (1, mask.shape[1]) if flipped else (mask.shape[0], 1)
        first = (lax.axis_index("ctx") + block) * rows
        query_pos = first + lax.broadcasted_iota(jnp.int32, line, query_dim)
        key_first = first - hops * rows + rows - mask.shape[key_dim]
        key_pos = key_first + lax.broadcasted_iota(jnp.int32, mask.shape, key_dim)
        seen = (key_pos >= user_starts(lengths, query_pos)) & (key_pos <= query_pos)
        value = jnp.where(seen, 1.0, 0.0).astype(F32)
        if mask.shape == (rows, rows):
            mask[...] = value
            continue
        at = 0 if mask.shape[0] == rows else 1
        is_late = jnp.where(far_start(lengths, block, hops, rows) > cut, 1.0, 0.0).astype(F32)
        late[8 * at : 8 * at + 8, :] = jnp.full((8, rows), is_late, F32)
        mask[...] = value * (is_late if at else 1.0 - is_late)
    for copy in copies:
        copy.wait()
    query, key, value = held[:3]
    pair = Pair(masks[0], table, heads, 0, near=near)
    attend([pair], heads, scaling, query, [key], [value], None, out)


def forward_kernel(hops, heads, scaling, table, near, mask, query, key, value, total, out):
    pair = Pair(mask, table, heads, hops, near=near)
    attend([pair], heads, scaling, query, [key], [value], total, out)


def normed_rows(attention):
    center = attention - jnp.mean(attention, axis=1, keepdims=True)
    inverse = lax.rsqrt(jnp.mean(center * center, axis=1, keepdims=True) + EPSILON)
    return center * inverse, inverse


def weights_kernel(hops, heads, scaling, table, near, mask, query, key, weights):
    pair = Pair(mask, table, heads, hops, near=near)
    rows, width = query.shape[0], query.shape[1] // heads

    def scores(head):
        cols = columns(head, width)
        return contract(query[:, cols], key[:, cols], 1, 1)

    def weigh(head, found):
        half = pair.half_logits(found, head, scaling)
        lines = columns(head, rows)
        weights[lines, :] = ((half + half * jnp.tanh(half)) * pair.mask).astype(BF16)

    in_stages(heads, scores, weigh)


def norm_kernel(heads, *refs):
    weights, value, total, out_grad, update_gate, gain = refs[:6]
    attention, attn_grad, gain_grad = refs[6:]
    width = total.shape[1] // heads
    for head in range(heads):
        cols, lines = columns(head, width), columns(head, total.shape[0])
        attention[:, cols] = total[:, cols] + contract(weights[lines, :], value[:, cols], 1, 0)
    rows, features = attention.shape
    step = 16
    gain_row = gain[...]
    gain_sum = jnp.zeros((8, features), F32)
    for low in range(0, rows, step):
        span = slice(low, low + step)
        normed, inverse = normed_rows(attention[span, :])
        gated = out_grad[span, :].astype(F32) * update_gate[span, :].astype(F32)
        product = gated * normed
        for part in range(0, step, 8):
            gain_sum = gain_sum + product[part : part + 8, :]
        pushed = gated * gain_row
        attn_grad[span, :] = (
            inverse
            * (
                pushed
                - jnp.mean(pushed, axis=1, keepdims=True)
                - normed * jnp.mean(pushed * normed, axis=1, keepdims=True)
            )
        ).astype(BF16)
    gain_grad[...] = jnp.sum(gain_sum, axis=0, keepdims=True)


def backward_query_kernel(hop_list, heads, scaling, *refs):
    count = len(hop_list)
    table, near, masks, refs = refs[0], refs[1], refs[2 : 2 + count], refs[2 + count :]
    query, grad, keys, values = refs[0], refs[1], refs[2 : 2 + count], refs[2 + count : 2 + 2 * count]
    gain_in, query_out, small_out = refs[2 + 2 * count :]
    rows, width = query.shape[0], query.shape[1] // heads
    pairs = [Pair(mask, table, heads, hops, near=near) for mask, hops in zip(masks, hop_list)]
    lanes = small_out.shape[1]
    lines = gain_in.shape[1] // lanes
    levels = small_out.shape[0] - lines
    lane = lax.broadcasted_iota(jnp.int32, (levels, lanes), 1)
    level_row = lax.broadcasted_iota(jnp.int32, (levels, lanes), 0)
    group = lax.broadcasted_iota(jnp.int32, (8, rows), 0)
    distance = (group - lax.broadcasted_iota(jnp.int32, (8, rows), 1)) & (rows - 1)
    bucket = sum((distance >= 2**level).astype(jnp.int32) for level in range(levels - 1))
    own = pairs[0].distance >= 0
    bias_total = [jnp.zeros((levels, lanes), F32)]

    def bias_sums(grads):
        close = jnp.where(own, grads[0], grads[1])
        rest = sum(grads[2:], jnp.where(own, grads[1], 0.0))
        by_place, far = jnp.zeros((8, rows), F32), jnp.zeros((8, rows), F32)
        for low in range(0, rows, 8):
            part = close[low : low + 8, :]
            by_place = by_place + (pltpu.roll(part, rows - low, 1) if low else part)
            far = far + rest[low : low + 8, :]
        sums = jnp.where(level_row == levels - 1, jnp.sum(far, axis=0, keepdims=True), 0.0)
        for level in range(levels):
            row = jnp.sum(jnp.where(bucket == level, by_place, 0.0), axis=0, keepdims=True)
            sums = sums + jnp.where(level_row == level, row, 0.0)
        return sums

    def scores(head):
        cols = columns(head, width)
        query_h, grad_h = query[:, cols], grad[:, cols]
        return [
            (contract(query_h, key[:, cols], 1, 1), contract(grad_h, value[:, cols], 1, 1))
            for key, value in zip(keys, values)
        ]

    def differentiate(head, found):
        cols = columns(head, width)
        query_part, grads = None, []
        for pair, key, (score, weight_grad) in zip(pairs, keys, found):
            half = pair.half_logits(score, head, scaling)
            grads.append(weight_grad * (slope_of(half, jnp.tanh(half)) * pair.mask))
            added = contract(grads[-1].astype(BF16), key[:, cols], 1, 0)
            query_part = added if query_part is None else query_part + added
        query_out[:, cols] = (query_part * scaling).astype(BF16)
        sums = jnp.sum(bias_sums(grads), axis=1, keepdims=True)
        bias_total[0] = jnp.where(lane == head, sums, bias_total[0])

    in_stages(heads, scores, differentiate, 1)
    for line in range(lines):
        small_out[line : line + 1, :] = gain_in[:, line * lanes : (line + 1) * lanes]
    small_out[lines:, :] = bias_total[0]


def add_key_grads(hops, heads, scaling, table, mask, query, grad, key, value, sums, store):
    width = query.shape[1] // heads
    pair = Pair(mask, table, heads, hops, True)

    def scores(head):
        cols = columns(head, width)
        score = contract(key[:, cols], query[:, cols], 1, 1)
        return score, contract(value[:, cols], grad[:, cols], 1, 1)

    def differentiate(head, found):
        cols = columns(head, width)
        half = pair.half_logits(found[0], head, scaling)
        tanh = jnp.tanh(half)
        rounded = (found[1] * (slope_of(half, tanh) * pair.mask)).astype(BF16)
        weights = ((half + half * tanh) * pair.mask).astype(BF16)
        parts = [contract(rounded, query[:, cols], 1, 0), contract(weights, grad[:, cols], 1, 0)]
        store(head, cols, *[part + held[:, cols] for part, held in zip(parts, sums)] or parts)

    in_stages(heads, scores, differentiate)


def into(key_out, value_out):
    def store(head, cols, key_part, value_part):
        key_out[:, cols] = key_part
        value_out[:, cols] = value_part

    return store


def next_key_kernel(hops, heads, scaling, *refs):
    add_key_grads(hops, heads, scaling, *refs[:6], refs[6:-2], into(*refs[-2:]))


def gate_and_key_kernel(hops, heads, scaling, *refs):
    attention, out_grad, gain, query_grad = refs[8:12]
    gate_out, query_out, key_out, value_out, held, written = refs[12:]
    rows, step = attention.shape[0], 16
    part = rows // 4
    copies = []

    def write(source, target, low):
        lines = slice(low, low + part)
        copies.append(
            pltpu.make_async_copy(source.at[lines], target.at[lines], written.at[len(copies)])
        )
        copies[-1].start()

    for low in range(0, rows, part):
        write(query_grad, query_out, low)
    gain_row = gain[...]
    for low in range(0, rows, step):
        span = slice(low, low + step)
        normed, _ = normed_rows(attention[span, :])
        held[span, :] = (out_grad[span, :].astype(F32) * normed * gain_row).astype(BF16)
        if (low + step) % part == 0:
            write(held, gate_out, low + step - part)
    add_key_grads(hops, heads, scaling, *refs[:6], refs[6:8], into(key_out, value_out))
    for copy in copies:
        copy.wait()


def message_kernel(heads, *refs):
    weights, slopes, late, query, grad, value, out = refs
    cut, width = out.shape[0], query.shape[1] // heads
    tail = query.shape[0] - cut
    is_late = late[8:9, :width] > 0.5

    def scores(head):
        cols = columns(head, width)
        return contract(value[cut:, cols], grad[:, cols], 1, 1)

    def choose(head, found):
        cols, lines = columns(head, width), columns(head, tail)
        rounded = (found * slopes[lines, :]).astype(BF16)
        parts = [
            contract(rounded, query[:, cols], 1, 0),
            contract(weights[lines, :], grad[:, cols], 1, 0),
        ]
        for at, part in enumerate(parts):
            lines = slice(at * tail, (at + 1) * tail)
            out[lines, cols] = jnp.where(is_late, part, grad[lines, cols].astype(F32)).astype(BF16)
        out[2 * tail :, cols] = grad[2 * tail : cut, cols]

    in_stages(heads, scores, choose)


def slopes_kernel(hops, heads, scaling, table, mask, query, key, weights, slopes):
    pair = Pair(mask, table, heads, hops, True)
    rows, cut, width = mask.shape[0], mask.shape[1], query.shape[1] // heads
    first = key.shape[0] - rows

    def scores(head):
        cols = columns(head, width)
        return contract(key[first:, cols], query[:cut, cols], 1, 1)

    def derive(head, found):
        half = pair.half_logits(found, head, scaling)
        tanh = jnp.tanh(half)
        lines = columns(head, rows)
        weights[lines, :] = ((half + half * tanh) * pair.mask).astype(BF16)
        slopes[lines, :] = slope_of(half, tanh) * pair.mask

    in_stages(heads, scores, derive)


def last_kernel(heads, scaling, *refs):
    weights, slopes, late, query, message, value, key_in, value_in = refs[:8]
    outs, held, written = refs[8:10], refs[10:12], refs[12]
    rows, cut, width = query.shape[0], message.shape[0], query.shape[1] // heads
    tail = rows - cut
    is_late = late[0:1, :width]
    copies = []

    def write(at, cols):
        source, target = held[at].at[:, cols], outs[at].at[:, cols]
        copies.append(pltpu.make_async_copy(source, target, written.at[len(copies)]))
        copies[-1].start()

    def scores(head):
        cols = columns(head, width)
        return contract(value[:, cols], message[:, cols], 1, 1)

    def differentiate(head, found):
        cols, lines = columns(head, width), columns(head, rows)
        rounded = (found * slopes[lines, :]).astype(BF16)
        parts = [
            contract(rounded, query[:cut, cols], 1, 0),
            contract(weights[lines, :], message[:, cols], 1, 0),
        ]
        for at, (part, before) in enumerate(zip(parts, (key_in, value_in))):
            factor = 1.0 if at else scaling
            held[at][:cut, cols] = ((before[:cut, cols] + part[:cut]) * factor).astype(BF16)
            sent = message[at * tail : (at + 1) * tail, cols].astype(F32) * is_late
            held[at][cut:, cols] = ((before[cut:, cols] + part[cut:] + sent) * factor).astype(BF16)
        for at in (0, 1):
            write(at, cols)

    in_stages(heads, scores, differentiate)
    for copy in copies:
        copy.wait()


def sum_kernel(*refs):
    gain_out, bias_out = refs[-2:]
    total = added_up([piece[...] for piece in refs[:-2]])
    lines = gain_out.shape[0]
    gain_out[...] = total[:lines]
    bias_out[...] = total[lines:, : bias_out.shape[1]]


def on_device(kernel, outs, args, smem=(), ahead=(), far=(), far_outs=0, scratch=()):
    count = len(smem) + len(far) + len(args)
    far = [pltpu.with_memory_space_constraint(array, pltpu.HBM) for array in far]

    def body(*refs):
        kernel(*refs[:count], *refs[count + len(ahead) :])

    vmem, anywhere = pl.BlockSpec(memory_space=pltpu.VMEM), pl.BlockSpec(memory_space=pl.ANY)
    return pl.pallas_call(
        body,
        out_shape=outs,
        in_specs=[pl.BlockSpec(memory_space=pltpu.SMEM)] * len(smem)
        + [pl.BlockSpec(memory_space=pltpu.HBM)] * len(far)
        + [vmem] * len(args)
        + [anywhere] * len(ahead),
        out_specs=[anywhere] * far_outs + [vmem] * (len(outs) - far_outs),
        scratch_shapes=scratch,
        compiler_params=pltpu.CompilerParams(vmem_limit_bytes=VMEM_LIMIT),
        cost_estimate=pl.CostEstimate(flops=1000000, bytes_accessed=100000, transcendentals=0),
    )(*smem, *far, *args, *ahead)


def rounds_of(axes):
    rounds = []
    for axis in axes:
        size = lax.axis_size(axis)
        step = 1
        while step < size:
            radix = 4 if size // step >= 4 else 2
            rounds.append((axis, [step * at for at in range(1, radix)]))
            step = radix * step
    return rounds


def exchanged(array, axis, distances):
    size = lax.axis_size(axis)
    found = [
        lax.ppermute(array, axis, [(i, i ^ distance) for i in range(size)])
        for distance in reversed(distances)
    ]
    return [array] + found[::-1]


def added_up(pieces):
    while len(pieces) > 1:
        pieces = [left + right for left, right in zip(pieces[::2], pieces[1::2])]
    return pieces[0]


def local(queries, key_rows, value_rows, update_gate, out_grad, user_lengths, rel_bias, norm_gain):
    rows, features = queries.shape[1:]
    levels, heads = rel_bias.shape
    scaling = (features // heads) ** (-0.5)
    reach = min(3, lax.axis_size("ctx") // 2)
    wide = jax.ShapeDtypeStruct((rows, features), F32)
    narrow = jax.ShapeDtypeStruct((rows, features), BF16)
    inputs = (queries[0], key_rows[0], value_rows[0], update_gate[0], out_grad[0], norm_gain[None])

    arrived = [passed_along(inputs[at], "ctx", by) for at, by in ((1, 1), (2, 1), (0, -1))]

    hop_list = tuple(range(reach + 1))
    plan = [(0, hops, False) for hops in hop_list] + [(hops, hops, True) for hops in hop_list]
    plan += [(reach - 1, reach, True)]
    cut = rows - rows // 4
    shapes = [(rows, rows)] * (len(plan) - 2) + [(rows, cut), (rows - cut, rows), (16, rows)]
    outs = [jax.ShapeDtypeStruct((count * heads, rows), F32) for count in (levels, rows)]
    outs += [jax.ShapeDtypeStruct(shape, F32) for shape in shapes]
    outs += [jax.ShapeDtypeStruct(array.shape, array.dtype) for array in inputs] + [wide]
    table, near, *found = on_device(
        partial(first_kernel, plan, cut, heads, scaling),
        outs,
        (),
        (user_lengths, rel_bias),
        far=inputs,
        scratch=[pltpu.SemaphoreType.DMA((len(inputs),))],
    )
    masks, flipped = found[: reach + 1], found[reach + 1 : 2 * reach + 2]
    sender_mask, late, query, key, value, gate, grad, gain, attention = found[2 * reach + 2 :]

    later_queries = [query, arrived[2]]
    keys, values = [key, arrived[0]], [value, arrived[1]]
    for hops in range(1, reach):
        keys.append(passed_along(keys[-1], "ctx", 1, hops + 1))
        values.append(passed_along(values[-1], "ctx", 1, hops + 1))
        later_queries.append(passed_along(later_queries[-1], "ctx", -1, hops + 1))
    for hops in range(1, reach):
        (attention,) = on_device(
            partial(forward_kernel, hops, heads, scaling),
            [wide],
            (table, near, masks[hops], query, keys[hops], values[hops], attention),
            ahead=later_queries[hops : hops + 1],
        )
    stacked = (heads * rows, rows)
    (far_weights,) = on_device(
        partial(weights_kernel, reach, heads, scaling),
        [jax.ShapeDtypeStruct(stacked, BF16)],
        (table, near, masks[-1], query, keys[-1]),
        ahead=[attention],
    )
    attention, attn_grad, gain_part = on_device(
        partial(norm_kernel, heads),
        [wide, narrow, jax.ShapeDtypeStruct((1, features), F32)],
        (far_weights, values[-1], attention, grad, gate, gain),
    )

    lanes = features // 8
    query_grad, sums = on_device(
        partial(backward_query_kernel, hop_list, heads, scaling),
        [narrow, jax.ShapeDtypeStruct((8 + levels, lanes), F32)],
        (table, near, *masks, query, attn_grad, *keys, *values, gain_part),
        ahead=later_queries[reach:],
    )
    later_grads = [attn_grad, passed_along(attn_grad, "ctx", -1)]
    pieces = [sums]
    for axis, distances in rounds_of(("dp",)):
        pieces = exchanged(added_up(pieces), axis, distances)

    def key_operands(hops):
        later = (later_queries[hops], later_grads[hops])
        return (table, flipped[hops], *later, key, value)

    key_grads = on_device(
        partial(next_key_kernel, 0, heads, scaling),
        [wide] * 2,
        key_operands(0),
    )
    sent_tables = on_device(
        partial(slopes_kernel, reach, heads, scaling),
        [jax.ShapeDtypeStruct((heads * (rows - cut), rows), kind) for kind in (BF16, F32)],
        (table, sender_mask, later_queries[reach - 1], keys[1]),
    )
    far_tables = on_device(
        partial(slopes_kernel, reach, heads, scaling),
        [jax.ShapeDtypeStruct((heads * rows, cut), kind) for kind in (BF16, F32)],
        (table, flipped[reach], later_queries[reach], key),
    )
    for hops in range(1, reach):
        arrived, *pieces = lax.optimization_barrier((later_grads[hops], *pieces))
        if hops + 1 == reach:
            (arrived,) = on_device(
                partial(message_kernel, heads),
                [jax.ShapeDtypeStruct((cut, features), BF16)],
                (*sent_tables, late, later_queries[hops], arrived, values[1]),
                ahead=[key_grads[0], far_tables[0]],
            )
        later_grads.append(passed_along(arrived, "ctx", -1, hops + 1))
        if hops == 1:
            gate_grad, query_grad, *key_grads = on_device(
                partial(gate_and_key_kernel, hops, heads, scaling),
                [narrow, narrow, wide, wide],
                (*key_operands(hops), *key_grads, attention, grad, gain, query_grad),
                far_outs=2,
                scratch=[pltpu.VMEM((rows, features), BF16), pltpu.SemaphoreType.DMA((8,))],
            )
        else:
            key_grads = on_device(
                partial(next_key_kernel, hops, heads, scaling),
                [wide] * 2,
                (*key_operands(hops), *key_grads),
            )
    for axis, distances in rounds_of(("ctx",)):
        pieces = exchanged(added_up(pieces), axis, distances)
    key_grad, value_grad = on_device(
        partial(last_kernel, heads, scaling),
        [narrow, narrow],
        (*far_tables, late, later_queries[reach], later_grads[reach], value, *key_grads),
        far_outs=2,
        scratch=[pltpu.VMEM((rows, features), BF16)] * 2 + [pltpu.SemaphoreType.DMA((2 * heads,))],
    )
    key_grad, value_grad, pieces[0] = lax.optimization_barrier((key_grad, value_grad, pieces[0]))
    gain_grad, bias_grad = on_device(
        sum_kernel,
        [jax.ShapeDtypeStruct((8, lanes), F32), jax.ShapeDtypeStruct((levels, heads), F32)],
        pieces,
    )
    return (
        query_grad[None],
        key_grad[None],
        value_grad[None],
        gate_grad[None],
        bias_grad,
        gain_grad.reshape(features),
    )


def solution(mesh):
    in_specs = (
        P(("groups", "dp"), "ctx", None),
        P(("groups", "dp"), "ctx", None),
        P(("groups", "dp"), "ctx", None),
        P(("groups", "dp"), "ctx", None),
        P(("groups", "dp"), "ctx", None),
        P(("groups", "dp"), None),
        P(),
        P(),
    )
    out_specs = (
        P(("groups", "dp"), "ctx", None),
        P(("groups", "dp"), "ctx", None),
        P(("groups", "dp"), "ctx", None),
        P(("groups", "dp"), "ctx", None),
        P("groups", None),
        P("groups"),
    )
    return jax.shard_map(local, mesh=mesh, in_specs=in_specs, out_specs=out_specs, check_vma=False)
```

```python
from functools import partial

import jax
import jax.numpy as jnp
from jax import lax
from jax.experimental import pallas as pl
from jax.experimental.pallas import tpu as pltpu
from jax.sharding import PartitionSpec as P

EPSILON = 1e-05
VMEM_LIMIT = 24 * 1024 * 1024
F32 = jnp.float32
BF16 = jnp.bfloat16


def passed_along(array, axis, by, hop=1):
    size = lax.axis_size(axis)
    first, last = (hop - 1, size - 2) if by > 0 else (1, size - hop)
    return lax.ppermute(array, axis, [(i, i + by) for i in range(first, last + 1)])


def contract(left, right, left_dim, right_dim):
    return lax.dot_general(
        left, right, (((left_dim,), (right_dim,)), ((), ())), preferred_element_type=F32
    )


def user_starts(lengths, query_pos):
    end = jnp.int32(0)
    start = jnp.zeros(query_pos.shape, jnp.int32)
    for user in range(lengths.shape[1]):
        end = end + lengths[0, user]
        start = jnp.where(query_pos >= end, end, start)
    return start


class Pair:
    def __init__(self, mask, table, heads, hops, flipped=False, near=None):
        rows = table.shape[1]
        self.table, self.heads, self.levels = table, heads, table.shape[0] // heads
        self.mask, self.hops, self.near = mask[...], hops, near
        self.far = (hops - 1) * rows + 1 >= 2 ** (self.levels - 2)
        if not self.far:
            query_dim, key_dim = (1, 0) if flipped else (0, 1)
            query_row = lax.broadcasted_iota(jnp.int32, mask.shape, query_dim)
            key_row = lax.broadcasted_iota(jnp.int32, mask.shape, key_dim)
            self.distance = query_row - key_row + hops * rows

    def half_bias(self, head):
        def level_row(level):
            at = level * self.heads + head
            return self.table[at : at + 1, : self.mask.shape[1]]

        value = level_row(self.levels - 1)
        if self.far:
            return value
        if self.near is not None:
            rows = self.mask.shape[0]
            close = self.near[head * rows : (head + 1) * rows, :]
            return close if self.hops == 0 else jnp.where(self.distance < rows, close, value)
        for level in range(self.levels - 2, -1, -1):
            value = jnp.where(self.distance < 2**level, level_row(level), value)
        return value

    def half_logits(self, scores, head, scaling):
        return scores * (0.5 * scaling) + self.half_bias(head)


def slope_of(half, tanh):
    return (0.5 + 0.5 * tanh) * (1.0 + half * (1.0 - tanh))


def columns(head, width):
    return slice(head * width, (head + 1) * width)


def in_stages(count, first, second, ahead=3):
    held = [first(i) for i in range(min(ahead, count))]
    for i in range(count):
        if i + ahead < count:
            held.append(first(i + ahead))
        second(i, held.pop(0))


def attend(pairs, heads, scaling, query, keys, values, total, out):
    width = query.shape[1] // heads

    def scores(head):
        cols = columns(head, width)
        return [contract(query[:, cols], key[:, cols], 1, 1) for key in keys]

    def weigh(head, found):
        cols = columns(head, width)
        part = None if total is None else total[:, cols]
        for pair, score, value in zip(pairs, found, values):
            half = pair.half_logits(score, head, scaling)
            weights = ((half + half * jnp.tanh(half)) * pair.mask).astype(BF16)
            added = contract(weights, value[:, cols], 1, 0)
            part = added if part is None else part + added
        out[:, cols] = part.astype(out.dtype)

    in_stages(heads, scores, weigh)


def far_start(lengths, block, reach, rows):
    first = (lax.axis_index("ctx") + block) * rows
    end, start = jnp.int32(0), jnp.int32(0)
    for user in range(lengths.shape[1]):
        end = end + lengths[0, user]
        start = jnp.where(first >= end, end, start)
    return start - (first - reach * rows)


def first_kernel(plan, cut, heads, scaling, lengths, bias, *refs):
    inputs, refs = refs[:6], refs[6:]
    table, near, masks, refs = refs[0], refs[1], refs[2 : 2 + len(plan)], refs[2 + len(plan) :]
    late, refs = refs[0], refs[1:]
    held, out, arrived = refs[:6], refs[6], refs[7]
    copies = [
        pltpu.make_async_copy(source, target, arrived.at[at])
        for at, (source, target) in enumerate(zip(inputs, held))
    ]
    for copy in copies:
        copy.start()
    levels = bias.shape[0]
    for level in range(levels):
        for head in range(heads):
            at = level * heads + head
            table[at : at + 1, :] = jnp.full((1, table.shape[1]), 0.5 * bias[level, head], F32)
    rows = masks[0].shape[0]
    apart = lax.broadcasted_iota(jnp.int32, (rows, rows), 0)
    apart = (apart - lax.broadcasted_iota(jnp.int32, (rows, rows), 1)) & (rows - 1)
    for head in range(heads):
        value = table[(levels - 1) * heads + head : (levels - 1) * heads + head + 1, :]
        for level in range(levels - 2, -1, -1):
            at = level * heads + head
            value = jnp.where(apart < 2**level, table[at : at + 1, :], value)
        near[head * rows : (head + 1) * rows, :] = value
    for (block, hops, flipped), mask in zip(plan, masks):
        query_dim, key_dim = (1, 0) if flipped else (0, 1)
        line = (1, mask.shape[1]) if flipped else (mask.shape[0], 1)
        first = (lax.axis_index("ctx") + block) * rows
        query_pos = first + lax.broadcasted_iota(jnp.int32, line, query_dim)
        key_first = first - hops * rows + rows - mask.shape[key_dim]
        key_pos = key_first + lax.broadcasted_iota(jnp.int32, mask.shape, key_dim)
        seen = (key_pos >= user_starts(lengths, query_pos)) & (key_pos <= query_pos)
        value = jnp.where(seen, 1.0, 0.0).astype(F32)
        if mask.shape == (rows, rows):
            mask[...] = value
            continue
        at = 0 if mask.shape[0] == rows else 1
        is_late = jnp.where(far_start(lengths, block, hops, rows) > cut, 1.0, 0.0).astype(F32)
        late[8 * at : 8 * at + 8, :] = jnp.full((8, rows), is_late, F32)
        mask[...] = value * (is_late if at else 1.0 - is_late)
    for copy in copies:
        copy.wait()
    query, key, value = held[:3]
    pair = Pair(masks[0], table, heads, 0, near=near)
    attend([pair], heads, scaling, query, [key], [value], None, out)


def forward_kernel(hops, heads, scaling, table, near, mask, query, key, value, total, out):
    pair = Pair(mask, table, heads, hops, near=near)
    attend([pair], heads, scaling, query, [key], [value], total, out)


def normed_rows(attention):
    center = attention - jnp.mean(attention, axis=1, keepdims=True)
    inverse = lax.rsqrt(jnp.mean(center * center, axis=1, keepdims=True) + EPSILON)
    return center * inverse, inverse


def weights_kernel(hops, heads, scaling, table, near, mask, query, key, weights):
    pair = Pair(mask, table, heads, hops, near=near)
    rows, width = query.shape[0], query.shape[1] // heads

    def scores(head):
        cols = columns(head, width)
        return contract(query[:, cols], key[:, cols], 1, 1)

    def weigh(head, found):
        half = pair.half_logits(found, head, scaling)
        lines = columns(head, rows)
        weights[lines, :] = ((half + half * jnp.tanh(half)) * pair.mask).astype(BF16)

    in_stages(heads, scores, weigh)


def norm_kernel(heads, *refs):
    weights, value, total, out_grad, update_gate, gain = refs[:6]
    attention, attn_grad, gain_grad = refs[6:]
    width = total.shape[1] // heads
    for head in range(heads):
        cols, lines = columns(head, width), columns(head, total.shape[0])
        attention[:, cols] = total[:, cols] + contract(weights[lines, :], value[:, cols], 1, 0)
    rows, features = attention.shape
    step = 16
    gain_row = gain[...]
    gain_sum = jnp.zeros((8, features), F32)
    for low in range(0, rows, step):
        span = slice(low, low + step)
        normed, inverse = normed_rows(attention[span, :])
        gated = out_grad[span, :].astype(F32) * update_gate[span, :].astype(F32)
        product = gated * normed
        for part in range(0, step, 8):
            gain_sum = gain_sum + product[part : part + 8, :]
        pushed = gated * gain_row
        attn_grad[span, :] = (
            inverse
            * (
                pushed
                - jnp.mean(pushed, axis=1, keepdims=True)
                - normed * jnp.mean(pushed * normed, axis=1, keepdims=True)
            )
        ).astype(BF16)
    gain_grad[...] = jnp.sum(gain_sum, axis=0, keepdims=True)


def backward_query_kernel(hop_list, heads, scaling, *refs):
    count = len(hop_list)
    table, near, masks, refs = refs[0], refs[1], refs[2 : 2 + count], refs[2 + count :]
    query, grad, keys, values = refs[0], refs[1], refs[2 : 2 + count], refs[2 + count : 2 + 2 * count]
    gain_in, query_out, small_out = refs[2 + 2 * count :]
    rows, width = query.shape[0], query.shape[1] // heads
    pairs = [Pair(mask, table, heads, hops, near=near) for mask, hops in zip(masks, hop_list)]
    lanes = small_out.shape[1]
    lines = gain_in.shape[1] // lanes
    levels = small_out.shape[0] - lines
    lane = lax.broadcasted_iota(jnp.int32, (levels, lanes), 1)
    level_row = lax.broadcasted_iota(jnp.int32, (levels, lanes), 0)
    group = lax.broadcasted_iota(jnp.int32, (8, rows), 0)
    distance = (group - lax.broadcasted_iota(jnp.int32, (8, rows), 1)) & (rows - 1)
    bucket = sum((distance >= 2**level).astype(jnp.int32) for level in range(levels - 1))
    own = pairs[0].distance >= 0
    bias_total = [jnp.zeros((levels, lanes), F32)]

    def bias_sums(grads):
        close = jnp.where(own, grads[0], grads[1])
        rest = sum(grads[2:], jnp.where(own, grads[1], 0.0))
        by_place, far = jnp.zeros((8, rows), F32), jnp.zeros((8, rows), F32)
        for low in range(0, rows, 8):
            part = close[low : low + 8, :]
            by_place = by_place + (pltpu.roll(part, rows - low, 1) if low else part)
            far = far + rest[low : low + 8, :]
        sums = jnp.where(level_row == levels - 1, jnp.sum(far, axis=0, keepdims=True), 0.0)
        for level in range(levels):
            row = jnp.sum(jnp.where(bucket == level, by_place, 0.0), axis=0, keepdims=True)
            sums = sums + jnp.where(level_row == level, row, 0.0)
        return sums

    def scores(head):
        cols = columns(head, width)
        query_h, grad_h = query[:, cols], grad[:, cols]
        return [
            (contract(query_h, key[:, cols], 1, 1), contract(grad_h, value[:, cols], 1, 1))
            for key, value in zip(keys, values)
        ]

    def differentiate(head, found):
        cols = columns(head, width)
        query_part, grads = None, []
        for pair, key, (score, weight_grad) in zip(pairs, keys, found):
            half = pair.half_logits(score, head, scaling)
            grads.append(weight_grad * (slope_of(half, jnp.tanh(half)) * pair.mask))
            added = contract(grads[-1].astype(BF16), key[:, cols], 1, 0)
            query_part = added if query_part is None else query_part + added
        query_out[:, cols] = (query_part * scaling).astype(BF16)
        sums = jnp.sum(bias_sums(grads), axis=1, keepdims=True)
        bias_total[0] = jnp.where(lane == head, sums, bias_total[0])

    in_stages(heads, scores, differentiate, 1)
    for line in range(lines):
        small_out[line : line + 1, :] = gain_in[:, line * lanes : (line + 1) * lanes]
    small_out[lines:, :] = bias_total[0]


def add_key_grads(hops, heads, scaling, table, mask, query, grad, key, value, sums, store):
    width = query.shape[1] // heads
    pair = Pair(mask, table, heads, hops, True)

    def scores(head):
        cols = columns(head, width)
        score = contract(key[:, cols], query[:, cols], 1, 1)
        return score, contract(value[:, cols], grad[:, cols], 1, 1)

    def differentiate(head, found):
        cols = columns(head, width)
        half = pair.half_logits(found[0], head, scaling)
        tanh = jnp.tanh(half)
        rounded = (found[1] * (slope_of(half, tanh) * pair.mask)).astype(BF16)
        weights = ((half + half * tanh) * pair.mask).astype(BF16)
        parts = [contract(rounded, query[:, cols], 1, 0), contract(weights, grad[:, cols], 1, 0)]
        store(head, cols, *[part + held[:, cols] for part, held in zip(parts, sums)] or parts)

    in_stages(heads, scores, differentiate)


def into(key_out, value_out):
    def store(head, cols, key_part, value_part):
        key_out[:, cols] = key_part
        value_out[:, cols] = value_part

    return store


def next_key_kernel(hops, heads, scaling, *refs):
    add_key_grads(hops, heads, scaling, *refs[:6], refs[6:-2], into(*refs[-2:]))


def gate_and_key_kernel(hops, heads, scaling, *refs):
    attention, out_grad, gain, query_grad = refs[6:10]
    gate_out, query_out, key_out, value_out, held, written = refs[10:]
    rows, step = attention.shape[0], 16
    part = rows // 4
    copies = []

    def write(source, target, low):
        lines = slice(low, low + part)
        copies.append(
            pltpu.make_async_copy(source.at[lines], target.at[lines], written.at[len(copies)])
        )
        copies[-1].start()

    for low in range(0, rows, part):
        write(query_grad, query_out, low)
    gain_row = gain[...]
    for low in range(0, rows, step):
        span = slice(low, low + step)
        normed, _ = normed_rows(attention[span, :])
        held[span, :] = (out_grad[span, :].astype(F32) * normed * gain_row).astype(BF16)
        if (low + step) % part == 0:
            write(held, gate_out, low + step - part)
    add_key_grads(hops, heads, scaling, *refs[:6], (), into(key_out, value_out))
    for copy in copies:
        copy.wait()


def message_kernel(heads, *refs):
    weights, slopes, late, query, grad, value, out = refs
    cut, width = out.shape[0], query.shape[1] // heads
    tail = query.shape[0] - cut
    is_late = late[8:9, :width] > 0.5

    def scores(head):
        cols = columns(head, width)
        return contract(value[cut:, cols], grad[:, cols], 1, 1)

    def choose(head, found):
        cols, lines = columns(head, width), columns(head, tail)
        rounded = (found * slopes[lines, :]).astype(BF16)
        parts = [
            contract(rounded, query[:, cols], 1, 0),
            contract(weights[lines, :], grad[:, cols], 1, 0),
        ]
        for at, part in enumerate(parts):
            lines = slice(at * tail, (at + 1) * tail)
            out[lines, cols] = jnp.where(is_late, part, grad[lines, cols].astype(F32)).astype(BF16)
        out[2 * tail :, cols] = grad[2 * tail : cut, cols]

    in_stages(heads, scores, choose)


def slopes_kernel(hops, heads, scaling, table, mask, query, key, weights, slopes):
    pair = Pair(mask, table, heads, hops, True)
    rows, cut, width = mask.shape[0], mask.shape[1], query.shape[1] // heads
    first = key.shape[0] - rows

    def scores(head):
        cols = columns(head, width)
        return contract(key[first:, cols], query[:cut, cols], 1, 1)

    def derive(head, found):
        half = pair.half_logits(found, head, scaling)
        tanh = jnp.tanh(half)
        lines = columns(head, rows)
        weights[lines, :] = ((half + half * tanh) * pair.mask).astype(BF16)
        slopes[lines, :] = slope_of(half, tanh) * pair.mask

    in_stages(heads, scores, derive)


def last_kernel(heads, scaling, *refs):
    weights, slopes, late, query, message, value, key_in, value_in = refs[:8]
    outs, held, written = refs[8:10], refs[10:12], refs[12]
    rows, cut, width = query.shape[0], message.shape[0], query.shape[1] // heads
    tail = rows - cut
    is_late = late[0:1, :width]
    copies = []

    def write(at, cols):
        source, target = held[at].at[:, cols], outs[at].at[:, cols]
        copies.append(pltpu.make_async_copy(source, target, written.at[len(copies)]))
        copies[-1].start()

    def scores(head):
        cols = columns(head, width)
        return contract(value[:, cols], message[:, cols], 1, 1)

    def differentiate(head, found):
        cols, lines = columns(head, width), columns(head, rows)
        rounded = (found * slopes[lines, :]).astype(BF16)
        parts = [
            contract(rounded, query[:cut, cols], 1, 0),
            contract(weights[lines, :], message[:, cols], 1, 0),
        ]
        for at, (part, before) in enumerate(zip(parts, (key_in, value_in))):
            factor = 1.0 if at else scaling
            held[at][:cut, cols] = ((before[:cut, cols] + part[:cut]) * factor).astype(BF16)
            sent = message[at * tail : (at + 1) * tail, cols].astype(F32) * is_late
            held[at][cut:, cols] = ((before[cut:, cols] + part[cut:] + sent) * factor).astype(BF16)
        for at in (0, 1):
            write(at, cols)

    in_stages(heads, scores, differentiate)
    for copy in copies:
        copy.wait()


def sum_kernel(*refs):
    gain_out, bias_out = refs[-2:]
    total = added_up([piece[...] for piece in refs[:-2]])
    lines = gain_out.shape[0]
    gain_out[...] = total[:lines]
    bias_out[...] = total[lines:, : bias_out.shape[1]]


def on_device(kernel, outs, args, smem=(), ahead=(), far=(), far_outs=0, scratch=()):
    count = len(smem) + len(far) + len(args)
    far = [pltpu.with_memory_space_constraint(array, pltpu.HBM) for array in far]

    def body(*refs):
        kernel(*refs[:count], *refs[count + len(ahead) :])

    vmem, anywhere = pl.BlockSpec(memory_space=pltpu.VMEM), pl.BlockSpec(memory_space=pl.ANY)
    return pl.pallas_call(
        body,
        out_shape=outs,
        in_specs=[pl.BlockSpec(memory_space=pltpu.SMEM)] * len(smem)
        + [pl.BlockSpec(memory_space=pltpu.HBM)] * len(far)
        + [vmem] * len(args)
        + [anywhere] * len(ahead),
        out_specs=[anywhere] * far_outs + [vmem] * (len(outs) - far_outs),
        scratch_shapes=scratch,
        compiler_params=pltpu.CompilerParams(vmem_limit_bytes=VMEM_LIMIT),
        cost_estimate=pl.CostEstimate(flops=1000000, bytes_accessed=100000, transcendentals=0),
    )(*smem, *far, *args, *ahead)


def rounds_of(axes):
    rounds = []
    for axis in axes:
        size = lax.axis_size(axis)
        step = 1
        while step < size:
            radix = 4 if size // step >= 4 else 2
            rounds.append((axis, [step * at for at in range(1, radix)]))
            step = radix * step
    return rounds


def exchanged(array, axis, distances):
    size = lax.axis_size(axis)
    found = [
        lax.ppermute(array, axis, [(i, i ^ distance) for i in range(size)])
        for distance in reversed(distances)
    ]
    return [array] + found[::-1]


def added_up(pieces):
    while len(pieces) > 1:
        pieces = [left + right for left, right in zip(pieces[::2], pieces[1::2])]
    return pieces[0]


def local(queries, key_rows, value_rows, update_gate, out_grad, user_lengths, rel_bias, norm_gain):
    rows, features = queries.shape[1:]
    levels, heads = rel_bias.shape
    scaling = (features // heads) ** (-0.5)
    reach = min(3, lax.axis_size("ctx") // 2)
    wide = jax.ShapeDtypeStruct((rows, features), F32)
    narrow = jax.ShapeDtypeStruct((rows, features), BF16)
    inputs = (queries[0], key_rows[0], value_rows[0], update_gate[0], out_grad[0], norm_gain[None])

    arrived = [passed_along(inputs[at], "ctx", by) for at, by in ((1, 1), (2, 1), (0, -1))]

    hop_list = tuple(range(reach + 1))
    plan = [(0, hops, False) for hops in hop_list] + [(hops, hops, True) for hops in hop_list]
    plan += [(reach - 1, reach, True)]
    cut = rows - rows // 4
    shapes = [(rows, rows)] * (len(plan) - 2) + [(rows, cut), (rows - cut, rows), (16, rows)]
    outs = [jax.ShapeDtypeStruct((count * heads, rows), F32) for count in (levels, rows)]
    outs += [jax.ShapeDtypeStruct(shape, F32) for shape in shapes]
    outs += [jax.ShapeDtypeStruct(array.shape, array.dtype) for array in inputs] + [wide]
    table, near, *found = on_device(
        partial(first_kernel, plan, cut, heads, scaling),
        outs,
        (),
        (user_lengths, rel_bias),
        far=inputs,
        scratch=[pltpu.SemaphoreType.DMA((len(inputs),))],
    )
    masks, flipped = found[: reach + 1], found[reach + 1 : 2 * reach + 2]
    sender_mask, late, query, key, value, gate, grad, gain, attention = found[2 * reach + 2 :]

    later_queries = [query, arrived[2]]
    keys, values = [key, arrived[0]], [value, arrived[1]]
    for hops in range(1, reach):
        keys.append(passed_along(keys[-1], "ctx", 1, hops + 1))
        values.append(passed_along(values[-1], "ctx", 1, hops + 1))
        later_queries.append(passed_along(later_queries[-1], "ctx", -1, hops + 1))
    for hops in range(1, reach):
        (attention,) = on_device(
            partial(forward_kernel, hops, heads, scaling),
            [wide],
            (table, near, masks[hops], query, keys[hops], values[hops], attention),
            ahead=later_queries[hops : hops + 1],
        )
    stacked = (heads * rows, rows)
    (far_weights,) = on_device(
        partial(weights_kernel, reach, heads, scaling),
        [jax.ShapeDtypeStruct(stacked, BF16)],
        (table, near, masks[-1], query, keys[-1]),
        ahead=[attention],
    )
    attention, attn_grad, gain_part = on_device(
        partial(norm_kernel, heads),
        [wide, narrow, jax.ShapeDtypeStruct((1, features), F32)],
        (far_weights, values[-1], attention, grad, gate, gain),
    )

    lanes = features // 8
    query_grad, sums = on_device(
        partial(backward_query_kernel, hop_list, heads, scaling),
        [narrow, jax.ShapeDtypeStruct((8 + levels, lanes), F32)],
        (table, near, *masks, query, attn_grad, *keys, *values, gain_part),
        ahead=later_queries[reach:],
    )
    later_grads = [attn_grad, passed_along(attn_grad, "ctx", -1)]
    pieces = [sums]
    for axis, distances in rounds_of(("dp",)):
        pieces = exchanged(added_up(pieces), axis, distances)

    def key_operands(hops):
        later = (later_queries[hops], later_grads[hops])
        return (table, flipped[hops], *later, key, value)

    gate_grad, query_grad, *key_grads = on_device(
        partial(gate_and_key_kernel, 0, heads, scaling),
        [narrow, narrow, wide, wide],
        (*key_operands(0), attention, grad, gain, query_grad),
        far_outs=2,
        scratch=[pltpu.VMEM((rows, features), BF16), pltpu.SemaphoreType.DMA((8,))],
    )
    sent_tables = on_device(
        partial(slopes_kernel, reach, heads, scaling),
        [jax.ShapeDtypeStruct((heads * (rows - cut), rows), kind) for kind in (BF16, F32)],
        (table, sender_mask, later_queries[reach - 1], keys[1]),
    )
    far_tables = on_device(
        partial(slopes_kernel, reach, heads, scaling),
        [jax.ShapeDtypeStruct((heads * rows, cut), kind) for kind in (BF16, F32)],
        (table, flipped[reach], later_queries[reach], key),
    )
    for hops in range(1, reach):
        arrived, *pieces = lax.optimization_barrier((later_grads[hops], *pieces))
        if hops + 1 == reach:
            (arrived,) = on_device(
                partial(message_kernel, heads),
                [jax.ShapeDtypeStruct((cut, features), BF16)],
                (*sent_tables, late, later_queries[hops], arrived, values[1]),
                ahead=[key_grads[0], far_tables[0]],
            )
        later_grads.append(passed_along(arrived, "ctx", -1, hops + 1))
        key_grads = on_device(
            partial(next_key_kernel, hops, heads, scaling),
            [wide] * 2,
            (*key_operands(hops), *key_grads),
        )
    for axis, distances in rounds_of(("ctx",)):
        pieces = exchanged(added_up(pieces), axis, distances)
    key_grad, value_grad = on_device(
        partial(last_kernel, heads, scaling),
        [narrow, narrow],
        (*far_tables, late, later_queries[reach], later_grads[reach], value, *key_grads),
        far_outs=2,
        scratch=[pltpu.VMEM((rows, features), BF16)] * 2 + [pltpu.SemaphoreType.DMA((2 * heads,))],
    )
    key_grad, value_grad, pieces[0] = lax.optimization_barrier((key_grad, value_grad, pieces[0]))
    gain_grad, bias_grad = on_device(
        sum_kernel,
        [jax.ShapeDtypeStruct((8, lanes), F32), jax.ShapeDtypeStruct((levels, heads), F32)],
        pieces[::-1],
    )
    return (
        query_grad[None],
        key_grad[None],
        value_grad[None],
        gate_grad[None],
        bias_grad,
        gain_grad.reshape(features),
    )


def solution(mesh):
    in_specs = (
        P(("groups", "dp"), "ctx", None),
        P(("groups", "dp"), "ctx", None),
        P(("groups", "dp"), "ctx", None),
        P(("groups", "dp"), "ctx", None),
        P(("groups", "dp"), "ctx", None),
        P(("groups", "dp"), None),
        P(),
        P(),
    )
    out_specs = (
        P(("groups", "dp"), "ctx", None),
        P(("groups", "dp"), "ctx", None),
        P(("groups", "dp"), "ctx", None),
        P(("groups", "dp"), "ctx", None),
        P("groups", None),
        P("groups"),
    )
    return jax.shard_map(local, mesh=mesh, in_specs=in_specs, out_specs=out_specs, check_vma=False)
```
